32 devices in a mesh: seq: 32 (over z, y, x, core).
Axes of the slice: x: 2, y: 2, z: 4, core: 2. Of those that a mesh axis runs over, the one named last changes fastest.
Arguments:
- tokens: float32 [4096, 256], P('seq'), may hold values from -6 to 6
- resets: int32 [4096], P('seq'), may hold values from 0 to 1, as said below
- pad_mask: int32 [4096], P('seq'), may hold values 0 or 1
- norm_gain: float32 [1, 256], replicated, may hold values from 0.5 to 1.5
- w_in: float32 [1, 256, 1024], replicated, may hold values from -0.375 to 0.375
- conv_w: float32 [1, 4, 512], replicated, may hold values from -3 to 3
- conv_b: float32 [1, 512], replicated, may hold values from -3 to 3
- w_x: float32 [1, 512, 48], replicated, may hold values from -0.25 to 0.25
- w_dt: float32 [1, 16, 512], replicated, may hold values from -1.5 to 1.5
- dt_bias: float32 [1, 512], replicated, may hold values from -7 to -2.5
- a_log: float32 [1, 512, 16], replicated, may hold values from -10 to 1
- d_skip: float32 [1, 512], replicated, may hold values from 0.5 to 1.5
- w_out: float32 [1, 512, 256], replicated, may hold values from -0.25 to 0.25
- grad_out: float32 [4096, 256], P('seq'), may hold values from -6 to 6
Outputs:
- mixed: float32 [4096, 256], P('seq')
- grad_tokens: float32 [4096, 256], P('seq')
- grad_norm_gain: float32 [1, 256], replicated
- grad_w_in: float32 [1, 256, 1024], replicated
- grad_conv_w: float32 [1, 4, 512], replicated
- grad_conv_b: float32 [1, 512], replicated
- grad_w_x: float32 [1, 512, 48], replicated
- grad_w_dt: float32 [1, 16, 512], replicated
- grad_dt_bias: float32 [1, 512], replicated
- grad_a_log: float32 [1, 512, 16], replicated
- grad_d_skip: float32 [1, 512], replicated
- grad_w_out: float32 [1, 512, 256], replicated
The draws below stay inside these ranges and needn't reach their ends.
Inputs may be any that keep to these rules, and one draw needn't show every extreme that they name: `resets`: 1 marks the first token of a contig. One contig begins within the first 65 tokens and ends within the last 64 tokens, with no 1 inside it.
All inputs are finite; a program needn't handle non-finite values. No bound on the sum of `pad_mask` on one device may be relied on, other than what follows from the above.
Results may differ from the reference program's by a relative error of at most 0.0003.
Values sent between devices are 32-bit elements; how exact they have to be, the bound alone decides.
No kernel may reach another device: no remote copies, remote signals or barrier semaphores. Data moves between devices by JAX's collectives and lax.ppermute only.
A program may use at most 192 MiB of HBM per device.

```python
import math
import jax
import jax.numpy as jnp
from jax import lax

D = 256
INNER = 512
STATE = 16
RANK = 16
CONV = 4
LAYERS = 1
TOK_DEV = 128
TOKENS = 4096


def draw_resets(key, part):
    key = jax.random.fold_in(key, 11)
    first_key, last_key, sprinkle_key = jax.random.split(key, 3)
    begin_at = jax.random.randint(first_key, (), 1, TOK_DEV // 2 + 1)
    end_at = TOKENS - jax.random.randint(last_key, (), 1, TOK_DEV // 2 + 1)
    position = jnp.arange(TOKENS)
    sprinkle = jax.random.randint(sprinkle_key, (TOKENS,), 0, 16) == 0
    outside = (position < begin_at) | (position > end_at)
    flags = sprinkle & outside | (position == begin_at) | (position == end_at + 1)
    return flags.astype(jnp.int32)


def plant(result, stream_key, smallest, high):
    dims = result.shape
    index_at = [jax.random.randint(jax.random.fold_in(stream_key, axis), (), 0, dims[axis]) for axis in range(len(dims))]
    result = result.at[tuple(index_at)].set(smallest)
    longest = dims.index(max(dims))
    index_at[longest] = (index_at[longest] + 1) % dims[longest]
    return result.at[tuple(index_at)].set(high)


def level_of(rng, dims, cuts, least, largest):
    def one(axis_at, blocks):
        draws = jax.random.uniform(jax.random.fold_in(jax.random.fold_in(rng, 6), axis_at), (blocks,), jnp.float32, least / len(cuts), largest / len(cuts))
        return jnp.repeat(jnp.exp(draws), dims[axis_at] // blocks).reshape((-1,) + (1,) * (len(dims) - axis_at - 1))

    gain = one(*cuts[0])
    for cut in cuts[1:]:
        gain = gain * one(*cut)
    return gain


def gaussian(key, extent, deviation, most, pieces=(), kind=jnp.bfloat16):
    level = level_of(key, extent, pieces, -0.22, 0.18) if pieces else 1.0
    array = jax.random.normal(key, extent, jnp.float32) * deviation * level
    return jnp.minimum(jnp.maximum(array, -most), most).astype(kind)


def setup_inputs(seed: int = 0) -> dict:
    streams_of = jax.random.split(jax.random.key(seed), 15)
    tokens = gaussian(streams_of[0], (TOKENS, D), 1.0, 6.0, ((0, 32),), jnp.float32)
    resets = draw_resets(jax.random.fold_in(streams_of[14], 71), 0)
    pad_mask = plant((jax.random.randint(streams_of[2], (TOKENS,), 0, 16) < 15).astype(jnp.int32), jax.random.fold_in(streams_of[2], 1), 0, 1)
    norm_gain = jnp.clip(1.0 + 0.1 * jax.random.normal(streams_of[3], (LAYERS, D), jnp.float32), 0.5, 1.5)
    w_in = gaussian(streams_of[4], (LAYERS, D, 2 * INNER), D ** -0.5, 0.375, (), jnp.float32)
    conv_w = gaussian(streams_of[5], (LAYERS, CONV, INNER), CONV ** -0.5, 3.0, (), jnp.float32)
    conv_b = gaussian(streams_of[6], (LAYERS, INNER), 0.5, 3.0, (), jnp.float32)
    w_x = gaussian(streams_of[7], (LAYERS, INNER, RANK + 2 * STATE), INNER ** -0.5, 0.25, (), jnp.float32)
    w_dt = gaussian(streams_of[8], (LAYERS, RANK, INNER), RANK ** -0.5, 1.5, (), jnp.float32)
    dt_bias = jnp.clip(jax.random.uniform(streams_of[9], (LAYERS, INNER), jnp.float32, -7.0, -2.5), -7.0, -2.5)
    a_log = jnp.clip(jax.random.uniform(streams_of[10], (LAYERS, INNER, STATE), jnp.float32, -10.0, 1.0), -10.0, 1.0)
    d_skip = jnp.clip(jax.random.uniform(streams_of[11], (LAYERS, INNER), jnp.float32, 0.5, 1.5), 0.5, 1.5)
    w_out = gaussian(streams_of[12], (LAYERS, INNER, D), INNER ** -0.5, 0.25, (), jnp.float32)
    grad_out = gaussian(streams_of[13], (TOKENS, D), 1.0, 6.0, ((0, 32),), jnp.float32)
    return dict(tokens=tokens, resets=resets, pad_mask=pad_mask, norm_gain=norm_gain, w_in=w_in, conv_w=conv_w, conv_b=conv_b, w_x=w_x, w_dt=w_dt, dt_bias=dt_bias, a_log=a_log, d_skip=d_skip, w_out=w_out, grad_out=grad_out)


@jax.custom_vjp
def low(v):
    return lax.optimization_barrier(v.astype(jnp.bfloat16)).astype(jnp.float32)

@jax.custom_vjp
def low_back(v):
    return v

def low_keep(v):
    return (low(v), None)

def low_pass(kept, grad):
    return (grad,)

def back_keep(v):
    return (v, None)

def back_low(kept, grad):
    return (low(grad),)
low.defvjp(low_keep, low_pass)
low_back.defvjp(back_keep, back_low)
epsilon = 1e-05
precise = lax.Precision.HIGHEST

def matmul(left, right):
    return jnp.dot(left, right, precision=precise, preferred_element_type=jnp.float32)

def prepare(extended, cut_rows, conv_w, conv_b, w_x, w_dt, dt_bias):
    padded = jnp.concatenate([jnp.ones((3,), jnp.float32), cut_rows])
    valid_one = padded[3:]
    valid_two = valid_one * padded[2:-1]
    valid_three = valid_two * padded[1:-2]
    summed = conv_b + conv_w[0] * extended[3:]
    summed = summed + conv_w[1] * (valid_one[:, None] * extended[2:-1])
    summed = summed + conv_w[2] * (valid_two[:, None] * extended[1:-2])
    summed = summed + conv_w[3] * (valid_three[:, None] * extended[:-3])
    conv_out = jax.nn.silu(summed)
    doubled = matmul(conv_out, w_x)
    rank_width = w_dt.shape[0]
    state_width = (w_x.shape[1] - rank_width) // 2
    delta = jax.nn.softplus(matmul(doubled[:, :rank_width], w_dt) + dt_bias)
    return (conv_out, delta, doubled[:, rank_width:rank_width + state_width], doubled[:, rank_width + state_width:])

def ref_scan(conv_out, delta, b_rows, c_rows, cut_rows, a_neg):
    length, inner_dim = conv_out.shape
    block_len = math.gcd(length, 256)
    block_count = length // block_len

    def per_token(carried, row):
        x_row, d_row, b_row, c_row, k_row = row
        carried = jnp.exp(d_row[:, None] * a_neg) * k_row * carried + (d_row * x_row)[:, None] * b_row[None, :]
        return (carried, lax.optimization_barrier(jnp.sum(carried * c_row[None, :], axis=1)))

    def one_block(carried, rows):
        return lax.scan(per_token, carried, rows)
    rows = (conv_out.reshape(block_count, block_len, inner_dim), delta.reshape(block_count, block_len, inner_dim), b_rows.reshape(block_count, block_len, -1), c_rows.reshape(block_count, block_len, -1), cut_rows.reshape(block_count, block_len))
    start_state = jnp.zeros(a_neg.shape, jnp.float32)
    unused, outputs = lax.scan(jax.checkpoint(one_block), start_state, rows)
    return outputs.reshape(length, inner_dim)

def mixer_dir(xb_rows, z_rows, cut_rows, conv_w, conv_b, w_x, w_dt, dt_bias, a_log, d_skip):
    extended = jnp.concatenate([jnp.zeros((3, xb_rows.shape[1]), jnp.float32), xb_rows], axis=0)
    conv_out, delta, b_rows, c_rows = prepare(extended, cut_rows, conv_w, conv_b, w_x, w_dt, dt_bias)
    a_neg = -jnp.exp(a_log)
    y_rows = ref_scan(conv_out, delta, b_rows, c_rows, cut_rows, a_neg) + d_skip * conv_out
    return y_rows * jax.nn.silu(z_rows)

def layer_fn(inputs, cut_fwd, cut_back, pad_rows, norm_gain, w_in, conv_w, conv_b, w_x, w_dt, dt_bias, a_log, d_skip, w_out):
    inner_dim = w_in.shape[1] // 2
    factor = lax.rsqrt(lax.optimization_barrier(jnp.mean(inputs * inputs, axis=1, keepdims=True)) + epsilon)
    normed = inputs * factor * norm_gain
    fwd_proj = matmul(normed, w_in)
    rev_proj = matmul(normed[:, ::-1], w_in)
    out_fwd = mixer_dir(fwd_proj[:, :inner_dim] * pad_rows[:, None], fwd_proj[:, inner_dim:], cut_fwd, conv_w, conv_b, w_x, w_dt, dt_bias, a_log, d_skip)
    out_rev = mixer_dir((rev_proj[:, :inner_dim] * pad_rows[:, None])[::-1], rev_proj[:, inner_dim:][::-1], cut_back[::-1], conv_w, conv_b, w_x, w_dt, dt_bias, a_log, d_skip)[::-1]
    return inputs + matmul(out_fwd, w_out) + matmul(out_rev, w_out)[:, ::-1]

def reference(tokens, resets, pad_mask, norm_gain, w_in, conv_w, conv_b, w_x, w_dt, dt_bias, a_log, d_skip, w_out, grad_out):
    keep_rows = 1.0 - resets.astype(jnp.float32)
    cut_back = jnp.concatenate([keep_rows[1:], jnp.ones((1,), jnp.float32)])
    pad_rows = pad_mask.astype(jnp.float32)

    def network(start_rows, *weights):
        current = start_rows
        for layer_no in range(norm_gain.shape[0]):
            chosen = [weight_arr[layer_no] for weight_arr in weights]
            current = jax.checkpoint(layer_fn)(current, keep_rows, cut_back, pad_rows, *chosen)
        return current
    mixed, backward = jax.vjp(network, tokens, norm_gain, w_in, conv_w, conv_b, w_x, w_dt, dt_bias, a_log, d_skip, w_out)
    grads = backward(grad_out)
    return (mixed, grads[0], grads[1], grads[2], grads[3], grads[4], grads[5], grads[6], grads[7], grads[8], grads[9], grads[10])
```

```python
import jax
import jax.numpy as jnp
from jax import lax
from jax.experimental import pallas as pl
from jax.experimental.pallas import tpu as pltpu
from jax.sharding import PartitionSpec as P

F32 = jnp.float32
BF16 = jnp.bfloat16
EPS = 1e-05
LOG2E = 1.4426950408889634
LN2 = 0.6931471805599453
BIG = 1e9
CH = 8
LANE = 128
VMEM_LIMIT = 56 * 1024 * 1024


def nn(a, b):
    return lax.dot_general(a, b, (((1,), (0,)), ((), ())), preferred_element_type=F32)


def nt(a, b):
    return lax.dot_general(a, b, (((1,), (1,)), ((), ())), preferred_element_type=F32)


def tn(a, b):
    return lax.dot_general(a, b, (((0,), (0,)), ((), ())), preferred_element_type=F32)


def split(x):
    high = x.astype(BF16)
    return high, (x - high.astype(F32)).astype(BF16)


def split3(x):
    high = x.astype(BF16)
    rest = x - high.astype(F32)
    mid = rest.astype(BF16)
    return high, mid, (rest - mid.astype(F32)).astype(BF16)


def mm(dot, a, b):
    ah, al = a if isinstance(a, tuple) else split(a)
    bh, bl = b if isinstance(b, tuple) else split(b)
    return dot(ah, bh) + (dot(ah, bl) + dot(al, bh))


def flip_matrix(size):
    rows = lax.broadcasted_iota(jnp.int32, (size, size), 0)
    cols = lax.broadcasted_iota(jnp.int32, (size, size), 1)
    return jnp.where(rows + cols == size - 1, 1.0, 0.0).astype(BF16)


def flipped(x):
    flip = flip_matrix(x.shape[1])
    high, mid, low = split3(x)
    return nn(high, flip) + (nn(mid, flip) + nn(low, flip))


def order_matrix(length):
    steps = length // CH
    rows = lax.broadcasted_iota(jnp.int32, (length, length), 0)
    cols = lax.broadcasted_iota(jnp.int32, (length, length), 1)
    token = (rows & (CH - 1)) * steps + (rows >> 3)
    return jnp.where(cols == token, 1.0, 0.0)


def exact(dot, order, x):
    high, mid, low = split3(x)
    order = order.astype(BF16)
    return dot(order, high) + (dot(order, mid) + dot(order, low))


def ordered(ref):
    return exact(nn, order_matrix(ref.shape[0]), ref[...])


def store_ordered(ref, value):
    ref[...] = exact(tn, order_matrix(ref.shape[0]), value)


def spread(row):
    length = row.shape[1]
    picked = (order_matrix(length) * row).astype(BF16)
    return nn(picked, jnp.ones((length, LANE), BF16))


def sigmoid(x):
    return 1.0 / (1.0 + jnp.exp(-x))


def normalize(x, gain):
    factor = lax.rsqrt(jnp.mean(x * x, axis=1, keepdims=True) + EPS)
    return factor, x * factor * gain


def both_orders(normed):
    flip = flip_matrix(normed.shape[1])
    high, low = split(normed)
    return (
        jnp.concatenate([high, nn(high, flip).astype(BF16)], axis=0),
        jnp.concatenate([low, nn(low, flip).astype(BF16)], axis=0),
    )


def params():
    return pltpu.CompilerParams(vmem_limit_bytes=VMEM_LIMIT)


def project_kernel(tok, pad, gain, w_in, gout, w_out, xb_o, z_o, go_o, gy_o):
    inner = w_out.shape[0]
    x = ordered(tok)
    normed = normalize(x, gain[...])[1]
    proj = mm(nn, both_orders(normed), split(w_in[...]))
    pad_col = spread(pad[...].astype(F32))
    pad_all = jnp.concatenate([pad_col, pad_col], axis=0)
    g = ordered(gout)
    gh, gl = both_orders(g)
    go = mm(nt, (gh, gl), split(w_out[...]))
    for lt in range(inner // LANE):
        cols = slice(lt * LANE, (lt + 1) * LANE)
        z = proj[:, inner + lt * LANE : inner + (lt + 1) * LANE]
        xb_o[:, cols] = proj[:, cols] * pad_all
        z_o[:, cols] = z
        go_o[:, cols] = go[:, cols]
        gy_o[:, cols] = go[:, cols] * (z * sigmoid(z))


def project(tok, pad, gain, w_in, gout, w_out):
    length, inner = tok.shape[0], w_out.shape[0]
    big = jax.ShapeDtypeStruct((2 * length, inner), F32)
    return pl.pallas_call(
        project_kernel,
        out_shape=(big, big, big, big),
        compiler_params=params(),
        name="project",
    )(tok, pad, gain, w_in, gout, w_out)


def pick_sides(from_sibling, from_other):
    odd = (lax.axis_index("seq") & 1) == 1
    left = jnp.where(odd, from_sibling, from_other)
    right = jnp.where(odd, from_other, from_sibling)
    return left, right


def rows_of(ref, first, count, cols):
    block = ref[pl.ds(pl.multiple_of(first, CH), count), cols]
    return [jnp.broadcast_to(block[n : n + 1], (CH, LANE)) for n in range(count)]


def sub_iota():
    return lax.broadcasted_iota(jnp.int32, (CH, LANE), 0)


def shifted(value, up):
    return pltpu.roll(value, 1 if up else CH - 1, 0)


def chunk_weights(total, up):
    sub = sub_iota()
    found = []
    width = total
    for reach in (1, 2, 4):
        inside = (sub >= reach) if up else (sub < CH - reach)
        found.append(jnp.where(inside, width, BIG))
        width = width + pltpu.roll(width, reach if up else CH - reach, 0)
    return found


def outside_sum(total, up):
    sub = sub_iota()
    value = jnp.where((sub >= 1) if up else (sub < CH - 1), shifted(total, up), 0.0)
    for reach in (1, 2, 4):
        inside = (sub >= reach) if up else (sub < CH - reach)
        value = value + jnp.where(inside, pltpu.roll(value, reach if up else CH - reach, 0), 0.0)
    return value


def chunk_scan(value, weights, a2, up):
    for reach, weight in zip((1, 2, 4), weights):
        value = value + jnp.exp2(weight * a2) * pltpu.roll(value, reach if up else CH - reach, 0)
    sub = sub_iota()
    enter = jnp.where((sub >= 1) if up else (sub < CH - 1), shifted(value, up), 0.0)
    leave = value[CH - 1 : CH] if up else value[0:1]
    return enter, leave


def prepare_kernel(
    sib, oth, keep, gain, w_in, conv_w, conv_b, w_x, w_dt, dt_bias, a_log, xb, gy,
    xc_o, dt_o, sig_o, conv_o, mask_o, dbl_o, xbh_o, sx_o, mx_o, sum_o,
    ext, de_s, dx_s, bc_s, a2_s,
):
    inner, rank = w_x.shape[0], w_dt.shape[0]
    state = a_log.shape[0]
    length = xb.shape[0] // 2
    steps = length // CH
    tiles = inner // LANE
    left, right = pick_sides(sib[...], oth[...])
    hn_l = normalize(left, gain[...])[1]
    hn_r = normalize(right, gain[...])[1]
    flip = flip_matrix(hn_r.shape[1])
    lh, ll = split(hn_l)
    rh, rl = split(hn_r)
    halo = (
        jnp.concatenate([lh, nn(rh, flip).astype(BF16)], axis=0),
        jnp.concatenate([ll, nn(rl, flip).astype(BF16)], axis=0),
    )
    xbh = mm(nn, halo, split(w_in[:, :inner]))
    xbh_o[...] = xbh
    lane = lax.broadcasted_iota(jnp.int32, (1, length), 1)
    here = 1.0 - keep[...].astype(F32)
    before, after = left[3:4, :length], right[3:4, :length]

    def back(k):
        return jnp.where(lane < k, pltpu.roll(before, k, 1), pltpu.roll(here, k, 1))

    def ahead(k):
        return jnp.where(
            lane >= length - k,
            pltpu.roll(after, length - k, 1),
            pltpu.roll(here, length - k, 1),
        )

    f1 = here
    f2 = f1 * back(1)
    f3 = f2 * back(2)
    r1 = ahead(1)
    r2 = r1 * ahead(2)
    r3 = r2 * ahead(3)
    for i, row in enumerate((f1, f2, f3, r1, r2, r3)):
        mask_o[i * length : (i + 1) * length, :] = spread(row)

    sub = sub_iota()

    def conv_tile(lt, carry):
        cols = pl.ds(pl.multiple_of(lt * LANE, LANE), LANE)
        xbh_t = xbh_o[:, cols]
        taps = [conv_w[k : k + 1, cols] for k in range(4)]
        bias = conv_b[:, cols]
        xf = [xb[j * CH : (j + 1) * CH, cols] for j in range(steps)]
        edge = [
            jnp.where(sub == 0, xbh_t[b : b + 1], pltpu.roll(xf[steps - 3 + b], 1, 0))
            for b in range(3)
        ]
        xf = edge + xf
        for j in range(steps):
            rows = slice(j * CH, (j + 1) * CH)
            v = bias + taps[0] * xf[j + 3]
            for k in range(1, 4):
                v = v + taps[k] * (mask_o[(k - 1) * length + j * CH : (k - 1) * length + (j + 1) * CH, :] * xf[j + 3 - k])
            conv_o[rows, cols] = v
            xc_o[rows, cols] = v * sigmoid(v)
        xr = [xb[length + j * CH : length + (j + 1) * CH, cols] for j in range(steps)]
        xr = xr + [
            jnp.where(sub == CH - 1, xbh_t[8 + b : 9 + b], pltpu.roll(xr[b], CH - 1, 0))
            for b in range(3)
        ]
        for j in range(steps):
            rows = slice(length + j * CH, length + (j + 1) * CH)
            v = bias + taps[0] * xr[j]
            for k in range(1, 4):
                v = v + taps[k] * (mask_o[(k + 2) * length + j * CH : (k + 2) * length + (j + 1) * CH, :] * xr[j + k])
            conv_o[rows, cols] = v
            xc_o[rows, cols] = v * sigmoid(v)
        return carry

    lax.fori_loop(0, tiles, conv_tile, 0)
    dbl = mm(nn, xc_o[...], w_x[...])
    dbl_o[...] = dbl
    pre_all = mm(nn, dbl[:, :rank], w_dt[...])
    expand_bc(dbl, rank, state, bc_s)
    a2_s[...] = jnp.exp(a_log[...]) * (-LOG2E)
    for lt in range(tiles):
        cols = slice(lt * LANE, (lt + 1) * LANE)
        pre = pre_all[:, cols] + dt_bias[:, cols]
        e = jnp.exp(-jnp.abs(pre))
        u = 1.0 + e
        log1p = jnp.where(u == 1.0, e, jnp.log(u) * (e / (u - 1.0)))
        dt = jnp.maximum(pre, 0.0) + log1p
        dt_o[:, cols] = dt
        sig_o[:, cols] = jnp.where(pre >= 0.0, 1.0, e) / u
        dx_s[:, cols] = dt * xc_o[:, cols]
        cut = jnp.concatenate([mask_o[:length], mask_o[3 * length : 4 * length]], axis=0)
        de_s[:, cols] = dt + BIG * (1.0 - cut)

    half = state // 2
    for dirn in range(2):
        order = range(steps) if dirn == 0 else range(steps - 1, -1, -1)
        base = dirn * length

        def tile(lt, carry, dirn=dirn, order=order, base=base):
            cols = pl.ds(pl.multiple_of(lt * LANE, LANE), LANE)
            total = jnp.zeros((CH, LANE), F32)
            for j in range(steps):
                total = total + de_s[base + j * CH : base + (j + 1) * CH, cols]
            up = dirn == 0
            w_s = chunk_weights(total, up)
            w_m = chunk_weights(total, not up)
            whole = jnp.sum(total, axis=0, keepdims=True)
            sum_o[4 * state + dirn : 4 * state + dirn + 1, cols] = whole

            def some(part, carry):
                n0 = part * half
                a2 = rows_of(a2_s, n0, half, cols)
                h = [jnp.zeros((CH, LANE), F32) for _ in range(half)]
                run = [jnp.ones((CH, LANE), F32) for _ in range(half)]
                m = [jnp.zeros((CH, LANE), F32) for _ in range(half)]
                for j in order:
                    rows = slice(base + j * CH, base + (j + 1) * CH)
                    de, dx, gyj = de_s[rows, cols], dx_s[rows, cols], gy[rows, cols]
                    for n in range(half):
                        at_b = pl.ds(pl.multiple_of((n0 + n) * LANE, LANE), LANE)
                        at_c = pl.ds(pl.multiple_of((state + n0 + n) * LANE, LANE), LANE)
                        d = jnp.exp2(de * a2[n])
                        h[n] = d * h[n] + dx * bc_s[rows, at_b]
                        run[n] = run[n] * d
                        m[n] = m[n] + run[n] * (gyj * bc_s[rows, at_c])
                s_row, m_row = (0, 3) if dirn == 0 else (2, 1)
                s_leave, m_leave = [], []
                for n in range(half):
                    enter, leave = chunk_scan(h[n], w_s, a2[n], up)
                    sx_o[dirn, n0 + n, :, cols] = enter
                    s_leave.append(leave)
                    enter, leave = chunk_scan(m[n], w_m, a2[n], not up)
                    mx_o[dirn, n0 + n, :, cols] = enter
                    m_leave.append(leave)
                for row, leave in ((s_row, s_leave), (m_row, m_leave)):
                    at = pl.multiple_of(row * state + n0, CH)
                    sum_o[pl.ds(at, half), cols] = jnp.concatenate(leave, axis=0)
                return carry

            return lax.fori_loop(0, 2, some, carry)

        lax.fori_loop(0, tiles, tile, 0)
    sum_o[4 * state + 2 :, :] = jnp.zeros((sum_o.shape[0] - 4 * state - 2, inner), F32)


def expand_bc(dbl, rank, state, bc_s):
    pieces = split3(dbl[:, rank:])
    width = dbl.shape[1] - rank
    lhs = jnp.concatenate(pieces, axis=1)
    rows = lax.broadcasted_iota(jnp.int32, (3 * width, width * LANE), 0)
    cols = lax.broadcasted_iota(jnp.int32, (3 * width, width * LANE), 1)
    entry = cols >> 7
    hit = (rows == entry) | (rows == entry + width) | (rows == entry + 2 * width)
    bc_s[...] = nn(lhs, jnp.where(hit, 1.0, 0.0).astype(BF16))


def prepare(sib, oth, keep, gain, w_in, conv_w, conv_b, w_x, w_dt, dt_bias, a_log, xb, gy):
    rows, inner = xb.shape
    state, width = a_log.shape[0], w_x.shape[1]
    big = jax.ShapeDtypeStruct((rows, inner), F32)
    edge = jax.ShapeDtypeStruct((2, state, CH, inner), F32)
    return pl.pallas_call(
        prepare_kernel,
        out_shape=(
            big, big, big, big,
            jax.ShapeDtypeStruct((3 * rows, LANE), F32),
            jax.ShapeDtypeStruct((rows, width), F32),
            jax.ShapeDtypeStruct((2 * CH, inner), F32),
            edge, edge,
            jax.ShapeDtypeStruct((4 * state + 8, inner), F32),
        ),
        scratch_shapes=[
            pltpu.VMEM((8, LANE), F32),
            pltpu.VMEM((rows, inner), F32),
            pltpu.VMEM((rows, inner), F32),
            pltpu.VMEM((rows, 2 * state * LANE), F32),
            pltpu.VMEM((state, inner), F32),
        ],
        compiler_params=params(),
        name="prepare",
    )(sib, oth, keep, gain, w_in, conv_w, conv_b, w_x, w_dt, dt_bias, a_log, xb, gy)


def join_kernel(bit, a_log, mine, theirs, total):
    state = a_log.shape[0]
    a2 = jnp.exp(a_log[...]) * (-LOG2E)
    upper_me = ((lax.axis_index("seq") >> bit) & 1) == 1
    low = jnp.where(upper_me, theirs[...], mine[...])
    high = jnp.where(upper_me, mine[...], theirs[...])
    f_row, r_row = 4 * state, 4 * state + 1

    def part(value, i):
        return value[i * state : (i + 1) * state]

    p_f = jnp.exp2(high[f_row : f_row + 1] * a2)
    p_r = jnp.exp2(high[r_row : r_row + 1] * a2)
    total[:state] = part(low, 0) * p_f + part(high, 0)
    total[state : 2 * state] = part(low, 1) * p_r + part(high, 1)
    p_f = jnp.exp2(low[f_row : f_row + 1] * a2)
    p_r = jnp.exp2(low[r_row : r_row + 1] * a2)
    total[2 * state : 3 * state] = part(high, 2) * p_r + part(low, 2)
    total[3 * state : 4 * state] = part(high, 3) * p_f + part(low, 3)
    total[4 * state :] = mine[4 * state :] + theirs[4 * state :]


def join(bit, a_log, mine, theirs):
    return pl.pallas_call(
        lambda *refs: join_kernel(bit, *refs),
        out_shape=jax.ShapeDtypeStruct(mine.shape, F32),
        compiler_params=params(),
        name="join",
    )(a_log, mine, theirs)


def enter_kernel(bits, a_log, *refs):
    theirs, out = refs[:-1], refs[-1]
    state, inner = a_log.shape
    a2 = jnp.exp(a_log[...]) * (-LOG2E)
    me = lax.axis_index("seq")
    f_row, r_row = 4 * state, 4 * state + 1
    out[...] = jnp.zeros(out.shape, F32)
    early = [jnp.zeros((1, inner), F32)] * 2
    late = [jnp.zeros((1, inner), F32)] * 2
    for bit, ref in zip(bits, theirs):
        upper = ((me >> bit) & 1) == 1
        use_low = jnp.where(upper, 1.0, 0.0)
        use_high = 1.0 - use_low
        df, dr = ref[f_row : f_row + 1], ref[r_row : r_row + 1]
        out[:state] += use_low * (ref[:state] * jnp.exp2(early[0] * a2))
        out[state : 2 * state] += use_low * (ref[state : 2 * state] * jnp.exp2(early[1] * a2))
        out[2 * state : 3 * state] += use_high * (ref[2 * state : 3 * state] * jnp.exp2(late[1] * a2))
        out[3 * state :] += use_high * (ref[3 * state : 4 * state] * jnp.exp2(late[0] * a2))
        early = [early[0] + use_low * df, early[1] + use_low * dr]
        late = [late[0] + use_high * df, late[1] + use_high * dr]


def enter(bits, a_log, theirs):
    state, inner = a_log.shape
    return pl.pallas_call(
        lambda *refs: enter_kernel(bits, *refs),
        out_shape=jax.ShapeDtypeStruct((4 * state, inner), F32),
        compiler_params=params(),
        name="enter",
    )(a_log, *theirs)


def main_kernel(
    rs_bits,
    tok, gout, pad, sib, oth, gain, w_in, conv_w, w_x, w_dt, a_log, d_skip, w_out,
    xb, z, go, gy, xc, dt, sig, conv, mask, dbl, xbh, sx, mx, car,
    mixed_o, gtok_o, to_sib, to_oth, *rest,
):
    outs, (de_s, dx_s, bc_s, a2_s, h_s, y_s, sb_s, sa_s, accb, accc, ga_s, gp_s, gpre_s, xcg_s, gscr) = rest[: rs_bits + 1], rest[rs_bits + 1 :]
    inner, rank = w_x.shape[0], w_dt.shape[0]
    feat = w_in.shape[0]
    state = a_log.shape[0]
    rows2 = xb.shape[0]
    length = rows2 // 2
    steps = length // CH
    tiles = inner // LANE
    half = state // 2
    sub = sub_iota()

    expand_bc(dbl[...], rank, state, bc_s)
    a2_s[...] = jnp.exp(a_log[...]) * (-LOG2E)
    accb[...] = jnp.zeros(accb.shape, F32)
    accc[...] = jnp.zeros(accc.shape, F32)
    ga_s[...] = jnp.zeros(ga_s.shape, F32)
    for lt in range(tiles):
        cols = slice(lt * LANE, (lt + 1) * LANE)
        cut = jnp.concatenate([mask[:length], mask[3 * length : 4 * length]], axis=0)
        de_s[:, cols] = dt[:, cols] + BIG * (1.0 - cut)
        dx_s[:, cols] = dt[:, cols] * xc[:, cols]

    for dirn in range(2):
        order = list(range(steps)) if dirn == 0 else list(range(steps - 1, -1, -1))
        base = dirn * length
        s_row, m_row = (0, 3) if dirn == 0 else (2, 1)

        def tile(lt, carry, dirn=dirn, order=order, base=base, s_row=s_row, m_row=m_row):
            cols = pl.ds(pl.multiple_of(lt * LANE, LANE), LANE)
            total = jnp.zeros((CH, LANE), F32)
            for j in range(steps):
                total = total + de_s[base + j * CH : base + (j + 1) * CH, cols]
            up = dirn == 0
            w_s = outside_sum(total, up)
            w_m = outside_sum(total, not up)

            def block(j):
                return slice(base + j * CH, base + (j + 1) * CH)

            def some(part, carry):
                n0 = part * half
                a2 = rows_of(a2_s, n0, half, cols)
                at_b = [pl.ds(pl.multiple_of((n0 + n) * LANE, LANE), LANE) for n in range(half)]
                at_c = [
                    pl.ds(pl.multiple_of((state + n0 + n) * LANE, LANE), LANE)
                    for n in range(half)
                ]
                h = []
                enter_h = rows_of(car, s_row * state + n0, half, cols)
                for n in range(half):
                    h.append(sx[dirn, n0 + n, :, cols] + jnp.exp2(w_s * a2[n]) * enter_h[n])
                    h_s[0, n] = h[n]
                for at, j in enumerate(order):
                    rows = block(j)
                    de, dx = de_s[rows, cols], dx_s[rows, cols]
                    y = None
                    for n in range(half):
                        h[n] = jnp.exp2(de * a2[n]) * h[n] + dx * bc_s[rows, at_b[n]]
                        h_s[at + 1, n] = h[n]
                        term = h[n] * bc_s[rows, at_c[n]]
                        y = term if y is None else y + term
                    y_s[rows, cols] = y + y_s[rows, cols]
                q = []
                ga = []
                enter_q = rows_of(car, m_row * state + n0, half, cols)
                for n in range(half):
                    q.append(mx[dirn, n0 + n, :, cols] + jnp.exp2(w_m * a2[n]) * enter_q[n])
                    ga.append(jnp.zeros((CH, LANE), F32))
                for at in range(steps - 1, -1, -1):
                    rows = block(order[at])
                    de, dx, gyj = de_s[rows, cols], dx_s[rows, cols], gy[rows, cols]
                    sb = sa = None
                    for n in range(half):
                        gh = gyj * bc_s[rows, at_c[n]] + q[n]
                        accc[rows, at_b[n]] += gyj * h_s[at + 1, n]
                        accb[rows, at_b[n]] += gh * dx
                        term_b = gh * bc_s[rows, at_b[n]]
                        q[n] = jnp.exp2(de * a2[n]) * gh
                        r = q[n] * h_s[at, n]
                        term_a = a2[n] * r
                        ga[n] = ga[n] + de * r
                        sb = term_b if sb is None else sb + term_b
                        sa = term_a if sa is None else sa + term_a
                    sb_s[rows, cols] = sb + sb_s[rows, cols]
                    sa_s[rows, cols] = sa + sa_s[rows, cols]
                for n in range(half):
                    ga_s[n0 + n, :, cols] += ga[n]
                return carry

            zero = jnp.zeros((CH, LANE), F32)
            for j in range(steps):
                y_s[block(j), cols] = zero
                sb_s[block(j), cols] = zero
                sa_s[block(j), cols] = zero
            return lax.fori_loop(0, 2, some, carry)

        lax.fori_loop(0, tiles, tile, 0)

    small = {}
    skip_rows, bias_rows = [], []
    for lt in range(tiles):
        cols = slice(lt * LANE, (lt + 1) * LANE)
        zt, xct, gyt = z[:, cols], xc[:, cols], gy[:, cols]
        s = sigmoid(zt)
        gate = zt * s
        y = y_s[:, cols] + d_skip[:, cols] * xct
        y_s[:, cols] = y * gate
        gp_s[:, inner + lt * LANE : inner + (lt + 1) * LANE] = go[:, cols] * y * (s * (1.0 + zt * (1.0 - s)))
        g_dt = xct * sb_s[:, cols] + LN2 * sa_s[:, cols]
        g_pre = g_dt * sig[:, cols]
        gpre_s[:, cols] = g_pre
        xcg_s[:, cols] = d_skip[:, cols] * gyt + dt[:, cols] * sb_s[:, cols]
        skip_rows.append(jnp.sum(gyt * xct, axis=0, keepdims=True))
        bias_rows.append(jnp.sum(g_pre, axis=0, keepdims=True))
    small["skip"] = jnp.concatenate(skip_rows, axis=1)
    small["dtb"] = jnp.concatenate(bias_rows, axis=1)

    x = ordered(tok)
    g_all = both_orders(ordered(gout))
    out_parts = split(y_s[...])
    w_out_parts = split(w_out[...])
    sb_s[:, :feat] = mm(nn, out_parts, w_out_parts)
    sa_s[:length, :feat] = flipped(sb_s[length:, :feat])
    store_ordered(mixed_o, x + (sb_s[:length, :feat] + sa_s[:length, :feat]))
    gw_out = mm(tn, out_parts, g_all)

    lanes = state * LANE
    e_row = lax.broadcasted_iota(jnp.int32, (lanes, LANE), 0) >> 7
    e_col = lax.broadcasted_iota(jnp.int32, (lanes, LANE), 1)
    pick_b = jnp.where(e_col == e_row + rank, 1.0, 0.0).astype(BF16)
    pick_c = jnp.where(e_col == e_row + rank + state, 1.0, 0.0).astype(BF16)
    bh, bl = split(accb[...])
    ch, cl = split(accc[...])
    g_bc = nn(bh, pick_b) + nn(bl, pick_b) + nn(ch, pick_c) + nn(cl, pick_c)
    gpre_parts = split(gpre_s[...])
    w_dt_parts = split(w_dt[...])
    g_rank = mm(nt, gpre_parts, w_dt_parts)
    width = rank + 2 * state
    g_dbl = jnp.concatenate([g_rank, g_bc[:, rank:width]], axis=1)
    g_dbl_parts = split(g_dbl)
    gw_dt = mm(tn, split(dbl[:, :rank]), gpre_parts)
    gw_x = mm(tn, g_dbl_parts, split(xc[...]))
    xcg_s[...] += mm(nt, g_dbl_parts, split(w_x[...]))

    cw_rows = [[] for _ in range(4)]
    cb_rows = []
    halo_f, halo_r = [], []
    for lt in range(tiles):
        cols = slice(lt * LANE, (lt + 1) * LANE)
        taps = [conv_w[k : k + 1, cols] for k in range(4)]
        xbh_t = xbh[:, cols]
        xf = [xb[j * CH : (j + 1) * CH, cols] for j in range(steps)]
        xf = [
            jnp.where(sub == 0, xbh_t[b : b + 1], pltpu.roll(xf[steps - 3 + b], 1, 0))
            for b in range(3)
        ] + xf
        gcw = [jnp.zeros((CH, LANE), F32) for _ in range(4)]
        gcb = jnp.zeros((CH, LANE), F32)
        grads = [None] * (steps + 3)
        for j in range(steps):
            rows = slice(j * CH, (j + 1) * CH)
            v = conv[rows, cols]
            s = sigmoid(v)
            u = xcg_s[rows, cols] * (s * (1.0 + v * (1.0 - s)))
            gcb = gcb + u
            for k in range(4):
                uk = u if k == 0 else u * mask[(k - 1) * length + j * CH : (k - 1) * length + (j + 1) * CH, :]
                gcw[k] = gcw[k] + uk * xf[j + 3 - k]
                add = taps[k] * uk
                at = j + 3 - k
                grads[at] = add if grads[at] is None else grads[at] + add
        for b in range(3):
            halo_f.append(grads[b][0:1])
            at = steps + b
            grads[at] = grads[at] + jnp.where(sub == CH - 1, 0.0, pltpu.roll(grads[b], CH - 1, 0))
        for j in range(steps):
            gp_s[j * CH : (j + 1) * CH, cols] = grads[j + 3]
        xr = [xb[length + j * CH : length + (j + 1) * CH, cols] for j in range(steps)]
        xr = xr + [
            jnp.where(sub == CH - 1, xbh_t[8 + b : 9 + b], pltpu.roll(xr[b], CH - 1, 0))
            for b in range(3)
        ]
        grads = [None] * (steps + 3)
        for j in range(steps):
            rows = slice(length + j * CH, length + (j + 1) * CH)
            v = conv[rows, cols]
            s = sigmoid(v)
            u = xcg_s[rows, cols] * (s * (1.0 + v * (1.0 - s)))
            gcb = gcb + u
            for k in range(4):
                uk = u if k == 0 else u * mask[(k + 2) * length + j * CH : (k + 2) * length + (j + 1) * CH, :]
                gcw[k] = gcw[k] + uk * xr[j + k]
                add = taps[k] * uk
                grads[j + k] = add if grads[j + k] is None else grads[j + k] + add
        for b in range(3):
            halo_r.append(grads[steps + b][CH - 1 : CH])
            grads[b] = grads[b] + jnp.where(sub == 0, 0.0, pltpu.roll(grads[steps + b], 1, 0))
        for j in range(steps):
            gp_s[length + j * CH : length + (j + 1) * CH, cols] = grads[j]
        for k in range(4):
            cw_rows[k].append(jnp.sum(gcw[k], axis=0, keepdims=True))
        cb_rows.append(jnp.sum(gcb, axis=0, keepdims=True))
    pad_col = spread(pad[...].astype(F32))
    pad_all = jnp.concatenate([pad_col, pad_col], axis=0)
    for lt in range(tiles):
        cols = slice(lt * LANE, (lt + 1) * LANE)
        gp_s[:, cols] *= pad_all

    blank = jnp.zeros((5, inner), F32)

    def gather(found):
        return jnp.concatenate(
            [jnp.concatenate([found[lt * 3 + b] for lt in range(tiles)], axis=1) for b in range(3)]
            + [blank],
            axis=0,
        )

    gh = jnp.concatenate([gather(halo_f), gather(halo_r)], axis=0)
    gh_parts = split(gh)
    left, right = pick_sides(sib[...], oth[...])
    factor_l, hn_l = normalize(left, gain[...])
    factor_r, hn_r = normalize(right, gain[...])
    flip = flip_matrix(feat)
    lh, ll = split(hn_l)
    rh, rl = split(hn_r)
    halo = (
        jnp.concatenate([lh, nn(rh, flip).astype(BF16)], axis=0),
        jnp.concatenate([ll, nn(rl, flip).astype(BF16)], axis=0),
    )

    factor, normed = normalize(x, gain[...])
    n_parts = both_orders(normed)
    w_in_parts = split(w_in[...])
    gp_parts = split(gp_s[...])
    gw_in = mm(tn, n_parts, gp_parts)
    gw_in_halo = mm(tn, halo, gh_parts)
    back = mm(nt, gp_parts, w_in_parts)
    g_normed = back[:length] + flipped(back[length:])
    back_h = mm(nt, gh_parts, (w_in_parts[0][:, :inner], w_in_parts[1][:, :inner]))
    gn_l = back_h[:CH]
    gn_r = flipped(back_h[CH:])

    def norm_back(x, factor, gn):
        scaled = gn * gain[...]
        return factor * scaled - x * (factor * factor * factor * jnp.mean(scaled * x, axis=1, keepdims=True))

    store_ordered(gtok_o, ordered(gout) + norm_back(x, factor, g_normed))
    to_left = norm_back(left, factor_l, gn_l)
    to_right = norm_back(right, factor_r, gn_r)
    odd = (lax.axis_index("seq") & 1) == 1
    to_sib[...] = jnp.where(odd, to_left, to_right)
    to_oth[...] = jnp.where(odd, to_right, to_left)
    three = lax.broadcasted_iota(jnp.int32, (CH, feat), 0) < 3
    g_gain = (
        jnp.sum(g_normed * (x * factor), axis=0, keepdims=True)
        + jnp.sum(jnp.where(three, gn_l * (left * factor_l) + gn_r * (right * factor_r), 0.0), axis=0, keepdims=True)
    )

    ga = jnp.concatenate([jnp.sum(ga_s[n], axis=0, keepdims=True) for n in range(state)], axis=0)
    few = jnp.concatenate(
        [gw_x, ga * (a2_s[...] * LN2), gw_dt]
        + [jnp.concatenate(cw_rows[k], axis=1) for k in range(4)]
        + [
            jnp.concatenate(cb_rows, axis=1),
            small["dtb"],
            small["skip"],
            jnp.concatenate([g_gain, jnp.zeros((1, inner - feat), F32)], axis=1),
        ],
        axis=0,
    )
    pieces = 1 << rs_bits
    mine = reverse_bits(lax.axis_index("seq"), rs_bits)
    in_rows, out_rows = feat // pieces, inner // pieces
    for p in range(pieces):
        slot = mine ^ reverse_bits(p, rs_bits)
        at = 0
        for lt in range(2 * tiles):
            value = gw_in[p * in_rows : (p + 1) * in_rows, lt * LANE : (lt + 1) * LANE]
            if lt < tiles:
                value = value + gw_in_halo[p * in_rows : (p + 1) * in_rows, lt * LANE : (lt + 1) * LANE]
            gscr[slot, at : at + in_rows, :] = value
            at += in_rows
        for lt in range(feat // LANE):
            gscr[slot, at : at + out_rows, :] = gw_out[p * out_rows : (p + 1) * out_rows, lt * LANE : (lt + 1) * LANE]
            at += out_rows
        for t in range(2 * p, 2 * p + 2):
            rb, lt = t // tiles, t % tiles
            if rb * CH < few.shape[0]:
                gscr[slot, at : at + CH, :] = few[rb * CH : (rb + 1) * CH, lt * LANE : (lt + 1) * LANE]
            else:
                gscr[slot, at : at + CH, :] = jnp.zeros((CH, LANE), F32)
            at += CH
    top = pieces
    for i in range(rs_bits):
        outs[i][...] = gscr[top // 2 : top]
        top //= 2
    outs[rs_bits][...] = gscr[0:1]


def reverse_bits(value, bits):
    found = 0
    for i in range(bits):
        found = found | (((value >> i) & 1) << (bits - 1 - i))
    return found


def piece_rows(rs_bits, feat, inner):
    pieces = 1 << rs_bits
    return (feat * 2 * inner + inner * feat) // LANE // pieces + 16 * 32 // pieces


def main(rs_bits, *arrays):
    tok, w_in, a_log, xb, dbl = arrays[0], arrays[6], arrays[10], arrays[13], arrays[22]
    length, feat = tok.shape
    rows2, inner = xb.shape
    state, rank = a_log.shape[0], arrays[9].shape[0]
    width = dbl.shape[1]
    tall = piece_rows(rs_bits, feat, inner)
    sizes = [1 << (rs_bits - 1 - i) for i in range(rs_bits)] + [1]
    big = pltpu.VMEM((rows2, inner), F32)
    return pl.pallas_call(
        lambda *refs: main_kernel(rs_bits, *refs),
        out_shape=(
            jax.ShapeDtypeStruct((length, feat), F32),
            jax.ShapeDtypeStruct((length, feat), F32),
            jax.ShapeDtypeStruct((CH, feat), F32),
            jax.ShapeDtypeStruct((CH, feat), F32),
        )
        + tuple(jax.ShapeDtypeStruct((size, tall, LANE), F32) for size in sizes),
        scratch_shapes=[
            big, big,
            pltpu.VMEM((rows2, 2 * state * LANE), F32),
            pltpu.VMEM((state, inner), F32),
            pltpu.VMEM((length // CH + 1, state // 2, CH, LANE), F32),
            big, big, big,
            pltpu.VMEM((rows2, state * LANE), F32),
            pltpu.VMEM((rows2, state * LANE), F32),
            pltpu.VMEM((state, CH, inner), F32),
            pltpu.VMEM((rows2, 2 * inner), F32),
            big, big,
            pltpu.VMEM((1 << rs_bits, tall, LANE), F32),
        ],
        compiler_params=params(),
        name="main",
    )(*arrays)


def unpack_kernel(
    rs_bits, near, far, gtok, from_sib, from_oth, pad,
    gtok_o, gain_o, w_in_o, conv_w_o, conv_b_o, w_x_o, w_dt_o, dt_bias_o, a_log_o, d_skip_o, w_out_o, few_s,
):
    feat = w_in_o.shape[0]
    inner = w_out_o.shape[0]
    tiles = inner // LANE
    pieces = 1 << rs_bits
    mine = reverse_bits(lax.axis_index("seq"), rs_bits)
    in_rows, out_rows = feat // pieces, inner // pieces
    for slot in range(pieces):
        source = near if slot < pieces // 2 else far
        i = slot % (pieces // 2)
        p = reverse_bits(mine ^ slot, rs_bits)
        at = 0
        rows = pl.ds(pl.multiple_of(p * in_rows, in_rows), in_rows)
        for lt in range(2 * tiles):
            w_in_o[rows, lt * LANE : (lt + 1) * LANE] = source[i, at : at + in_rows, :]
            at += in_rows
        rows = pl.ds(pl.multiple_of(p * out_rows, out_rows), out_rows)
        for lt in range(feat // LANE):
            w_out_o[rows, lt * LANE : (lt + 1) * LANE] = source[i, at : at + out_rows, :]
            at += out_rows
        few_s[p] = source[i, at : at + 2 * CH, :]

    def few_rows(first, count):
        found = []
        for lt in range(tiles):
            t = first // CH * tiles + lt
            found.append(few_s[t // 2, (t % 2) * CH + first % CH : (t % 2) * CH + first % CH + count, :])
        return jnp.concatenate(found, axis=1)

    width, state = w_x_o.shape[1], a_log_o.shape[1]
    rank = w_dt_o.shape[0]
    w_x_o[...] = jnp.concatenate([few_rows(r, CH) for r in range(0, width, CH)], axis=0).T
    at = width
    a_log_o[...] = jnp.concatenate([few_rows(r, CH) for r in range(at, at + state, CH)], axis=0).T
    at += state
    w_dt_o[...] = jnp.concatenate([few_rows(r, CH) for r in range(at, at + rank, CH)], axis=0)
    at += rank
    conv_w_o[...] = few_rows(at, 4)
    conv_b_o[...] = few_rows(at + 4, 1)
    dt_bias_o[...] = few_rows(at + 5, 1)
    d_skip_o[...] = few_rows(at + 6, 1)
    gain_o[...] = few_rows(at + 7, 1)[:, :feat]

    left, right = pick_sides(from_sib[...], from_oth[...])
    length = gtok.shape[0]
    row = lax.broadcasted_iota(jnp.int32, (length, feat), 0)
    sub = lax.broadcasted_iota(jnp.int32, (CH, feat), 0)
    padded = spread_plain(pad[...].astype(F32), feat)
    first = jnp.where(sub < 3, left, 0.0)
    last = jnp.where(sub >= CH - 3, pltpu.roll(right, CH - 3, 0), 0.0)
    gtok_o[...] = gtok[...]
    gtok_o[:CH] = gtok[:CH] + padded[:CH] * first
    gtok_o[length - CH :] = gtok[length - CH :] + padded[length - CH :] * last


def spread_plain(row, width):
    length = row.shape[1]
    rows = lax.broadcasted_iota(jnp.int32, (length, length), 0)
    cols = lax.broadcasted_iota(jnp.int32, (length, length), 1)
    picked = (jnp.where(rows == cols, 1.0, 0.0) * row).astype(BF16)
    return nn(picked, jnp.ones((length, width), BF16))


def unpack(rs_bits, near, far, gtok, from_sib, from_oth, pad, state, rank):
    length, feat = gtok.shape
    pieces = 1 << rs_bits
    inner = 4 * LANE if state is None else state[1]
    width = rank + 2 * state[0]
    shape = lambda *dims: jax.ShapeDtypeStruct(dims, F32)
    return pl.pallas_call(
        lambda *refs: unpack_kernel(rs_bits, *refs),
        out_shape=(
            shape(length, feat),
            shape(1, feat),
            shape(feat, 2 * inner),
            shape(4, inner),
            shape(1, inner),
            shape(inner, width),
            shape(rank, inner),
            shape(1, inner),
            shape(inner, state[0]),
            shape(1, inner),
            shape(inner, feat),
        ),
        scratch_shapes=[pltpu.VMEM((pieces, 2 * CH, LANE), F32)],
        compiler_params=params(),
        name="unpack",
    )(near, far, gtok, from_sib, from_oth, pad)


def body(tokens, resets, pad_mask, norm_gain, w_in, conv_w, conv_b, w_x, w_dt, dt_bias, a_log, d_skip, w_out, grad_out):
    count = lax.axis_size("seq")
    bits = count.bit_length() - 1
    rs_bits = min(5, bits)
    odd = (lax.axis_index("seq") & 1) == 1
    length, feat = tokens.shape
    keep_row, pad_row = resets.reshape(1, length), pad_mask.reshape(1, length)
    gain, a_log_t = norm_gain, a_log[0].T

    def swap(value, bit):
        return lax.ppermute(value, "seq", [(i, i ^ (1 << bit)) for i in range(count)])

    across = [(i, i + 1) for i in range(1, count - 1, 2)] + [(i + 1, i) for i in range(1, count - 1, 2)]

    def swap_across(value):
        return lax.ppermute(value, "seq", across)

    kept = jnp.pad(1.0 - resets.astype(F32), (0, feat - length))[None]
    real = pad_mask.astype(F32)[:, None]
    fill = jnp.zeros((4, feat), F32)
    first = jnp.concatenate([tokens[:3] * real[:3], kept, fill], axis=0)
    last = jnp.concatenate([tokens[-3:] * real[-3:], kept, fill], axis=0)
    oth = swap_across(jnp.where(odd, last, first))
    sib = swap(jnp.where(odd, first, last), 0)

    xb, z, go, gy = project(tokens, pad_row, gain, w_in[0], grad_out, w_out[0])
    xc, dt, sig, conv, mask, dbl, xbh, sx, mx, total = prepare(
        sib, oth, keep_row, gain, w_in[0], conv_w[0], conv_b, w_x[0], w_dt[0], dt_bias, a_log_t, xb, gy
    )
    theirs = []
    for bit in range(bits):
        theirs.append(swap(total, bit))
        if bit < bits - 1:
            total = join(bit, a_log_t, total, theirs[-1])
    car = enter(tuple(range(bits)), a_log_t, theirs)
    found = main(
        rs_bits,
        tokens, grad_out, pad_row, sib, oth, gain, w_in[0], conv_w[0], w_x[0], w_dt[0], a_log_t, d_skip, w_out[0],
        xb, z, go, gy, xc, dt, sig, conv, mask, dbl, xbh, sx, mx, car,
    )
    mixed, gtok, to_sib, to_oth = found[:4]
    parts = list(found[4:])

    for bit in range(rs_bits):
        got = swap(parts[bit], bit)
        for later in range(bit + 1, rs_bits + 1):
            size = parts[later].shape[0]
            start = size if later < rs_bits else 0
            parts[later] = parts[later] + got[start : start + size]
    own = parts[rs_bits]
    for bit in range(rs_bits, bits):
        own = own + swap(own, bit)
    from_sib, from_oth = swap(to_sib, 0), swap_across(to_oth)
    for bit in range(rs_bits - 1, 0, -1):
        own = jnp.concatenate([own, swap(own, bit)], axis=0)
    far = swap(own, 0)
    outs = unpack(rs_bits, own, far, gtok, from_sib, from_oth, pad_row, a_log_t.shape, w_dt.shape[1])
    gtok, g_gain, g_w_in, g_conv_w, g_conv_b, g_w_x, g_w_dt, g_dt_bias, g_a_log, g_d_skip, g_w_out = outs
    return (
        mixed, gtok, g_gain, g_w_in[None], g_conv_w[None], g_conv_b, g_w_x[None], g_w_dt[None],
        g_dt_bias, g_a_log[None], g_d_skip, g_w_out[None],
    )


def solution(mesh):
    rows, whole = P("seq", None), P()
    return jax.shard_map(
        body,
        mesh=mesh,
        in_specs=(rows, P("seq"), P("seq")) + (whole,) * 10 + (rows,),
        out_specs=(rows, rows) + (whole,) * 10,
        check_vma=False,
    )
```

```python
import jax
import jax.numpy as jnp
from jax import lax
from jax.experimental import pallas as pl
from jax.experimental.pallas import tpu as pltpu
from jax.sharding import PartitionSpec as P

F32 = jnp.float32
BF16 = jnp.bfloat16
EPS = 1e-05
LOG2E = 1.4426950408889634
LN2 = 0.6931471805599453
BIG = 1e9
CH = 8
LANE = 128
MIB = 1024 * 1024


def nn(a, b):
    return lax.dot_general(a, b, (((1,), (0,)), ((), ())), preferred_element_type=F32)


def nt(a, b):
    return lax.dot_general(a, b, (((1,), (1,)), ((), ())), preferred_element_type=F32)


def tn(a, b):
    return lax.dot_general(a, b, (((0,), (0,)), ((), ())), preferred_element_type=F32)


def split(x):
    high = x.astype(BF16)
    return high, (x - high.astype(F32)).astype(BF16)


def split3(x):
    high = x.astype(BF16)
    rest = x - high.astype(F32)
    mid = rest.astype(BF16)
    return high, mid, (rest - mid.astype(F32)).astype(BF16)


def mm(dot, a, b):
    ah, al = a if isinstance(a, tuple) else split(a)
    bh, bl = b if isinstance(b, tuple) else split(b)
    return dot(ah, bh) + (dot(ah, bl) + dot(al, bh))


def flip_matrix(size):
    rows = lax.broadcasted_iota(jnp.int32, (size, size), 0)
    cols = lax.broadcasted_iota(jnp.int32, (size, size), 1)
    return jnp.where(rows + cols == size - 1, 1.0, 0.0).astype(BF16)


def flipped(x):
    flip = flip_matrix(x.shape[1])
    high, mid, low = split3(x)
    return nn(high, flip) + (nn(mid, flip) + nn(low, flip))


def order_matrix(length):
    steps = length // CH
    rows = lax.broadcasted_iota(jnp.int32, (length, length), 0)
    cols = lax.broadcasted_iota(jnp.int32, (length, length), 1)
    token = (rows & (CH - 1)) * steps + (rows >> 3)
    return jnp.where(cols == token, 1.0, 0.0)


def exact(dot, order, x):
    high, mid, low = split3(x)
    order = order.astype(BF16)
    return dot(order, high) + (dot(order, mid) + dot(order, low))


def ordered(ref):
    return exact(nn, order_matrix(ref.shape[0]), ref[...])


def store_ordered(ref, value):
    ref[...] = exact(tn, order_matrix(ref.shape[0]), value)


def spread(row):
    length = row.shape[1]
    picked = (order_matrix(length) * row).astype(BF16)
    return nn(picked, jnp.ones((length, LANE), BF16))


def sigmoid(x):
    return 1.0 / (1.0 + jnp.exp(-x))


def normalize(x, gain):
    factor = lax.rsqrt(jnp.mean(x * x, axis=1, keepdims=True) + EPS)
    return factor, x * factor * gain


def both_orders(normed):
    flip = flip_matrix(normed.shape[1])
    high, low = split(normed)
    return (
        jnp.concatenate([high, nn(high, flip).astype(BF16)], axis=0),
        jnp.concatenate([low, nn(low, flip).astype(BF16)], axis=0),
    )


def params(mib):
    return pltpu.CompilerParams(vmem_limit_bytes=mib * MIB)


def in_hbm(*arrays):
    return tuple(pltpu.with_memory_space_constraint(x, pltpu.HBM) for x in arrays)


def edges_kernel(first_rows, last_rows, resets, pad, to_sib, to_oth):
    length = resets.shape[1]
    sub = lax.broadcasted_iota(jnp.int32, (CH, length), 0)
    lane = lax.broadcasted_iota(jnp.int32, (CH, length), 1)
    real = pad[...].astype(F32)
    row = lax.broadcasted_iota(jnp.int32, first_rows.shape, 0)
    kept = 1.0 - resets[...].astype(F32)
    kept = jnp.concatenate([kept, jnp.zeros((1, first_rows.shape[1] - length), F32)], axis=1)

    def message(rows, start):
        col = jnp.sum(jnp.where(lane == sub + start, real, 0.0), axis=1, keepdims=True)
        return jnp.where(row < 3, rows * col, jnp.where(row == 3, kept, 0.0))

    first = message(first_rows[...], 0)
    last = message(pltpu.roll(last_rows[...], 3, 0), length - 3)
    odd = (lax.axis_index("seq") & 1) == 1
    to_sib[...] = jnp.where(odd, first, last)
    to_oth[...] = jnp.where(odd, last, first)


def edges(tok, resets, pad):
    length, feat = tok.shape
    shape = jax.ShapeDtypeStruct((CH, feat), F32)
    whole = lambda *dims: pl.BlockSpec(dims, lambda i: (0, 0))
    return pl.pallas_call(
        edges_kernel,
        grid=(1,),
        in_specs=[
            whole(CH, feat),
            pl.BlockSpec((CH, feat), lambda i: (length // CH - 1, 0)),
            whole(1, length),
            whole(1, length),
        ],
        out_specs=(whole(CH, feat), whole(CH, feat)),
        out_shape=(shape, shape),
        compiler_params=params(2),
        name="edges",
    )(*in_hbm(tok, tok, resets, pad))


def project_kernel(tok, pad, gain, w_in, gout, w_out, *refs):
    more = (len(refs) - 10) // 2
    xb_o, z_o, go_o, gy_o, *kept = refs[more:]
    for ref, kept_o in zip((tok, pad, gain, w_in, gout, w_out) + refs[:more], kept):
        kept_o[...] = ref[...]
    inner = w_out.shape[0]
    x = ordered(tok)
    normed = normalize(x, gain[...])[1]
    proj = mm(nn, both_orders(normed), split(w_in[...]))
    pad_col = spread(pad[...].astype(F32))
    pad_all = jnp.concatenate([pad_col, pad_col], axis=0)
    g = ordered(gout)
    gh, gl = both_orders(g)
    go = mm(nt, (gh, gl), split(w_out[...]))
    for lt in range(inner // LANE):
        cols = slice(lt * LANE, (lt + 1) * LANE)
        z = proj[:, inner + lt * LANE : inner + (lt + 1) * LANE]
        xb_o[:, cols] = proj[:, cols] * pad_all
        z_o[:, cols] = z
        go_o[:, cols] = go[:, cols]
        gy_o[:, cols] = go[:, cols] * (z * sigmoid(z))


def project(*arrays):
    tok, w_out = arrays[0], arrays[5]
    length, inner = tok.shape[0], w_out.shape[0]
    big = jax.ShapeDtypeStruct((2 * length, inner), F32)
    found = pl.pallas_call(
        project_kernel,
        out_shape=(big, big, big, big) + tuple(jax.ShapeDtypeStruct(x.shape, x.dtype) for x in arrays),
        compiler_params=params(8),
        name="project",
    )(*in_hbm(*arrays))
    return found[:4], found[4:]


def pick_sides(from_sibling, from_other):
    odd = (lax.axis_index("seq") & 1) == 1
    left = jnp.where(odd, from_sibling, from_other)
    right = jnp.where(odd, from_other, from_sibling)
    return left, right


def rows_of(ref, first, count, cols):
    block = ref[pl.ds(pl.multiple_of(first, CH), count), cols]
    return [jnp.broadcast_to(block[n : n + 1], (CH, LANE)) for n in range(count)]


def sub_iota():
    return lax.broadcasted_iota(jnp.int32, (CH, LANE), 0)


def shifted(value, up):
    return pltpu.roll(value, 1 if up else CH - 1, 0)


def chunk_weights(total, up):
    sub = sub_iota()
    found = []
    width = total
    for reach in (1, 2, 4):
        inside = (sub >= reach) if up else (sub < CH - reach)
        found.append(jnp.where(inside, width, BIG))
        width = width + pltpu.roll(width, reach if up else CH - reach, 0)
    return found


def outside_sum(total, up):
    sub = sub_iota()
    value = jnp.where((sub >= 1) if up else (sub < CH - 1), shifted(total, up), 0.0)
    for reach in (1, 2, 4):
        inside = (sub >= reach) if up else (sub < CH - reach)
        value = value + jnp.where(inside, pltpu.roll(value, reach if up else CH - reach, 0), 0.0)
    return value


def chunk_scan(value, weights, a2, up):
    for reach, weight in zip((1, 2, 4), weights):
        value = value + jnp.exp2(weight * a2) * pltpu.roll(value, reach if up else CH - reach, 0)
    sub = sub_iota()
    enter = jnp.where((sub >= 1) if up else (sub < CH - 1), shifted(value, up), 0.0)
    leave = value[CH - 1 : CH] if up else value[0:1]
    return enter, leave


def prepare_kernel(
    sib, oth, keep, gain, w_in, conv_w, conv_b, w_x, w_dt, dt_bias, a_log, xb, gy,
    xc_o, dt_o, sig_o, conv_o, mask_o, dbl_o, xbh_o, sx_o, mx_o, sum_o, de_s, dx_s, bc_s, a2_s, decay_o,
    leave_s,
):
    inner, rank = w_x.shape[1], w_dt.shape[0]
    state = a_log.shape[0]
    length = xb.shape[0] // 2
    steps = length // CH
    tiles = inner // LANE
    left, right = pick_sides(sib[...], oth[...])
    hn_l = normalize(left, gain[...])[1]
    hn_r = normalize(right, gain[...])[1]
    flip = flip_matrix(hn_r.shape[1])
    lh, ll = split(hn_l)
    rh, rl = split(hn_r)
    halo = (
        jnp.concatenate([lh, nn(rh, flip).astype(BF16)], axis=0),
        jnp.concatenate([ll, nn(rl, flip).astype(BF16)], axis=0),
    )
    xbh = mm(nn, halo, split(w_in[:, :inner]))
    xbh_o[...] = xbh
    lane = lax.broadcasted_iota(jnp.int32, (1, length), 1)
    here = 1.0 - keep[...].astype(F32)
    before, after = left[3:4, :length], right[3:4, :length]

    def back(k):
        return jnp.where(lane < k, pltpu.roll(before, k, 1), pltpu.roll(here, k, 1))

    def ahead(k):
        return jnp.where(
            lane >= length - k,
            pltpu.roll(after, length - k, 1),
            pltpu.roll(here, length - k, 1),
        )

    f1 = here
    f2 = f1 * back(1)
    f3 = f2 * back(2)
    r1 = ahead(1)
    r2 = r1 * ahead(2)
    r3 = r2 * ahead(3)
    for i, row in enumerate((f1, f2, f3, r1, r2, r3)):
        mask_o[i * length : (i + 1) * length, :] = spread(row)

    sub = sub_iota()

    def conv_tile(lt, carry):
        cols = pl.ds(pl.multiple_of(lt * LANE, LANE), LANE)
        xbh_t = xbh_o[:, cols]
        taps = [conv_w[k : k + 1, cols] for k in range(4)]
        bias = conv_b[:, cols]
        xf = [xb[j * CH : (j + 1) * CH, cols] for j in range(steps)]
        edge = [
            jnp.where(sub == 0, xbh_t[b : b + 1], pltpu.roll(xf[steps - 3 + b], 1, 0))
            for b in range(3)
        ]
        xf = edge + xf
        for j in range(steps):
            rows = slice(j * CH, (j + 1) * CH)
            v = bias + taps[0] * xf[j + 3]
            for k in range(1, 4):
                v = v + taps[k] * (mask_o[(k - 1) * length + j * CH : (k - 1) * length + (j + 1) * CH, :] * xf[j + 3 - k])
            conv_o[rows, cols] = v
            xc_o[rows, cols] = v * sigmoid(v)
        xr = [xb[length + j * CH : length + (j + 1) * CH, cols] for j in range(steps)]
        xr = xr + [
            jnp.where(sub == CH - 1, xbh_t[8 + b : 9 + b], pltpu.roll(xr[b], CH - 1, 0))
            for b in range(3)
        ]
        for j in range(steps):
            rows = slice(length + j * CH, length + (j + 1) * CH)
            v = bias + taps[0] * xr[j]
            for k in range(1, 4):
                v = v + taps[k] * (mask_o[(k + 2) * length + j * CH : (k + 2) * length + (j + 1) * CH, :] * xr[j + k])
            conv_o[rows, cols] = v
            xc_o[rows, cols] = v * sigmoid(v)
        return carry

    lax.fori_loop(0, tiles, conv_tile, 0)
    dbl = mm(nt, xc_o[...], w_x[...])
    dbl_o[...] = dbl
    pre_all = mm(nn, dbl[:, :rank], w_dt[...])
    expand_bc(dbl, rank, state, bc_s)
    a2 = jnp.exp(a_log[...]) * (-LOG2E)
    for n in range(state):
        a2_s[n] = jnp.broadcast_to(a2[n : n + 1], (CH, inner))
    for lt in range(tiles):
        cols = slice(lt * LANE, (lt + 1) * LANE)
        pre = pre_all[:, cols] + dt_bias[:, cols]
        e = jnp.exp(-jnp.abs(pre))
        u = 1.0 + e
        log1p = jnp.where(u == 1.0, e, jnp.log(u) * (e / (u - 1.0)))
        dt = jnp.maximum(pre, 0.0) + log1p
        dt_o[:, cols] = dt
        sig_o[:, cols] = jnp.where(pre >= 0.0, 1.0, e) / u
        dx_s[:, cols] = dt * xc_o[:, cols]
        cut = jnp.concatenate([mask_o[:length], mask_o[3 * length : 4 * length]], axis=0)
        de_s[:, cols] = dt + BIG * (1.0 - cut)

    group = 4
    cols_of = [slice(t * LANE, (t + 1) * LANE) for t in range(tiles)]
    for dirn in range(2):
        order = list(range(steps)) if dirn == 0 else list(range(steps - 1, -1, -1))
        base = dirn * length
        up = dirn == 0
        s_row, m_row = (0, 3) if dirn == 0 else (2, 1)
        totals = []
        for cols in cols_of:
            total = jnp.zeros((CH, LANE), F32)
            for j in range(steps):
                total = total + de_s[base + j * CH : base + (j + 1) * CH, cols]
            sum_o[4 * state + dirn : 4 * state + dirn + 1, cols] = jnp.sum(total, axis=0, keepdims=True)
            totals.append(total)

        def some(g, carry, order=order, base=base, up=up, dirn=dirn, s_row=s_row, m_row=m_row, totals=totals):
            n0 = g * group
            at_b, at_c = lanes_of(n0, group), lanes_of(state + n0, group)
            keys = [(n, t) for n in range(group) for t in range(tiles)]
            a2 = {(n, t): a2_s[n0 + n, :, cols_of[t]] for n, t in keys}
            h, m = {}, {}
            for at, j in enumerate(order):
                rows = slice(base + j * CH, base + (j + 1) * CH)
                de = [de_s[rows, c] for c in cols_of]
                dx = [dx_s[rows, c] for c in cols_of]
                for n in range(group):
                    b_n = bc_s[rows, at_b[n]]
                    for t, cols in enumerate(cols_of):
                        d = jnp.exp2(de[t] * a2[n, t])
                        decay_o[dirn, at, n0 + n, :, cols] = d
                        h[n, t] = dx[t] * b_n if at == 0 else d * h[n, t] + dx[t] * b_n
            for at in range(steps - 1, -1, -1):
                rows = slice(base + order[at] * CH, base + (order[at] + 1) * CH)
                gyj = [gy[rows, c] for c in cols_of]
                for n in range(group):
                    c_n = bc_s[rows, at_c[n]]
                    for t, cols in enumerate(cols_of):
                        own = gyj[t] * c_n
                        d = decay_o[dirn, at, n0 + n, :, cols]
                        m[n, t] = d * (own if at == steps - 1 else own + m[n, t])
            for t in range(tiles):
                w_s, w_m = chunk_weights(totals[t], up), chunk_weights(totals[t], not up)
                for n in range(group):
                    enter, leave = chunk_scan(h[n, t], w_s, a2[n, t], up)
                    sx_o[dirn, n0 + n, :, cols_of[t]] = enter
                    leave_s[s_row * state + n0 + n, :, cols_of[t]] = jnp.broadcast_to(leave, (CH, LANE))
                    enter, leave = chunk_scan(m[n, t], w_m, a2[n, t], not up)
                    mx_o[dirn, n0 + n, :, cols_of[t]] = enter
                    leave_s[m_row * state + n0 + n, :, cols_of[t]] = jnp.broadcast_to(leave, (CH, LANE))
            return carry

        lax.fori_loop(0, state // group, some, 0)
    for row in range(0, 4 * state, CH):
        for cols in cols_of:
            sum_o[row : row + CH, cols] = jnp.concatenate([leave_s[row + i, 0:1, cols] for i in range(CH)], axis=0)
    sum_o[4 * state + 2 :, :] = jnp.zeros((sum_o.shape[0] - 4 * state - 2, inner), F32)


def lanes_of(first, count):
    return [pl.ds(pl.multiple_of((first + n) * LANE, LANE), LANE) for n in range(count)]


def expand_bc(dbl, rank, state, bc_s):
    pieces = split3(dbl[:, rank:])
    width = dbl.shape[1] - rank
    lhs = jnp.concatenate(pieces, axis=1)
    rows = lax.broadcasted_iota(jnp.int32, (3 * width, width * LANE), 0)
    cols = lax.broadcasted_iota(jnp.int32, (3 * width, width * LANE), 1)
    entry = cols >> 7
    hit = (rows == entry) | (rows == entry + width) | (rows == entry + 2 * width)
    bc_s[...] = nn(lhs, jnp.where(hit, 1.0, 0.0).astype(BF16))


def prepare(sib, oth, keep, gain, w_in, conv_w, conv_b, w_x, w_dt, dt_bias, a_log, xb, gy):
    rows, inner = xb.shape
    state, width = a_log.shape[0], w_x.shape[0]
    big = pltpu.VMEM((rows, inner), F32)
    edge = pltpu.VMEM((2, state, CH, inner), F32)
    return pl.pallas_call(
        prepare_kernel,
        out_shape=(
            big, big, big, big,
            pltpu.VMEM((3 * rows, LANE), F32),
            pltpu.VMEM((rows, width), F32),
            pltpu.VMEM((2 * CH, inner), F32),
            edge, edge,
            pltpu.VMEM((4 * state + 8, inner), F32),
            big, big,
            pltpu.VMEM((rows, 2 * state * LANE), F32),
            pltpu.VMEM((state, CH, inner), F32),
            pltpu.VMEM((2, rows // 2 // CH, state, CH, inner), F32),
        ),
        scratch_shapes=[pltpu.VMEM((4 * state, CH, inner), F32)],
        compiler_params=params(8),
        name="prepare",
    )(sib, oth, keep, gain, w_in, conv_w, conv_b, w_x, w_dt, dt_bias, a_log, xb, gy)


def summary_parts(ref_value, state):
    return [ref_value[i * state : (i + 1) * state] for i in range(4)]


def pair_kernel(a2_s, mine, theirs, out):
    state, half = a2_s.shape[0], out.shape[1]
    core = lax.axis_index("seq") & 1
    cols = pl.ds(pl.multiple_of(core * half, half), half)
    a2 = half_a2(a2_s, half)
    me, it = mine[:, cols], theirs[:, cols]
    low, high = jnp.where(core == 1, it, me), jnp.where(core == 1, me, it)
    put_total(out, joined(low, high, a2, state), state)


def joined(low, high, a2, state):
    low_f, low_r = low[4 * state : 4 * state + 1], low[4 * state + 1 : 4 * state + 2]
    high_f, high_r = high[4 * state : 4 * state + 1], high[4 * state + 1 : 4 * state + 2]
    lows, highs = summary_parts(low, state), summary_parts(high, state)
    return [
        lows[0] * jnp.exp2(high_f * a2) + highs[0],
        lows[1] * jnp.exp2(high_r * a2) + highs[1],
        highs[2] * jnp.exp2(low_r * a2) + lows[2],
        highs[3] * jnp.exp2(low_f * a2) + lows[3],
        low_f + high_f,
        low_r + high_r,
    ]


def put_total(out, parts, state):
    for i in range(4):
        out[i * state : (i + 1) * state] = parts[i]
    rest = jnp.zeros((out.shape[0] - 4 * state - 2, out.shape[1]), F32)
    out[4 * state :] = jnp.concatenate([parts[4], parts[5], rest], axis=0)


def half_a2(a2_s, half):
    core = lax.axis_index("seq") & 1
    cols = pl.ds(pl.multiple_of(core * half, half), half)
    return jnp.concatenate([a2_s[n, 0:1, cols] for n in range(a2_s.shape[0])], axis=0)


def stage_kernel(first, halves, a2_s, *refs):
    outs = 1 + len(halves) if halves else 2
    members, out, held = refs[: -outs - 1], refs[-outs - 1 : -1], refs[-1]
    count = len(members)
    state, half = a2_s.shape[0], out[0].shape[1]
    a2 = half_a2(a2_s, half)
    at = (lax.axis_index("seq") >> first) & (count - 1)
    for i, ref in enumerate(members):
        held[at ^ i] = ref[...]
    zero, none = jnp.zeros((state, half), F32), jnp.zeros((1, half), F32)

    def run_through(order, rows, reach):
        run = [zero, zero, none, none]
        seen = list(run)
        for i in order:
            seen = [jnp.where(at == i, now, old) for now, old in zip(run, seen)]
            df, dr = held[i, 4 * state : 4 * state + 1], held[i, 4 * state + 1 : 4 * state + 2]
            decays = [jnp.exp2((df, dr)[w] * a2) for w in reach]
            run = [run[k] * decays[k] + held[i, rows[k] * state : (rows[k] + 1) * state] for k in range(2)] + [
                run[2] + df,
                run[3] + dr,
            ]
        return run, seen

    right, seen = run_through(range(count), (0, 1), (0, 1))
    left, seen_left = run_through(range(count - 1, -1, -1), (2, 3), (1, 0))
    enter = out[0]
    enter[:state], enter[state : 2 * state] = seen[0], seen[1]
    enter[2 * state : 3 * state], enter[3 * state : 4 * state] = seen_left[0], seen_left[1]
    blank = jnp.zeros((CH, half), F32)
    enter[4 * state :] = jnp.concatenate([seen[2], seen[3], seen_left[2], seen_left[3], blank[:4]], axis=0)
    sums = jnp.concatenate([right[2], right[3], blank[:6]], axis=0)
    if halves:
        me = lax.axis_index("seq")
        for ref, apart in zip(out[1:], halves):
            later = (me ^ apart) > me
            ref[:state] = jnp.where(later, right[0], left[0])
            ref[state : 2 * state] = jnp.where(later, right[1], left[1])
            ref[2 * state :] = sums
    else:
        for i, value in enumerate((right[0], right[1], left[0], left[1])):
            out[1][i * state : (i + 1) * state] = value
        out[1][4 * state :] = sums


def last_kernel(first, a2_s, *refs):
    theirs, out, held = refs[:-2], refs[-2], refs[-1]
    count = len(theirs) + 1
    state, half = a2_s.shape[0], out.shape[1]
    a2 = half_a2(a2_s, half)
    at = (lax.axis_index("seq") >> first) & (count - 1)
    held[at] = jnp.zeros(held.shape[1:], F32)
    for i, ref in enumerate(theirs):
        held[at ^ (i + 1)] = ref[...]

    def run_through(order, reach, inside):
        run = [jnp.zeros((state, half), F32)] * 2
        for i in order:
            sums = held[i, 2 * state : 2 * state + 1], held[i, 2 * state + 1 : 2 * state + 2]
            for k in range(2):
                longer = run[k] * jnp.exp2(sums[reach[k]] * a2) + held[i, k * state : (k + 1) * state]
                run[k] = jnp.where(inside(i), longer, run[k])
        return run

    found = run_through(range(count - 1), (0, 1), lambda i: i < at)
    found = found + run_through(range(count - 1, 0, -1), (1, 0), lambda i: i > at)
    for i in range(4):
        out[i * state : (i + 1) * state] = found[i]


def pair(a2_s, mine, theirs):
    rows, inner = mine.shape
    return pl.pallas_call(
        pair_kernel,
        out_shape=jax.ShapeDtypeStruct((rows, inner // 2), F32),
        compiler_params=params(2),
        name="pair",
    )(a2_s, mine, theirs)


def stage(first, halves, a2_s, members):
    shape = jax.ShapeDtypeStruct(members[0].shape, F32)
    part = jax.ShapeDtypeStruct((2 * a2_s.shape[0] + CH, members[0].shape[1]), F32)
    return pl.pallas_call(
        lambda *refs: stage_kernel(first, halves, *refs),
        out_shape=(shape,) + (part,) * len(halves) if halves else (shape, shape),
        scratch_shapes=[pltpu.VMEM((len(members),) + members[0].shape, F32)],
        compiler_params=params(4),
        name="stage",
    )(a2_s, *members)


def last_stage(first, a2_s, theirs):
    return pl.pallas_call(
        lambda *refs: last_kernel(first, *refs),
        out_shape=jax.ShapeDtypeStruct((4 * a2_s.shape[0], theirs[0].shape[1]), F32),
        scratch_shapes=[pltpu.VMEM((len(theirs) + 1,) + theirs[0].shape, F32)],
        compiler_params=params(4),
        name="stage",
    )(a2_s, *theirs)


def enter_kernel(a2_s, *refs):
    stages, out = refs[:-1], refs[-1]
    state, half = a2_s.shape[0], out.shape[1]
    a2 = half_a2(a2_s, half)
    value = [stages[-1][i * state : (i + 1) * state] for i in range(4)]
    for ref in reversed(stages[:-1]):
        reach = [ref[4 * state + i : 4 * state + i + 1] for i in range(4)]
        value = [
            ref[i * state : (i + 1) * state] + value[i] * jnp.exp2(reach[w] * a2)
            for i, w in ((0, 0), (1, 1), (2, 3), (3, 2))
        ]
    for i in range(4):
        out[i * state : (i + 1) * state] = value[i]


def enter(a2_s, stages):
    half = stages[0].shape[1]
    return pl.pallas_call(
        enter_kernel,
        out_shape=jax.ShapeDtypeStruct((4 * a2_s.shape[0], half), F32),
        compiler_params=params(2),
        name="enter",
    )(a2_s, *stages)


def carry_in(car_s, a2_s, mine_half, other_half, sibling):
    state, inner = a2_s.shape[0], a2_s.shape[2]
    half = inner // 2
    odd = (lax.axis_index("seq") & 1) == 1
    a2 = jnp.concatenate([a2_s[n, 0:1, :] for n in range(state)], axis=0)
    left, right = jnp.where(odd, other_half[...], mine_half[...]), jnp.where(odd, mine_half[...], other_half[...])
    into = jnp.concatenate([left, right], axis=1)
    df, dr = sibling[4 * state : 4 * state + 1], sibling[4 * state + 1 : 4 * state + 2]
    for i, reach, through in ((0, df, odd), (1, dr, odd), (2, dr, ~odd), (3, df, ~odd)):
        rows = slice(i * state, (i + 1) * state)
        value = jnp.where(through, into[rows] * jnp.exp2(reach * a2) + sibling[rows], into[rows])
        for n in range(state):
            car_s[i * state + n] = jnp.broadcast_to(value[n : n + 1], (CH, inner))


def forward_kernel(
    mine_half, other_half, sibling, sx, de_s, dx_s, bc_s, a2_s, decay,
    y_s, h_s, car_o,
    before_s,
):
    rows2, inner = de_s.shape
    length = rows2 // 2
    steps = length // CH
    tiles = inner // LANE
    state = a2_s.shape[0]
    carry_in(car_o, a2_s, mine_half, other_half, sibling)
    y_s[...] = jnp.zeros(y_s.shape, F32)
    group = 4
    cols_of = [slice(t * LANE, (t + 1) * LANE) for t in range(tiles)]
    for dirn in range(2):
        order = list(range(steps)) if dirn == 0 else list(range(steps - 1, -1, -1))
        base = dirn * length
        s_row = 0 if dirn == 0 else 2
        for cols in cols_of:
            total = jnp.zeros((CH, LANE), F32)
            for j in range(steps):
                total = total + de_s[base + j * CH : base + (j + 1) * CH, cols]
            before_s[:, cols] = outside_sum(total, dirn == 0)

        def some(g, carry, dirn=dirn, order=order, base=base, s_row=s_row):
            n0 = g * group
            at_b, at_c = lanes_of(n0, group), lanes_of(state + n0, group)
            h = {}
            for n in range(group):
                for t, cols in enumerate(cols_of):
                    into = jnp.exp2(before_s[:, cols] * a2_s[n0 + n, :, cols]) * car_o[s_row * state + n0 + n, :, cols]
                    h[n, t] = sx[dirn, n0 + n, :, cols] + into
                    h_s[dirn, 0, n0 + n, :, cols] = h[n, t]
            for at, j in enumerate(order):
                rows = slice(base + j * CH, base + (j + 1) * CH)
                dx = [dx_s[rows, c] for c in cols_of]
                y = [None] * tiles
                for n in range(group):
                    b_n, c_n = bc_s[rows, at_b[n]], bc_s[rows, at_c[n]]
                    for t, cols in enumerate(cols_of):
                        h[n, t] = decay[dirn, at, n0 + n, :, cols] * h[n, t] + dx[t] * b_n
                        h_s[dirn, at + 1, n0 + n, :, cols] = h[n, t]
                        term = h[n, t] * c_n
                        y[t] = term if n == 0 else y[t] + term
                for t, cols in enumerate(cols_of):
                    y_s[rows, cols] += y[t]
            return carry

        lax.fori_loop(0, state // group, some, 0)


def forward(mine_half, other_half, sibling, sx, de, dx, bc, a2, decay):
    rows2, inner = de.shape
    state = a2.shape[0]
    steps = rows2 // 2 // CH
    return pl.pallas_call(
        forward_kernel,
        out_shape=(
            jax.ShapeDtypeStruct((rows2, inner), F32),
            jax.ShapeDtypeStruct((2, steps + 1, state, CH, inner), F32),
            jax.ShapeDtypeStruct((4 * state, CH, inner), F32),
        ),
        scratch_shapes=[pltpu.VMEM((CH, inner), F32)],
        compiler_params=params(4),
        name="forward",
    )(mine_half, other_half, sibling, sx, de, dx, bc, a2, decay)


def ready_kernel(
    rank, tok, gout, gain, w_in, w_out, d_skip, z, go, conv, xc, gy,
    x_o, g_o, nth_o, ntl_o, gh_o, gl_o, wih_o, wil_o, wfh_o, wfl_o, woh_o, wol_o, vfh_o, vfl_o,
    gate_o, zgrad_o, cgrad_o, xch_o, xcl_o, skip_o, pickb_o, pickc_o,
):
    feat, inner = gain.shape[1], w_out.shape[0]
    x = ordered(tok)
    x_o[...] = x
    g = ordered(gout)
    g_o[...] = g
    high, low = both_orders(normalize(x, gain[...])[1])
    nth_o[...] = high.astype(F32).T.astype(BF16)
    ntl_o[...] = low.astype(F32).T.astype(BF16)
    gh_o[...], gl_o[...] = both_orders(g)
    flip = flip_matrix(feat)
    high, low = split(w_in[...])
    wih_o[...], wil_o[...] = high, low
    wfh_o[...], wfl_o[...] = nn(flip, high).astype(BF16), nn(flip, low).astype(BF16)
    high, low = split(w_out[...])
    woh_o[...], wol_o[...] = high, low
    vfh_o[...], vfl_o[...] = nn(high, flip).astype(BF16), nn(low, flip).astype(BF16)
    xch_o[...], xcl_o[...] = split(xc[...])
    for lt in range(inner // LANE):
        cols = slice(lt * LANE, (lt + 1) * LANE)
        zt, v = z[:, cols], conv[:, cols]
        s = sigmoid(zt)
        gate_o[:, cols] = zt * s
        zgrad_o[:, cols] = go[:, cols] * (s * (1.0 + zt * (1.0 - s)))
        s = sigmoid(v)
        cgrad_o[:, cols] = s * (1.0 + v * (1.0 - s))
        skip_o[:, cols] = jnp.sum(gy[:, cols] * xc[:, cols], axis=0, keepdims=True)
    row = lax.broadcasted_iota(jnp.int32, pickb_o.shape, 0) >> 7
    col = lax.broadcasted_iota(jnp.int32, pickb_o.shape, 1)
    pickb_o[...] = jnp.where(col == row + rank, 1.0, 0.0).astype(BF16)
    pickc_o[...] = jnp.where(col == row + (rank + pickb_o.shape[0] // LANE), 1.0, 0.0).astype(BF16)


def ready(rank, state, tok, gout, gain, w_in, w_out, d_skip, z, go, conv, xc, gy):
    length, feat = tok.shape
    rows2, inner = z.shape
    f32 = lambda *dims: jax.ShapeDtypeStruct(dims, F32)
    b16 = lambda *dims: jax.ShapeDtypeStruct(dims, BF16)
    both = lambda *dims: (b16(*dims), b16(*dims))
    return pl.pallas_call(
        lambda *refs: ready_kernel(rank, *refs),
        out_shape=(f32(length, feat), f32(length, feat))
        + both(feat, rows2) + both(rows2, feat) + both(feat, 2 * inner) + both(feat, 2 * inner)
        + both(inner, feat) + both(inner, feat)
        + (f32(rows2, inner), f32(rows2, inner), f32(rows2, inner))
        + both(rows2, inner) + (f32(1, inner),) + both(state * LANE, LANE),
        compiler_params=params(8),
        name="ready",
    )(tok, gout, gain, w_in, w_out, d_skip, z, go, conv, xc, gy)


def early_kernel(
    rs_bits, x, nth, ntl, gh, gl, woh, wol, vfh, vfl, gate, zgrad, d_skip, xc, y_s,
    mixed_o, gzh_o, gzl_o, pieces_o,
):
    rows2, inner = xc.shape
    length = rows2 // 2
    y = y_s[...] + d_skip[...] * xc[...]
    gz = split(zgrad[...] * y)
    gzh_o[...], gzl_o[...] = gz
    out = split(y * gate[...])
    gw_out = mm(tn, out, (gh[...], gl[...]))
    gw_in = mm(nn, (nth[...], ntl[...]), gz)
    put_pieces(rs_bits, pieces_o, [(gw_in, None), (gw_out, None)])
    fwd = mm(nn, (out[0][:length], out[1][:length]), (woh[...], wol[...]))
    rev = mm(nn, (out[0][length:], out[1][length:]), (vfh[...], vfl[...]))
    store_ordered(mixed_o, x[...] + (fwd + rev))


def early(rs_bits, x, nth, ntl, gh, gl, woh, wol, vfh, vfl, gate, zgrad, d_skip, xc, y):
    length, feat = x.shape
    rows2, inner = xc.shape
    pieces = 1 << rs_bits
    tall = 2 * feat * inner // LANE // pieces
    gz = jax.ShapeDtypeStruct((rows2, inner), BF16)
    return pl.pallas_call(
        lambda *refs: early_kernel(rs_bits, *refs),
        out_shape=(jax.ShapeDtypeStruct((length, feat), F32), gz, gz, jax.ShapeDtypeStruct((pieces, tall, LANE), F32)),
        compiler_params=params(8),
        name="early",
    )(x, nth, ntl, gh, gl, woh, wol, vfh, vfl, gate, zgrad, d_skip, xc, y)


def put_pieces(rs_bits, pieces_o, arrays, few=None):
    pieces = 1 << rs_bits
    mine = reverse_bits(lax.axis_index("seq"), rs_bits)
    for p in range(pieces):
        slot = mine ^ reverse_bits(p, rs_bits)
        at = 0
        for value, more in arrays:
            tall = value.shape[0] // pieces
            for lt in range(value.shape[1] // LANE):
                where = (slice(p * tall, (p + 1) * tall), slice(lt * LANE, (lt + 1) * LANE))
                block = value[where] if more is None else value[where] + more[where]
                pieces_o[slot, at : at + tall, :] = block
                at += tall
        if few is not None:
            tiles = few.shape[1] // LANE
            top = pieces // tiles * CH
            rest = (few.shape[0] - top) * tiles // pieces
            rb, lt = p // tiles, p % tiles
            pieces_o[slot, at : at + CH, :] = few[rb * CH : (rb + 1) * CH, lt * LANE : (lt + 1) * LANE]
            rows = []
            for v in range(rest * p, rest * (p + 1)):
                rb, lt = top + v // tiles, v % tiles
                rows.append(few[rb : rb + 1, lt * LANE : (lt + 1) * LANE])
            zeros = jnp.zeros((4, LANE), F32)
            rows = [zeros] + rows + [zeros[: 4 - rest]]
            pieces_o[slot, at + CH : at + 2 * CH, :] = jnp.concatenate(rows, axis=0)
            pieces_o[slot, at + 2 * CH : at + 3 * CH, :] = jnp.zeros((CH, LANE), F32)


def row_vectors(rows):
    return jnp.concatenate(
        [rows[b : b + 1, lt * LANE : (lt + 1) * LANE] for b in range(3) for lt in range(rows.shape[1] // LANE)],
        axis=0,
    )


def backward_kernel(
    dirn, mx, car, h_s, de_s, dx_s, bc_s, a2_s, decay, gy,
    sb_s, sa_s, accb, accc, ga_s,
    after_s,
):
    rows2, inner = de_s.shape
    length = rows2 // 2
    steps = length // CH
    tiles = inner // LANE
    state = a2_s.shape[0]
    order = list(range(steps)) if dirn == 0 else list(range(steps - 1, -1, -1))
    base = dirn * length
    m_row = 3 if dirn == 0 else 1
    group = 2
    cols_of = [slice(t * LANE, (t + 1) * LANE) for t in range(tiles)]
    sb_s[...] = jnp.zeros(sb_s.shape, F32)
    sa_s[...] = jnp.zeros(sa_s.shape, F32)
    for cols in cols_of:
        total = jnp.zeros((CH, LANE), F32)
        for j in range(steps):
            total = total + de_s[base + j * CH : base + (j + 1) * CH, cols]
        after_s[:, cols] = outside_sum(total, dirn != 0)

    def some(g, carry):
        n0 = g * group
        at_b, at_c = lanes_of(n0, group), lanes_of(state + n0, group)
        a2, q, ga = {}, {}, {}
        for n in range(group):
            for t, cols in enumerate(cols_of):
                a2[n, t] = a2_s[n0 + n, :, cols]
                into = jnp.exp2(after_s[:, cols] * a2[n, t]) * car[m_row * state + n0 + n, :, cols]
                q[n, t] = mx[dirn, n0 + n, :, cols] + into
                ga[n, t] = jnp.zeros((CH, LANE), F32)
        for at in range(steps - 1, -1, -1):
            j = order[at]
            rows = slice(base + j * CH, base + (j + 1) * CH)
            here = slice(j * CH, (j + 1) * CH)
            de = [de_s[rows, c] for c in cols_of]
            dx = [dx_s[rows, c] for c in cols_of]
            gyj = [gy[rows, c] for c in cols_of]
            sb, sa = [None] * tiles, [None] * tiles
            for n in range(group):
                b_n, c_n = bc_s[rows, at_b[n]], bc_s[rows, at_c[n]]
                to_b = to_c = None
                for t, cols in enumerate(cols_of):
                    gh = gyj[t] * c_n + q[n, t]
                    term_c = gyj[t] * h_s[dirn, at + 1, n0 + n, :, cols]
                    term_b = gh * dx[t]
                    to_b = term_b if t == 0 else to_b + term_b
                    to_c = term_c if t == 0 else to_c + term_c
                    q[n, t] = decay[dirn, at, n0 + n, :, cols] * gh
                    r = q[n, t] * h_s[dirn, at, n0 + n, :, cols]
                    ga[n, t] = ga[n, t] + de[t] * r
                    sb[t] = gh * b_n if n == 0 else sb[t] + gh * b_n
                    sa[t] = a2[n, t] * r if n == 0 else sa[t] + a2[n, t] * r
                accb[here, at_b[n]] = to_b
                accc[here, at_b[n]] = to_c
            for t, cols in enumerate(cols_of):
                sb_s[here, cols] += sb[t]
                sa_s[here, cols] += sa[t]
        for n in range(group):
            for t, cols in enumerate(cols_of):
                ga_s[n0 + n, :, cols] = ga[n, t]
        return carry

    lax.fori_loop(0, state // group, some, 0)


def backward(dirn, mx, car, h, de, dx, bc, a2, decay, gy):
    rows2, inner = de.shape
    state = a2.shape[0]
    length = rows2 // 2
    half = jax.ShapeDtypeStruct((length, inner), F32)
    acc = jax.ShapeDtypeStruct((length, state * LANE), F32)
    return pl.pallas_call(
        lambda *refs: backward_kernel(dirn, *refs),
        out_shape=(half, half, acc, acc, jax.ShapeDtypeStruct((state, CH, inner), F32)),
        scratch_shapes=[pltpu.VMEM((CH, inner), F32)],
        compiler_params=params(4),
        name="backward",
    )(mx, car, h, de, dx, bc, a2, decay, gy)


def inner_kernel(
    pad, conv_w, w_x, w_dt, d_skip, a2_s,
    xb, gy, xc, dt, sig, cgrad, mask, dbl, xbh, xch, xcl, skip_sum, pick_b, pick_c,
    sb_f, sa_f, accb_f, accc_f, ga_f, sb_r, sa_r, accb_r, accc_r, ga_r,
    gxh_o, gxl_o, halo_o, few_o,
    gp_s, gpre_s, xcg_s,
):
    inner, rank = w_x.shape[1], w_dt.shape[0]
    state = a2_s.shape[0]
    rows2 = xb.shape[0]
    length = rows2 // 2
    steps = length // CH
    tiles = inner // LANE
    sub = sub_iota()

    bias_rows = []
    for lt in range(tiles):
        cols = slice(lt * LANE, (lt + 1) * LANE)
        bias = jnp.zeros((1, LANE), F32)
        for dirn, sb, sa in ((0, sb_f, sa_f), (1, sb_r, sa_r)):
            rows = slice(dirn * length, (dirn + 1) * length)
            g_pre = (xc[rows, cols] * sb[:, cols] + LN2 * sa[:, cols]) * sig[rows, cols]
            gpre_s[rows, cols] = g_pre
            xcg_s[rows, cols] = d_skip[:, cols] * gy[rows, cols] + dt[rows, cols] * sb[:, cols]
            bias = bias + jnp.sum(g_pre, axis=0, keepdims=True)
        bias_rows.append(bias)

    b_parts = split(jnp.concatenate([accb_f[...], accb_r[...]], axis=0))
    c_parts = split(jnp.concatenate([accc_f[...], accc_r[...]], axis=0))
    g_bc = (nn(b_parts[0], pick_b[...]) + nn(b_parts[1], pick_b[...])) + (
        nn(c_parts[0], pick_c[...]) + nn(c_parts[1], pick_c[...])
    )
    gpre_parts = split(gpre_s[...])
    w_dt_parts = split(w_dt[...])
    g_rank = mm(nt, gpre_parts, w_dt_parts)
    width = rank + 2 * state
    g_dbl = jnp.concatenate([g_rank, g_bc[:, rank:width]], axis=1)
    g_dbl_parts = split(g_dbl)
    few_o[width + state : width + state + rank, :] = mm(tn, split(dbl[:, :rank]), gpre_parts)
    few_o[:width, :] = mm(tn, g_dbl_parts, (xch[...], xcl[...]))
    xcg_s[...] += mm(nn, g_dbl_parts, split(w_x[...]))

    cw_rows = [[] for _ in range(4)]
    cb_rows = []
    halo_f, halo_r = [], []
    for lt in range(tiles):
        cols = slice(lt * LANE, (lt + 1) * LANE)
        taps = [conv_w[k : k + 1, cols] for k in range(4)]
        xbh_t = xbh[:, cols]
        xf = [xb[j * CH : (j + 1) * CH, cols] for j in range(steps)]
        xf = [
            jnp.where(sub == 0, xbh_t[b : b + 1], pltpu.roll(xf[steps - 3 + b], 1, 0))
            for b in range(3)
        ] + xf
        gcw = [jnp.zeros((CH, LANE), F32) for _ in range(4)]
        gcb = jnp.zeros((CH, LANE), F32)
        grads = [None] * (steps + 3)
        for j in range(steps):
            rows = slice(j * CH, (j + 1) * CH)
            u = xcg_s[rows, cols] * cgrad[rows, cols]
            gcb = gcb + u
            for k in range(4):
                uk = u if k == 0 else u * mask[(k - 1) * length + j * CH : (k - 1) * length + (j + 1) * CH, :]
                gcw[k] = gcw[k] + uk * xf[j + 3 - k]
                add = taps[k] * uk
                at = j + 3 - k
                grads[at] = add if grads[at] is None else grads[at] + add
        for b in range(3):
            halo_f.append(grads[b][0:1])
            at = steps + b
            grads[at] = grads[at] + jnp.where(sub == CH - 1, 0.0, pltpu.roll(grads[b], CH - 1, 0))
        for j in range(steps):
            gp_s[j * CH : (j + 1) * CH, cols] = grads[j + 3]
        xr = [xb[length + j * CH : length + (j + 1) * CH, cols] for j in range(steps)]
        xr = xr + [
            jnp.where(sub == CH - 1, xbh_t[8 + b : 9 + b], pltpu.roll(xr[b], CH - 1, 0))
            for b in range(3)
        ]
        grads = [None] * (steps + 3)
        for j in range(steps):
            rows = slice(length + j * CH, length + (j + 1) * CH)
            u = xcg_s[rows, cols] * cgrad[rows, cols]
            gcb = gcb + u
            for k in range(4):
                uk = u if k == 0 else u * mask[(k + 2) * length + j * CH : (k + 2) * length + (j + 1) * CH, :]
                gcw[k] = gcw[k] + uk * xr[j + k]
                add = taps[k] * uk
                grads[j + k] = add if grads[j + k] is None else grads[j + k] + add
        for b in range(3):
            halo_r.append(grads[steps + b][CH - 1 : CH])
            grads[b] = grads[b] + jnp.where(sub == 0, 0.0, pltpu.roll(grads[steps + b], 1, 0))
        for j in range(steps):
            gp_s[length + j * CH : length + (j + 1) * CH, cols] = grads[j]
        for k in range(4):
            cw_rows[k].append(jnp.sum(gcw[k], axis=0, keepdims=True))
        cb_rows.append(jnp.sum(gcb, axis=0, keepdims=True))
    pad_col = spread(pad[...].astype(F32))
    pad_all = jnp.concatenate([pad_col, pad_col], axis=0)
    for lt in range(tiles):
        cols = slice(lt * LANE, (lt + 1) * LANE)
        gxh_o[:, cols], gxl_o[:, cols] = split(gp_s[:, cols] * pad_all)

    blank = jnp.zeros((5, inner), F32)

    def gather(found):
        return jnp.concatenate(
            [jnp.concatenate([found[lt * 3 + b] for lt in range(tiles)], axis=1) for b in range(3)]
            + [blank],
            axis=0,
        )

    halo_o[...] = jnp.concatenate([gather(halo_f), gather(halo_r)], axis=0)
    ga = jnp.concatenate(
        [jnp.sum(ga_f[n] + ga_r[n], axis=0, keepdims=True) * (a2_s[n, 0:1, :] * LN2) for n in range(state)], axis=0
    )
    few_o[width : width + state, :] = ga
    few_o[width + state + rank :, :] = jnp.concatenate(
        [jnp.concatenate(cw_rows[k], axis=1) for k in range(4)]
        + [
            jnp.concatenate(cb_rows, axis=1),
            jnp.concatenate(bias_rows, axis=1),
            skip_sum[...],
            jnp.zeros((1, inner), F32),
        ],
        axis=0,
    )


def inner_back(*arrays):
    w_x, w_dt, a2, xb = arrays[2], arrays[3], arrays[5], arrays[6]
    rows2, inner = xb.shape
    few = w_x.shape[0] + a2.shape[0] + w_dt.shape[0] + CH
    big = pltpu.VMEM((rows2, inner), F32)
    part = jax.ShapeDtypeStruct((rows2, inner), BF16)
    return pl.pallas_call(
        inner_kernel,
        out_shape=(
            part, part,
            jax.ShapeDtypeStruct((2 * CH, inner), F32),
            jax.ShapeDtypeStruct((few, inner), F32),
        ),
        scratch_shapes=[big, big, big],
        compiler_params=params(8),
        name="inner",
    )(*arrays)


def tail_kernel(
    rs_bits, sib, oth, gain, x_s, g_s, nth, ntl, wih, wil, wfh, wfl, gzh, gzl, gxh, gxl, halo, few,
    gtok_o, to_left_o, to_right_o, pieces_o,
):
    feat = gain.shape[1]
    rows2, inner = gxh.shape
    length = rows2 // 2
    left, right = pick_sides(sib[...], oth[...])
    factor_l, hn_l = normalize(left, gain[...])
    factor_r, hn_r = normalize(right, gain[...])
    flip = flip_matrix(feat)
    lh, ll = split(hn_l)
    rh, rl = split(hn_r)
    edge = (
        jnp.concatenate([lh, nn(rh, flip).astype(BF16)], axis=0),
        jnp.concatenate([ll, nn(rl, flip).astype(BF16)], axis=0),
    )
    x, g = x_s[...], g_s[...]
    factor = normalize(x, gain[...])[0]
    gh_parts = split(halo[...])
    gw_in = mm(nn, (nth[...], ntl[...]), (gxh[...], gxl[...]))
    gw_in_halo = mm(tn, edge, gh_parts)
    w_xb = (wih[:, :inner], wil[:, :inner])
    g_normed = (
        mm(nt, (gxh[:length], gxl[:length]), w_xb)
        + mm(nt, (gzh[:length], gzl[:length]), (wih[:, inner:], wil[:, inner:]))
    ) + (
        mm(nt, (gxh[length:], gxl[length:]), (wfh[:, :inner], wfl[:, :inner]))
        + mm(nt, (gzh[length:], gzl[length:]), (wfh[:, inner:], wfl[:, inner:]))
    )
    back_h = mm(nt, gh_parts, w_xb)
    gn_l = back_h[:CH]
    gn_r = flipped(back_h[CH:])

    def norm_back(x, factor, gn):
        scaled = gn * gain[...]
        return factor * scaled - x * (factor * factor * factor * jnp.mean(scaled * x, axis=1, keepdims=True))

    store_ordered(gtok_o, g + norm_back(x, factor, g_normed))
    to_left = norm_back(left, factor_l, gn_l)
    to_right = norm_back(right, factor_r, gn_r)
    to_left_o[...] = to_left
    to_right_o[...] = to_right
    three = lax.broadcasted_iota(jnp.int32, (CH, feat), 0) < 3
    g_gain = (
        jnp.sum(g_normed * (x * factor), axis=0, keepdims=True)
        + jnp.sum(jnp.where(three, gn_l * (left * factor_l) + gn_r * (right * factor_r), 0.0), axis=0, keepdims=True)
    )
    few_all = jnp.concatenate(
        [few[: few.shape[0] - CH, :], few[few.shape[0] - CH : few.shape[0] - 1, :]]
        + [jnp.concatenate([g_gain, jnp.zeros((1, inner - feat), F32)], axis=1)],
        axis=0,
    )
    put_pieces(rs_bits, pieces_o, [(gw_in, gw_in_halo)], few_all)
    pieces = 1 << rs_bits
    me = lax.axis_index("seq") & (pieces - 1)
    mine = reverse_bits(me, rs_bits)
    at = pieces_o.shape[1] - 2 * CH

    @pl.when(me < pieces - 1)
    def _():
        slot = mine ^ reverse_bits(me + 1, rs_bits)
        vectors = row_vectors(to_right)
        pieces_o[slot, at : at + 4, :] = vectors[:4]
        pieces_o[slot, at + CH : at + CH + 2, :] = vectors[4:]

    @pl.when(me > 0)
    def _():
        slot = mine ^ reverse_bits(me - 1, rs_bits)
        pieces_o[slot, at + CH + 2 : at + 2 * CH, :] = row_vectors(to_left)


def reverse_bits(value, bits):
    found = 0
    for i in range(bits):
        found = found | (((value >> i) & 1) << (bits - 1 - i))
    return found


def tail(rs_bits, *arrays):
    x, gxh = arrays[3], arrays[13]
    length, feat = x.shape
    inner = gxh.shape[1]
    pieces = 1 << rs_bits
    tall = feat * inner // LANE // pieces + 3 * CH
    return pl.pallas_call(
        lambda *refs: tail_kernel(rs_bits, *refs),
        out_shape=(
            jax.ShapeDtypeStruct((length, feat), F32),
            jax.ShapeDtypeStruct((CH, feat), F32),
            jax.ShapeDtypeStruct((CH, feat), F32),
            jax.ShapeDtypeStruct((pieces, tall, LANE), F32),
        ),
        compiler_params=params(8),
        name="tail",
    )(*arrays)


def unpack_kernel(
    rs_bits, near, far, gtok, halo, pad,
    gtok_o, gain_o, w_in_o, conv_w_o, conv_b_o, w_x_o, w_dt_o, dt_bias_o, a_log_o, d_skip_o, w_out_o, few_s, rest_s,
):
    feat = w_in_o.shape[0]
    inner = w_out_o.shape[0]
    tiles = inner // LANE
    pieces = 1 << rs_bits
    mine = reverse_bits(lax.axis_index("seq"), rs_bits)
    in_rows, out_rows = feat // pieces, inner // pieces
    for slot in range(pieces):
        source = near if slot < pieces // 2 else far
        i = slot % (pieces // 2)
        p = reverse_bits(mine ^ slot, rs_bits)
        at = 0
        in_at = pl.ds(pl.multiple_of(p * in_rows, in_rows), in_rows)
        out_at = pl.ds(pl.multiple_of(p * out_rows, out_rows), out_rows)
        for lt in range(tiles):
            w_in_o[in_at, inner + lt * LANE : inner + (lt + 1) * LANE] = source[i, at : at + in_rows, :]
            at += in_rows
        for lt in range(feat // LANE):
            w_out_o[out_at, lt * LANE : (lt + 1) * LANE] = source[i, at : at + out_rows, :]
            at += out_rows
        for lt in range(tiles):
            w_in_o[in_at, lt * LANE : (lt + 1) * LANE] = source[i, at : at + in_rows, :]
            at += in_rows
        few_s[p] = source[i, at : at + CH, :]
        rest_s[p] = source[i, at + CH : at + 2 * CH, :]

    top = pieces // tiles * CH
    total = w_x_o.shape[0] + a_log_o.shape[0] + w_dt_o.shape[0] + CH
    rest = (total - top) * tiles // pieces

    def few_rows(first, count):
        found = []
        for lt in range(tiles):
            if first < top:
                found.append(few_s[first // CH * tiles + lt])
                continue
            rows = []
            for row in range(first, first + count):
                v = (row - top) * tiles + lt
                rows.append(rest_s[v // rest, 4 + v % rest : 5 + v % rest, :])
            found.append(jnp.concatenate(rows, axis=0) if count > 1 else rows[0])
        return jnp.concatenate(found, axis=1)

    width, state = w_x_o.shape[0], a_log_o.shape[0]
    rank = w_dt_o.shape[0]
    w_x_o[...] = jnp.concatenate([few_rows(r, CH) for r in range(0, width, CH)], axis=0)
    at = width
    a_log_o[...] = jnp.concatenate([few_rows(r, CH) for r in range(at, at + state, CH)], axis=0)
    at += state
    w_dt_o[...] = jnp.concatenate([few_rows(r, CH) for r in range(at, at + rank, CH)], axis=0)
    at += rank
    conv_w_o[...] = few_rows(at, 4)
    conv_b_o[...] = few_rows(at + 4, 1)
    dt_bias_o[...] = few_rows(at + 5, 1)
    d_skip_o[...] = few_rows(at + 6, 1)
    gain_o[...] = few_rows(at + 7, 1)[:, :feat]

    length = gtok.shape[0]
    per = feat // LANE
    padded = spread_plain(pad[...].astype(F32), feat)

    def three(first):
        rows = [
            jnp.concatenate([halo[first + b * per + lt : first + b * per + lt + 1, :] for lt in range(per)], axis=1)
            for b in range(3)
        ]
        return rows, jnp.zeros((CH - 3, feat), F32)

    rows, blank = three(0)
    first = jnp.concatenate(rows + [blank], axis=0)
    rows, blank = three(3 * per)
    last = jnp.concatenate([blank] + rows, axis=0)
    gtok_o[...] = gtok[...]
    gtok_o[:CH] = gtok[:CH] + padded[:CH] * first
    gtok_o[length - CH :] = gtok[length - CH :] + padded[length - CH :] * last


def spread_plain(row, width):
    length = row.shape[1]
    rows = lax.broadcasted_iota(jnp.int32, (length, length), 0)
    cols = lax.broadcasted_iota(jnp.int32, (length, length), 1)
    picked = (jnp.where(rows == cols, 1.0, 0.0) * row).astype(BF16)
    return nn(picked, jnp.ones((length, width), BF16))


def unpack(rs_bits, near, far, gtok, halo, pad, state, rank):
    length, feat = gtok.shape
    pieces = 1 << rs_bits
    inner = state[1]
    width = rank + 2 * state[0]
    shape = lambda *dims: jax.ShapeDtypeStruct(dims, F32)
    return pl.pallas_call(
        lambda *refs: unpack_kernel(rs_bits, *refs),
        out_shape=(
            shape(length, feat),
            shape(1, feat),
            shape(feat, 2 * inner),
            shape(4, inner),
            shape(1, inner),
            shape(width, inner),
            shape(rank, inner),
            shape(1, inner),
            shape(state[0], inner),
            shape(1, inner),
            shape(inner, feat),
        ),
        scratch_shapes=[pltpu.VMEM((pieces, CH, LANE), F32)] * 2,
        compiler_params=params(6),
        name="unpack",
    )(near, far, gtok, halo, pad)


def body(tokens, resets, pad_mask, norm_gain, w_in, conv_w, conv_b, w_x, w_dt, dt_bias, a_log, d_skip, w_out, grad_out):
    count = lax.axis_size("seq")
    bits = count.bit_length() - 1
    rs_bits = min(5, bits)
    length = tokens.shape[0]
    keep_row, pad_row = resets.reshape(1, length), pad_mask.reshape(1, length)

    def exchange(value, apart):
        return lax.ppermute(value, "seq", [(i, i ^ apart) for i in range(count)])

    def swap(value, bit):
        return exchange(value, 1 << bit)

    across = [(i, i + 1) for i in range(1, count - 1, 2)] + [(i + 1, i) for i in range(1, count - 1, 2)]

    def swap_across(value):
        return lax.ppermute(value, "seq", across)

    to_sib, to_oth = edges(tokens, keep_row, pad_row)
    oth = swap_across(to_oth)
    sib = swap(to_sib, 0)
    (xb, z, go, gy), kept = project(
        tokens, pad_row, norm_gain, w_in[0], grad_out, w_out[0],
        keep_row, conv_w[0], conv_b, w_x[0].T, w_dt[0], dt_bias, a_log[0].T, d_skip,
    )
    (tok, pad, gain, w_in_0, gout, w_out_0, keep, conv_w_0, conv_b_0, w_x_t, w_dt_0, dt_bias_0, a_log_t, skip) = kept
    xc, dt, sig, conv, mask, dbl, xbh, sx, mx, total, de, dx, bc, a2, decay = prepare(
        sib, oth, keep, gain, w_in_0, conv_w_0, conv_b_0, w_x_t, w_dt_0, dt_bias_0, a_log_t, xb, gy
    )

    sibling = swap(total, 0)
    group = pair(a2, total, sibling)
    group, gate_in = lax.optimization_barrier((group, (z, go, conv, xc, gy)))
    at_hand = ready(w_dt.shape[1], a_log.shape[2], tok, gout, gain, w_in_0, w_out_0, skip, *gate_in)
    stages = []
    steps = [range(first, min(first + 2, bits)) for first in range(1, bits, 2)]
    step = steps[-1]
    distances = [i << step[0] for i in range(1, 1 << len(step))]
    for first_step in steps[:-1]:
        members = [group] + [exchange(group, i << first_step[0]) for i in range(1, 1 << len(first_step))]
        halves = distances if first_step is steps[-2] else ()
        entering, *group = stage(first_step[0], halves, a2, members)
        stages.append(entering)
        if not halves:
            (group,) = group
    group, at_hand = lax.optimization_barrier((group, at_hand))
    theirs = [exchange(value, apart) for value, apart in zip(group, distances)]
    stages.append(last_stage(step[0], a2, theirs))
    mine_half = enter(a2, stages)
    other_half = swap(mine_half, 0)

    y, h, car = forward(mine_half, other_half, sibling, sx, de, dx, bc, a2, decay)
    def reduced(part, step):
        size = part.shape[0] >> len(step)
        total = part[:size]
        for i in range(1, 1 << len(step)):
            slot = reverse_bits(i, len(step))
            total = total + exchange(part[slot * size : (slot + 1) * size], i << step[0])
        return total

    (x, g, nth, ntl, gh, gl, wih, wil, wfh, wfl, woh, wol, vfh, vfl, gate, zgrad, cgrad, xch, xcl, skip_sum,
     pick_b, pick_c) = at_hand
    rs_steps = [range(0, 1)] + [range(first, min(first + 2, rs_bits)) for first in range(1, rs_bits, 2)]
    mixed, gzh, gzl, part_a = early(rs_bits, x, nth, ntl, gh, gl, woh, wol, vfh, vfl, gate, zgrad, skip, xc, y)
    part_a, h = lax.optimization_barrier((part_a, h))
    part_a = reduced(part_a, range(0, 1))
    back_f = backward(0, mx, car, h, de, dx, bc, a2, decay, gy)
    part_a, back_f, h = lax.optimization_barrier((part_a, back_f, h))
    part_a = reduced(part_a, rs_steps[1])
    back_r = backward(1, mx, car, h, de, dx, bc, a2, decay, gy)
    gxh, gxl, halo_g, few = inner_back(
        pad, conv_w_0, w_x_t, w_dt_0, skip, a2,
        xb, gy, xc, dt, sig, cgrad, mask, dbl, xbh, xch, xcl, skip_sum, pick_b, pick_c, *back_f, *back_r,
    )
    part_a, gxh = lax.optimization_barrier((part_a, gxh))
    gtok, to_left, to_right, part_b = tail(
        rs_bits, sib, oth, gain, x, g, nth, ntl, wih, wil, wfh, wfl, gzh, gzl, gxh, gxl, halo_g, few
    )
    part_b = reduced(part_b, rs_steps[0])
    part_b = reduced(part_b, rs_steps[1])
    own = jnp.concatenate([part_a, part_b], axis=1)
    for step in rs_steps[2:]:
        own = reduced(own, step)
    for bit in range(rs_bits, bits):
        own = own + swap(own, bit)
    tall = own.shape[1]
    halo = jnp.concatenate([own[0, tall - 16 : tall - 12], own[0, tall - 8 :]], axis=0)
    if bits > rs_bits:
        pairs = [(i, i + 1) for i in range(count - 1)]
        from_left = lax.ppermute(to_right, "seq", pairs)[:3]
        from_right = lax.ppermute(to_left, "seq", [(j, i) for i, j in pairs])[:3]
        halo = jnp.concatenate([from_left.reshape(-1, LANE), from_right.reshape(-1, LANE)], axis=0)
    own = own[:, : tall - 8]
    for step in reversed(rs_steps[1:]):
        parts = [own] + [exchange(own, reverse_bits(i, len(step)) << step[0]) for i in range(1, 1 << len(step))]
        own = jnp.concatenate(parts, axis=0)
    far = swap(own, 0)
    outs = unpack(rs_bits, own, far, gtok, halo, pad, a_log_t.shape, w_dt.shape[1])
    gtok, g_gain, g_w_in, g_conv_w, g_conv_b, g_w_x, g_w_dt, g_dt_bias, g_a_log, g_d_skip, g_w_out = outs
    return (
        mixed, gtok, g_gain, g_w_in[None], g_conv_w[None], g_conv_b, g_w_x.T[None], g_w_dt[None],
        g_dt_bias, g_a_log.T[None], g_d_skip, g_w_out[None],
    )


def solution(mesh):
    rows, whole = P("seq", None), P()
    return jax.shard_map(
        body,
        mesh=mesh,
        in_specs=(rows, P("seq"), P("seq")) + (whole,) * 10 + (rows,),
        out_specs=(rows, rows) + (whole,) * 10,
        check_vma=False,
    )
```

```python
import jax
import jax.numpy as jnp
from jax import lax
from jax.experimental import pallas as pl
from jax.experimental.pallas import tpu as pltpu
from jax.sharding import PartitionSpec as P

F32 = jnp.float32
BF16 = jnp.bfloat16
EPS = 1e-05
LOG2E = 1.4426950408889634
LN2 = 0.6931471805599453
BIG = 1e9
CH = 8
LANE = 128
MIB = 1024 * 1024


def nn(a, b):
    return lax.dot_general(a, b, (((1,), (0,)), ((), ())), preferred_element_type=F32)


def nt(a, b):
    return lax.dot_general(a, b, (((1,), (1,)), ((), ())), preferred_element_type=F32)


def tn(a, b):
    return lax.dot_general(a, b, (((0,), (0,)), ((), ())), preferred_element_type=F32)


def split(x):
    high = x.astype(BF16)
    return high, (x - high.astype(F32)).astype(BF16)


def split3(x):
    high = x.astype(BF16)
    rest = x - high.astype(F32)
    mid = rest.astype(BF16)
    return high, mid, (rest - mid.astype(F32)).astype(BF16)


def mm(dot, a, b):
    ah, al = a if isinstance(a, tuple) else split(a)
    bh, bl = b if isinstance(b, tuple) else split(b)
    return dot(ah, bh) + (dot(ah, bl) + dot(al, bh))


def flip_matrix(size):
    rows = lax.broadcasted_iota(jnp.int32, (size, size), 0)
    cols = lax.broadcasted_iota(jnp.int32, (size, size), 1)
    return jnp.where(rows + cols == size - 1, 1.0, 0.0).astype(BF16)


def flipped(x):
    flip = flip_matrix(x.shape[1])
    high, mid, low = split3(x)
    return nn(high, flip) + (nn(mid, flip) + nn(low, flip))


def order_matrix(length):
    steps = length // CH
    rows = lax.broadcasted_iota(jnp.int32, (length, length), 0)
    cols = lax.broadcasted_iota(jnp.int32, (length, length), 1)
    token = (rows & (CH - 1)) * steps + (rows >> 3)
    return jnp.where(cols == token, 1.0, 0.0)


def exact(dot, order, x):
    high, mid, low = split3(x)
    order = order.astype(BF16)
    return dot(order, high) + (dot(order, mid) + dot(order, low))


def ordered(ref):
    return exact(nn, order_matrix(ref.shape[0]), ref[...])


def store_ordered(ref, value):
    ref[...] = exact(tn, order_matrix(ref.shape[0]), value)


def spread(row):
    length = row.shape[1]
    picked = (order_matrix(length) * row).astype(BF16)
    return nn(picked, jnp.ones((length, LANE), BF16))


def sigmoid(x):
    return 1.0 / (1.0 + jnp.exp(-x))


def normalize(x, gain):
    factor = lax.rsqrt(jnp.mean(x * x, axis=1, keepdims=True) + EPS)
    return factor, x * factor * gain


def both_orders(normed):
    flip = flip_matrix(normed.shape[1])
    high, low = split(normed)
    return (
        jnp.concatenate([high, nn(high, flip).astype(BF16)], axis=0),
        jnp.concatenate([low, nn(low, flip).astype(BF16)], axis=0),
    )


def params(mib):
    return pltpu.CompilerParams(vmem_limit_bytes=mib * MIB)


def in_hbm(*arrays):
    return tuple(pltpu.with_memory_space_constraint(x, pltpu.HBM) for x in arrays)


def edges_kernel(tok, resets, pad, *refs):
    more = (len(refs) - 5) // 2
    to_sib, to_oth, *kept = refs[more:]
    for ref, kept_o in zip((tok, resets, pad) + refs[:more], kept):
        kept_o[...] = ref[...]
    length, feat = tok.shape
    sub = lax.broadcasted_iota(jnp.int32, (CH, length), 0)
    lane = lax.broadcasted_iota(jnp.int32, (CH, length), 1)
    real = pad[...].astype(F32)
    row = lax.broadcasted_iota(jnp.int32, (CH, feat), 0)
    flags = 1.0 - resets[...].astype(F32)
    flags = jnp.concatenate([flags, jnp.zeros((1, feat - length), F32)], axis=1)

    def message(rows, start):
        col = jnp.sum(jnp.where(lane == sub + start, real, 0.0), axis=1, keepdims=True)
        return jnp.where(row < 3, rows * col, jnp.where(row == 3, flags, 0.0))

    first = message(tok[:CH, :], 0)
    last = message(pltpu.roll(tok[length - CH :, :], 3, 0), length - 3)
    odd = (lax.axis_index("seq") & 1) == 1
    to_sib[...] = jnp.where(odd, first, last)
    to_oth[...] = jnp.where(odd, last, first)


def edges(*arrays):
    shape = jax.ShapeDtypeStruct((CH, arrays[0].shape[1]), F32)
    found = pl.pallas_call(
        edges_kernel,
        out_shape=(shape, shape) + tuple(jax.ShapeDtypeStruct(x.shape, x.dtype) for x in arrays),
        compiler_params=params(8),
        name="edges",
    )(*in_hbm(*arrays))
    return found[0], found[1], found[2:]


def project_kernel(tok, pad, gain, w_in, gout, w_out, xb_o, z_o, go_o, gy_o):
    inner = w_out.shape[0]
    x = ordered(tok)
    normed = normalize(x, gain[...])[1]
    proj = mm(nn, both_orders(normed), split(w_in[...]))
    pad_col = spread(pad[...].astype(F32))
    pad_all = jnp.concatenate([pad_col, pad_col], axis=0)
    g = ordered(gout)
    gh, gl = both_orders(g)
    go = mm(nt, (gh, gl), split(w_out[...]))
    for lt in range(inner // LANE):
        cols = slice(lt * LANE, (lt + 1) * LANE)
        z = proj[:, inner + lt * LANE : inner + (lt + 1) * LANE]
        xb_o[:, cols] = proj[:, cols] * pad_all
        z_o[:, cols] = z
        go_o[:, cols] = go[:, cols]
        gy_o[:, cols] = go[:, cols] * (z * sigmoid(z))


def project(tok, pad, gain, w_in, gout, w_out):
    big = jax.ShapeDtypeStruct((2 * tok.shape[0], w_out.shape[0]), F32)
    return pl.pallas_call(
        project_kernel,
        out_shape=(big, big, big, big),
        compiler_params=params(8),
        name="project",
    )(tok, pad, gain, w_in, gout, w_out)


def pick_sides(from_sibling, from_other):
    odd = (lax.axis_index("seq") & 1) == 1
    left = jnp.where(odd, from_sibling, from_other)
    right = jnp.where(odd, from_other, from_sibling)
    return left, right


def rows_of(ref, first, count, cols):
    block = ref[pl.ds(pl.multiple_of(first, CH), count), cols]
    return [jnp.broadcast_to(block[n : n + 1], (CH, LANE)) for n in range(count)]


def sub_iota():
    return lax.broadcasted_iota(jnp.int32, (CH, LANE), 0)


def shifted(value, up):
    return pltpu.roll(value, 1 if up else CH - 1, 0)


def chunk_weights(total, up):
    sub = sub_iota()
    found = []
    width = total
    for reach in (1, 2, 4):
        inside = (sub >= reach) if up else (sub < CH - reach)
        found.append(jnp.where(inside, width, BIG))
        width = width + pltpu.roll(width, reach if up else CH - reach, 0)
    return found


def outside_sum(total, up):
    sub = sub_iota()
    value = jnp.where((sub >= 1) if up else (sub < CH - 1), shifted(total, up), 0.0)
    for reach in (1, 2, 4):
        inside = (sub >= reach) if up else (sub < CH - reach)
        value = value + jnp.where(inside, pltpu.roll(value, reach if up else CH - reach, 0), 0.0)
    return value


def chunk_scan(value, weights, a2, up):
    for reach, weight in zip((1, 2, 4), weights):
        value = value + jnp.exp2(weight * a2) * pltpu.roll(value, reach if up else CH - reach, 0)
    sub = sub_iota()
    enter = jnp.where((sub >= 1) if up else (sub < CH - 1), shifted(value, up), 0.0)
    leave = value[CH - 1 : CH] if up else value[0:1]
    return enter, leave


def prepare_kernel(
    sib, oth, keep, gain, w_in, conv_w, conv_b, w_x, w_dt, dt_bias, a_log, xb, gy,
    xc_o, dt_o, sig_o, conv_o, mask_o, dbl_o, xbh_o, sx_o, mx_o, sum_o, de_s, dx_s, bc_s, a2_s, decay_o,
    leave_s,
):
    inner, rank = w_x.shape[1], w_dt.shape[0]
    state = a_log.shape[0]
    length = xb.shape[0] // 2
    steps = length // CH
    tiles = inner // LANE
    left, right = pick_sides(sib[...], oth[...])
    hn_l = normalize(left, gain[...])[1]
    hn_r = normalize(right, gain[...])[1]
    flip = flip_matrix(hn_r.shape[1])
    lh, ll = split(hn_l)
    rh, rl = split(hn_r)
    halo = (
        jnp.concatenate([lh, nn(rh, flip).astype(BF16)], axis=0),
        jnp.concatenate([ll, nn(rl, flip).astype(BF16)], axis=0),
    )
    xbh = mm(nn, halo, split(w_in[:, :inner]))
    xbh_o[...] = xbh
    lane = lax.broadcasted_iota(jnp.int32, (1, length), 1)
    here = 1.0 - keep[...].astype(F32)
    before, after = left[3:4, :length], right[3:4, :length]

    def back(k):
        return jnp.where(lane < k, pltpu.roll(before, k, 1), pltpu.roll(here, k, 1))

    def ahead(k):
        return jnp.where(
            lane >= length - k,
            pltpu.roll(after, length - k, 1),
            pltpu.roll(here, length - k, 1),
        )

    f1 = here
    f2 = f1 * back(1)
    f3 = f2 * back(2)
    r1 = ahead(1)
    r2 = r1 * ahead(2)
    r3 = r2 * ahead(3)
    for i, row in enumerate((f1, f2, f3, r1, r2, r3)):
        mask_o[i * length : (i + 1) * length, :] = spread(row)

    sub = sub_iota()

    def conv_tile(lt, carry):
        cols = pl.ds(pl.multiple_of(lt * LANE, LANE), LANE)
        xbh_t = xbh_o[:, cols]
        taps = [conv_w[k : k + 1, cols] for k in range(4)]
        bias = conv_b[:, cols]
        xf = [xb[j * CH : (j + 1) * CH, cols] for j in range(steps)]
        edge = [
            jnp.where(sub == 0, xbh_t[b : b + 1], pltpu.roll(xf[steps - 3 + b], 1, 0))
            for b in range(3)
        ]
        xf = edge + xf
        for j in range(steps):
            rows = slice(j * CH, (j + 1) * CH)
            v = bias + taps[0] * xf[j + 3]
            for k in range(1, 4):
                v = v + taps[k] * (mask_o[(k - 1) * length + j * CH : (k - 1) * length + (j + 1) * CH, :] * xf[j + 3 - k])
            conv_o[rows, cols] = v
            xc_o[rows, cols] = v * sigmoid(v)
        xr = [xb[length + j * CH : length + (j + 1) * CH, cols] for j in range(steps)]
        xr = xr + [
            jnp.where(sub == CH - 1, xbh_t[8 + b : 9 + b], pltpu.roll(xr[b], CH - 1, 0))
            for b in range(3)
        ]
        for j in range(steps):
            rows = slice(length + j * CH, length + (j + 1) * CH)
            v = bias + taps[0] * xr[j]
            for k in range(1, 4):
                v = v + taps[k] * (mask_o[(k + 2) * length + j * CH : (k + 2) * length + (j + 1) * CH, :] * xr[j + k])
            conv_o[rows, cols] = v
            xc_o[rows, cols] = v * sigmoid(v)
        return carry

    lax.fori_loop(0, tiles, conv_tile, 0)
    dbl = mm(nt, xc_o[...], w_x[...])
    dbl_o[...] = dbl
    pre_all = mm(nn, dbl[:, :rank], w_dt[...])
    expand_bc(dbl, rank, state, bc_s)
    a2 = jnp.exp(a_log[...]) * (-LOG2E)
    for n in range(state):
        a2_s[n] = jnp.broadcast_to(a2[n : n + 1], (CH, inner))
    for lt in range(tiles):
        cols = slice(lt * LANE, (lt + 1) * LANE)
        pre = pre_all[:, cols] + dt_bias[:, cols]
        e = jnp.exp(-jnp.abs(pre))
        u = 1.0 + e
        log1p = jnp.where(u == 1.0, e, jnp.log(u) * (e / (u - 1.0)))
        dt = jnp.maximum(pre, 0.0) + log1p
        dt_o[:, cols] = dt
        sig_o[:, cols] = jnp.where(pre >= 0.0, 1.0, e) / u
        dx_s[:, cols] = dt * xc_o[:, cols]
        cut = jnp.concatenate([mask_o[:length], mask_o[3 * length : 4 * length]], axis=0)
        de_s[:, cols] = dt + BIG * (1.0 - cut)

    group = 4
    cols_of = [slice(t * LANE, (t + 1) * LANE) for t in range(tiles)]
    for dirn in range(2):
        order = list(range(steps)) if dirn == 0 else list(range(steps - 1, -1, -1))
        base = dirn * length
        up = dirn == 0
        s_row, m_row = (0, 3) if dirn == 0 else (2, 1)
        totals = []
        for cols in cols_of:
            total = jnp.zeros((CH, LANE), F32)
            for j in range(steps):
                total = total + de_s[base + j * CH : base + (j + 1) * CH, cols]
            sum_o[4 * state + dirn : 4 * state + dirn + 1, cols] = jnp.sum(total, axis=0, keepdims=True)
            totals.append(total)

        def some(g, carry, order=order, base=base, up=up, dirn=dirn, s_row=s_row, m_row=m_row, totals=totals):
            n0 = g * group
            at_b, at_c = lanes_of(n0, group), lanes_of(state + n0, group)
            keys = [(n, t) for n in range(group) for t in range(tiles)]
            a2 = {(n, t): a2_s[n0 + n, :, cols_of[t]] for n, t in keys}
            h, m = {}, {}
            for at, j in enumerate(order):
                rows = slice(base + j * CH, base + (j + 1) * CH)
                de = [de_s[rows, c] for c in cols_of]
                dx = [dx_s[rows, c] for c in cols_of]
                for n in range(group):
                    b_n = bc_s[rows, at_b[n]]
                    for t, cols in enumerate(cols_of):
                        d = jnp.exp2(de[t] * a2[n, t])
                        decay_o[dirn, at, n0 + n, :, cols] = d
                        h[n, t] = dx[t] * b_n if at == 0 else d * h[n, t] + dx[t] * b_n
            for at in range(steps - 1, -1, -1):
                rows = slice(base + order[at] * CH, base + (order[at] + 1) * CH)
                gyj = [gy[rows, c] for c in cols_of]
                for n in range(group):
                    c_n = bc_s[rows, at_c[n]]
                    for t, cols in enumerate(cols_of):
                        own = gyj[t] * c_n
                        d = decay_o[dirn, at, n0 + n, :, cols]
                        m[n, t] = d * (own if at == steps - 1 else own + m[n, t])
            for t in range(tiles):
                w_s, w_m = chunk_weights(totals[t], up), chunk_weights(totals[t], not up)
                for n in range(group):
                    enter, leave = chunk_scan(h[n, t], w_s, a2[n, t], up)
                    sx_o[dirn, n0 + n, :, cols_of[t]] = enter
                    leave_s[s_row * state + n0 + n, :, cols_of[t]] = jnp.broadcast_to(leave, (CH, LANE))
                    enter, leave = chunk_scan(m[n, t], w_m, a2[n, t], not up)
                    mx_o[dirn, n0 + n, :, cols_of[t]] = enter
                    leave_s[m_row * state + n0 + n, :, cols_of[t]] = jnp.broadcast_to(leave, (CH, LANE))
            return carry

        lax.fori_loop(0, state // group, some, 0)
    for row in range(0, 4 * state, CH):
        for cols in cols_of:
            sum_o[row : row + CH, cols] = jnp.concatenate([leave_s[row + i, 0:1, cols] for i in range(CH)], axis=0)
    sum_o[4 * state + 2 :, :] = jnp.zeros((sum_o.shape[0] - 4 * state - 2, inner), F32)


def lanes_of(first, count):
    return [pl.ds(pl.multiple_of((first + n) * LANE, LANE), LANE) for n in range(count)]


def expand_bc(dbl, rank, state, bc_s):
    pieces = split3(dbl[:, rank:])
    width = dbl.shape[1] - rank
    lhs = jnp.concatenate(pieces, axis=1)
    rows = lax.broadcasted_iota(jnp.int32, (3 * width, width * LANE), 0)
    cols = lax.broadcasted_iota(jnp.int32, (3 * width, width * LANE), 1)
    entry = cols >> 7
    hit = (rows == entry) | (rows == entry + width) | (rows == entry + 2 * width)
    bc_s[...] = nn(lhs, jnp.where(hit, 1.0, 0.0).astype(BF16))


def prepare(sib, oth, keep, gain, w_in, conv_w, conv_b, w_x, w_dt, dt_bias, a_log, xb, gy):
    rows, inner = xb.shape
    state, width = a_log.shape[0], w_x.shape[0]
    big = pltpu.VMEM((rows, inner), F32)
    edge = pltpu.VMEM((2, state, CH, inner), F32)
    return pl.pallas_call(
        prepare_kernel,
        out_shape=(
            big, big, big, big,
            pltpu.VMEM((3 * rows, LANE), F32),
            pltpu.VMEM((rows, width), F32),
            pltpu.VMEM((2 * CH, inner), F32),
            edge, edge,
            pltpu.VMEM((4 * state + 8, inner), F32),
            big, big,
            pltpu.VMEM((rows, 2 * state * LANE), F32),
            pltpu.VMEM((state, CH, inner), F32),
            pltpu.VMEM((2, rows // 2 // CH, state, CH, inner), F32),
        ),
        scratch_shapes=[pltpu.VMEM((4 * state, CH, inner), F32)],
        compiler_params=params(8),
        name="prepare",
    )(sib, oth, keep, gain, w_in, conv_w, conv_b, w_x, w_dt, dt_bias, a_log, xb, gy)


def summary_parts(ref_value, state):
    return [ref_value[i * state : (i + 1) * state] for i in range(4)]


def pair_kernel(a2_s, mine, theirs, out):
    state, half = a2_s.shape[0], out.shape[1]
    core = lax.axis_index("seq") & 1
    cols = pl.ds(pl.multiple_of(core * half, half), half)
    a2 = half_a2(a2_s, half)
    me, it = mine[:, cols], theirs[:, cols]
    low, high = jnp.where(core == 1, it, me), jnp.where(core == 1, me, it)
    put_total(out, joined(low, high, a2, state), state)


def joined(low, high, a2, state):
    low_f, low_r = low[4 * state : 4 * state + 1], low[4 * state + 1 : 4 * state + 2]
    high_f, high_r = high[4 * state : 4 * state + 1], high[4 * state + 1 : 4 * state + 2]
    lows, highs = summary_parts(low, state), summary_parts(high, state)
    return [
        lows[0] * jnp.exp2(high_f * a2) + highs[0],
        lows[1] * jnp.exp2(high_r * a2) + highs[1],
        highs[2] * jnp.exp2(low_r * a2) + lows[2],
        highs[3] * jnp.exp2(low_f * a2) + lows[3],
        low_f + high_f,
        low_r + high_r,
    ]


def put_total(out, parts, state):
    for i in range(4):
        out[i * state : (i + 1) * state] = parts[i]
    rest = jnp.zeros((out.shape[0] - 4 * state - 2, out.shape[1]), F32)
    out[4 * state :] = jnp.concatenate([parts[4], parts[5], rest], axis=0)


def half_a2(a2_s, half):
    core = lax.axis_index("seq") & 1
    cols = pl.ds(pl.multiple_of(core * half, half), half)
    return jnp.concatenate([a2_s[n, 0:1, cols] for n in range(a2_s.shape[0])], axis=0)


def stage_kernel(first, halves, a2_s, *refs):
    outs = 1 + len(halves) if halves else 2
    members, out, held = refs[: -outs - 1], refs[-outs - 1 : -1], refs[-1]
    count = len(members)
    state, half = a2_s.shape[0], out[0].shape[1]
    a2 = half_a2(a2_s, half)
    at = (lax.axis_index("seq") >> first) & (count - 1)
    for i, ref in enumerate(members):
        held[at ^ i] = ref[...]
    zero, none = jnp.zeros((state, half), F32), jnp.zeros((1, half), F32)

    def run_through(order, rows, reach):
        run = [zero, zero, none, none]
        seen = list(run)
        for i in order:
            seen = [jnp.where(at == i, now, old) for now, old in zip(run, seen)]
            df, dr = held[i, 4 * state : 4 * state + 1], held[i, 4 * state + 1 : 4 * state + 2]
            decays = [jnp.exp2((df, dr)[w] * a2) for w in reach]
            run = [run[k] * decays[k] + held[i, rows[k] * state : (rows[k] + 1) * state] for k in range(2)] + [
                run[2] + df,
                run[3] + dr,
            ]
        return run, seen

    right, seen = run_through(range(count), (0, 1), (0, 1))
    left, seen_left = run_through(range(count - 1, -1, -1), (2, 3), (1, 0))
    enter = out[0]
    enter[:state], enter[state : 2 * state] = seen[0], seen[1]
    enter[2 * state : 3 * state], enter[3 * state : 4 * state] = seen_left[0], seen_left[1]
    blank = jnp.zeros((CH, half), F32)
    enter[4 * state :] = jnp.concatenate([seen[2], seen[3], seen_left[2], seen_left[3], blank[:4]], axis=0)
    sums = jnp.concatenate([right[2], right[3], blank[:6]], axis=0)
    if halves:
        me = lax.axis_index("seq")
        for ref, apart in zip(out[1:], halves):
            later = (me ^ apart) > me
            ref[:state] = jnp.where(later, right[0], left[0])
            ref[state : 2 * state] = jnp.where(later, right[1], left[1])
            ref[2 * state :] = sums
    else:
        for i, value in enumerate((right[0], right[1], left[0], left[1])):
            out[1][i * state : (i + 1) * state] = value
        out[1][4 * state :] = sums


def last_kernel(first, a2_s, *refs):
    theirs, out, held = refs[:-2], refs[-2], refs[-1]
    count = len(theirs) + 1
    state, half = a2_s.shape[0], out.shape[1]
    a2 = half_a2(a2_s, half)
    at = (lax.axis_index("seq") >> first) & (count - 1)
    held[at] = jnp.zeros(held.shape[1:], F32)
    for i, ref in enumerate(theirs):
        held[at ^ (i + 1)] = ref[...]

    def run_through(order, reach, inside):
        run = [jnp.zeros((state, half), F32)] * 2
        for i in order:
            sums = held[i, 2 * state : 2 * state + 1], held[i, 2 * state + 1 : 2 * state + 2]
            for k in range(2):
                longer = run[k] * jnp.exp2(sums[reach[k]] * a2) + held[i, k * state : (k + 1) * state]
                run[k] = jnp.where(inside(i), longer, run[k])
        return run

    found = run_through(range(count - 1), (0, 1), lambda i: i < at)
    found = found + run_through(range(count - 1, 0, -1), (1, 0), lambda i: i > at)
    for i in range(4):
        out[i * state : (i + 1) * state] = found[i]


def pair(a2_s, mine, theirs):
    rows, inner = mine.shape
    return pl.pallas_call(
        pair_kernel,
        out_shape=jax.ShapeDtypeStruct((rows, inner // 2), F32),
        compiler_params=params(2),
        name="pair",
    )(a2_s, mine, theirs)


def stage(first, halves, a2_s, members):
    shape = jax.ShapeDtypeStruct(members[0].shape, F32)
    part = jax.ShapeDtypeStruct((2 * a2_s.shape[0] + CH, members[0].shape[1]), F32)
    return pl.pallas_call(
        lambda *refs: stage_kernel(first, halves, *refs),
        out_shape=(shape,) + (part,) * len(halves) if halves else (shape, shape),
        scratch_shapes=[pltpu.VMEM((len(members),) + members[0].shape, F32)],
        compiler_params=params(4),
        name="stage",
    )(a2_s, *members)


def last_stage(first, a2_s, theirs):
    return pl.pallas_call(
        lambda *refs: last_kernel(first, *refs),
        out_shape=jax.ShapeDtypeStruct((4 * a2_s.shape[0], theirs[0].shape[1]), F32),
        scratch_shapes=[pltpu.VMEM((len(theirs) + 1,) + theirs[0].shape, F32)],
        compiler_params=params(4),
        name="stage",
    )(a2_s, *theirs)


def enter_kernel(a2_s, *refs):
    stages, out = refs[:-1], refs[-1]
    state, half = a2_s.shape[0], out.shape[1]
    a2 = half_a2(a2_s, half)
    value = [stages[-1][i * state : (i + 1) * state] for i in range(4)]
    for ref in reversed(stages[:-1]):
        reach = [ref[4 * state + i : 4 * state + i + 1] for i in range(4)]
        value = [
            ref[i * state : (i + 1) * state] + value[i] * jnp.exp2(reach[w] * a2)
            for i, w in ((0, 0), (1, 1), (2, 3), (3, 2))
        ]
    for i in range(4):
        out[i * state : (i + 1) * state] = value[i]


def enter(a2_s, stages):
    half = stages[0].shape[1]
    return pl.pallas_call(
        enter_kernel,
        out_shape=jax.ShapeDtypeStruct((4 * a2_s.shape[0], half), F32),
        compiler_params=params(2),
        name="enter",
    )(a2_s, *stages)


def carry_in(car_s, a2_s, mine_half, other_half, sibling):
    state, inner = a2_s.shape[0], a2_s.shape[2]
    half = inner // 2
    odd = (lax.axis_index("seq") & 1) == 1
    a2 = jnp.concatenate([a2_s[n, 0:1, :] for n in range(state)], axis=0)
    left, right = jnp.where(odd, other_half[...], mine_half[...]), jnp.where(odd, mine_half[...], other_half[...])
    into = jnp.concatenate([left, right], axis=1)
    df, dr = sibling[4 * state : 4 * state + 1], sibling[4 * state + 1 : 4 * state + 2]
    for i, reach, through in ((0, df, odd), (1, dr, odd), (2, dr, ~odd), (3, df, ~odd)):
        rows = slice(i * state, (i + 1) * state)
        value = jnp.where(through, into[rows] * jnp.exp2(reach * a2) + sibling[rows], into[rows])
        for n in range(state):
            car_s[i * state + n] = jnp.broadcast_to(value[n : n + 1], (CH, inner))


def forward_kernel(
    mine_half, other_half, sibling, sx, de_s, dx_s, bc_s, a2_s, decay,
    y_s, h_s, car_o,
    before_s,
):
    rows2, inner = de_s.shape
    length = rows2 // 2
    steps = length // CH
    tiles = inner // LANE
    state = a2_s.shape[0]
    carry_in(car_o, a2_s, mine_half, other_half, sibling)
    y_s[...] = jnp.zeros(y_s.shape, F32)
    group = 4
    cols_of = [slice(t * LANE, (t + 1) * LANE) for t in range(tiles)]
    for dirn in range(2):
        order = list(range(steps)) if dirn == 0 else list(range(steps - 1, -1, -1))
        base = dirn * length
        s_row = 0 if dirn == 0 else 2
        for cols in cols_of:
            total = jnp.zeros((CH, LANE), F32)
            for j in range(steps):
                total = total + de_s[base + j * CH : base + (j + 1) * CH, cols]
            before_s[:, cols] = outside_sum(total, dirn == 0)

        def some(g, carry, dirn=dirn, order=order, base=base, s_row=s_row):
            n0 = g * group
            at_b, at_c = lanes_of(n0, group), lanes_of(state + n0, group)
            h = {}
            for n in range(group):
                for t, cols in enumerate(cols_of):
                    into = jnp.exp2(before_s[:, cols] * a2_s[n0 + n, :, cols]) * car_o[s_row * state + n0 + n, :, cols]
                    h[n, t] = sx[dirn, n0 + n, :, cols] + into
                    h_s[dirn, 0, n0 + n, :, cols] = h[n, t]
            for at, j in enumerate(order):
                rows = slice(base + j * CH, base + (j + 1) * CH)
                dx = [dx_s[rows, c] for c in cols_of]
                y = [None] * tiles
                for n in range(group):
                    b_n, c_n = bc_s[rows, at_b[n]], bc_s[rows, at_c[n]]
                    for t, cols in enumerate(cols_of):
                        h[n, t] = decay[dirn, at, n0 + n, :, cols] * h[n, t] + dx[t] * b_n
                        h_s[dirn, at + 1, n0 + n, :, cols] = h[n, t]
                        term = h[n, t] * c_n
                        y[t] = term if n == 0 else y[t] + term
                for t, cols in enumerate(cols_of):
                    y_s[rows, cols] += y[t]
            return carry

        lax.fori_loop(0, state // group, some, 0)


def forward(mine_half, other_half, sibling, sx, de, dx, bc, a2, decay):
    rows2, inner = de.shape
    state = a2.shape[0]
    steps = rows2 // 2 // CH
    return pl.pallas_call(
        forward_kernel,
        out_shape=(
            jax.ShapeDtypeStruct((rows2, inner), F32),
            jax.ShapeDtypeStruct((2, steps + 1, state, CH, inner), F32),
            jax.ShapeDtypeStruct((4 * state, CH, inner), F32),
        ),
        scratch_shapes=[pltpu.VMEM((CH, inner), F32)],
        compiler_params=params(4),
        name="forward",
    )(mine_half, other_half, sibling, sx, de, dx, bc, a2, decay)


def ready_kernel(
    rank, tok, gout, gain, w_in, w_out, d_skip, z, go, conv, xc, gy,
    x_o, g_o, nth_o, ntl_o, gh_o, gl_o, wih_o, wil_o, wfh_o, wfl_o, woh_o, wol_o, vfh_o, vfl_o,
    gate_o, zgrad_o, cgrad_o, xch_o, xcl_o, skip_o, pickb_o, pickc_o,
):
    feat, inner = gain.shape[1], w_out.shape[0]
    x = ordered(tok)
    x_o[...] = x
    g = ordered(gout)
    g_o[...] = g
    high, low = both_orders(normalize(x, gain[...])[1])
    nth_o[...] = high.astype(F32).T.astype(BF16)
    ntl_o[...] = low.astype(F32).T.astype(BF16)
    gh_o[...], gl_o[...] = both_orders(g)
    flip = flip_matrix(feat)
    high, low = split(w_in[...])
    wih_o[...], wil_o[...] = high, low
    wfh_o[...], wfl_o[...] = nn(flip, high).astype(BF16), nn(flip, low).astype(BF16)
    high, low = split(w_out[...])
    woh_o[...], wol_o[...] = high, low
    vfh_o[...], vfl_o[...] = nn(high, flip).astype(BF16), nn(low, flip).astype(BF16)
    xch_o[...], xcl_o[...] = split(xc[...])
    for lt in range(inner // LANE):
        cols = slice(lt * LANE, (lt + 1) * LANE)
        zt, v = z[:, cols], conv[:, cols]
        s = sigmoid(zt)
        gate_o[:, cols] = zt * s
        zgrad_o[:, cols] = go[:, cols] * (s * (1.0 + zt * (1.0 - s)))
        s = sigmoid(v)
        cgrad_o[:, cols] = s * (1.0 + v * (1.0 - s))
        skip_o[:, cols] = jnp.sum(gy[:, cols] * xc[:, cols], axis=0, keepdims=True)
    row = lax.broadcasted_iota(jnp.int32, pickb_o.shape, 0) >> 7
    col = lax.broadcasted_iota(jnp.int32, pickb_o.shape, 1)
    pickb_o[...] = jnp.where(col == row + rank, 1.0, 0.0).astype(BF16)
    pickc_o[...] = jnp.where(col == row + (rank + pickb_o.shape[0] // LANE), 1.0, 0.0).astype(BF16)


def ready(rank, state, tok, gout, gain, w_in, w_out, d_skip, z, go, conv, xc, gy):
    length, feat = tok.shape
    rows2, inner = z.shape
    f32 = lambda *dims: jax.ShapeDtypeStruct(dims, F32)
    b16 = lambda *dims: jax.ShapeDtypeStruct(dims, BF16)
    both = lambda *dims: (b16(*dims), b16(*dims))
    return pl.pallas_call(
        lambda *refs: ready_kernel(rank, *refs),
        out_shape=(f32(length, feat), f32(length, feat))
        + both(feat, rows2) + both(rows2, feat) + both(feat, 2 * inner) + both(feat, 2 * inner)
        + both(inner, feat) + both(inner, feat)
        + (f32(rows2, inner), f32(rows2, inner), f32(rows2, inner))
        + both(rows2, inner) + (f32(1, inner),) + both(state * LANE, LANE),
        compiler_params=params(8),
        name="ready",
    )(tok, gout, gain, w_in, w_out, d_skip, z, go, conv, xc, gy)


def early_kernel(
    rs_bits, x, nth, ntl, gh, gl, woh, wol, vfh, vfl, gate, zgrad, d_skip, xc, y_s,
    mixed_o, gzh_o, gzl_o, pieces_o,
):
    rows2, inner = xc.shape
    length = rows2 // 2
    y = y_s[...] + d_skip[...] * xc[...]
    gz = split(zgrad[...] * y)
    gzh_o[...], gzl_o[...] = gz
    out = split(y * gate[...])
    gw_out = mm(tn, out, (gh[...], gl[...]))
    gw_in = mm(nn, (nth[...], ntl[...]), gz)
    put_pieces(rs_bits, pieces_o, [(gw_in, None), (gw_out, None)])
    fwd = mm(nn, (out[0][:length], out[1][:length]), (woh[...], wol[...]))
    rev = mm(nn, (out[0][length:], out[1][length:]), (vfh[...], vfl[...]))
    store_ordered(mixed_o, x[...] + (fwd + rev))


def early(rs_bits, x, nth, ntl, gh, gl, woh, wol, vfh, vfl, gate, zgrad, d_skip, xc, y):
    length, feat = x.shape
    rows2, inner = xc.shape
    pieces = 1 << rs_bits
    tall = 2 * feat * inner // LANE // pieces
    gz = jax.ShapeDtypeStruct((rows2, inner), BF16)
    return pl.pallas_call(
        lambda *refs: early_kernel(rs_bits, *refs),
        out_shape=(jax.ShapeDtypeStruct((length, feat), F32), gz, gz, jax.ShapeDtypeStruct((pieces, tall, LANE), F32)),
        compiler_params=params(8),
        name="early",
    )(x, nth, ntl, gh, gl, woh, wol, vfh, vfl, gate, zgrad, d_skip, xc, y)


def put_pieces(rs_bits, pieces_o, arrays, few=None):
    pieces = 1 << rs_bits
    mine = reverse_bits(lax.axis_index("seq"), rs_bits)
    for p in range(pieces):
        slot = mine ^ reverse_bits(p, rs_bits)
        at = 0
        for value, more in arrays:
            tall = value.shape[0] // pieces
            for lt in range(value.shape[1] // LANE):
                where = (slice(p * tall, (p + 1) * tall), slice(lt * LANE, (lt + 1) * LANE))
                block = value[where] if more is None else value[where] + more[where]
                pieces_o[slot, at : at + tall, :] = block
                at += tall
        if few is not None:
            tiles = few.shape[1] // LANE
            top = pieces // tiles * CH
            rest = (few.shape[0] - top) * tiles // pieces
            rb, lt = p // tiles, p % tiles
            pieces_o[slot, at : at + CH, :] = few[rb * CH : (rb + 1) * CH, lt * LANE : (lt + 1) * LANE]
            rows = []
            for v in range(rest * p, rest * (p + 1)):
                rb, lt = top + v // tiles, v % tiles
                rows.append(few[rb : rb + 1, lt * LANE : (lt + 1) * LANE])
            zeros = jnp.zeros((4, LANE), F32)
            rows = [zeros] + rows + [zeros[: 4 - rest]]
            pieces_o[slot, at + CH : at + 2 * CH, :] = jnp.concatenate(rows, axis=0)
            pieces_o[slot, at + 2 * CH : at + 3 * CH, :] = jnp.zeros((CH, LANE), F32)


def row_vectors(rows):
    return jnp.concatenate(
        [rows[b : b + 1, lt * LANE : (lt + 1) * LANE] for b in range(3) for lt in range(rows.shape[1] // LANE)],
        axis=0,
    )


def backward_kernel(
    dirn, mx, car, h_s, de_s, dx_s, bc_s, a2_s, decay, gy,
    sb_s, sa_s, accb, accc, ga_s,
    after_s,
):
    rows2, inner = de_s.shape
    length = rows2 // 2
    steps = length // CH
    tiles = inner // LANE
    state = a2_s.shape[0]
    order = list(range(steps)) if dirn == 0 else list(range(steps - 1, -1, -1))
    base = dirn * length
    m_row = 3 if dirn == 0 else 1
    group = 2
    cols_of = [slice(t * LANE, (t + 1) * LANE) for t in range(tiles)]
    sb_s[...] = jnp.zeros(sb_s.shape, F32)
    sa_s[...] = jnp.zeros(sa_s.shape, F32)
    for cols in cols_of:
        total = jnp.zeros((CH, LANE), F32)
        for j in range(steps):
            total = total + de_s[base + j * CH : base + (j + 1) * CH, cols]
        after_s[:, cols] = outside_sum(total, dirn != 0)

    def some(g, carry):
        n0 = g * group
        at_b, at_c = lanes_of(n0, group), lanes_of(state + n0, group)
        a2, q, ga = {}, {}, {}
        for n in range(group):
            for t, cols in enumerate(cols_of):
                a2[n, t] = a2_s[n0 + n, :, cols]
                into = jnp.exp2(after_s[:, cols] * a2[n, t]) * car[m_row * state + n0 + n, :, cols]
                q[n, t] = mx[dirn, n0 + n, :, cols] + into
                ga[n, t] = jnp.zeros((CH, LANE), F32)
        for at in range(steps - 1, -1, -1):
            j = order[at]
            rows = slice(base + j * CH, base + (j + 1) * CH)
            here = slice(j * CH, (j + 1) * CH)
            de = [de_s[rows, c] for c in cols_of]
            dx = [dx_s[rows, c] for c in cols_of]
            gyj = [gy[rows, c] for c in cols_of]
            sb, sa = [None] * tiles, [None] * tiles
            for n in range(group):
                b_n, c_n = bc_s[rows, at_b[n]], bc_s[rows, at_c[n]]
                to_b = to_c = None
                for t, cols in enumerate(cols_of):
                    gh = gyj[t] * c_n + q[n, t]
                    term_c = gyj[t] * h_s[dirn, at + 1, n0 + n, :, cols]
                    term_b = gh * dx[t]
                    to_b = term_b if t == 0 else to_b + term_b
                    to_c = term_c if t == 0 else to_c + term_c
                    q[n, t] = decay[dirn, at, n0 + n, :, cols] * gh
                    r = q[n, t] * h_s[dirn, at, n0 + n, :, cols]
                    ga[n, t] = ga[n, t] + de[t] * r
                    sb[t] = gh * b_n if n == 0 else sb[t] + gh * b_n
                    sa[t] = a2[n, t] * r if n == 0 else sa[t] + a2[n, t] * r
                accb[here, at_b[n]] = to_b
                accc[here, at_b[n]] = to_c
            for t, cols in enumerate(cols_of):
                sb_s[here, cols] += sb[t]
                sa_s[here, cols] += sa[t]
        for n in range(group):
            for t, cols in enumerate(cols_of):
                ga_s[n0 + n, :, cols] = ga[n, t]
        return carry

    lax.fori_loop(0, state // group, some, 0)


def backward(dirn, mx, car, h, de, dx, bc, a2, decay, gy):
    rows2, inner = de.shape
    state = a2.shape[0]
    length = rows2 // 2
    half = jax.ShapeDtypeStruct((length, inner), F32)
    acc = jax.ShapeDtypeStruct((length, state * LANE), F32)
    return pl.pallas_call(
        lambda *refs: backward_kernel(dirn, *refs),
        out_shape=(half, half, acc, acc, jax.ShapeDtypeStruct((state, CH, inner), F32)),
        scratch_shapes=[pltpu.VMEM((CH, inner), F32)],
        compiler_params=params(4),
        name="backward",
    )(mx, car, h, de, dx, bc, a2, decay, gy)


def inner_kernel(
    pad, conv_w, w_x, w_dt, d_skip, a2_s,
    xb, gy, xc, dt, sig, cgrad, mask, dbl, xbh, xch, xcl, skip_sum, pick_b, pick_c,
    sb_f, sa_f, accb_f, accc_f, ga_f, sb_r, sa_r, accb_r, accc_r, ga_r,
    gxh_o, gxl_o, halo_o, few_o,
    gp_s, gpre_s, xcg_s,
):
    inner, rank = w_x.shape[1], w_dt.shape[0]
    state = a2_s.shape[0]
    rows2 = xb.shape[0]
    length = rows2 // 2
    steps = length // CH
    tiles = inner // LANE
    sub = sub_iota()

    bias_rows = []
    for lt in range(tiles):
        cols = slice(lt * LANE, (lt + 1) * LANE)
        bias = jnp.zeros((1, LANE), F32)
        for dirn, sb, sa in ((0, sb_f, sa_f), (1, sb_r, sa_r)):
            rows = slice(dirn * length, (dirn + 1) * length)
            g_pre = (xc[rows, cols] * sb[:, cols] + LN2 * sa[:, cols]) * sig[rows, cols]
            gpre_s[rows, cols] = g_pre
            xcg_s[rows, cols] = d_skip[:, cols] * gy[rows, cols] + dt[rows, cols] * sb[:, cols]
            bias = bias + jnp.sum(g_pre, axis=0, keepdims=True)
        bias_rows.append(bias)

    b_parts = split(jnp.concatenate([accb_f[...], accb_r[...]], axis=0))
    c_parts = split(jnp.concatenate([accc_f[...], accc_r[...]], axis=0))
    g_bc = (nn(b_parts[0], pick_b[...]) + nn(b_parts[1], pick_b[...])) + (
        nn(c_parts[0], pick_c[...]) + nn(c_parts[1], pick_c[...])
    )
    gpre_parts = split(gpre_s[...])
    w_dt_parts = split(w_dt[...])
    g_rank = mm(nt, gpre_parts, w_dt_parts)
    width = rank + 2 * state
    g_dbl = jnp.concatenate([g_rank, g_bc[:, rank:width]], axis=1)
    g_dbl_parts = split(g_dbl)
    few_o[width + state : width + state + rank, :] = mm(tn, split(dbl[:, :rank]), gpre_parts)
    few_o[:width, :] = mm(tn, g_dbl_parts, (xch[...], xcl[...]))
    xcg_s[...] += mm(nn, g_dbl_parts, split(w_x[...]))

    cw_rows = [[] for _ in range(4)]
    cb_rows = []
    halo_f, halo_r = [], []
    for lt in range(tiles):
        cols = slice(lt * LANE, (lt + 1) * LANE)
        taps = [conv_w[k : k + 1, cols] for k in range(4)]
        xbh_t = xbh[:, cols]
        xf = [xb[j * CH : (j + 1) * CH, cols] for j in range(steps)]
        xf = [
            jnp.where(sub == 0, xbh_t[b : b + 1], pltpu.roll(xf[steps - 3 + b], 1, 0))
            for b in range(3)
        ] + xf
        gcw = [jnp.zeros((CH, LANE), F32) for _ in range(4)]
        gcb = jnp.zeros((CH, LANE), F32)
        grads = [None] * (steps + 3)
        for j in range(steps):
            rows = slice(j * CH, (j + 1) * CH)
            u = xcg_s[rows, cols] * cgrad[rows, cols]
            gcb = gcb + u
            for k in range(4):
                uk = u if k == 0 else u * mask[(k - 1) * length + j * CH : (k - 1) * length + (j + 1) * CH, :]
                gcw[k] = gcw[k] + uk * xf[j + 3 - k]
                add = taps[k] * uk
                at = j + 3 - k
                grads[at] = add if grads[at] is None else grads[at] + add
        for b in range(3):
            halo_f.append(grads[b][0:1])
            at = steps + b
            grads[at] = grads[at] + jnp.where(sub == CH - 1, 0.0, pltpu.roll(grads[b], CH - 1, 0))
        for j in range(steps):
            gp_s[j * CH : (j + 1) * CH, cols] = grads[j + 3]
        xr = [xb[length + j * CH : length + (j + 1) * CH, cols] for j in range(steps)]
        xr = xr + [
            jnp.where(sub == CH - 1, xbh_t[8 + b : 9 + b], pltpu.roll(xr[b], CH - 1, 0))
            for b in range(3)
        ]
        grads = [None] * (steps + 3)
        for j in range(steps):
            rows = slice(length + j * CH, length + (j + 1) * CH)
            u = xcg_s[rows, cols] * cgrad[rows, cols]
            gcb = gcb + u
            for k in range(4):
                uk = u if k == 0 else u * mask[(k + 2) * length + j * CH : (k + 2) * length + (j + 1) * CH, :]
                gcw[k] = gcw[k] + uk * xr[j + k]
                add = taps[k] * uk
                grads[j + k] = add if grads[j + k] is None else grads[j + k] + add
        for b in range(3):
            halo_r.append(grads[steps + b][CH - 1 : CH])
            grads[b] = grads[b] + jnp.where(sub == 0, 0.0, pltpu.roll(grads[steps + b], 1, 0))
        for j in range(steps):
            gp_s[length + j * CH : length + (j + 1) * CH, cols] = grads[j]
        for k in range(4):
            cw_rows[k].append(jnp.sum(gcw[k], axis=0, keepdims=True))
        cb_rows.append(jnp.sum(gcb, axis=0, keepdims=True))
    pad_col = spread(pad[...].astype(F32))
    pad_all = jnp.concatenate([pad_col, pad_col], axis=0)
    for lt in range(tiles):
        cols = slice(lt * LANE, (lt + 1) * LANE)
        gxh_o[:, cols], gxl_o[:, cols] = split(gp_s[:, cols] * pad_all)

    blank = jnp.zeros((5, inner), F32)

    def gather(found):
        return jnp.concatenate(
            [jnp.concatenate([found[lt * 3 + b] for lt in range(tiles)], axis=1) for b in range(3)]
            + [blank],
            axis=0,
        )

    halo_o[...] = jnp.concatenate([gather(halo_f), gather(halo_r)], axis=0)
    ga = jnp.concatenate(
        [jnp.sum(ga_f[n] + ga_r[n], axis=0, keepdims=True) * (a2_s[n, 0:1, :] * LN2) for n in range(state)], axis=0
    )
    few_o[width : width + state, :] = ga
    few_o[width + state + rank :, :] = jnp.concatenate(
        [jnp.concatenate(cw_rows[k], axis=1) for k in range(4)]
        + [
            jnp.concatenate(cb_rows, axis=1),
            jnp.concatenate(bias_rows, axis=1),
            skip_sum[...],
            jnp.zeros((1, inner), F32),
        ],
        axis=0,
    )


def inner_back(*arrays):
    w_x, w_dt, a2, xb = arrays[2], arrays[3], arrays[5], arrays[6]
    rows2, inner = xb.shape
    few = w_x.shape[0] + a2.shape[0] + w_dt.shape[0] + CH
    big = pltpu.VMEM((rows2, inner), F32)
    part = jax.ShapeDtypeStruct((rows2, inner), BF16)
    return pl.pallas_call(
        inner_kernel,
        out_shape=(
            part, part,
            jax.ShapeDtypeStruct((2 * CH, inner), F32),
            jax.ShapeDtypeStruct((few, inner), F32),
        ),
        scratch_shapes=[big, big, big],
        compiler_params=params(8),
        name="inner",
    )(*arrays)


def tail_kernel(
    rs_bits, sib, oth, gain, x_s, g_s, nth, ntl, wih, wil, wfh, wfl, gzh, gzl, gxh, gxl, halo, few,
    gtok_o, to_left_o, to_right_o, pieces_o,
):
    feat = gain.shape[1]
    rows2, inner = gxh.shape
    length = rows2 // 2
    left, right = pick_sides(sib[...], oth[...])
    factor_l, hn_l = normalize(left, gain[...])
    factor_r, hn_r = normalize(right, gain[...])
    flip = flip_matrix(feat)
    lh, ll = split(hn_l)
    rh, rl = split(hn_r)
    edge = (
        jnp.concatenate([lh, nn(rh, flip).astype(BF16)], axis=0),
        jnp.concatenate([ll, nn(rl, flip).astype(BF16)], axis=0),
    )
    x, g = x_s[...], g_s[...]
    factor = normalize(x, gain[...])[0]
    gh_parts = split(halo[...])
    gw_in = mm(nn, (nth[...], ntl[...]), (gxh[...], gxl[...]))
    gw_in_halo = mm(tn, edge, gh_parts)
    w_xb = (wih[:, :inner], wil[:, :inner])
    g_normed = (
        mm(nt, (gxh[:length], gxl[:length]), w_xb)
        + mm(nt, (gzh[:length], gzl[:length]), (wih[:, inner:], wil[:, inner:]))
    ) + (
        mm(nt, (gxh[length:], gxl[length:]), (wfh[:, :inner], wfl[:, :inner]))
        + mm(nt, (gzh[length:], gzl[length:]), (wfh[:, inner:], wfl[:, inner:]))
    )
    back_h = mm(nt, gh_parts, w_xb)
    gn_l = back_h[:CH]
    gn_r = flipped(back_h[CH:])

    def norm_back(x, factor, gn):
        scaled = gn * gain[...]
        return factor * scaled - x * (factor * factor * factor * jnp.mean(scaled * x, axis=1, keepdims=True))

    store_ordered(gtok_o, g + norm_back(x, factor, g_normed))
    to_left = norm_back(left, factor_l, gn_l)
    to_right = norm_back(right, factor_r, gn_r)
    to_left_o[...] = to_left
    to_right_o[...] = to_right
    three = lax.broadcasted_iota(jnp.int32, (CH, feat), 0) < 3
    g_gain = (
        jnp.sum(g_normed * (x * factor), axis=0, keepdims=True)
        + jnp.sum(jnp.where(three, gn_l * (left * factor_l) + gn_r * (right * factor_r), 0.0), axis=0, keepdims=True)
    )
    few_all = jnp.concatenate(
        [few[: few.shape[0] - CH, :], few[few.shape[0] - CH : few.shape[0] - 1, :]]
        + [jnp.concatenate([g_gain, jnp.zeros((1, inner - feat), F32)], axis=1)],
        axis=0,
    )
    put_pieces(rs_bits, pieces_o, [(gw_in, gw_in_halo)], few_all)
    pieces = 1 << rs_bits
    me = lax.axis_index("seq") & (pieces - 1)
    mine = reverse_bits(me, rs_bits)
    at = pieces_o.shape[1] - 2 * CH

    @pl.when(me < pieces - 1)
    def _():
        slot = mine ^ reverse_bits(me + 1, rs_bits)
        vectors = row_vectors(to_right)
        pieces_o[slot, at : at + 4, :] = vectors[:4]
        pieces_o[slot, at + CH : at + CH + 2, :] = vectors[4:]

    @pl.when(me > 0)
    def _():
        slot = mine ^ reverse_bits(me - 1, rs_bits)
        pieces_o[slot, at + CH + 2 : at + 2 * CH, :] = row_vectors(to_left)


def reverse_bits(value, bits):
    found = 0
    for i in range(bits):
        found = found | (((value >> i) & 1) << (bits - 1 - i))
    return found


def tail(rs_bits, *arrays):
    x, gxh = arrays[3], arrays[13]
    length, feat = x.shape
    inner = gxh.shape[1]
    pieces = 1 << rs_bits
    tall = feat * inner // LANE // pieces + 3 * CH
    return pl.pallas_call(
        lambda *refs: tail_kernel(rs_bits, *refs),
        out_shape=(
            jax.ShapeDtypeStruct((length, feat), F32),
            jax.ShapeDtypeStruct((CH, feat), F32),
            jax.ShapeDtypeStruct((CH, feat), F32),
            jax.ShapeDtypeStruct((pieces, tall, LANE), F32),
        ),
        compiler_params=params(8),
        name="tail",
    )(*arrays)


def unpack_kernel(rs_bits, parts, *refs):
    sources, refs = refs[:parts], refs[parts:]
    (gtok, halo, pad, gtok_o, gain_o, w_in_o, conv_w_o, conv_b_o, w_x_o, w_dt_o, dt_bias_o, a_log_o, d_skip_o, w_out_o,
     few_s, rest_s) = refs
    feat = w_in_o.shape[0]
    inner = w_out_o.shape[0]
    tiles = inner // LANE
    pieces = 1 << rs_bits
    mine = reverse_bits(lax.axis_index("seq"), rs_bits)
    in_rows, out_rows = feat // pieces, inner // pieces
    for slot in range(pieces):
        source = sources[slot * parts // pieces]
        i = slot % (pieces // parts)
        p = reverse_bits(mine ^ slot, rs_bits)
        at = 0
        in_at = pl.ds(pl.multiple_of(p * in_rows, in_rows), in_rows)
        out_at = pl.ds(pl.multiple_of(p * out_rows, out_rows), out_rows)
        for lt in range(tiles):
            w_in_o[in_at, inner + lt * LANE : inner + (lt + 1) * LANE] = source[i, at : at + in_rows, :]
            at += in_rows
        for lt in range(feat // LANE):
            w_out_o[out_at, lt * LANE : (lt + 1) * LANE] = source[i, at : at + out_rows, :]
            at += out_rows
        for lt in range(tiles):
            w_in_o[in_at, lt * LANE : (lt + 1) * LANE] = source[i, at : at + in_rows, :]
            at += in_rows
        few_s[p] = source[i, at : at + CH, :]
        rest_s[p] = source[i, at + CH : at + 2 * CH, :]

    top = pieces // tiles * CH
    total = w_x_o.shape[0] + a_log_o.shape[0] + w_dt_o.shape[0] + CH
    rest = (total - top) * tiles // pieces

    def few_rows(first, count):
        found = []
        for lt in range(tiles):
            if first < top:
                found.append(few_s[first // CH * tiles + lt])
                continue
            rows = []
            for row in range(first, first + count):
                v = (row - top) * tiles + lt
                rows.append(rest_s[v // rest, 4 + v % rest : 5 + v % rest, :])
            found.append(jnp.concatenate(rows, axis=0) if count > 1 else rows[0])
        return jnp.concatenate(found, axis=1)

    width, state = w_x_o.shape[0], a_log_o.shape[0]
    rank = w_dt_o.shape[0]
    w_x_o[...] = jnp.concatenate([few_rows(r, CH) for r in range(0, width, CH)], axis=0)
    at = width
    a_log_o[...] = jnp.concatenate([few_rows(r, CH) for r in range(at, at + state, CH)], axis=0)
    at += state
    w_dt_o[...] = jnp.concatenate([few_rows(r, CH) for r in range(at, at + rank, CH)], axis=0)
    at += rank
    conv_w_o[...] = few_rows(at, 4)
    conv_b_o[...] = few_rows(at + 4, 1)
    dt_bias_o[...] = few_rows(at + 5, 1)
    d_skip_o[...] = few_rows(at + 6, 1)
    gain_o[...] = few_rows(at + 7, 1)[:, :feat]

    length = gtok.shape[0]
    per = feat // LANE
    padded = spread_plain(pad[...].astype(F32), feat)

    def three(first):
        rows = [
            jnp.concatenate([halo[first + b * per + lt : first + b * per + lt + 1, :] for lt in range(per)], axis=1)
            for b in range(3)
        ]
        return rows, jnp.zeros((CH - 3, feat), F32)

    rows, blank = three(0)
    first = jnp.concatenate(rows + [blank], axis=0)
    rows, blank = three(3 * per)
    last = jnp.concatenate([blank] + rows, axis=0)
    gtok_o[...] = gtok[...]
    gtok_o[:CH] = gtok[:CH] + padded[:CH] * first
    gtok_o[length - CH :] = gtok[length - CH :] + padded[length - CH :] * last


def spread_plain(row, width):
    length = row.shape[1]
    rows = lax.broadcasted_iota(jnp.int32, (length, length), 0)
    cols = lax.broadcasted_iota(jnp.int32, (length, length), 1)
    picked = (jnp.where(rows == cols, 1.0, 0.0) * row).astype(BF16)
    return nn(picked, jnp.ones((length, width), BF16))


def unpack(rs_bits, parts, gtok, halo, pad, state, rank):
    length, feat = gtok.shape
    pieces = 1 << rs_bits
    inner = state[1]
    width = rank + 2 * state[0]
    shape = lambda *dims: jax.ShapeDtypeStruct(dims, F32)
    return pl.pallas_call(
        lambda *refs: unpack_kernel(rs_bits, len(parts), *refs),
        out_shape=(
            shape(length, feat),
            shape(1, feat),
            shape(feat, 2 * inner),
            shape(4, inner),
            shape(1, inner),
            shape(width, inner),
            shape(rank, inner),
            shape(1, inner),
            shape(state[0], inner),
            shape(1, inner),
            shape(inner, feat),
        ),
        scratch_shapes=[pltpu.VMEM((pieces, CH, LANE), F32)] * 2,
        compiler_params=params(6),
        name="unpack",
    )(*parts, gtok, halo, pad)


def body(tokens, resets, pad_mask, norm_gain, w_in, conv_w, conv_b, w_x, w_dt, dt_bias, a_log, d_skip, w_out, grad_out):
    count = lax.axis_size("seq")
    bits = count.bit_length() - 1
    rs_bits = min(5, bits)
    length = tokens.shape[0]
    keep_row, pad_row = resets.reshape(1, length), pad_mask.reshape(1, length)

    def exchange(value, apart):
        return lax.ppermute(value, "seq", [(i, i ^ apart) for i in range(count)])

    def swap(value, bit):
        return exchange(value, 1 << bit)

    across = [(i, i + 1) for i in range(1, count - 1, 2)] + [(i + 1, i) for i in range(1, count - 1, 2)]

    def swap_across(value):
        return lax.ppermute(value, "seq", across)

    to_sib, to_oth, kept = edges(
        tokens, keep_row, pad_row, norm_gain, w_in[0], grad_out, w_out[0],
        conv_w[0], conv_b, w_x[0].T, w_dt[0], dt_bias, a_log[0].T, d_skip,
    )
    (tok, keep, pad, gain, w_in_0, gout, w_out_0, conv_w_0, conv_b_0, w_x_t, w_dt_0, dt_bias_0, a_log_t, skip) = kept
    oth = swap_across(to_oth)
    sib = swap(to_sib, 0)
    xb, z, go, gy = project(tok, pad, gain, w_in_0, gout, w_out_0)
    xc, dt, sig, conv, mask, dbl, xbh, sx, mx, total, de, dx, bc, a2, decay = prepare(
        sib, oth, keep, gain, w_in_0, conv_w_0, conv_b_0, w_x_t, w_dt_0, dt_bias_0, a_log_t, xb, gy
    )

    sibling = swap(total, 0)
    group = pair(a2, total, sibling)
    group, gate_in = lax.optimization_barrier((group, (z, go, conv, xc, gy)))
    at_hand = ready(w_dt.shape[1], a_log.shape[2], tok, gout, gain, w_in_0, w_out_0, skip, *gate_in)
    stages = []
    steps = [range(first, min(first + 2, bits)) for first in range(1, bits, 2)]
    step = steps[-1]
    distances = [i << step[0] for i in range(1, 1 << len(step))]
    for first_step in steps[:-1]:
        members = [group] + [exchange(group, i << first_step[0]) for i in range(1, 1 << len(first_step))]
        halves = distances if first_step is steps[-2] else ()
        entering, *group = stage(first_step[0], halves, a2, members)
        stages.append(entering)
        if not halves:
            (group,) = group
    group, at_hand = lax.optimization_barrier((group, at_hand))
    theirs = [exchange(value, apart) for value, apart in zip(group, distances)]
    stages.append(last_stage(step[0], a2, theirs))
    mine_half = enter(a2, stages)
    other_half = swap(mine_half, 0)

    y, h, car = forward(mine_half, other_half, sibling, sx, de, dx, bc, a2, decay)
    def reduced(part, step):
        size = part.shape[0] >> len(step)
        total = part[:size]
        for i in ((3, 1, 2) if len(step) == 2 else (1,)):
            slot = reverse_bits(i, len(step))
            total = total + exchange(part[slot * size : (slot + 1) * size], i << step[0])
        return total

    (x, g, nth, ntl, gh, gl, wih, wil, wfh, wfl, woh, wol, vfh, vfl, gate, zgrad, cgrad, xch, xcl, skip_sum,
     pick_b, pick_c) = at_hand
    rs_steps = [range(0, 1)] + [range(first, min(first + 2, rs_bits)) for first in range(1, rs_bits, 2)]
    mixed, gzh, gzl, part_a = early(rs_bits, x, nth, ntl, gh, gl, woh, wol, vfh, vfl, gate, zgrad, skip, xc, y)
    part_a, h = lax.optimization_barrier((part_a, h))
    part_a = reduced(part_a, range(0, 1))
    back_f = backward(0, mx, car, h, de, dx, bc, a2, decay, gy)
    part_a, back_f, h = lax.optimization_barrier((part_a, back_f, h))
    part_a = reduced(part_a, range(1, 2))
    back_r = backward(1, mx, car, h, de, dx, bc, a2, decay, gy)
    gxh, gxl, halo_g, few = inner_back(
        pad, conv_w_0, w_x_t, w_dt_0, skip, a2,
        xb, gy, xc, dt, sig, cgrad, mask, dbl, xbh, xch, xcl, skip_sum, pick_b, pick_c, *back_f, *back_r,
    )
    gtok, to_left, to_right, part_b = tail(
        rs_bits, sib, oth, gain, x, g, nth, ntl, wih, wil, wfh, wfl, gzh, gzl, gxh, gxl, halo_g, few
    )
    part_a, part_b = lax.optimization_barrier((part_a, part_b))
    part_a, part_b = reduced(part_a, range(2, 3)), reduced(part_b, rs_steps[0])
    part_b = reduced(part_b, rs_steps[1])
    own = jnp.concatenate([part_a, part_b], axis=1)
    for step in rs_steps[2:]:
        own = reduced(own, step)
    for bit in range(rs_bits, bits):
        own = own + swap(own, bit)
    tall = own.shape[1]
    halo = jnp.concatenate([own[0, tall - 16 : tall - 12], own[0, tall - 8 :]], axis=0)
    if bits > rs_bits:
        pairs = [(i, i + 1) for i in range(count - 1)]
        from_left = lax.ppermute(to_right, "seq", pairs)[:3]
        from_right = lax.ppermute(to_left, "seq", [(j, i) for i, j in pairs])[:3]
        halo = jnp.concatenate([from_left.reshape(-1, LANE), from_right.reshape(-1, LANE)], axis=0)
    own = own[:, : tall - 8]
    for step in reversed(rs_steps[1:]):
        near = [exchange(own, reverse_bits(i, len(step)) << step[0]) for i in range((1 << len(step)) - 1, 0, -1)]
        near = [own] + near[::-1]
        if step is not rs_steps[1]:
            own = jnp.concatenate(near, axis=0)
    far = [swap(part, 0) for part in near]
    outs = unpack(rs_bits, near + far, gtok, halo, pad, a_log_t.shape, w_dt.shape[1])
    gtok, g_gain, g_w_in, g_conv_w, g_conv_b, g_w_x, g_w_dt, g_dt_bias, g_a_log, g_d_skip, g_w_out = outs
    return (
        mixed, gtok, g_gain, g_w_in[None], g_conv_w[None], g_conv_b, g_w_x.T[None], g_w_dt[None],
        g_dt_bias, g_a_log.T[None], g_d_skip, g_w_out[None],
    )


def solution(mesh):
    rows, whole = P("seq", None), P()
    return jax.shard_map(
        body,
        mesh=mesh,
        in_specs=(rows, P("seq"), P("seq")) + (whole,) * 10 + (rows,),
        out_specs=(rows, rows) + (whole,) * 10,
        check_vma=False,
    )
```

```python
import jax
import jax.numpy as jnp
from jax import lax
from jax.experimental import pallas as pl
from jax.experimental.pallas import tpu as pltpu
from jax.sharding import PartitionSpec as P

F32 = jnp.float32
BF16 = jnp.bfloat16
EPS = 1e-05
LOG2E = 1.4426950408889634
LN2 = 0.6931471805599453
BIG = 1e9
CH = 8
LANE = 128
MIB = 1024 * 1024


def nn(a, b):
    return lax.dot_general(a, b, (((1,), (0,)), ((), ())), preferred_element_type=F32)


def nt(a, b):
    return lax.dot_general(a, b, (((1,), (1,)), ((), ())), preferred_element_type=F32)


def tn(a, b):
    return lax.dot_general(a, b, (((0,), (0,)), ((), ())), preferred_element_type=F32)


def split(x):
    high = x.astype(BF16)
    return high, (x - high.astype(F32)).astype(BF16)


def split3(x):
    high = x.astype(BF16)
    rest = x - high.astype(F32)
    mid = rest.astype(BF16)
    return high, mid, (rest - mid.astype(F32)).astype(BF16)


def mm(dot, a, b):
    ah, al = a if isinstance(a, tuple) else split(a)
    bh, bl = b if isinstance(b, tuple) else split(b)
    return dot(ah, bh) + (dot(ah, bl) + dot(al, bh))


def flip_matrix(size):
    rows = lax.broadcasted_iota(jnp.int32, (size, size), 0)
    cols = lax.broadcasted_iota(jnp.int32, (size, size), 1)
    return jnp.where(rows + cols == size - 1, 1.0, 0.0).astype(BF16)


def flipped(x):
    flip = flip_matrix(x.shape[1])
    high, mid, low = split3(x)
    return nn(high, flip) + (nn(mid, flip) + nn(low, flip))


def order_matrix(length):
    steps = length // CH
    rows = lax.broadcasted_iota(jnp.int32, (length, length), 0)
    cols = lax.broadcasted_iota(jnp.int32, (length, length), 1)
    token = (rows & (CH - 1)) * steps + (rows >> 3)
    return jnp.where(cols == token, 1.0, 0.0)


def exact(dot, order, x):
    high, mid, low = split3(x)
    order = order.astype(BF16)
    return dot(order, high) + (dot(order, mid) + dot(order, low))


def ordered(ref):
    return exact(nn, order_matrix(ref.shape[0]), ref[...])


def store_ordered(ref, value):
    ref[...] = exact(tn, order_matrix(ref.shape[0]), value)


def spread(row, order=None):
    length = row.shape[1]
    picked = ((order_matrix(length) if order is None else order) * row).astype(BF16)
    return nn(picked, jnp.ones((length, LANE), BF16))


def sigmoid(x):
    return 1.0 / (1.0 + jnp.exp(-x))


def normalize(x, gain):
    factor = lax.rsqrt(jnp.mean(x * x, axis=1, keepdims=True) + EPS)
    return factor, x * factor * gain


def both_orders(normed):
    flip = flip_matrix(normed.shape[1])
    high, low = split(normed)
    return (
        jnp.concatenate([high, nn(high, flip).astype(BF16)], axis=0),
        jnp.concatenate([low, nn(low, flip).astype(BF16)], axis=0),
    )


def params(mib):
    return pltpu.CompilerParams(vmem_limit_bytes=mib * MIB)


def in_hbm(*arrays):
    return tuple(pltpu.with_memory_space_constraint(x, pltpu.HBM) for x in arrays)


def edges_kernel(tok, resets, pad, *refs):
    more = (len(refs) - 5) // 2
    to_sib, to_oth, *kept = refs[more:]
    for ref, kept_o in zip((tok, resets, pad) + refs[:more], kept):
        kept_o[...] = ref[...]
    length, feat = tok.shape
    sub = lax.broadcasted_iota(jnp.int32, (CH, length), 0)
    lane = lax.broadcasted_iota(jnp.int32, (CH, length), 1)
    real = pad[...].astype(F32)
    row = lax.broadcasted_iota(jnp.int32, (CH, feat), 0)
    flags = 1.0 - resets[...].astype(F32)
    flags = jnp.concatenate([flags, jnp.zeros((1, feat - length), F32)], axis=1)

    def message(rows, start):
        col = jnp.sum(jnp.where(lane == sub + start, real, 0.0), axis=1, keepdims=True)
        return jnp.where(row < 3, rows * col, jnp.where(row == 3, flags, 0.0))

    first = message(tok[:CH, :], 0)
    last = message(pltpu.roll(tok[length - CH :, :], 3, 0), length - 3)
    odd = (lax.axis_index("seq") & 1) == 1
    to_sib[...] = jnp.where(odd, first, last)
    to_oth[...] = jnp.where(odd, last, first)


def edges(*arrays):
    shape = jax.ShapeDtypeStruct((CH, arrays[0].shape[1]), F32)
    found = pl.pallas_call(
        edges_kernel,
        out_shape=(shape, shape) + tuple(jax.ShapeDtypeStruct(x.shape, x.dtype) for x in arrays),
        compiler_params=params(8),
        name="edges",
    )(*in_hbm(*arrays))
    return found[0], found[1], found[2:]


def project_kernel(tok, pad, gain, w_in, gout, w_out, a_log, xb_o, z_o, go_o, gy_o, wih_o, wil_o, spread_o, a2_o):
    inner = w_out.shape[0]
    x = ordered(tok)
    normed = normalize(x, gain[...])[1]
    w_parts = split(w_in[...])
    wih_o[...], wil_o[...] = w_parts
    proj = mm(nn, both_orders(normed), w_parts)
    pad_col = spread(pad[...].astype(F32))
    pad_all = jnp.concatenate([pad_col, pad_col], axis=0)
    g = ordered(gout)
    gh, gl = both_orders(g)
    go = mm(nt, (gh, gl), split(w_out[...]))
    for lt in range(inner // LANE):
        cols = slice(lt * LANE, (lt + 1) * LANE)
        z = proj[:, inner + lt * LANE : inner + (lt + 1) * LANE]
        xb_o[:, cols] = proj[:, cols] * pad_all
        z_o[:, cols] = z
        go_o[:, cols] = go[:, cols]
        gy_o[:, cols] = go[:, cols] * (z * sigmoid(z))
    width = spread_o.shape[0] // 3
    row = lax.broadcasted_iota(jnp.int32, spread_o.shape, 0)
    entry = lax.broadcasted_iota(jnp.int32, spread_o.shape, 1) >> 7
    row = jnp.where(row >= 2 * width, row - 2 * width, jnp.where(row >= width, row - width, row))
    spread_o[...] = jnp.where(row == entry, 1.0, 0.0).astype(BF16)
    a2 = jnp.exp(a_log[...]) * (-LOG2E)
    for n in range(a2.shape[0]):
        a2_o[n] = jnp.broadcast_to(a2[n : n + 1], (CH, inner))


def project(tok, pad, gain, w_in, gout, w_out, a_log):
    big = jax.ShapeDtypeStruct((2 * tok.shape[0], w_out.shape[0]), F32)
    part = jax.ShapeDtypeStruct(w_in.shape, BF16)
    state, inner = a_log.shape
    return pl.pallas_call(
        project_kernel,
        out_shape=(
            big, big, big, big, part, part,
            jax.ShapeDtypeStruct((6 * state, 2 * state * LANE), BF16),
            jax.ShapeDtypeStruct((state, CH, inner), F32),
        ),
        compiler_params=params(8),
        name="project",
    )(tok, pad, gain, w_in, gout, w_out, a_log)


def pick_sides(from_sibling, from_other):
    odd = (lax.axis_index("seq") & 1) == 1
    left = jnp.where(odd, from_sibling, from_other)
    right = jnp.where(odd, from_other, from_sibling)
    return left, right


def rows_of(ref, first, count, cols):
    block = ref[pl.ds(pl.multiple_of(first, CH), count), cols]
    return [jnp.broadcast_to(block[n : n + 1], (CH, LANE)) for n in range(count)]


def sub_iota():
    return lax.broadcasted_iota(jnp.int32, (CH, LANE), 0)


def shifted(value, up):
    return pltpu.roll(value, 1 if up else CH - 1, 0)


def chunk_weights(total, up):
    sub = sub_iota()
    found = []
    width = total
    for reach in (1, 2, 4):
        inside = (sub >= reach) if up else (sub < CH - reach)
        found.append(jnp.where(inside, width, BIG))
        width = width + pltpu.roll(width, reach if up else CH - reach, 0)
    return found


def outside_sum(total, up):
    sub = sub_iota()
    value = jnp.where((sub >= 1) if up else (sub < CH - 1), shifted(total, up), 0.0)
    for reach in (1, 2, 4):
        inside = (sub >= reach) if up else (sub < CH - reach)
        value = value + jnp.where(inside, pltpu.roll(value, reach if up else CH - reach, 0), 0.0)
    return value


def chunk_scan(value, weights, a2, up):
    for reach, weight in zip((1, 2, 4), weights):
        value = value + jnp.exp2(weight * a2) * pltpu.roll(value, reach if up else CH - reach, 0)
    sub = sub_iota()
    enter = jnp.where((sub >= 1) if up else (sub < CH - 1), shifted(value, up), 0.0)
    leave = value[CH - 1 : CH] if up else value[0:1]
    return enter, leave


def prepare_kernel(
    sib, oth, keep, gain, wih, wil, conv_w, conv_b, w_x, w_dt, dt_bias, spread_s, a2_s, xb, gy,
    xc_o, dt_o, pre_o, conv_o, mask_o, dbl_o, xbh_o, sx_o, mx_o, sum_o, de_s, dx_s, bc_s, decay_o, drive_o,
    leave_s,
):
    inner, rank = w_x.shape[1], w_dt.shape[0]
    state = a2_s.shape[0]
    length = xb.shape[0] // 2
    steps = length // CH
    tiles = inner // LANE
    left, right = pick_sides(sib[...], oth[...])
    hn_l = normalize(left, gain[...])[1]
    hn_r = normalize(right, gain[...])[1]
    flip = flip_matrix(hn_r.shape[1])
    lh, ll = split(hn_l)
    rh, rl = split(hn_r)
    halo = (
        jnp.concatenate([lh, nn(rh, flip).astype(BF16)], axis=0),
        jnp.concatenate([ll, nn(rl, flip).astype(BF16)], axis=0),
    )
    xbh = mm(nn, halo, (wih[:, :inner], wil[:, :inner]))
    xbh_o[...] = xbh
    lane = lax.broadcasted_iota(jnp.int32, (1, length), 1)
    here = 1.0 - keep[...].astype(F32)
    before, after = left[3:4, :length], right[3:4, :length]

    def back(k):
        return jnp.where(lane < k, pltpu.roll(before, k, 1), pltpu.roll(here, k, 1))

    def ahead(k):
        return jnp.where(
            lane >= length - k,
            pltpu.roll(after, length - k, 1),
            pltpu.roll(here, length - k, 1),
        )

    f1 = here
    f2 = f1 * back(1)
    f3 = f2 * back(2)
    r1 = ahead(1)
    r2 = r1 * ahead(2)
    r3 = r2 * ahead(3)
    token_order = order_matrix(length)
    for i, row in enumerate((f1, f2, f3, r1, r2, r3)):
        mask_o[i * length : (i + 1) * length, :] = spread(row, token_order)

    sub = sub_iota()

    def conv_tile(lt, carry):
        cols = pl.ds(pl.multiple_of(lt * LANE, LANE), LANE)
        xbh_t = xbh_o[:, cols]
        taps = [conv_w[k : k + 1, cols] for k in range(4)]
        bias = conv_b[:, cols]
        xf = [xb[j * CH : (j + 1) * CH, cols] for j in range(steps)]
        edge = [
            jnp.where(sub == 0, xbh_t[b : b + 1], pltpu.roll(xf[steps - 3 + b], 1, 0))
            for b in range(3)
        ]
        xf = edge + xf
        for j in range(steps):
            rows = slice(j * CH, (j + 1) * CH)
            v = bias + taps[0] * xf[j + 3]
            for k in range(1, 4):
                v = v + taps[k] * (mask_o[(k - 1) * length + j * CH : (k - 1) * length + (j + 1) * CH, :] * xf[j + 3 - k])
            conv_o[rows, cols] = v
            xc_o[rows, cols] = v * sigmoid(v)
        xr = [xb[length + j * CH : length + (j + 1) * CH, cols] for j in range(steps)]
        xr = xr + [
            jnp.where(sub == CH - 1, xbh_t[8 + b : 9 + b], pltpu.roll(xr[b], CH - 1, 0))
            for b in range(3)
        ]
        for j in range(steps):
            rows = slice(length + j * CH, length + (j + 1) * CH)
            v = bias + taps[0] * xr[j]
            for k in range(1, 4):
                v = v + taps[k] * (mask_o[(k + 2) * length + j * CH : (k + 2) * length + (j + 1) * CH, :] * xr[j + k])
            conv_o[rows, cols] = v
            xc_o[rows, cols] = v * sigmoid(v)
        return carry

    lax.fori_loop(0, tiles, conv_tile, 0)
    dbl = mm(nt, xc_o[...], w_x[...])
    dbl_o[...] = dbl
    pre_all = mm(nn, dbl[:, :rank], w_dt[...])
    bc_s[...] = nn(jnp.concatenate(split3(dbl[:, rank:]), axis=1), spread_s[...])
    for lt in range(tiles):
        cols = slice(lt * LANE, (lt + 1) * LANE)
        pre = pre_all[:, cols] + dt_bias[:, cols]
        e = jnp.exp(-jnp.abs(pre))
        u = 1.0 + e
        log1p = jnp.where(u == 1.0, e, jnp.log(u) * (e / (u - 1.0)))
        dt = jnp.maximum(pre, 0.0) + log1p
        dt_o[:, cols] = dt
        pre_o[:, cols] = pre
        dx_s[:, cols] = dt * xc_o[:, cols]
        cut = jnp.concatenate([mask_o[:length], mask_o[3 * length : 4 * length]], axis=0)
        de_s[:, cols] = dt + BIG * (1.0 - cut)

    group = 8
    cols_of = [slice(t * LANE, (t + 1) * LANE) for t in range(tiles)]
    for dirn in range(2):
        order = list(range(steps)) if dirn == 0 else list(range(steps - 1, -1, -1))
        base = dirn * length
        up = dirn == 0
        s_row, m_row = (0, 3) if dirn == 0 else (2, 1)
        totals = []
        for cols in cols_of:
            total = jnp.zeros((CH, LANE), F32)
            for j in range(steps):
                total = total + de_s[base + j * CH : base + (j + 1) * CH, cols]
            sum_o[4 * state + dirn : 4 * state + dirn + 1, cols] = jnp.sum(total, axis=0, keepdims=True)
            totals.append(total)

        def some(g, carry, order=order, base=base, up=up, dirn=dirn, s_row=s_row, m_row=m_row, totals=totals):
            n0 = g * group
            at_b, at_c = lanes_of(n0, group), lanes_of(state + n0, group)
            keys = [(n, t) for n in range(group) for t in range(tiles)]
            a2 = {(n, t): a2_s[n0 + n, :, cols_of[t]] for n, t in keys}
            h, m = {}, {}
            for at, j in enumerate(order):
                rows = slice(base + j * CH, base + (j + 1) * CH)
                de = [de_s[rows, c] for c in cols_of]
                dx = [dx_s[rows, c] for c in cols_of]
                for n in range(group):
                    b_n = bc_s[rows, at_b[n]]
                    for t, cols in enumerate(cols_of):
                        d = jnp.exp2(de[t] * a2[n, t])
                        decay_o[dirn, at, n0 + n, :, cols] = d
                        drive = dx[t] * b_n
                        drive_o[dirn, at, n0 + n, :, cols] = drive
                        h[n, t] = drive if at == 0 else d * h[n, t] + drive
            for at in range(steps - 1, -1, -1):
                rows = slice(base + order[at] * CH, base + (order[at] + 1) * CH)
                gyj = [gy[rows, c] for c in cols_of]
                for n in range(group):
                    c_n = bc_s[rows, at_c[n]]
                    for t, cols in enumerate(cols_of):
                        own = gyj[t] * c_n
                        d = decay_o[dirn, at, n0 + n, :, cols]
                        m[n, t] = d * (own if at == steps - 1 else own + m[n, t])
            for t in range(tiles):
                w_s, w_m = chunk_weights(totals[t], up), chunk_weights(totals[t], not up)
                for n in range(group):
                    enter, leave = chunk_scan(h[n, t], w_s, a2[n, t], up)
                    sx_o[dirn, n0 + n, :, cols_of[t]] = enter
                    leave_s[s_row * state + n0 + n, :, cols_of[t]] = jnp.broadcast_to(leave, (CH, LANE))
                    enter, leave = chunk_scan(m[n, t], w_m, a2[n, t], not up)
                    mx_o[dirn, n0 + n, :, cols_of[t]] = enter
                    leave_s[m_row * state + n0 + n, :, cols_of[t]] = jnp.broadcast_to(leave, (CH, LANE))
            return carry

        lax.fori_loop(0, state // group, some, 0)
    for row in range(0, 4 * state, CH):
        for cols in cols_of:
            sum_o[row : row + CH, cols] = jnp.concatenate([leave_s[row + i, 0:1, cols] for i in range(CH)], axis=0)
    sum_o[4 * state + 2 :, :] = jnp.zeros((sum_o.shape[0] - 4 * state - 2, inner), F32)


def lanes_of(first, count):
    return [pl.ds(pl.multiple_of((first + n) * LANE, LANE), LANE) for n in range(count)]


def prepare(sib, oth, keep, gain, wih, wil, conv_w, conv_b, w_x, w_dt, dt_bias, spread_s, a2, xb, gy):
    rows, inner = xb.shape
    state, width = a2.shape[0], w_x.shape[0]
    big = pltpu.VMEM((rows, inner), F32)
    edge = pltpu.VMEM((2, state, CH, inner), F32)
    return pl.pallas_call(
        prepare_kernel,
        out_shape=(
            big, big, big, big,
            pltpu.VMEM((3 * rows, LANE), F32),
            pltpu.VMEM((rows, width), F32),
            pltpu.VMEM((2 * CH, inner), F32),
            edge, edge,
            pltpu.VMEM((4 * state + 8, inner), F32),
            big, big,
            pltpu.VMEM((rows, 2 * state * LANE), F32),
            pltpu.VMEM((2, rows // 2 // CH, state, CH, inner), F32),
            pltpu.VMEM((2, rows // 2 // CH, state, CH, inner), F32),
        ),
        scratch_shapes=[pltpu.VMEM((4 * state, CH, inner), F32)],
        compiler_params=params(8),
        name="prepare",
    )(sib, oth, keep, gain, wih, wil, conv_w, conv_b, w_x, w_dt, dt_bias, spread_s, a2, xb, gy)


def summary_parts(ref_value, state):
    return [ref_value[i * state : (i + 1) * state] for i in range(4)]


def pair_kernel(a2_s, mine, theirs, out):
    state, half = a2_s.shape[0], out.shape[1]
    core = lax.axis_index("seq") & 1
    cols = pl.ds(pl.multiple_of(core * half, half), half)
    a2 = half_a2(a2_s, half)
    me, it = mine[:, cols], theirs[:, cols]
    low, high = jnp.where(core == 1, it, me), jnp.where(core == 1, me, it)
    put_total(out, joined(low, high, a2, state), state)


def joined(low, high, a2, state):
    low_f, low_r = low[4 * state : 4 * state + 1], low[4 * state + 1 : 4 * state + 2]
    high_f, high_r = high[4 * state : 4 * state + 1], high[4 * state + 1 : 4 * state + 2]
    lows, highs = summary_parts(low, state), summary_parts(high, state)
    return [
        lows[0] * jnp.exp2(high_f * a2) + highs[0],
        lows[1] * jnp.exp2(high_r * a2) + highs[1],
        highs[2] * jnp.exp2(low_r * a2) + lows[2],
        highs[3] * jnp.exp2(low_f * a2) + lows[3],
        low_f + high_f,
        low_r + high_r,
    ]


def put_total(out, parts, state):
    for i in range(4):
        out[i * state : (i + 1) * state] = parts[i]
    rest = jnp.zeros((out.shape[0] - 4 * state - 2, out.shape[1]), F32)
    out[4 * state :] = jnp.concatenate([parts[4], parts[5], rest], axis=0)


def half_a2(a2_s, half):
    core = lax.axis_index("seq") & 1
    cols = pl.ds(pl.multiple_of(core * half, half), half)
    return jnp.concatenate([a2_s[n, 0:1, cols] for n in range(a2_s.shape[0])], axis=0)


def stage_kernel(first, halves, a2_s, *refs):
    outs = 1 + len(halves) if halves else 2
    members, out, held = refs[: -outs - 1], refs[-outs - 1 : -1], refs[-1]
    count = len(members)
    state, half = a2_s.shape[0], out[0].shape[1]
    a2 = half_a2(a2_s, half)
    at = (lax.axis_index("seq") >> first) & (count - 1)
    for i, ref in enumerate(members):
        held[at ^ i] = ref[...]
    zero, none = jnp.zeros((state, half), F32), jnp.zeros((1, half), F32)

    def run_through(order, rows, reach):
        run = [zero, zero, none, none]
        seen = list(run)
        for i in order:
            seen = [jnp.where(at == i, now, old) for now, old in zip(run, seen)]
            df, dr = held[i, 4 * state : 4 * state + 1], held[i, 4 * state + 1 : 4 * state + 2]
            decays = [jnp.exp2((df, dr)[w] * a2) for w in reach]
            run = [run[k] * decays[k] + held[i, rows[k] * state : (rows[k] + 1) * state] for k in range(2)] + [
                run[2] + df,
                run[3] + dr,
            ]
        return run, seen

    right, seen = run_through(range(count), (0, 1), (0, 1))
    left, seen_left = run_through(range(count - 1, -1, -1), (2, 3), (1, 0))
    enter = out[0]
    enter[:state], enter[state : 2 * state] = seen[0], seen[1]
    enter[2 * state : 3 * state], enter[3 * state : 4 * state] = seen_left[0], seen_left[1]
    blank = jnp.zeros((CH, half), F32)
    enter[4 * state :] = jnp.concatenate([seen[2], seen[3], seen_left[2], seen_left[3], blank[:4]], axis=0)
    sums = jnp.concatenate([right[2], right[3], blank[:6]], axis=0)
    if halves:
        me = lax.axis_index("seq")
        for ref, apart in zip(out[1:], halves):
            later = (me ^ apart) > me
            ref[:state] = jnp.where(later, right[0], left[0])
            ref[state : 2 * state] = jnp.where(later, right[1], left[1])
            ref[2 * state :] = sums
    else:
        for i, value in enumerate((right[0], right[1], left[0], left[1])):
            out[1][i * state : (i + 1) * state] = value
        out[1][4 * state :] = sums


def last_kernel(first, a2_s, *refs):
    theirs, out, held = refs[:-2], refs[-2], refs[-1]
    count = len(theirs) + 1
    state, half = a2_s.shape[0], out.shape[1]
    a2 = half_a2(a2_s, half)
    at = (lax.axis_index("seq") >> first) & (count - 1)
    held[at] = jnp.zeros(held.shape[1:], F32)
    for i, ref in enumerate(theirs):
        held[at ^ (i + 1)] = ref[...]

    def run_through(order, reach, inside):
        run = [jnp.zeros((state, half), F32)] * 2
        for i in order:
            sums = held[i, 2 * state : 2 * state + 1], held[i, 2 * state + 1 : 2 * state + 2]
            for k in range(2):
                longer = run[k] * jnp.exp2(sums[reach[k]] * a2) + held[i, k * state : (k + 1) * state]
                run[k] = jnp.where(inside(i), longer, run[k])
        return run

    found = run_through(range(count - 1), (0, 1), lambda i: i < at)
    found = found + run_through(range(count - 1, 0, -1), (1, 0), lambda i: i > at)
    for i in range(4):
        out[i * state : (i + 1) * state] = found[i]


def pair(a2_s, mine, theirs):
    rows, inner = mine.shape
    return pl.pallas_call(
        pair_kernel,
        out_shape=jax.ShapeDtypeStruct((rows, inner // 2), F32),
        compiler_params=params(2),
        name="pair",
    )(a2_s, mine, theirs)


def stage(first, halves, a2_s, members):
    shape = jax.ShapeDtypeStruct(members[0].shape, F32)
    part = jax.ShapeDtypeStruct((2 * a2_s.shape[0] + CH, members[0].shape[1]), F32)
    return pl.pallas_call(
        lambda *refs: stage_kernel(first, halves, *refs),
        out_shape=(shape,) + (part,) * len(halves) if halves else (shape, shape),
        scratch_shapes=[pltpu.VMEM((len(members),) + members[0].shape, F32)],
        compiler_params=params(4),
        name="stage",
    )(a2_s, *members)


def last_stage(first, a2_s, theirs):
    return pl.pallas_call(
        lambda *refs: last_kernel(first, *refs),
        out_shape=jax.ShapeDtypeStruct((4 * a2_s.shape[0], theirs[0].shape[1]), F32),
        scratch_shapes=[pltpu.VMEM((len(theirs) + 1,) + theirs[0].shape, F32)],
        compiler_params=params(4),
        name="stage",
    )(a2_s, *theirs)


def enter_kernel(a2_s, *refs):
    stages, out = refs[:-1], refs[-1]
    state, half = a2_s.shape[0], out.shape[1]
    a2 = half_a2(a2_s, half)
    value = [stages[-1][i * state : (i + 1) * state] for i in range(4)]
    for ref in reversed(stages[:-1]):
        reach = [ref[4 * state + i : 4 * state + i + 1] for i in range(4)]
        value = [
            ref[i * state : (i + 1) * state] + value[i] * jnp.exp2(reach[w] * a2)
            for i, w in ((0, 0), (1, 1), (2, 3), (3, 2))
        ]
    for i in range(4):
        out[i * state : (i + 1) * state] = value[i]


def enter(a2_s, stages):
    half = stages[0].shape[1]
    return pl.pallas_call(
        enter_kernel,
        out_shape=jax.ShapeDtypeStruct((4 * a2_s.shape[0], half), F32),
        compiler_params=params(2),
        name="enter",
    )(a2_s, *stages)


def carry_in(car_s, a2_s, mine_half, other_half, sibling):
    state, inner = a2_s.shape[0], a2_s.shape[2]
    half = inner // 2
    odd = (lax.axis_index("seq") & 1) == 1
    a2 = jnp.concatenate([a2_s[n, 0:1, :] for n in range(state)], axis=0)
    left, right = jnp.where(odd, other_half[...], mine_half[...]), jnp.where(odd, mine_half[...], other_half[...])
    into = jnp.concatenate([left, right], axis=1)
    df, dr = sibling[4 * state : 4 * state + 1], sibling[4 * state + 1 : 4 * state + 2]
    for i, reach, through in ((0, df, odd), (1, dr, odd), (2, dr, ~odd), (3, df, ~odd)):
        rows = slice(i * state, (i + 1) * state)
        value = jnp.where(through, into[rows] * jnp.exp2(reach * a2) + sibling[rows], into[rows])
        for n in range(state):
            car_s[i * state + n] = jnp.broadcast_to(value[n : n + 1], (CH, inner))


def forward_kernel(
    mine_half, other_half, sibling, sx, de_s, dx_s, bc_s, a2_s, decay, drive,
    y_s, h_s, car_o,
    before_s,
):
    rows2, inner = de_s.shape
    length = rows2 // 2
    steps = length // CH
    tiles = inner // LANE
    state = a2_s.shape[0]
    carry_in(car_o, a2_s, mine_half, other_half, sibling)
    y_s[...] = jnp.zeros(y_s.shape, F32)
    group = 4
    cols_of = [slice(t * LANE, (t + 1) * LANE) for t in range(tiles)]
    for dirn in range(2):
        order = list(range(steps)) if dirn == 0 else list(range(steps - 1, -1, -1))
        base = dirn * length
        s_row = 0 if dirn == 0 else 2
        for cols in cols_of:
            total = jnp.zeros((CH, LANE), F32)
            for j in range(steps):
                total = total + de_s[base + j * CH : base + (j + 1) * CH, cols]
            before_s[:, cols] = outside_sum(total, dirn == 0)

        def some(g, carry, dirn=dirn, order=order, base=base, s_row=s_row):
            n0 = g * group
            at_b, at_c = lanes_of(n0, group), lanes_of(state + n0, group)
            h = {}
            for n in range(group):
                for t, cols in enumerate(cols_of):
                    into = jnp.exp2(before_s[:, cols] * a2_s[n0 + n, :, cols]) * car_o[s_row * state + n0 + n, :, cols]
                    h[n, t] = sx[dirn, n0 + n, :, cols] + into
                    h_s[dirn, 0, n0 + n, :, cols] = h[n, t]
            for at, j in enumerate(order):
                rows = slice(base + j * CH, base + (j + 1) * CH)
                dx = [dx_s[rows, c] for c in cols_of]
                y = [None] * tiles
                for n in range(group):
                    c_n = bc_s[rows, at_c[n]]
                    for t, cols in enumerate(cols_of):
                        h[n, t] = decay[dirn, at, n0 + n, :, cols] * h[n, t] + drive[dirn, at, n0 + n, :, cols]
                        h_s[dirn, at + 1, n0 + n, :, cols] = h[n, t]
                        term = h[n, t] * c_n
                        y[t] = term if n == 0 else y[t] + term
                for t, cols in enumerate(cols_of):
                    y_s[rows, cols] += y[t]
            return carry

        lax.fori_loop(0, state // group, some, 0)


def forward(mine_half, other_half, sibling, sx, de, dx, bc, a2, decay, drive):
    rows2, inner = de.shape
    state = a2.shape[0]
    steps = rows2 // 2 // CH
    return pl.pallas_call(
        forward_kernel,
        out_shape=(
            jax.ShapeDtypeStruct((rows2, inner), F32),
            jax.ShapeDtypeStruct((2, steps + 1, state, CH, inner), F32),
            jax.ShapeDtypeStruct((4 * state, CH, inner), F32),
        ),
        scratch_shapes=[pltpu.VMEM((CH, inner), F32)],
        compiler_params=params(4),
        name="forward",
    )(mine_half, other_half, sibling, sx, de, dx, bc, a2, decay, drive)


def ready_kernel(
    rank, tok, gout, gain, wih, wil, w_out, d_skip, z, go, conv, pre, xc, gy,
    x_o, g_o, nth_o, ntl_o, gh_o, gl_o, wfh_o, wfl_o, woh_o, wol_o, vfh_o, vfl_o,
    gate_o, zgrad_o, cgrad_o, sig_o, xch_o, xcl_o, skip_o, pickb_o, pickc_o,
):
    feat, inner = gain.shape[1], w_out.shape[0]
    x = ordered(tok)
    x_o[...] = x
    g = ordered(gout)
    g_o[...] = g
    high, low = both_orders(normalize(x, gain[...])[1])
    nth_o[...] = high.astype(F32).T.astype(BF16)
    ntl_o[...] = low.astype(F32).T.astype(BF16)
    gh_o[...], gl_o[...] = both_orders(g)
    flip = flip_matrix(feat)
    wfh_o[...], wfl_o[...] = nn(flip, wih[...]).astype(BF16), nn(flip, wil[...]).astype(BF16)
    high, low = split(w_out[...])
    woh_o[...], wol_o[...] = high, low
    vfh_o[...], vfl_o[...] = nn(high, flip).astype(BF16), nn(low, flip).astype(BF16)
    xch_o[...], xcl_o[...] = split(xc[...])
    for lt in range(inner // LANE):
        cols = slice(lt * LANE, (lt + 1) * LANE)
        zt, v = z[:, cols], conv[:, cols]
        s = sigmoid(zt)
        gate_o[:, cols] = zt * s
        zgrad_o[:, cols] = go[:, cols] * (s * (1.0 + zt * (1.0 - s)))
        s = sigmoid(v)
        cgrad_o[:, cols] = s * (1.0 + v * (1.0 - s))
        sig_o[:, cols] = sigmoid(pre[:, cols])
        skip_o[:, cols] = jnp.sum(gy[:, cols] * xc[:, cols], axis=0, keepdims=True)
    row = lax.broadcasted_iota(jnp.int32, pickb_o.shape, 0) >> 6
    col = lax.broadcasted_iota(jnp.int32, pickb_o.shape, 1)
    pickb_o[...] = jnp.where(col == row + rank, 1.0, 0.0).astype(BF16)
    pickc_o[...] = jnp.where(col == row + (rank + pickb_o.shape[0] // (LANE // 2)), 1.0, 0.0).astype(BF16)


def ready(rank, state, tok, gout, gain, wih, wil, w_out, d_skip, z, go, conv, pre, xc, gy):
    length, feat = tok.shape
    rows2, inner = z.shape
    f32 = lambda *dims: jax.ShapeDtypeStruct(dims, F32)
    b16 = lambda *dims: jax.ShapeDtypeStruct(dims, BF16)
    both = lambda *dims: (b16(*dims), b16(*dims))
    return pl.pallas_call(
        lambda *refs: ready_kernel(rank, *refs),
        out_shape=(f32(length, feat), f32(length, feat))
        + both(feat, rows2) + both(rows2, feat) + both(feat, 2 * inner)
        + both(inner, feat) + both(inner, feat)
        + (f32(rows2, inner),) * 4
        + both(rows2, inner) + (f32(1, inner),) + both(state * LANE // 2, LANE),
        compiler_params=params(8),
        name="ready",
    )(tok, gout, gain, wih, wil, w_out, d_skip, z, go, conv, pre, xc, gy)


def early_kernel(
    rs_bits, nth, ntl, gh, gl, gate, zgrad, d_skip, xc, y_s, gzh_o, gzl_o, outh_o, outl_o, pieces_o,
):
    y = y_s[...] + d_skip[...] * xc[...]
    gz = split(zgrad[...] * y)
    gzh_o[...], gzl_o[...] = gz
    out = split(y * gate[...])
    gw_out = mm(tn, out, (gh[...], gl[...]))
    gw_in = mm(nn, (nth[...], ntl[...]), gz)
    outh_o[...], outl_o[...] = out
    put_pieces(rs_bits, pieces_o, [(gw_in, None), (gw_out, None)])


def early(rs_bits, nth, ntl, gh, gl, gate, zgrad, d_skip, xc, y):
    feat = nth.shape[0]
    rows2, inner = xc.shape
    pieces = 1 << rs_bits
    tall = 2 * feat * inner // LANE // pieces
    gz = jax.ShapeDtypeStruct((rows2, inner), BF16)
    return pl.pallas_call(
        lambda *refs: early_kernel(rs_bits, *refs),
        out_shape=(gz, gz, gz, gz, jax.ShapeDtypeStruct((pieces, tall, LANE), F32)),
        compiler_params=params(8),
        name="early",
    )(nth, ntl, gh, gl, gate, zgrad, d_skip, xc, y)


def put_pieces(rs_bits, pieces_o, arrays, few=None):
    pieces = 1 << rs_bits
    mine = reverse_bits(lax.axis_index("seq"), rs_bits)
    for p in range(pieces):
        slot = mine ^ reverse_bits(p, rs_bits)
        at = 0
        for value, more in arrays:
            tall = value.shape[0] // pieces
            for lt in range(value.shape[1] // LANE):
                where = (slice(p * tall, (p + 1) * tall), slice(lt * LANE, (lt + 1) * LANE))
                block = value[where] if more is None else value[where] + more[where]
                pieces_o[slot, at : at + tall, :] = block
                at += tall
        if few is not None:
            tiles = few.shape[1] // LANE
            top = pieces // tiles * CH
            rest = (few.shape[0] - top) * tiles // pieces
            rb, lt = p // tiles, p % tiles
            pieces_o[slot, at : at + CH, :] = few[rb * CH : (rb + 1) * CH, lt * LANE : (lt + 1) * LANE]
            rows = []
            for v in range(rest * p, rest * (p + 1)):
                rb, lt = top + v // tiles, v % tiles
                rows.append(few[rb : rb + 1, lt * LANE : (lt + 1) * LANE])
            zeros = jnp.zeros((4, LANE), F32)
            rows = [zeros] + rows + [zeros[: 4 - rest]]
            pieces_o[slot, at + CH : at + 2 * CH, :] = jnp.concatenate(rows, axis=0)
            pieces_o[slot, at + 2 * CH : at + 3 * CH, :] = jnp.zeros((CH, LANE), F32)


def row_vectors(rows):
    return jnp.concatenate(
        [rows[b : b + 1, lt * LANE : (lt + 1) * LANE] for b in range(3) for lt in range(rows.shape[1] // LANE)],
        axis=0,
    )


def backward_kernel(
    dirn, mx, car, h_s, de_s, dx_s, bc_s, a2_s, decay, gy,
    sb_s, sa_s, accb, accc, ga_s,
    after_s,
):
    rows2, inner = de_s.shape
    length = rows2 // 2
    steps = length // CH
    tiles = inner // LANE
    state = a2_s.shape[0]
    order = list(range(steps)) if dirn == 0 else list(range(steps - 1, -1, -1))
    base = dirn * length
    m_row = 3 if dirn == 0 else 1
    group = 2
    low = lax.broadcasted_iota(jnp.int32, (CH, LANE), 1) < LANE // 2
    cols_of = [slice(t * LANE, (t + 1) * LANE) for t in range(tiles)]
    sb_s[...] = jnp.zeros(sb_s.shape, F32)
    sa_s[...] = jnp.zeros(sa_s.shape, F32)
    for cols in cols_of:
        total = jnp.zeros((CH, LANE), F32)
        for j in range(steps):
            total = total + de_s[base + j * CH : base + (j + 1) * CH, cols]
        after_s[:, cols] = outside_sum(total, dirn != 0)

    def some(g, carry):
        n0 = g * group
        at_b, at_c = lanes_of(n0, group), lanes_of(state + n0, group)
        a2, q, ga = {}, {}, {}
        for n in range(group):
            for t, cols in enumerate(cols_of):
                a2[n, t] = a2_s[n0 + n, :, cols]
                into = jnp.exp2(after_s[:, cols] * a2[n, t]) * car[m_row * state + n0 + n, :, cols]
                q[n, t] = mx[dirn, n0 + n, :, cols] + into
                ga[n, t] = jnp.zeros((CH, LANE), F32)
        for time in range(steps - 1, -1, -1):
            j = order[time]
            rows = slice(base + j * CH, base + (j + 1) * CH)
            here = slice(j * CH, (j + 1) * CH)
            de = [de_s[rows, c] for c in cols_of]
            dx = [dx_s[rows, c] for c in cols_of]
            gyj = [gy[rows, c] for c in cols_of]
            sb, sa = [None] * tiles, [None] * tiles
            sums = []
            for n in range(group):
                b_n, c_n = bc_s[rows, at_b[n]], bc_s[rows, at_c[n]]
                to_b = to_c = None
                for t, cols in enumerate(cols_of):
                    gh = gyj[t] * c_n + q[n, t]
                    term_c = gyj[t] * h_s[dirn, time + 1, n0 + n, :, cols]
                    term_b = gh * dx[t]
                    to_b = term_b if t == 0 else to_b + term_b
                    to_c = term_c if t == 0 else to_c + term_c
                    q[n, t] = decay[dirn, time, n0 + n, :, cols] * gh
                    r = q[n, t] * h_s[dirn, time, n0 + n, :, cols]
                    ga[n, t] = ga[n, t] + de[t] * r
                    sb[t] = gh * b_n if n == 0 else sb[t] + gh * b_n
                    sa[t] = a2[n, t] * r if n == 0 else sa[t] + a2[n, t] * r
                sums.append((to_b, to_c))
            at = pl.ds(pl.multiple_of(g * LANE, LANE), LANE)
            for acc, one, two in ((accb, sums[0][0], sums[1][0]), (accc, sums[0][1], sums[1][1])):
                acc[here, at] = jnp.where(low, one, two) + pltpu.roll(jnp.where(low, two, one), LANE // 2, 1)
            for t, cols in enumerate(cols_of):
                sb_s[here, cols] += sb[t]
                sa_s[here, cols] += sa[t]
        for n in range(group):
            for t, cols in enumerate(cols_of):
                ga_s[n0 + n, :, cols] = ga[n, t]
        return carry

    lax.fori_loop(0, state // group, some, 0)


def backward(dirn, mx, car, h, de, dx, bc, a2, decay, gy):
    rows2, inner = de.shape
    state = a2.shape[0]
    length = rows2 // 2
    half = jax.ShapeDtypeStruct((length, inner), F32)
    acc = jax.ShapeDtypeStruct((length, state * LANE // 2), F32)
    return pl.pallas_call(
        lambda *refs: backward_kernel(dirn, *refs),
        out_shape=(half, half, acc, acc, jax.ShapeDtypeStruct((state, CH, inner), F32)),
        scratch_shapes=[pltpu.VMEM((CH, inner), F32)],
        compiler_params=params(4),
        name="backward",
    )(mx, car, h, de, dx, bc, a2, decay, gy)


def inner_kernel(
    pad, conv_w, w_x, w_dt, d_skip, a2_s,
    xb, gy, xc, dt, sig, cgrad, mask, dbl, xbh, xch, xcl, skip_sum, pick_b, pick_c,
    sb_f, sa_f, accb_f, accc_f, ga_f, sb_r, sa_r, accb_r, accc_r, ga_r,
    gxh_o, gxl_o, halo_o, few_o,
    gp_s, gpre_s, xcg_s,
):
    inner, rank = w_x.shape[1], w_dt.shape[0]
    state = a2_s.shape[0]
    rows2 = xb.shape[0]
    length = rows2 // 2
    steps = length // CH
    tiles = inner // LANE
    sub = sub_iota()

    bias_rows = []
    for lt in range(tiles):
        cols = slice(lt * LANE, (lt + 1) * LANE)
        bias = jnp.zeros((1, LANE), F32)
        for dirn, sb, sa in ((0, sb_f, sa_f), (1, sb_r, sa_r)):
            rows = slice(dirn * length, (dirn + 1) * length)
            g_pre = (xc[rows, cols] * sb[:, cols] + LN2 * sa[:, cols]) * sig[rows, cols]
            gpre_s[rows, cols] = g_pre
            xcg_s[rows, cols] = d_skip[:, cols] * gy[rows, cols] + dt[rows, cols] * sb[:, cols]
            bias = bias + jnp.sum(g_pre, axis=0, keepdims=True)
        bias_rows.append(bias)

    b_parts = split(jnp.concatenate([accb_f[...], accb_r[...]], axis=0))
    c_parts = split(jnp.concatenate([accc_f[...], accc_r[...]], axis=0))
    g_bc = (nn(b_parts[0], pick_b[...]) + nn(b_parts[1], pick_b[...])) + (
        nn(c_parts[0], pick_c[...]) + nn(c_parts[1], pick_c[...])
    )
    gpre_parts = split(gpre_s[...])
    w_dt_parts = split(w_dt[...])
    g_rank = mm(nt, gpre_parts, w_dt_parts)
    width = rank + 2 * state
    g_dbl = jnp.concatenate([g_rank, g_bc[:, rank:width]], axis=1)
    g_dbl_parts = split(g_dbl)
    few_o[width + state : width + state + rank, :] = mm(tn, split(dbl[:, :rank]), gpre_parts)
    few_o[:width, :] = mm(tn, g_dbl_parts, (xch[...], xcl[...]))
    xcg_s[...] += mm(nn, g_dbl_parts, split(w_x[...]))

    cw_rows = [[] for _ in range(4)]
    cb_rows = []
    halo_f, halo_r = [], []
    for lt in range(tiles):
        cols = slice(lt * LANE, (lt + 1) * LANE)
        taps = [conv_w[k : k + 1, cols] for k in range(4)]
        xbh_t = xbh[:, cols]
        xf = [xb[j * CH : (j + 1) * CH, cols] for j in range(steps)]
        xf = [
            jnp.where(sub == 0, xbh_t[b : b + 1], pltpu.roll(xf[steps - 3 + b], 1, 0))
            for b in range(3)
        ] + xf
        gcw = [jnp.zeros((CH, LANE), F32) for _ in range(4)]
        gcb = jnp.zeros((CH, LANE), F32)
        grads = [None] * (steps + 3)
        for j in range(steps):
            rows = slice(j * CH, (j + 1) * CH)
            u = xcg_s[rows, cols] * cgrad[rows, cols]
            gcb = gcb + u
            for k in range(4):
                uk = u if k == 0 else u * mask[(k - 1) * length + j * CH : (k - 1) * length + (j + 1) * CH, :]
                gcw[k] = gcw[k] + uk * xf[j + 3 - k]
                add = taps[k] * uk
                at = j + 3 - k
                grads[at] = add if grads[at] is None else grads[at] + add
        for b in range(3):
            halo_f.append(grads[b][0:1])
            at = steps + b
            grads[at] = grads[at] + jnp.where(sub == CH - 1, 0.0, pltpu.roll(grads[b], CH - 1, 0))
        for j in range(steps):
            gp_s[j * CH : (j + 1) * CH, cols] = grads[j + 3]
        xr = [xb[length + j * CH : length + (j + 1) * CH, cols] for j in range(steps)]
        xr = xr + [
            jnp.where(sub == CH - 1, xbh_t[8 + b : 9 + b], pltpu.roll(xr[b], CH - 1, 0))
            for b in range(3)
        ]
        grads = [None] * (steps + 3)
        for j in range(steps):
            rows = slice(length + j * CH, length + (j + 1) * CH)
            u = xcg_s[rows, cols] * cgrad[rows, cols]
            gcb = gcb + u
            for k in range(4):
                uk = u if k == 0 else u * mask[(k + 2) * length + j * CH : (k + 2) * length + (j + 1) * CH, :]
                gcw[k] = gcw[k] + uk * xr[j + k]
                add = taps[k] * uk
                grads[j + k] = add if grads[j + k] is None else grads[j + k] + add
        for b in range(3):
            halo_r.append(grads[steps + b][CH - 1 : CH])
            grads[b] = grads[b] + jnp.where(sub == 0, 0.0, pltpu.roll(grads[steps + b], 1, 0))
        for j in range(steps):
            gp_s[length + j * CH : length + (j + 1) * CH, cols] = grads[j]
        for k in range(4):
            cw_rows[k].append(jnp.sum(gcw[k], axis=0, keepdims=True))
        cb_rows.append(jnp.sum(gcb, axis=0, keepdims=True))
    pad_col = spread(pad[...].astype(F32))
    pad_all = jnp.concatenate([pad_col, pad_col], axis=0)
    for lt in range(tiles):
        cols = slice(lt * LANE, (lt + 1) * LANE)
        gxh_o[:, cols], gxl_o[:, cols] = split(gp_s[:, cols] * pad_all)

    blank = jnp.zeros((5, inner), F32)

    def gather(found):
        return jnp.concatenate(
            [jnp.concatenate([found[lt * 3 + b] for lt in range(tiles)], axis=1) for b in range(3)]
            + [blank],
            axis=0,
        )

    halo_o[...] = jnp.concatenate([gather(halo_f), gather(halo_r)], axis=0)
    ga = jnp.concatenate(
        [jnp.sum(ga_f[n] + ga_r[n], axis=0, keepdims=True) * (a2_s[n, 0:1, :] * LN2) for n in range(state)], axis=0
    )
    few_o[width : width + state, :] = ga
    few_o[width + state + rank :, :] = jnp.concatenate(
        [jnp.concatenate(cw_rows[k], axis=1) for k in range(4)]
        + [
            jnp.concatenate(cb_rows, axis=1),
            jnp.concatenate(bias_rows, axis=1),
            skip_sum[...],
            jnp.zeros((1, inner), F32),
        ],
        axis=0,
    )


def inner_back(*arrays):
    w_x, w_dt, a2, xb = arrays[2], arrays[3], arrays[5], arrays[6]
    rows2, inner = xb.shape
    few = w_x.shape[0] + a2.shape[0] + w_dt.shape[0] + CH
    big = pltpu.VMEM((rows2, inner), F32)
    part = jax.ShapeDtypeStruct((rows2, inner), BF16)
    return pl.pallas_call(
        inner_kernel,
        out_shape=(
            part, part,
            jax.ShapeDtypeStruct((2 * CH, inner), F32),
            jax.ShapeDtypeStruct((few, inner), F32),
        ),
        scratch_shapes=[big, big, big],
        compiler_params=params(8),
        name="inner",
    )(*arrays)


def tail_kernel(
    rs_bits, sib, oth, gain, x_s, nth, ntl, wih, wil, wfh, wfl, gzh, gzl, gxh, gxl, halo, few,
    normed_o, pieces_o, *edges_o,
):
    feat = gain.shape[1]
    rows2, inner = gxh.shape
    length = rows2 // 2
    left, right = pick_sides(sib[...], oth[...])
    factor_l, hn_l = normalize(left, gain[...])
    factor_r, hn_r = normalize(right, gain[...])
    flip = flip_matrix(feat)
    lh, ll = split(hn_l)
    rh, rl = split(hn_r)
    edge = (
        jnp.concatenate([lh, nn(rh, flip).astype(BF16)], axis=0),
        jnp.concatenate([ll, nn(rl, flip).astype(BF16)], axis=0),
    )
    x = x_s[...]
    factor = normalize(x, gain[...])[0]
    gh_parts = split(halo[...])
    gw_in = mm(nn, (nth[...], ntl[...]), (gxh[...], gxl[...]))
    gw_in_halo = mm(tn, edge, gh_parts)
    w_xb = (wih[:, :inner], wil[:, :inner])
    g_normed = (
        mm(nt, (gxh[:length], gxl[:length]), w_xb)
        + mm(nt, (gzh[:length], gzl[:length]), (wih[:, inner:], wil[:, inner:]))
    ) + (
        mm(nt, (gxh[length:], gxl[length:]), (wfh[:, :inner], wfl[:, :inner]))
        + mm(nt, (gzh[length:], gzl[length:]), (wfh[:, inner:], wfl[:, inner:]))
    )
    back_h = mm(nt, gh_parts, w_xb)
    gn_l = back_h[:CH]
    gn_r = flipped(back_h[CH:])

    normed_o[...] = g_normed
    to_left = norm_back(left, factor_l, gn_l, gain[...])
    to_right = norm_back(right, factor_r, gn_r, gain[...])
    for ref, value in zip(edges_o, (to_left, to_right)):
        ref[...] = value
    three = lax.broadcasted_iota(jnp.int32, (CH, feat), 0) < 3
    g_gain = (
        jnp.sum(g_normed * (x * factor), axis=0, keepdims=True)
        + jnp.sum(jnp.where(three, gn_l * (left * factor_l) + gn_r * (right * factor_r), 0.0), axis=0, keepdims=True)
    )
    few_all = jnp.concatenate(
        [few[: few.shape[0] - CH, :], few[few.shape[0] - CH : few.shape[0] - 1, :]]
        + [jnp.concatenate([g_gain, jnp.zeros((1, inner - feat), F32)], axis=1)],
        axis=0,
    )
    put_pieces(rs_bits, pieces_o, [(gw_in, gw_in_halo)], few_all)
    pieces = 1 << rs_bits
    me = lax.axis_index("seq") & (pieces - 1)
    mine = reverse_bits(me, rs_bits)
    at = pieces_o.shape[1] - 2 * CH

    @pl.when(me < pieces - 1)
    def _():
        slot = mine ^ reverse_bits(me + 1, rs_bits)
        vectors = row_vectors(to_right)
        pieces_o[slot, at : at + 4, :] = vectors[:4]
        pieces_o[slot, at + CH : at + CH + 2, :] = vectors[4:]

    @pl.when(me > 0)
    def _():
        slot = mine ^ reverse_bits(me - 1, rs_bits)
        pieces_o[slot, at + CH + 2 : at + 2 * CH, :] = row_vectors(to_left)


def reverse_bits(value, bits):
    found = 0
    for i in range(bits):
        found = found | (((value >> i) & 1) << (bits - 1 - i))
    return found


def norm_back(x, factor, gn, gain):
    scaled = gn * gain
    return factor * scaled - x * (factor * factor * factor * jnp.mean(scaled * x, axis=1, keepdims=True))


def finish_kernel(x_s, g, gain, g_normed, outh, outl, woh, wol, vfh, vfl, mixed_o, gtok_o):
    length = x_s.shape[0]
    x = x_s[...]
    fwd = mm(nn, (outh[:length], outl[:length]), (woh[...], wol[...]))
    rev = mm(nn, (outh[length:], outl[length:]), (vfh[...], vfl[...]))
    store_ordered(mixed_o, x + (fwd + rev))
    factor = normalize(x, gain[...])[0]
    store_ordered(gtok_o, g[...] + norm_back(x, factor, g_normed[...], gain[...]))


def finish(*arrays):
    shape = jax.ShapeDtypeStruct(arrays[0].shape, F32)
    return pl.pallas_call(
        finish_kernel,
        out_shape=(shape, shape),
        compiler_params=params(6),
        name="finish",
    )(*arrays)


def tail(rs_bits, alone, *arrays):
    x, gxh = arrays[3], arrays[12]
    length, feat = x.shape
    inner = gxh.shape[1]
    pieces = 1 << rs_bits
    tall = feat * inner // LANE // pieces + 3 * CH
    return pl.pallas_call(
        lambda *refs: tail_kernel(rs_bits, *refs),
        out_shape=(
            jax.ShapeDtypeStruct((length, feat), F32),
            jax.ShapeDtypeStruct((pieces, tall, LANE), F32),
        )
        + (jax.ShapeDtypeStruct((CH, feat), F32),) * (2 if alone else 0),
        compiler_params=params(8),
        name="tail",
    )(*arrays)


def unpack_kernel(rs_bits, parts, *refs):
    sources, refs = refs[:parts], refs[parts:]
    (gtok, halo, pad, gtok_o, gain_o, w_in_o, conv_w_o, conv_b_o, w_x_o, w_dt_o, dt_bias_o, a_log_o, d_skip_o, w_out_o,
     few_s, rest_s) = refs
    feat = w_in_o.shape[0]
    inner = w_out_o.shape[0]
    tiles = inner // LANE
    pieces = 1 << rs_bits
    mine = reverse_bits(lax.axis_index("seq"), rs_bits)
    in_rows, out_rows = feat // pieces, inner // pieces
    for slot in range(pieces):
        source = sources[slot * parts // pieces]
        i = slot % (pieces // parts)
        p = reverse_bits(mine ^ slot, rs_bits)
        at = 0
        in_at = pl.ds(pl.multiple_of(p * in_rows, in_rows), in_rows)
        out_at = pl.ds(pl.multiple_of(p * out_rows, out_rows), out_rows)
        for lt in range(tiles):
            w_in_o[in_at, inner + lt * LANE : inner + (lt + 1) * LANE] = source[i, at : at + in_rows, :]
            at += in_rows
        for lt in range(feat // LANE):
            w_out_o[out_at, lt * LANE : (lt + 1) * LANE] = source[i, at : at + out_rows, :]
            at += out_rows
        for lt in range(tiles):
            w_in_o[in_at, lt * LANE : (lt + 1) * LANE] = source[i, at : at + in_rows, :]
            at += in_rows
        few_s[p] = source[i, at : at + CH, :]
        rest_s[p] = source[i, at + CH : at + 2 * CH, :]

    top = pieces // tiles * CH
    total = w_x_o.shape[0] + a_log_o.shape[0] + w_dt_o.shape[0] + CH
    rest = (total - top) * tiles // pieces

    def few_rows(first, count):
        found = []
        for lt in range(tiles):
            if first < top:
                found.append(few_s[first // CH * tiles + lt])
                continue
            rows = []
            for row in range(first, first + count):
                v = (row - top) * tiles + lt
                rows.append(rest_s[v // rest, 4 + v % rest : 5 + v % rest, :])
            found.append(jnp.concatenate(rows, axis=0) if count > 1 else rows[0])
        return jnp.concatenate(found, axis=1)

    width, state = w_x_o.shape[0], a_log_o.shape[0]
    rank = w_dt_o.shape[0]
    w_x_o[...] = jnp.concatenate([few_rows(r, CH) for r in range(0, width, CH)], axis=0)
    at = width
    a_log_o[...] = jnp.concatenate([few_rows(r, CH) for r in range(at, at + state, CH)], axis=0)
    at += state
    w_dt_o[...] = jnp.concatenate([few_rows(r, CH) for r in range(at, at + rank, CH)], axis=0)
    at += rank
    conv_w_o[...] = few_rows(at, 4)
    conv_b_o[...] = few_rows(at + 4, 1)
    dt_bias_o[...] = few_rows(at + 5, 1)
    d_skip_o[...] = few_rows(at + 6, 1)
    gain_o[...] = few_rows(at + 7, 1)[:, :feat]

    length = gtok.shape[0]
    per = feat // LANE
    padded = spread_plain(pad[...].astype(F32), feat)

    def three(first):
        rows = [
            jnp.concatenate([halo[first + b * per + lt : first + b * per + lt + 1, :] for lt in range(per)], axis=1)
            for b in range(3)
        ]
        return rows, jnp.zeros((CH - 3, feat), F32)

    rows, blank = three(0)
    first = jnp.concatenate(rows + [blank], axis=0)
    rows, blank = three(3 * per)
    last = jnp.concatenate([blank] + rows, axis=0)
    gtok_o[...] = gtok[...]
    gtok_o[:CH] = gtok[:CH] + padded[:CH] * first
    gtok_o[length - CH :] = gtok[length - CH :] + padded[length - CH :] * last


def spread_plain(row, width):
    length = row.shape[1]
    rows = lax.broadcasted_iota(jnp.int32, (length, length), 0)
    cols = lax.broadcasted_iota(jnp.int32, (length, length), 1)
    picked = (jnp.where(rows == cols, 1.0, 0.0) * row).astype(BF16)
    return nn(picked, jnp.ones((length, width), BF16))


def unpack(rs_bits, parts, gtok, halo, pad, state, rank):
    length, feat = gtok.shape
    pieces = 1 << rs_bits
    inner = state[1]
    width = rank + 2 * state[0]
    shape = lambda *dims: jax.ShapeDtypeStruct(dims, F32)
    return pl.pallas_call(
        lambda *refs: unpack_kernel(rs_bits, len(parts), *refs),
        out_shape=(
            shape(length, feat),
            shape(1, feat),
            shape(feat, 2 * inner),
            shape(4, inner),
            shape(1, inner),
            shape(width, inner),
            shape(rank, inner),
            shape(1, inner),
            shape(state[0], inner),
            shape(1, inner),
            shape(inner, feat),
        ),
        scratch_shapes=[pltpu.VMEM((pieces, CH, LANE), F32)] * 2,
        compiler_params=params(6),
        name="unpack",
    )(*parts, gtok, halo, pad)


def body(tokens, resets, pad_mask, norm_gain, w_in, conv_w, conv_b, w_x, w_dt, dt_bias, a_log, d_skip, w_out, grad_out):
    count = lax.axis_size("seq")
    bits = count.bit_length() - 1
    rs_bits = min(5, bits)
    length = tokens.shape[0]
    keep_row, pad_row = resets.reshape(1, length), pad_mask.reshape(1, length)

    def exchange(value, apart):
        return lax.ppermute(value, "seq", [(i, i ^ apart) for i in range(count)])

    def swap(value, bit):
        return exchange(value, 1 << bit)

    across = [(i, i + 1) for i in range(1, count - 1, 2)] + [(i + 1, i) for i in range(1, count - 1, 2)]

    def swap_across(value):
        return lax.ppermute(value, "seq", across)

    to_sib, to_oth, kept = edges(
        tokens, keep_row, pad_row, norm_gain, w_in[0], grad_out, w_out[0],
        conv_w[0], conv_b, w_x[0].T, w_dt[0], dt_bias, a_log[0].T, d_skip,
    )
    (tok, keep, pad, gain, w_in_0, gout, w_out_0, conv_w_0, conv_b_0, w_x_t, w_dt_0, dt_bias_0, a_log_t, skip) = kept
    oth = swap_across(to_oth)
    sib = swap(to_sib, 0)
    xb, z, go, gy, wih, wil, spread_s, a2 = project(tok, pad, gain, w_in_0, gout, w_out_0, a_log_t)
    xc, dt, pre, conv, mask, dbl, xbh, sx, mx, total, de, dx, bc, decay, drive = prepare(
        sib, oth, keep, gain, wih, wil, conv_w_0, conv_b_0, w_x_t, w_dt_0, dt_bias_0, spread_s, a2, xb, gy
    )

    sibling = swap(total, 0)
    group = pair(a2, total, sibling)
    group, gate_in = lax.optimization_barrier((group, (z, go, conv, pre, xc, gy)))
    at_hand = ready(w_dt.shape[1], a_log.shape[2], tok, gout, gain, wih, wil, w_out_0, skip, *gate_in)
    stages = []
    steps = [range(first, min(first + 2, bits)) for first in range(1, bits, 2)]
    step = steps[-1]
    distances = [i << step[0] for i in range(1, 1 << len(step))]
    for first_step in steps[:-1]:
        members = [group] + [exchange(group, i << first_step[0]) for i in range(1, 1 << len(first_step))]
        halves = distances if first_step is steps[-2] else ()
        entering, *group = stage(first_step[0], halves, a2, members)
        stages.append(entering)
        if not halves:
            (group,) = group
    group, at_hand = lax.optimization_barrier((group, at_hand))
    theirs = [exchange(value, apart) for value, apart in zip(group, distances)]
    stages.append(last_stage(step[0], a2, theirs))
    mine_half = enter(a2, stages)
    other_half = swap(mine_half, 0)

    y, h, car = forward(mine_half, other_half, sibling, sx, de, dx, bc, a2, decay, drive)
    def reduced(part, step):
        size = part.shape[0] >> len(step)
        total = part[:size]
        for i in ((2, 3, 1) if len(step) == 2 else (1,)):
            slot = reverse_bits(i, len(step))
            total = total + exchange(part[slot * size : (slot + 1) * size], i << step[0])
        return total

    (x, g, nth, ntl, gh, gl, wfh, wfl, woh, wol, vfh, vfl, gate, zgrad, cgrad, sig, xch, xcl, skip_sum,
     pick_b, pick_c) = at_hand
    rs_steps = [range(0, 1)] + [range(first, min(first + 2, rs_bits)) for first in range(1, rs_bits, 2)]
    gzh, gzl, outh, outl, part_a = early(rs_bits, nth, ntl, gh, gl, gate, zgrad, skip, xc, y)
    part_a, h = lax.optimization_barrier((part_a, h))
    part_a = reduced(part_a, range(0, 1))
    back_f = backward(0, mx, car, h, de, dx, bc, a2, decay, gy)
    part_a, back_f, h = lax.optimization_barrier((part_a, back_f, h))
    part_a = reduced(part_a, range(1, 2))
    back_r = backward(1, mx, car, h, de, dx, bc, a2, decay, gy)
    gxh, gxl, halo_g, few = inner_back(
        pad, conv_w_0, w_x_t, w_dt_0, skip, a2,
        xb, gy, xc, dt, sig, cgrad, mask, dbl, xbh, xch, xcl, skip_sum, pick_b, pick_c, *back_f, *back_r,
    )
    g_normed, part_b, *to_sides = tail(
        rs_bits, bits > rs_bits, sib, oth, gain, x, nth, ntl, wih, wil, wfh, wfl, gzh, gzl, gxh, gxl, halo_g, few
    )
    part_a, part_b = lax.optimization_barrier((part_a, part_b))
    part_a, part_b = reduced(part_a, range(2, 3)), reduced(part_b, rs_steps[0])
    part_b, g_normed = lax.optimization_barrier((part_b, g_normed))
    part_b = reduced(part_b, rs_steps[1])
    mixed, gtok = finish(x, g, gain, g_normed, outh, outl, woh, wol, vfh, vfl)
    part_b, mixed, gtok = lax.optimization_barrier((part_b, mixed, gtok))
    own = jnp.concatenate([part_a, part_b], axis=1)
    for step in rs_steps[2:]:
        own = reduced(own, step)
    for bit in range(rs_bits, bits):
        own = own + swap(own, bit)
    tall = own.shape[1]
    halo = jnp.concatenate([own[0, tall - 16 : tall - 12], own[0, tall - 8 :]], axis=0)
    if bits > rs_bits:
        pairs = [(i, i + 1) for i in range(count - 1)]
        from_left = lax.ppermute(to_sides[1], "seq", pairs)[:3]
        from_right = lax.ppermute(to_sides[0], "seq", [(j, i) for i, j in pairs])[:3]
        halo = jnp.concatenate([from_left.reshape(-1, LANE), from_right.reshape(-1, LANE)], axis=0)
    own = own[:, : tall - 8]
    for step in reversed(rs_steps[1:]):
        near = [exchange(own, reverse_bits(i, len(step)) << step[0]) for i in range((1 << len(step)) - 1, 0, -1)]
        near = [own] + near[::-1]
        if step is not rs_steps[1]:
            own = jnp.concatenate(near, axis=0)
    far = [swap(part, 0) for part in near]
    outs = unpack(rs_bits, near + far, gtok, halo, pad, a_log_t.shape, w_dt.shape[1])
    gtok, g_gain, g_w_in, g_conv_w, g_conv_b, g_w_x, g_w_dt, g_dt_bias, g_a_log, g_d_skip, g_w_out = outs
    return (
        mixed, gtok, g_gain, g_w_in[None], g_conv_w[None], g_conv_b, g_w_x.T[None], g_w_dt[None],
        g_dt_bias, g_a_log.T[None], g_d_skip, g_w_out[None],
    )


def solution(mesh):
    rows, whole = P("seq", None), P()
    return jax.shard_map(
        body,
        mesh=mesh,
        in_specs=(rows, P("seq"), P("seq")) + (whole,) * 10 + (rows,),
        out_specs=(rows, rows) + (whole,) * 10,
        check_vma=False,
    )
```

```python
import jax
import jax.numpy as jnp
from jax import lax
from jax.experimental import pallas as pl
from jax.experimental.pallas import tpu as pltpu
from jax.sharding import PartitionSpec as P

F32 = jnp.float32
BF16 = jnp.bfloat16
EPS = 1e-05
LOG2E = 1.4426950408889634
LN2 = 0.6931471805599453
BIG = 1e9
CH = 8
LANE = 128
MIB = 1024 * 1024


def nn(a, b):
    return lax.dot_general(a, b, (((1,), (0,)), ((), ())), preferred_element_type=F32)


def nt(a, b):
    return lax.dot_general(a, b, (((1,), (1,)), ((), ())), preferred_element_type=F32)


def tn(a, b):
    return lax.dot_general(a, b, (((0,), (0,)), ((), ())), preferred_element_type=F32)


def split(x):
    high = x.astype(BF16)
    return high, (x - high.astype(F32)).astype(BF16)


def split3(x):
    high = x.astype(BF16)
    rest = x - high.astype(F32)
    mid = rest.astype(BF16)
    return high, mid, (rest - mid.astype(F32)).astype(BF16)


def mm(dot, a, b):
    ah, al = a if isinstance(a, tuple) else split(a)
    bh, bl = b if isinstance(b, tuple) else split(b)
    return dot(ah, bh) + (dot(ah, bl) + dot(al, bh))


def flip_matrix(size):
    rows = lax.broadcasted_iota(jnp.int32, (size, size), 0)
    cols = lax.broadcasted_iota(jnp.int32, (size, size), 1)
    return jnp.where(rows + cols == size - 1, 1.0, 0.0).astype(BF16)


def flipped(x):
    flip = flip_matrix(x.shape[1])
    high, mid, low = split3(x)
    return nn(high, flip) + (nn(mid, flip) + nn(low, flip))


def order_matrix(length):
    steps = length // CH
    rows = lax.broadcasted_iota(jnp.int32, (length, length), 0)
    cols = lax.broadcasted_iota(jnp.int32, (length, length), 1)
    token = (rows & (CH - 1)) * steps + (rows >> 3)
    return jnp.where(cols == token, 1.0, 0.0)


def exact(dot, order, x):
    high, mid, low = split3(x)
    order = order.astype(BF16)
    return dot(order, high) + (dot(order, mid) + dot(order, low))


def ordered(ref):
    return exact(nn, order_matrix(ref.shape[0]), ref[...])


def store_ordered(ref, value):
    ref[...] = exact(tn, order_matrix(ref.shape[0]), value)


def spread(row, order=None):
    length = row.shape[1]
    picked = ((order_matrix(length) if order is None else order) * row).astype(BF16)
    return nn(picked, jnp.ones((length, LANE), BF16))


def sigmoid(x):
    return 1.0 / (1.0 + jnp.exp(-x))


def normalize(x, gain):
    factor = lax.rsqrt(jnp.mean(x * x, axis=1, keepdims=True) + EPS)
    return factor, x * factor * gain


def both_orders(normed):
    flip = flip_matrix(normed.shape[1])
    high, low = split(normed)
    return (
        jnp.concatenate([high, nn(high, flip).astype(BF16)], axis=0),
        jnp.concatenate([low, nn(low, flip).astype(BF16)], axis=0),
    )


def params(mib):
    return pltpu.CompilerParams(vmem_limit_bytes=mib * MIB)


def in_hbm(*arrays):
    return tuple(pltpu.with_memory_space_constraint(x, pltpu.HBM) for x in arrays)


def edges_kernel(*refs):
    count = (len(refs) - 3) // 2
    far, to_sib, to_oth, near, arrived = refs[:count], refs[count], refs[count + 1], refs[count + 2 : -1], refs[-1]
    copies = [pltpu.make_async_copy(one, two, arrived.at[i]) for i, (one, two) in enumerate(zip(far, near))]
    for copy in copies:
        copy.start()
    for copy in copies[:3]:
        copy.wait()
    tok, resets, pad = near[:3]
    length, feat = tok.shape
    sub = lax.broadcasted_iota(jnp.int32, (CH, length), 0)
    lane = lax.broadcasted_iota(jnp.int32, (CH, length), 1)
    real = pad[...].astype(F32)
    row = lax.broadcasted_iota(jnp.int32, (CH, feat), 0)
    flags = 1.0 - resets[...].astype(F32)
    flags = jnp.concatenate([flags, jnp.zeros((1, feat - length), F32)], axis=1)

    def message(rows, start):
        col = jnp.sum(jnp.where(lane == sub + start, real, 0.0), axis=1, keepdims=True)
        return jnp.where(row < 3, rows * col, jnp.where(row == 3, flags, 0.0))

    first = message(tok[:CH, :], 0)
    last = message(pltpu.roll(tok[length - CH :, :], 3, 0), length - 3)
    odd = (lax.axis_index("seq") & 1) == 1
    to_sib[...] = jnp.where(odd, first, last)
    to_oth[...] = jnp.where(odd, last, first)
    for copy in copies[3:]:
        copy.wait()


def edges(*arrays):
    shape = jax.ShapeDtypeStruct((CH, arrays[0].shape[1]), F32)
    found = pl.pallas_call(
        edges_kernel,
        in_specs=[pl.BlockSpec(memory_space=pl.ANY)] * len(arrays),
        out_specs=(pl.BlockSpec(memory_space=pltpu.VMEM),) * (2 + len(arrays)),
        out_shape=(shape, shape) + tuple(jax.ShapeDtypeStruct(x.shape, x.dtype) for x in arrays),
        scratch_shapes=[pltpu.SemaphoreType.DMA((len(arrays),))],
        compiler_params=params(8),
        name="edges",
    )(*in_hbm(*arrays))
    return found[0], found[1], found[2:]


def project_kernel(tok, pad, gain, w_in, gout, w_out, a_log, xb_o, z_o, go_o, gy_o, wih_o, wil_o, spread_o, a2_o):
    inner = w_out.shape[0]
    x = ordered(tok)
    normed = normalize(x, gain[...])[1]
    w_parts = split(w_in[...])
    wih_o[...], wil_o[...] = w_parts
    proj = mm(nn, both_orders(normed), w_parts)
    pad_col = spread(pad[...].astype(F32))
    pad_all = jnp.concatenate([pad_col, pad_col], axis=0)
    g = ordered(gout)
    gh, gl = both_orders(g)
    go = mm(nt, (gh, gl), split(w_out[...]))
    for lt in range(inner // LANE):
        cols = slice(lt * LANE, (lt + 1) * LANE)
        z = proj[:, inner + lt * LANE : inner + (lt + 1) * LANE]
        xb_o[:, cols] = proj[:, cols] * pad_all
        z_o[:, cols] = z
        go_o[:, cols] = go[:, cols]
        gy_o[:, cols] = go[:, cols] * (z * sigmoid(z))
    width = spread_o.shape[0] // 3
    row = lax.broadcasted_iota(jnp.int32, spread_o.shape, 0)
    entry = lax.broadcasted_iota(jnp.int32, spread_o.shape, 1) >> 7
    row = jnp.where(row >= 2 * width, row - 2 * width, jnp.where(row >= width, row - width, row))
    spread_o[...] = jnp.where(row == entry, 1.0, 0.0).astype(BF16)
    a2 = jnp.exp(a_log[...]) * (-LOG2E)
    for n in range(a2.shape[0]):
        a2_o[n] = jnp.broadcast_to(a2[n : n + 1], (CH, inner))


def project(tok, pad, gain, w_in, gout, w_out, a_log):
    big = jax.ShapeDtypeStruct((2 * tok.shape[0], w_out.shape[0]), F32)
    part = jax.ShapeDtypeStruct(w_in.shape, BF16)
    state, inner = a_log.shape
    return pl.pallas_call(
        project_kernel,
        out_shape=(
            big, big, big, big, part, part,
            jax.ShapeDtypeStruct((6 * state, 2 * state * LANE), BF16),
            jax.ShapeDtypeStruct((state, CH, inner), F32),
        ),
        compiler_params=params(8),
        name="project",
    )(tok, pad, gain, w_in, gout, w_out, a_log)


def pick_sides(from_sibling, from_other):
    odd = (lax.axis_index("seq") & 1) == 1
    left = jnp.where(odd, from_sibling, from_other)
    right = jnp.where(odd, from_other, from_sibling)
    return left, right


def rows_of(ref, first, count, cols):
    block = ref[pl.ds(pl.multiple_of(first, CH), count), cols]
    return [jnp.broadcast_to(block[n : n + 1], (CH, LANE)) for n in range(count)]


def sub_iota():
    return lax.broadcasted_iota(jnp.int32, (CH, LANE), 0)


def shifted(value, up):
    return pltpu.roll(value, 1 if up else CH - 1, 0)


def chunk_weights(total, up):
    sub = sub_iota()
    found = []
    width = total
    for reach in (1, 2, 4):
        inside = (sub >= reach) if up else (sub < CH - reach)
        found.append(jnp.where(inside, width, BIG))
        width = width + pltpu.roll(width, reach if up else CH - reach, 0)
    return found


def outside_sum(total, up):
    sub = sub_iota()
    value = jnp.where((sub >= 1) if up else (sub < CH - 1), shifted(total, up), 0.0)
    for reach in (1, 2, 4):
        inside = (sub >= reach) if up else (sub < CH - reach)
        value = value + jnp.where(inside, pltpu.roll(value, reach if up else CH - reach, 0), 0.0)
    return value


def chunk_scan(value, weights, a2, up):
    for reach, weight in zip((1, 2, 4), weights):
        value = value + jnp.exp2(weight * a2) * pltpu.roll(value, reach if up else CH - reach, 0)
    sub = sub_iota()
    enter = jnp.where((sub >= 1) if up else (sub < CH - 1), shifted(value, up), 0.0)
    leave = value[CH - 1 : CH] if up else value[0:1]
    return enter, leave


def prepare_kernel(
    sib, oth, keep, gain, wih, wil, conv_w, conv_b, w_x, w_dt, dt_bias, spread_s, a2_s, xb, gy,
    xc_o, dt_o, pre_o, conv_o, mask_o, dbl_o, xbh_o, sx_o, mx_o, sum_o, de_s, dx_s, bc_s, decay_o, drive_o,
    leave_s,
):
    inner, rank = w_x.shape[1], w_dt.shape[0]
    state = a2_s.shape[0]
    length = xb.shape[0] // 2
    steps = length // CH
    tiles = inner // LANE
    left, right = pick_sides(sib[...], oth[...])
    hn_l = normalize(left, gain[...])[1]
    hn_r = normalize(right, gain[...])[1]
    flip = flip_matrix(hn_r.shape[1])
    lh, ll = split(hn_l)
    rh, rl = split(hn_r)
    halo = (
        jnp.concatenate([lh, nn(rh, flip).astype(BF16)], axis=0),
        jnp.concatenate([ll, nn(rl, flip).astype(BF16)], axis=0),
    )
    xbh = mm(nn, halo, (wih[:, :inner], wil[:, :inner]))
    xbh_o[...] = xbh
    lane = lax.broadcasted_iota(jnp.int32, (1, length), 1)
    here = 1.0 - keep[...].astype(F32)
    before, after = left[3:4, :length], right[3:4, :length]

    def back(k):
        return jnp.where(lane < k, pltpu.roll(before, k, 1), pltpu.roll(here, k, 1))

    def ahead(k):
        return jnp.where(
            lane >= length - k,
            pltpu.roll(after, length - k, 1),
            pltpu.roll(here, length - k, 1),
        )

    f1 = here
    f2 = f1 * back(1)
    f3 = f2 * back(2)
    r1 = ahead(1)
    r2 = r1 * ahead(2)
    r3 = r2 * ahead(3)
    token_order = order_matrix(length)
    for i, row in enumerate((f1, f2, f3, r1, r2, r3)):
        mask_o[i * length : (i + 1) * length, :] = spread(row, token_order)

    sub = sub_iota()

    def conv_tile(lt, carry):
        cols = pl.ds(pl.multiple_of(lt * LANE, LANE), LANE)
        xbh_t = xbh_o[:, cols]
        taps = [conv_w[k : k + 1, cols] for k in range(4)]
        bias = conv_b[:, cols]
        xf = [xb[j * CH : (j + 1) * CH, cols] for j in range(steps)]
        edge = [
            jnp.where(sub == 0, xbh_t[b : b + 1], pltpu.roll(xf[steps - 3 + b], 1, 0))
            for b in range(3)
        ]
        xf = edge + xf
        for j in range(steps):
            rows = slice(j * CH, (j + 1) * CH)
            v = bias + taps[0] * xf[j + 3]
            for k in range(1, 4):
                v = v + taps[k] * (mask_o[(k - 1) * length + j * CH : (k - 1) * length + (j + 1) * CH, :] * xf[j + 3 - k])
            conv_o[rows, cols] = v
            xc_o[rows, cols] = v * sigmoid(v)
        xr = [xb[length + j * CH : length + (j + 1) * CH, cols] for j in range(steps)]
        xr = xr + [
            jnp.where(sub == CH - 1, xbh_t[8 + b : 9 + b], pltpu.roll(xr[b], CH - 1, 0))
            for b in range(3)
        ]
        for j in range(steps):
            rows = slice(length + j * CH, length + (j + 1) * CH)
            v = bias + taps[0] * xr[j]
            for k in range(1, 4):
                v = v + taps[k] * (mask_o[(k + 2) * length + j * CH : (k + 2) * length + (j + 1) * CH, :] * xr[j + k])
            conv_o[rows, cols] = v
            xc_o[rows, cols] = v * sigmoid(v)
        return carry

    lax.fori_loop(0, tiles, conv_tile, 0)
    dbl = mm(nt, xc_o[...], w_x[...])
    dbl_o[...] = dbl
    pre_all = mm(nn, dbl[:, :rank], w_dt[...])
    bc_s[...] = nn(jnp.concatenate(split3(dbl[:, rank:]), axis=1), spread_s[...])
    for lt in range(tiles):
        cols = slice(lt * LANE, (lt + 1) * LANE)
        pre = pre_all[:, cols] + dt_bias[:, cols]
        e = jnp.exp(-jnp.abs(pre))
        u = 1.0 + e
        log1p = jnp.where(u == 1.0, e, jnp.log(u) * (e / (u - 1.0)))
        dt = jnp.maximum(pre, 0.0) + log1p
        dt_o[:, cols] = dt
        pre_o[:, cols] = pre
        dx_s[:, cols] = dt * xc_o[:, cols]
        cut = jnp.concatenate([mask_o[:length], mask_o[3 * length : 4 * length]], axis=0)
        de_s[:, cols] = dt + BIG * (1.0 - cut)

    group = 8
    cols_of = [slice(t * LANE, (t + 1) * LANE) for t in range(tiles)]
    for dirn in range(2):
        order = list(range(steps)) if dirn == 0 else list(range(steps - 1, -1, -1))
        base = dirn * length
        up = dirn == 0
        s_row, m_row = (0, 3) if dirn == 0 else (2, 1)
        totals = []
        for cols in cols_of:
            total = jnp.zeros((CH, LANE), F32)
            for j in range(steps):
                total = total + de_s[base + j * CH : base + (j + 1) * CH, cols]
            sum_o[4 * state + dirn : 4 * state + dirn + 1, cols] = jnp.sum(total, axis=0, keepdims=True)
            totals.append(total)

        def some(g, carry, order=order, base=base, up=up, dirn=dirn, s_row=s_row, m_row=m_row, totals=totals):
            n0 = g * group
            at_b, at_c = lanes_of(n0, group), lanes_of(state + n0, group)
            keys = [(n, t) for n in range(group) for t in range(tiles)]
            a2 = {(n, t): a2_s[n0 + n, :, cols_of[t]] for n, t in keys}
            h, m = {}, {}
            for at, j in enumerate(order):
                rows = slice(base + j * CH, base + (j + 1) * CH)
                de = [de_s[rows, c] for c in cols_of]
                dx = [dx_s[rows, c] for c in cols_of]
                for n in range(group):
                    b_n = bc_s[rows, at_b[n]]
                    for t, cols in enumerate(cols_of):
                        d = jnp.exp2(de[t] * a2[n, t])
                        decay_o[dirn, at, n0 + n, :, cols] = d
                        drive = dx[t] * b_n
                        drive_o[dirn, at, n0 + n, :, cols] = drive
                        h[n, t] = drive if at == 0 else d * h[n, t] + drive
            for at in range(steps - 1, -1, -1):
                rows = slice(base + order[at] * CH, base + (order[at] + 1) * CH)
                gyj = [gy[rows, c] for c in cols_of]
                for n in range(group):
                    c_n = bc_s[rows, at_c[n]]
                    for t, cols in enumerate(cols_of):
                        own = gyj[t] * c_n
                        d = decay_o[dirn, at, n0 + n, :, cols]
                        m[n, t] = d * (own if at == steps - 1 else own + m[n, t])
            for t in range(tiles):
                w_s, w_m = chunk_weights(totals[t], up), chunk_weights(totals[t], not up)
                for n in range(group):
                    enter, leave = chunk_scan(h[n, t], w_s, a2[n, t], up)
                    sx_o[dirn, n0 + n, :, cols_of[t]] = enter
                    leave_s[s_row * state + n0 + n, :, cols_of[t]] = jnp.broadcast_to(leave, (CH, LANE))
                    enter, leave = chunk_scan(m[n, t], w_m, a2[n, t], not up)
                    mx_o[dirn, n0 + n, :, cols_of[t]] = enter
                    leave_s[m_row * state + n0 + n, :, cols_of[t]] = jnp.broadcast_to(leave, (CH, LANE))
            return carry

        lax.fori_loop(0, state // group, some, 0)
    for row in range(0, 4 * state, CH):
        for cols in cols_of:
            sum_o[row : row + CH, cols] = jnp.concatenate([leave_s[row + i, 0:1, cols] for i in range(CH)], axis=0)
    sum_o[4 * state + 2 :, :] = jnp.zeros((sum_o.shape[0] - 4 * state - 2, inner), F32)


def lanes_of(first, count):
    return [pl.ds(pl.multiple_of((first + n) * LANE, LANE), LANE) for n in range(count)]


def prepare(sib, oth, keep, gain, wih, wil, conv_w, conv_b, w_x, w_dt, dt_bias, spread_s, a2, xb, gy):
    rows, inner = xb.shape
    state, width = a2.shape[0], w_x.shape[0]
    big = pltpu.VMEM((rows, inner), F32)
    edge = pltpu.VMEM((2, state, CH, inner), F32)
    return pl.pallas_call(
        prepare_kernel,
        out_shape=(
            big, big, big, big,
            pltpu.VMEM((3 * rows, LANE), F32),
            pltpu.VMEM((rows, width), F32),
            pltpu.VMEM((2 * CH, inner), F32),
            edge, edge,
            pltpu.VMEM((4 * state + 8, inner), F32),
            big, big,
            pltpu.VMEM((rows, 2 * state * LANE), F32),
            pltpu.VMEM((2, rows // 2 // CH, state, CH, inner), F32),
            pltpu.VMEM((2, rows // 2 // CH, state, CH, inner), F32),
        ),
        scratch_shapes=[pltpu.VMEM((4 * state, CH, inner), F32)],
        compiler_params=params(8),
        name="prepare",
    )(sib, oth, keep, gain, wih, wil, conv_w, conv_b, w_x, w_dt, dt_bias, spread_s, a2, xb, gy)


def summary_parts(ref_value, state):
    return [ref_value[i * state : (i + 1) * state] for i in range(4)]


def pair_kernel(a2_s, mine, theirs, out):
    state, half = a2_s.shape[0], out.shape[1]
    core = lax.axis_index("seq") & 1
    cols = pl.ds(pl.multiple_of(core * half, half), half)
    a2 = half_a2(a2_s, half)
    me, it = mine[:, cols], theirs[:, cols]
    low, high = jnp.where(core == 1, it, me), jnp.where(core == 1, me, it)
    put_total(out, joined(low, high, a2, state), state)


def joined(low, high, a2, state):
    low_f, low_r = low[4 * state : 4 * state + 1], low[4 * state + 1 : 4 * state + 2]
    high_f, high_r = high[4 * state : 4 * state + 1], high[4 * state + 1 : 4 * state + 2]
    lows, highs = summary_parts(low, state), summary_parts(high, state)
    return [
        lows[0] * jnp.exp2(high_f * a2) + highs[0],
        lows[1] * jnp.exp2(high_r * a2) + highs[1],
        highs[2] * jnp.exp2(low_r * a2) + lows[2],
        highs[3] * jnp.exp2(low_f * a2) + lows[3],
        low_f + high_f,
        low_r + high_r,
    ]


def put_total(out, parts, state):
    for i in range(4):
        out[i * state : (i + 1) * state] = parts[i]
    rest = jnp.zeros((out.shape[0] - 4 * state - 2, out.shape[1]), F32)
    out[4 * state :] = jnp.concatenate([parts[4], parts[5], rest], axis=0)


def half_a2(a2_s, half):
    core = lax.axis_index("seq") & 1
    cols = pl.ds(pl.multiple_of(core * half, half), half)
    return jnp.concatenate([a2_s[n, 0:1, cols] for n in range(a2_s.shape[0])], axis=0)


def stage_kernel(first, halves, a2_s, *refs):
    outs = 1 + len(halves) if halves else 2
    members, out, held = refs[: -outs - 1], refs[-outs - 1 : -1], refs[-1]
    count = len(members)
    state, half = a2_s.shape[0], out[0].shape[1]
    a2 = half_a2(a2_s, half)
    at = (lax.axis_index("seq") >> first) & (count - 1)
    for i, ref in enumerate(members):
        held[at ^ i] = ref[...]
    zero, none = jnp.zeros((state, half), F32), jnp.zeros((1, half), F32)

    def run_through(order, rows, reach):
        run = [zero, zero, none, none]
        seen = list(run)
        for i in order:
            seen = [jnp.where(at == i, now, old) for now, old in zip(run, seen)]
            df, dr = held[i, 4 * state : 4 * state + 1], held[i, 4 * state + 1 : 4 * state + 2]
            decays = [jnp.exp2((df, dr)[w] * a2) for w in reach]
            run = [run[k] * decays[k] + held[i, rows[k] * state : (rows[k] + 1) * state] for k in range(2)] + [
                run[2] + df,
                run[3] + dr,
            ]
        return run, seen

    right, seen = run_through(range(count), (0, 1), (0, 1))
    left, seen_left = run_through(range(count - 1, -1, -1), (2, 3), (1, 0))
    enter = out[0]
    enter[:state], enter[state : 2 * state] = seen[0], seen[1]
    enter[2 * state : 3 * state], enter[3 * state : 4 * state] = seen_left[0], seen_left[1]
    blank = jnp.zeros((CH, half), F32)
    enter[4 * state :] = jnp.concatenate([seen[2], seen[3], seen_left[2], seen_left[3], blank[:4]], axis=0)
    sums = jnp.concatenate([right[2], right[3], blank[:6]], axis=0)
    if halves:
        me = lax.axis_index("seq")
        for ref, apart in zip(out[1:], halves):
            later = (me ^ apart) > me
            ref[:state] = jnp.where(later, right[0], left[0])
            ref[state : 2 * state] = jnp.where(later, right[1], left[1])
            ref[2 * state :] = sums
    else:
        for i, value in enumerate((right[0], right[1], left[0], left[1])):
            out[1][i * state : (i + 1) * state] = value
        out[1][4 * state :] = sums


def last_kernel(first, a2_s, *refs):
    theirs, out, held = refs[:-2], refs[-2], refs[-1]
    count = len(theirs) + 1
    state, half = a2_s.shape[0], out.shape[1]
    a2 = half_a2(a2_s, half)
    at = (lax.axis_index("seq") >> first) & (count - 1)
    held[at] = jnp.zeros(held.shape[1:], F32)
    for i, ref in enumerate(theirs):
        held[at ^ (i + 1)] = ref[...]

    def run_through(order, reach, inside):
        run = [jnp.zeros((state, half), F32)] * 2
        for i in order:
            sums = held[i, 2 * state : 2 * state + 1], held[i, 2 * state + 1 : 2 * state + 2]
            for k in range(2):
                longer = run[k] * jnp.exp2(sums[reach[k]] * a2) + held[i, k * state : (k + 1) * state]
                run[k] = jnp.where(inside(i), longer, run[k])
        return run

    found = run_through(range(count - 1), (0, 1), lambda i: i < at)
    found = found + run_through(range(count - 1, 0, -1), (1, 0), lambda i: i > at)
    for i in range(4):
        out[i * state : (i + 1) * state] = found[i]


def pair(a2_s, mine, theirs):
    rows, inner = mine.shape
    return pl.pallas_call(
        pair_kernel,
        out_shape=jax.ShapeDtypeStruct((rows, inner // 2), F32),
        compiler_params=params(2),
        name="pair",
    )(a2_s, mine, theirs)


def stage(first, halves, a2_s, members):
    shape = jax.ShapeDtypeStruct(members[0].shape, F32)
    part = jax.ShapeDtypeStruct((2 * a2_s.shape[0] + CH, members[0].shape[1]), F32)
    return pl.pallas_call(
        lambda *refs: stage_kernel(first, halves, *refs),
        out_shape=(shape,) + (part,) * len(halves) if halves else (shape, shape),
        scratch_shapes=[pltpu.VMEM((len(members),) + members[0].shape, F32)],
        compiler_params=params(4),
        name="stage",
    )(a2_s, *members)


def last_stage(first, a2_s, theirs):
    return pl.pallas_call(
        lambda *refs: last_kernel(first, *refs),
        out_shape=jax.ShapeDtypeStruct((4 * a2_s.shape[0], theirs[0].shape[1]), F32),
        scratch_shapes=[pltpu.VMEM((len(theirs) + 1,) + theirs[0].shape, F32)],
        compiler_params=params(4),
        name="stage",
    )(a2_s, *theirs)


def enter_kernel(a2_s, *refs):
    stages, out = refs[:-1], refs[-1]
    state, half = a2_s.shape[0], out.shape[1]
    a2 = half_a2(a2_s, half)
    value = [stages[-1][i * state : (i + 1) * state] for i in range(4)]
    for ref in reversed(stages[:-1]):
        reach = [ref[4 * state + i : 4 * state + i + 1] for i in range(4)]
        value = [
            ref[i * state : (i + 1) * state] + value[i] * jnp.exp2(reach[w] * a2)
            for i, w in ((0, 0), (1, 1), (2, 3), (3, 2))
        ]
    for i in range(4):
        out[i * state : (i + 1) * state] = value[i]


def enter(a2_s, stages):
    half = stages[0].shape[1]
    return pl.pallas_call(
        enter_kernel,
        out_shape=jax.ShapeDtypeStruct((4 * a2_s.shape[0], half), F32),
        compiler_params=params(2),
        name="enter",
    )(a2_s, *stages)


def carry_in(car_s, a2_s, mine_half, other_half, sibling):
    state, inner = a2_s.shape[0], a2_s.shape[2]
    half = inner // 2
    odd = (lax.axis_index("seq") & 1) == 1
    a2 = jnp.concatenate([a2_s[n, 0:1, :] for n in range(state)], axis=0)
    left, right = jnp.where(odd, other_half[...], mine_half[...]), jnp.where(odd, mine_half[...], other_half[...])
    into = jnp.concatenate([left, right], axis=1)
    df, dr = sibling[4 * state : 4 * state + 1], sibling[4 * state + 1 : 4 * state + 2]
    for i, reach, through in ((0, df, odd), (1, dr, odd), (2, dr, ~odd), (3, df, ~odd)):
        rows = slice(i * state, (i + 1) * state)
        value = jnp.where(through, into[rows] * jnp.exp2(reach * a2) + sibling[rows], into[rows])
        for n in range(state):
            car_s[i * state + n] = jnp.broadcast_to(value[n : n + 1], (CH, inner))


def forward_kernel(
    mine_half, other_half, sibling, sx, de_s, dx_s, bc_s, a2_s, decay, drive,
    y_s, h_s, car_o,
    before_s,
):
    rows2, inner = de_s.shape
    length = rows2 // 2
    steps = length // CH
    tiles = inner // LANE
    state = a2_s.shape[0]
    carry_in(car_o, a2_s, mine_half, other_half, sibling)
    y_s[...] = jnp.zeros(y_s.shape, F32)
    group = 8
    cols_of = [slice(t * LANE, (t + 1) * LANE) for t in range(tiles)]
    for dirn in range(2):
        order = list(range(steps)) if dirn == 0 else list(range(steps - 1, -1, -1))
        base = dirn * length
        s_row = 0 if dirn == 0 else 2
        for cols in cols_of:
            total = jnp.zeros((CH, LANE), F32)
            for j in range(steps):
                total = total + de_s[base + j * CH : base + (j + 1) * CH, cols]
            before_s[:, cols] = outside_sum(total, dirn == 0)

        def some(g, carry, dirn=dirn, order=order, base=base, s_row=s_row):
            n0 = g * group
            at_b, at_c = lanes_of(n0, group), lanes_of(state + n0, group)
            h = {}
            for n in range(group):
                for t, cols in enumerate(cols_of):
                    into = jnp.exp2(before_s[:, cols] * a2_s[n0 + n, :, cols]) * car_o[s_row * state + n0 + n, :, cols]
                    h[n, t] = sx[dirn, n0 + n, :, cols] + into
                    h_s[dirn, 0, n0 + n, :, cols] = h[n, t]
            for at, j in enumerate(order):
                rows = slice(base + j * CH, base + (j + 1) * CH)
                dx = [dx_s[rows, c] for c in cols_of]
                y = [None] * tiles
                for n in range(group):
                    c_n = bc_s[rows, at_c[n]]
                    for t, cols in enumerate(cols_of):
                        h[n, t] = decay[dirn, at, n0 + n, :, cols] * h[n, t] + drive[dirn, at, n0 + n, :, cols]
                        h_s[dirn, at + 1, n0 + n, :, cols] = h[n, t]
                        term = h[n, t] * c_n
                        y[t] = term if n == 0 else y[t] + term
                for t, cols in enumerate(cols_of):
                    y_s[rows, cols] += y[t]
            return carry

        lax.fori_loop(0, state // group, some, 0)


def forward(mine_half, other_half, sibling, sx, de, dx, bc, a2, decay, drive):
    rows2, inner = de.shape
    state = a2.shape[0]
    steps = rows2 // 2 // CH
    return pl.pallas_call(
        forward_kernel,
        out_shape=(
            jax.ShapeDtypeStruct((rows2, inner), F32),
            jax.ShapeDtypeStruct((2, steps + 1, state, CH, inner), F32),
            jax.ShapeDtypeStruct((4 * state, CH, inner), F32),
        ),
        scratch_shapes=[pltpu.VMEM((CH, inner), F32)],
        compiler_params=params(4),
        name="forward",
    )(mine_half, other_half, sibling, sx, de, dx, bc, a2, decay, drive)


def ready_kernel(
    rank, tok, gout, gain, wih, wil, w_out, d_skip, z, go, conv, pre, xc, gy,
    x_o, g_o, nth_o, ntl_o, gh_o, gl_o, wfh_o, wfl_o, woh_o, wol_o, vfh_o, vfl_o,
    gate_o, zgrad_o, cgrad_o, sig_o, xch_o, xcl_o, skip_o, pickb_o, pickc_o,
):
    feat, inner = gain.shape[1], w_out.shape[0]
    x = ordered(tok)
    x_o[...] = x
    g = ordered(gout)
    g_o[...] = g
    high, low = both_orders(normalize(x, gain[...])[1])
    nth_o[...] = high.astype(F32).T.astype(BF16)
    ntl_o[...] = low.astype(F32).T.astype(BF16)
    gh_o[...], gl_o[...] = both_orders(g)
    flip = flip_matrix(feat)
    wfh_o[...], wfl_o[...] = nn(flip, wih[...]).astype(BF16), nn(flip, wil[...]).astype(BF16)
    high, low = split(w_out[...])
    woh_o[...], wol_o[...] = high, low
    vfh_o[...], vfl_o[...] = nn(high, flip).astype(BF16), nn(low, flip).astype(BF16)
    xch_o[...], xcl_o[...] = split(xc[...])
    for lt in range(inner // LANE):
        cols = slice(lt * LANE, (lt + 1) * LANE)
        zt, v = z[:, cols], conv[:, cols]
        s = sigmoid(zt)
        gate_o[:, cols] = zt * s
        zgrad_o[:, cols] = go[:, cols] * (s * (1.0 + zt * (1.0 - s)))
        s = sigmoid(v)
        cgrad_o[:, cols] = s * (1.0 + v * (1.0 - s))
        sig_o[:, cols] = sigmoid(pre[:, cols])
        skip_o[:, cols] = jnp.sum(gy[:, cols] * xc[:, cols], axis=0, keepdims=True)
    row = lax.broadcasted_iota(jnp.int32, pickb_o.shape, 0) >> 6
    col = lax.broadcasted_iota(jnp.int32, pickb_o.shape, 1)
    pickb_o[...] = jnp.where(col == row + rank, 1.0, 0.0).astype(BF16)
    pickc_o[...] = jnp.where(col == row + (rank + pickb_o.shape[0] // (LANE // 2)), 1.0, 0.0).astype(BF16)


def ready(rank, state, tok, gout, gain, wih, wil, w_out, d_skip, z, go, conv, pre, xc, gy):
    length, feat = tok.shape
    rows2, inner = z.shape
    f32 = lambda *dims: jax.ShapeDtypeStruct(dims, F32)
    b16 = lambda *dims: jax.ShapeDtypeStruct(dims, BF16)
    both = lambda *dims: (b16(*dims), b16(*dims))
    return pl.pallas_call(
        lambda *refs: ready_kernel(rank, *refs),
        out_shape=(f32(length, feat), f32(length, feat))
        + both(feat, rows2) + both(rows2, feat) + both(feat, 2 * inner)
        + both(inner, feat) + both(inner, feat)
        + (f32(rows2, inner),) * 4
        + both(rows2, inner) + (f32(1, inner),) + both(state * LANE // 2, LANE),
        compiler_params=params(8),
        name="ready",
    )(tok, gout, gain, wih, wil, w_out, d_skip, z, go, conv, pre, xc, gy)


def early_kernel(
    rs_bits, nth, ntl, gh, gl, gate, zgrad, d_skip, xc, y_s, gzh_o, gzl_o, outh_o, outl_o, pieces_o,
):
    y = y_s[...] + d_skip[...] * xc[...]
    gz = split(zgrad[...] * y)
    gzh_o[...], gzl_o[...] = gz
    out = split(y * gate[...])
    gw_out = mm(tn, out, (gh[...], gl[...]))
    gw_in = mm(nn, (nth[...], ntl[...]), gz)
    outh_o[...], outl_o[...] = out
    put_pieces(rs_bits, pieces_o, [(gw_in, None), (gw_out, None)])


def early(rs_bits, nth, ntl, gh, gl, gate, zgrad, d_skip, xc, y):
    feat = nth.shape[0]
    rows2, inner = xc.shape
    pieces = 1 << rs_bits
    tall = 2 * feat * inner // LANE // pieces
    gz = jax.ShapeDtypeStruct((rows2, inner), BF16)
    return pl.pallas_call(
        lambda *refs: early_kernel(rs_bits, *refs),
        out_shape=(gz, gz, gz, gz, jax.ShapeDtypeStruct((pieces, tall, LANE), F32)),
        compiler_params=params(8),
        name="early",
    )(nth, ntl, gh, gl, gate, zgrad, d_skip, xc, y)


def put_pieces(rs_bits, pieces_o, arrays, few=None):
    pieces = 1 << rs_bits
    mine = reverse_bits(lax.axis_index("seq"), rs_bits)
    for p in range(pieces):
        slot = mine ^ reverse_bits(p, rs_bits)
        at = 0
        for value, more in arrays:
            tall = value.shape[0] // pieces
            for lt in range(value.shape[1] // LANE):
                where = (slice(p * tall, (p + 1) * tall), slice(lt * LANE, (lt + 1) * LANE))
                block = value[where] if more is None else value[where] + more[where]
                pieces_o[slot, at : at + tall, :] = block
                at += tall
        if few is not None:
            tiles = few.shape[1] // LANE
            top = pieces // tiles * CH
            rest = (few.shape[0] - top) * tiles // pieces
            rb, lt = p // tiles, p % tiles
            pieces_o[slot, at : at + CH, :] = few[rb * CH : (rb + 1) * CH, lt * LANE : (lt + 1) * LANE]
            rows = []
            for v in range(rest * p, rest * (p + 1)):
                rb, lt = top + v // tiles, v % tiles
                rows.append(few[rb : rb + 1, lt * LANE : (lt + 1) * LANE])
            zeros = jnp.zeros((4, LANE), F32)
            rows = [zeros] + rows + [zeros[: 4 - rest]]
            pieces_o[slot, at + CH : at + 2 * CH, :] = jnp.concatenate(rows, axis=0)
            pieces_o[slot, at + 2 * CH : at + 3 * CH, :] = jnp.zeros((CH, LANE), F32)


def row_vectors(rows):
    return jnp.concatenate(
        [rows[b : b + 1, lt * LANE : (lt + 1) * LANE] for b in range(3) for lt in range(rows.shape[1] // LANE)],
        axis=0,
    )


def backward_kernel(
    dirn, mx, car, h_s, de_s, dx_s, bc_s, a2_s, decay, gy,
    sb_s, sa_s, accb, accc, ga_s,
    after_s,
):
    rows2, inner = de_s.shape
    length = rows2 // 2
    steps = length // CH
    tiles = inner // LANE
    state = a2_s.shape[0]
    order = list(range(steps)) if dirn == 0 else list(range(steps - 1, -1, -1))
    base = dirn * length
    m_row = 3 if dirn == 0 else 1
    group = 8
    low = lax.broadcasted_iota(jnp.int32, (CH, LANE), 1) < LANE // 2
    cols_of = [slice(t * LANE, (t + 1) * LANE) for t in range(tiles)]
    sb_s[...] = jnp.zeros(sb_s.shape, F32)
    sa_s[...] = jnp.zeros(sa_s.shape, F32)
    for cols in cols_of:
        total = jnp.zeros((CH, LANE), F32)
        for j in range(steps):
            total = total + de_s[base + j * CH : base + (j + 1) * CH, cols]
        after_s[:, cols] = outside_sum(total, dirn != 0)

    def some(g, carry):
        n0 = g * group
        at_b, at_c = lanes_of(n0, group), lanes_of(state + n0, group)
        a2, q, ga, now = {}, {}, {}, {}
        for n in range(group):
            for t, cols in enumerate(cols_of):
                a2[n, t] = a2_s[n0 + n, :, cols]
                into = jnp.exp2(after_s[:, cols] * a2[n, t]) * car[m_row * state + n0 + n, :, cols]
                q[n, t] = mx[dirn, n0 + n, :, cols] + into
                ga[n, t] = jnp.zeros((CH, LANE), F32)
                now[n, t] = h_s[dirn, steps, n0 + n, :, cols]
        for time in range(steps - 1, -1, -1):
            j = order[time]
            rows = slice(base + j * CH, base + (j + 1) * CH)
            here = slice(j * CH, (j + 1) * CH)
            de = [de_s[rows, c] for c in cols_of]
            dx = [dx_s[rows, c] for c in cols_of]
            gyj = [gy[rows, c] for c in cols_of]
            sb, sa = [None] * tiles, [None] * tiles
            sums = []
            for n in range(group):
                b_n, c_n = bc_s[rows, at_b[n]], bc_s[rows, at_c[n]]
                to_b = to_c = None
                for t, cols in enumerate(cols_of):
                    gh = gyj[t] * c_n + q[n, t]
                    term_c = gyj[t] * now[n, t]
                    term_b = gh * dx[t]
                    to_b = term_b if t == 0 else to_b + term_b
                    to_c = term_c if t == 0 else to_c + term_c
                    q[n, t] = decay[dirn, time, n0 + n, :, cols] * gh
                    now[n, t] = h_s[dirn, time, n0 + n, :, cols]
                    r = q[n, t] * now[n, t]
                    ga[n, t] = ga[n, t] + de[t] * r
                    sb[t] = gh * b_n if n == 0 else sb[t] + gh * b_n
                    sa[t] = a2[n, t] * r if n == 0 else sa[t] + a2[n, t] * r
                sums.append((to_b, to_c))
            for i, at in enumerate(lanes_of(g * (group // 2), group // 2)):
                for acc, one, two in zip((accb, accc), sums[2 * i], sums[2 * i + 1]):
                    acc[here, at] = jnp.where(low, one, two) + pltpu.roll(jnp.where(low, two, one), LANE // 2, 1)
            for t, cols in enumerate(cols_of):
                sb_s[here, cols] += sb[t]
                sa_s[here, cols] += sa[t]
        for n in range(group):
            for t, cols in enumerate(cols_of):
                ga_s[n0 + n, :, cols] = ga[n, t]
        return carry

    lax.fori_loop(0, state // group, some, 0)


def backward(dirn, mx, car, h, de, dx, bc, a2, decay, gy):
    rows2, inner = de.shape
    state = a2.shape[0]
    length = rows2 // 2
    half = jax.ShapeDtypeStruct((length, inner), F32)
    acc = jax.ShapeDtypeStruct((length, state * LANE // 2), F32)
    return pl.pallas_call(
        lambda *refs: backward_kernel(dirn, *refs),
        out_shape=(half, half, acc, acc, jax.ShapeDtypeStruct((state, CH, inner), F32)),
        scratch_shapes=[pltpu.VMEM((CH, inner), F32)],
        compiler_params=params(4),
        name="backward",
    )(mx, car, h, de, dx, bc, a2, decay, gy)


def inner_kernel(
    pad, conv_w, w_x, w_dt, d_skip, a2_s,
    xb, gy, xc, dt, sig, cgrad, mask, dbl, xbh, xch, xcl, skip_sum, pick_b, pick_c,
    sb_f, sa_f, accb_f, accc_f, ga_f, sb_r, sa_r, accb_r, accc_r, ga_r,
    gxh_o, gxl_o, halo_o, few_o,
    gp_s, gpre_s, xcg_s,
):
    inner, rank = w_x.shape[1], w_dt.shape[0]
    state = a2_s.shape[0]
    rows2 = xb.shape[0]
    length = rows2 // 2
    steps = length // CH
    tiles = inner // LANE
    sub = sub_iota()

    bias_rows = []
    for lt in range(tiles):
        cols = slice(lt * LANE, (lt + 1) * LANE)
        bias = jnp.zeros((1, LANE), F32)
        for dirn, sb, sa in ((0, sb_f, sa_f), (1, sb_r, sa_r)):
            rows = slice(dirn * length, (dirn + 1) * length)
            g_pre = (xc[rows, cols] * sb[:, cols] + LN2 * sa[:, cols]) * sig[rows, cols]
            gpre_s[rows, cols] = g_pre
            xcg_s[rows, cols] = d_skip[:, cols] * gy[rows, cols] + dt[rows, cols] * sb[:, cols]
            bias = bias + jnp.sum(g_pre, axis=0, keepdims=True)
        bias_rows.append(bias)

    b_parts = split(jnp.concatenate([accb_f[...], accb_r[...]], axis=0))
    c_parts = split(jnp.concatenate([accc_f[...], accc_r[...]], axis=0))
    g_bc = (nn(b_parts[0], pick_b[...]) + nn(b_parts[1], pick_b[...])) + (
        nn(c_parts[0], pick_c[...]) + nn(c_parts[1], pick_c[...])
    )
    gpre_parts = split(gpre_s[...])
    w_dt_parts = split(w_dt[...])
    g_rank = mm(nt, gpre_parts, w_dt_parts)
    width = rank + 2 * state
    g_dbl = jnp.concatenate([g_rank, g_bc[:, rank:width]], axis=1)
    g_dbl_parts = split(g_dbl)
    few_o[width + state : width + state + rank, :] = mm(tn, split(dbl[:, :rank]), gpre_parts)
    few_o[:width, :] = mm(tn, g_dbl_parts, (xch[...], xcl[...]))
    xcg_s[...] += mm(nn, g_dbl_parts, split(w_x[...]))

    cw_rows = [[] for _ in range(4)]
    cb_rows = []
    halo_f, halo_r = [], []
    for lt in range(tiles):
        cols = slice(lt * LANE, (lt + 1) * LANE)
        taps = [conv_w[k : k + 1, cols] for k in range(4)]
        xbh_t = xbh[:, cols]
        xf = [xb[j * CH : (j + 1) * CH, cols] for j in range(steps)]
        xf = [
            jnp.where(sub == 0, xbh_t[b : b + 1], pltpu.roll(xf[steps - 3 + b], 1, 0))
            for b in range(3)
        ] + xf
        gcw = [jnp.zeros((CH, LANE), F32) for _ in range(4)]
        gcb = jnp.zeros((CH, LANE), F32)
        grads = [None] * (steps + 3)
        for j in range(steps):
            rows = slice(j * CH, (j + 1) * CH)
            u = xcg_s[rows, cols] * cgrad[rows, cols]
            gcb = gcb + u
            for k in range(4):
                uk = u if k == 0 else u * mask[(k - 1) * length + j * CH : (k - 1) * length + (j + 1) * CH, :]
                gcw[k] = gcw[k] + uk * xf[j + 3 - k]
                add = taps[k] * uk
                at = j + 3 - k
                grads[at] = add if grads[at] is None else grads[at] + add
        for b in range(3):
            halo_f.append(grads[b][0:1])
            at = steps + b
            grads[at] = grads[at] + jnp.where(sub == CH - 1, 0.0, pltpu.roll(grads[b], CH - 1, 0))
        for j in range(steps):
            gp_s[j * CH : (j + 1) * CH, cols] = grads[j + 3]
        xr = [xb[length + j * CH : length + (j + 1) * CH, cols] for j in range(steps)]
        xr = xr + [
            jnp.where(sub == CH - 1, xbh_t[8 + b : 9 + b], pltpu.roll(xr[b], CH - 1, 0))
            for b in range(3)
        ]
        grads = [None] * (steps + 3)
        for j in range(steps):
            rows = slice(length + j * CH, length + (j + 1) * CH)
            u = xcg_s[rows, cols] * cgrad[rows, cols]
            gcb = gcb + u
            for k in range(4):
                uk = u if k == 0 else u * mask[(k + 2) * length + j * CH : (k + 2) * length + (j + 1) * CH, :]
                gcw[k] = gcw[k] + uk * xr[j + k]
                add = taps[k] * uk
                grads[j + k] = add if grads[j + k] is None else grads[j + k] + add
        for b in range(3):
            halo_r.append(grads[steps + b][CH - 1 : CH])
            grads[b] = grads[b] + jnp.where(sub == 0, 0.0, pltpu.roll(grads[steps + b], 1, 0))
        for j in range(steps):
            gp_s[length + j * CH : length + (j + 1) * CH, cols] = grads[j]
        for k in range(4):
            cw_rows[k].append(jnp.sum(gcw[k], axis=0, keepdims=True))
        cb_rows.append(jnp.sum(gcb, axis=0, keepdims=True))
    pad_col = spread(pad[...].astype(F32))
    pad_all = jnp.concatenate([pad_col, pad_col], axis=0)
    for lt in range(tiles):
        cols = slice(lt * LANE, (lt + 1) * LANE)
        gxh_o[:, cols], gxl_o[:, cols] = split(gp_s[:, cols] * pad_all)

    blank = jnp.zeros((5, inner), F32)

    def gather(found):
        return jnp.concatenate(
            [jnp.concatenate([found[lt * 3 + b] for lt in range(tiles)], axis=1) for b in range(3)]
            + [blank],
            axis=0,
        )

    halo_o[...] = jnp.concatenate([gather(halo_f), gather(halo_r)], axis=0)
    ga = jnp.concatenate(
        [jnp.sum(ga_f[n] + ga_r[n], axis=0, keepdims=True) * (a2_s[n, 0:1, :] * LN2) for n in range(state)], axis=0
    )
    few_o[width : width + state, :] = ga
    few_o[width + state + rank :, :] = jnp.concatenate(
        [jnp.concatenate(cw_rows[k], axis=1) for k in range(4)]
        + [
            jnp.concatenate(cb_rows, axis=1),
            jnp.concatenate(bias_rows, axis=1),
            skip_sum[...],
            jnp.zeros((1, inner), F32),
        ],
        axis=0,
    )


def inner_back(*arrays):
    w_x, w_dt, a2, xb = arrays[2], arrays[3], arrays[5], arrays[6]
    rows2, inner = xb.shape
    few = w_x.shape[0] + a2.shape[0] + w_dt.shape[0] + CH
    big = pltpu.VMEM((rows2, inner), F32)
    part = jax.ShapeDtypeStruct((rows2, inner), BF16)
    return pl.pallas_call(
        inner_kernel,
        out_shape=(
            part, part,
            jax.ShapeDtypeStruct((2 * CH, inner), F32),
            jax.ShapeDtypeStruct((few, inner), F32),
        ),
        scratch_shapes=[big, big, big],
        compiler_params=params(8),
        name="inner",
    )(*arrays)


def tail_kernel(
    rs_bits, sib, oth, gain, x_s, nth, ntl, wih, wil, wfh, wfl, gzh, gzl, gxh, gxl, halo, few,
    normed_o, pieces_o, *edges_o,
):
    feat = gain.shape[1]
    rows2, inner = gxh.shape
    length = rows2 // 2
    left, right = pick_sides(sib[...], oth[...])
    factor_l, hn_l = normalize(left, gain[...])
    factor_r, hn_r = normalize(right, gain[...])
    flip = flip_matrix(feat)
    lh, ll = split(hn_l)
    rh, rl = split(hn_r)
    edge = (
        jnp.concatenate([lh, nn(rh, flip).astype(BF16)], axis=0),
        jnp.concatenate([ll, nn(rl, flip).astype(BF16)], axis=0),
    )
    x = x_s[...]
    factor = normalize(x, gain[...])[0]
    gh_parts = split(halo[...])
    gw_in = mm(nn, (nth[...], ntl[...]), (gxh[...], gxl[...]))
    gw_in_halo = mm(tn, edge, gh_parts)
    w_xb = (wih[:, :inner], wil[:, :inner])
    g_normed = (
        mm(nt, (gxh[:length], gxl[:length]), w_xb)
        + mm(nt, (gzh[:length], gzl[:length]), (wih[:, inner:], wil[:, inner:]))
    ) + (
        mm(nt, (gxh[length:], gxl[length:]), (wfh[:, :inner], wfl[:, :inner]))
        + mm(nt, (gzh[length:], gzl[length:]), (wfh[:, inner:], wfl[:, inner:]))
    )
    back_h = mm(nt, gh_parts, w_xb)
    gn_l = back_h[:CH]
    gn_r = flipped(back_h[CH:])

    normed_o[...] = g_normed
    to_left = norm_back(left, factor_l, gn_l, gain[...])
    to_right = norm_back(right, factor_r, gn_r, gain[...])
    for ref, value in zip(edges_o, (to_left, to_right)):
        ref[...] = value
    three = lax.broadcasted_iota(jnp.int32, (CH, feat), 0) < 3
    g_gain = (
        jnp.sum(g_normed * (x * factor), axis=0, keepdims=True)
        + jnp.sum(jnp.where(three, gn_l * (left * factor_l) + gn_r * (right * factor_r), 0.0), axis=0, keepdims=True)
    )
    few_all = jnp.concatenate(
        [few[: few.shape[0] - CH, :], few[few.shape[0] - CH : few.shape[0] - 1, :]]
        + [jnp.concatenate([g_gain, jnp.zeros((1, inner - feat), F32)], axis=1)],
        axis=0,
    )
    put_pieces(rs_bits, pieces_o, [(gw_in, gw_in_halo)], few_all)
    pieces = 1 << rs_bits
    me = lax.axis_index("seq") & (pieces - 1)
    mine = reverse_bits(me, rs_bits)
    at = pieces_o.shape[1] - 2 * CH

    @pl.when(me < pieces - 1)
    def _():
        slot = mine ^ reverse_bits(me + 1, rs_bits)
        vectors = row_vectors(to_right)
        pieces_o[slot, at : at + 4, :] = vectors[:4]
        pieces_o[slot, at + CH : at + CH + 2, :] = vectors[4:]

    @pl.when(me > 0)
    def _():
        slot = mine ^ reverse_bits(me - 1, rs_bits)
        pieces_o[slot, at + CH + 2 : at + 2 * CH, :] = row_vectors(to_left)


def reverse_bits(value, bits):
    found = 0
    for i in range(bits):
        found = found | (((value >> i) & 1) << (bits - 1 - i))
    return found


def norm_back(x, factor, gn, gain):
    scaled = gn * gain
    return factor * scaled - x * (factor * factor * factor * jnp.mean(scaled * x, axis=1, keepdims=True))


def finish_kernel(x_s, g, gain, g_normed, outh, outl, woh, wol, vfh, vfl, mixed_o, gtok_o):
    length = x_s.shape[0]
    x = x_s[...]
    fwd = mm(nn, (outh[:length], outl[:length]), (woh[...], wol[...]))
    rev = mm(nn, (outh[length:], outl[length:]), (vfh[...], vfl[...]))
    store_ordered(mixed_o, x + (fwd + rev))
    factor = normalize(x, gain[...])[0]
    store_ordered(gtok_o, g[...] + norm_back(x, factor, g_normed[...], gain[...]))


def finish(*arrays):
    shape = jax.ShapeDtypeStruct(arrays[0].shape, F32)
    return pl.pallas_call(
        finish_kernel,
        out_shape=(shape, shape),
        compiler_params=params(6),
        name="finish",
    )(*arrays)


def tail(rs_bits, alone, *arrays):
    x, gxh = arrays[3], arrays[12]
    length, feat = x.shape
    inner = gxh.shape[1]
    pieces = 1 << rs_bits
    tall = feat * inner // LANE // pieces + 3 * CH
    return pl.pallas_call(
        lambda *refs: tail_kernel(rs_bits, *refs),
        out_shape=(
            jax.ShapeDtypeStruct((length, feat), F32),
            jax.ShapeDtypeStruct((pieces, tall, LANE), F32),
        )
        + (jax.ShapeDtypeStruct((CH, feat), F32),) * (2 if alone else 0),
        compiler_params=params(8),
        name="tail",
    )(*arrays)


def unpack_kernel(rs_bits, parts, *refs):
    sources, refs = refs[:parts], refs[parts:]
    (gtok, halo, pad, gtok_o, gain_o, w_in_o, conv_w_o, conv_b_o, w_x_o, w_dt_o, dt_bias_o, a_log_o, d_skip_o, w_out_o,
     few_s, rest_s) = refs
    feat = w_in_o.shape[0]
    inner = w_out_o.shape[0]
    tiles = inner // LANE
    pieces = 1 << rs_bits
    mine = reverse_bits(lax.axis_index("seq"), rs_bits)
    in_rows, out_rows = feat // pieces, inner // pieces
    for slot in range(pieces):
        source = sources[slot * parts // pieces]
        i = slot % (pieces // parts)
        p = reverse_bits(mine ^ slot, rs_bits)
        at = 0
        in_at = pl.ds(pl.multiple_of(p * in_rows, in_rows), in_rows)
        out_at = pl.ds(pl.multiple_of(p * out_rows, out_rows), out_rows)
        for lt in range(tiles):
            w_in_o[in_at, inner + lt * LANE : inner + (lt + 1) * LANE] = source[i, at : at + in_rows, :]
            at += in_rows
        for lt in range(feat // LANE):
            w_out_o[out_at, lt * LANE : (lt + 1) * LANE] = source[i, at : at + out_rows, :]
            at += out_rows
        for lt in range(tiles):
            w_in_o[in_at, lt * LANE : (lt + 1) * LANE] = source[i, at : at + in_rows, :]
            at += in_rows
        few_s[p] = source[i, at : at + CH, :]
        rest_s[p] = source[i, at + CH : at + 2 * CH, :]

    top = pieces // tiles * CH
    total = w_x_o.shape[0] + a_log_o.shape[0] + w_dt_o.shape[0] + CH
    rest = (total - top) * tiles // pieces

    def few_rows(first, count):
        found = []
        for lt in range(tiles):
            if first < top:
                found.append(few_s[first // CH * tiles + lt])
                continue
            rows = []
            for row in range(first, first + count):
                v = (row - top) * tiles + lt
                rows.append(rest_s[v // rest, 4 + v % rest : 5 + v % rest, :])
            found.append(jnp.concatenate(rows, axis=0) if count > 1 else rows[0])
        return jnp.concatenate(found, axis=1)

    width, state = w_x_o.shape[0], a_log_o.shape[0]
    rank = w_dt_o.shape[0]
    w_x_o[...] = jnp.concatenate([few_rows(r, CH) for r in range(0, width, CH)], axis=0)
    at = width
    a_log_o[...] = jnp.concatenate([few_rows(r, CH) for r in range(at, at + state, CH)], axis=0)
    at += state
    w_dt_o[...] = jnp.concatenate([few_rows(r, CH) for r in range(at, at + rank, CH)], axis=0)
    at += rank
    conv_w_o[...] = few_rows(at, 4)
    conv_b_o[...] = few_rows(at + 4, 1)
    dt_bias_o[...] = few_rows(at + 5, 1)
    d_skip_o[...] = few_rows(at + 6, 1)
    gain_o[...] = few_rows(at + 7, 1)[:, :feat]

    length = gtok.shape[0]
    per = feat // LANE
    padded = spread_plain(pad[...].astype(F32), feat)

    def three(first):
        rows = [
            jnp.concatenate([halo[first + b * per + lt : first + b * per + lt + 1, :] for lt in range(per)], axis=1)
            for b in range(3)
        ]
        return rows, jnp.zeros((CH - 3, feat), F32)

    rows, blank = three(0)
    first = jnp.concatenate(rows + [blank], axis=0)
    rows, blank = three(3 * per)
    last = jnp.concatenate([blank] + rows, axis=0)
    gtok_o[...] = gtok[...]
    gtok_o[:CH] = gtok[:CH] + padded[:CH] * first
    gtok_o[length - CH :] = gtok[length - CH :] + padded[length - CH :] * last


def spread_plain(row, width):
    length = row.shape[1]
    rows = lax.broadcasted_iota(jnp.int32, (length, length), 0)
    cols = lax.broadcasted_iota(jnp.int32, (length, length), 1)
    picked = (jnp.where(rows == cols, 1.0, 0.0) * row).astype(BF16)
    return nn(picked, jnp.ones((length, width), BF16))


def unpack(rs_bits, parts, gtok, halo, pad, state, rank):
    length, feat = gtok.shape
    pieces = 1 << rs_bits
    inner = state[1]
    width = rank + 2 * state[0]
    shape = lambda *dims: jax.ShapeDtypeStruct(dims, F32)
    return pl.pallas_call(
        lambda *refs: unpack_kernel(rs_bits, len(parts), *refs),
        out_shape=(
            shape(length, feat),
            shape(1, feat),
            shape(feat, 2 * inner),
            shape(4, inner),
            shape(1, inner),
            shape(width, inner),
            shape(rank, inner),
            shape(1, inner),
            shape(state[0], inner),
            shape(1, inner),
            shape(inner, feat),
        ),
        scratch_shapes=[pltpu.VMEM((pieces, CH, LANE), F32)] * 2,
        compiler_params=params(6),
        name="unpack",
    )(*parts, gtok, halo, pad)


def body(tokens, resets, pad_mask, norm_gain, w_in, conv_w, conv_b, w_x, w_dt, dt_bias, a_log, d_skip, w_out, grad_out):
    count = lax.axis_size("seq")
    bits = count.bit_length() - 1
    rs_bits = min(5, bits)
    length = tokens.shape[0]
    keep_row, pad_row = resets.reshape(1, length), pad_mask.reshape(1, length)

    def exchange(value, apart):
        return lax.ppermute(value, "seq", [(i, i ^ apart) for i in range(count)])

    def swap(value, bit):
        return exchange(value, 1 << bit)

    across = [(i, i + 1) for i in range(1, count - 1, 2)] + [(i + 1, i) for i in range(1, count - 1, 2)]

    def swap_across(value):
        return lax.ppermute(value, "seq", across)

    to_sib, to_oth, kept = edges(
        tokens, keep_row, pad_row, norm_gain, w_in[0], grad_out, w_out[0],
        conv_w[0], conv_b, w_x[0].T, w_dt[0], dt_bias, a_log[0].T, d_skip,
    )
    (tok, keep, pad, gain, w_in_0, gout, w_out_0, conv_w_0, conv_b_0, w_x_t, w_dt_0, dt_bias_0, a_log_t, skip) = kept
    oth = swap_across(to_oth)
    sib = swap(to_sib, 0)
    xb, z, go, gy, wih, wil, spread_s, a2 = project(tok, pad, gain, w_in_0, gout, w_out_0, a_log_t)
    xc, dt, pre, conv, mask, dbl, xbh, sx, mx, total, de, dx, bc, decay, drive = prepare(
        sib, oth, keep, gain, wih, wil, conv_w_0, conv_b_0, w_x_t, w_dt_0, dt_bias_0, spread_s, a2, xb, gy
    )

    sibling = swap(total, 0)
    group = pair(a2, total, sibling)
    group, gate_in = lax.optimization_barrier((group, (z, go, conv, pre, xc, gy)))
    at_hand = ready(w_dt.shape[1], a_log.shape[2], tok, gout, gain, wih, wil, w_out_0, skip, *gate_in)
    stages = []
    steps = [range(first, min(first + 2, bits)) for first in range(1, bits, 2)]
    step = steps[-1]
    distances = [i << step[0] for i in range(1, 1 << len(step))]
    for first_step in steps[:-1]:
        members = [group] + [exchange(group, i << first_step[0]) for i in range(1, 1 << len(first_step))]
        halves = distances if first_step is steps[-2] else ()
        entering, *group = stage(first_step[0], halves, a2, members)
        stages.append(entering)
        if not halves:
            (group,) = group
    group, at_hand = lax.optimization_barrier((group, at_hand))
    theirs = [exchange(value, apart) for value, apart in zip(group, distances)]
    stages.append(last_stage(step[0], a2, theirs))
    mine_half = enter(a2, stages)
    other_half = swap(mine_half, 0)

    y, h, car = forward(mine_half, other_half, sibling, sx, de, dx, bc, a2, decay, drive)
    def reduced(part, step):
        size = part.shape[0] >> len(step)
        total = part[:size]
        for i in ((2, 3, 1) if len(step) == 2 else (1,)):
            slot = reverse_bits(i, len(step))
            total = total + exchange(part[slot * size : (slot + 1) * size], i << step[0])
        return total

    (x, g, nth, ntl, gh, gl, wfh, wfl, woh, wol, vfh, vfl, gate, zgrad, cgrad, sig, xch, xcl, skip_sum,
     pick_b, pick_c) = at_hand
    rs_steps = [range(0, 1)] + [range(first, min(first + 2, rs_bits)) for first in range(1, rs_bits, 2)]
    gzh, gzl, outh, outl, part_a = early(rs_bits, nth, ntl, gh, gl, gate, zgrad, skip, xc, y)
    part_a, h = lax.optimization_barrier((part_a, h))
    part_a = reduced(part_a, range(0, 1))
    back_f = backward(0, mx, car, h, de, dx, bc, a2, decay, gy)
    part_a, back_f, h = lax.optimization_barrier((part_a, back_f, h))
    part_a = reduced(part_a, range(1, 2))
    back_r = backward(1, mx, car, h, de, dx, bc, a2, decay, gy)
    gxh, gxl, halo_g, few = inner_back(
        pad, conv_w_0, w_x_t, w_dt_0, skip, a2,
        xb, gy, xc, dt, sig, cgrad, mask, dbl, xbh, xch, xcl, skip_sum, pick_b, pick_c, *back_f, *back_r,
    )
    g_normed, part_b, *to_sides = tail(
        rs_bits, bits > rs_bits, sib, oth, gain, x, nth, ntl, wih, wil, wfh, wfl, gzh, gzl, gxh, gxl, halo_g, few
    )
    part_a, part_b = lax.optimization_barrier((part_a, part_b))
    part_a, part_b = reduced(part_a, range(2, 3)), reduced(part_b, rs_steps[0])
    part_b, g_normed = lax.optimization_barrier((part_b, g_normed))
    part_b = reduced(part_b, rs_steps[1])
    mixed, gtok = finish(x, g, gain, g_normed, outh, outl, woh, wol, vfh, vfl)
    part_b, mixed, gtok = lax.optimization_barrier((part_b, mixed, gtok))
    own = jnp.concatenate([part_a, part_b], axis=1)
    for step in rs_steps[2:]:
        own = reduced(own, step)
    for bit in range(rs_bits, bits):
        own = own + swap(own, bit)
    tall = own.shape[1]
    halo = jnp.concatenate([own[0, tall - 16 : tall - 12], own[0, tall - 8 :]], axis=0)
    if bits > rs_bits:
        pairs = [(i, i + 1) for i in range(count - 1)]
        from_left = lax.ppermute(to_sides[1], "seq", pairs)[:3]
        from_right = lax.ppermute(to_sides[0], "seq", [(j, i) for i, j in pairs])[:3]
        halo = jnp.concatenate([from_left.reshape(-1, LANE), from_right.reshape(-1, LANE)], axis=0)
    own = own[:, : tall - 8]
    for step in reversed(rs_steps[1:]):
        near = [exchange(own, reverse_bits(i, len(step)) << step[0]) for i in range((1 << len(step)) - 1, 0, -1)]
        near = [own] + near[::-1]
        if step is not rs_steps[1]:
            own = jnp.concatenate(near, axis=0)
    far = [swap(part, 0) for part in near]
    outs = unpack(rs_bits, near + far, gtok, halo, pad, a_log_t.shape, w_dt.shape[1])
    gtok, g_gain, g_w_in, g_conv_w, g_conv_b, g_w_x, g_w_dt, g_dt_bias, g_a_log, g_d_skip, g_w_out = outs
    return (
        mixed, gtok, g_gain, g_w_in[None], g_conv_w[None], g_conv_b, g_w_x.T[None], g_w_dt[None],
        g_dt_bias, g_a_log.T[None], g_d_skip, g_w_out[None],
    )


def solution(mesh):
    rows, whole = P("seq", None), P()
    return jax.shard_map(
        body,
        mesh=mesh,
        in_specs=(rows, P("seq"), P("seq")) + (whole,) * 10 + (rows,),
        out_specs=(rows, rows) + (whole,) * 10,
        check_vma=False,
    )
```

```python
import jax
import jax.numpy as jnp
from jax import lax
from jax.experimental import pallas as pl
from jax.experimental.pallas import tpu as pltpu
from jax.sharding import PartitionSpec as P

F32 = jnp.float32
BF16 = jnp.bfloat16
EPS = 1e-05
LOG2E = 1.4426950408889634
LN2 = 0.6931471805599453
BIG = 1e9
CH = 8
LANE = 128
MIB = 1024 * 1024


def nn(a, b):
    return lax.dot_general(a, b, (((1,), (0,)), ((), ())), preferred_element_type=F32)


def nt(a, b):
    return lax.dot_general(a, b, (((1,), (1,)), ((), ())), preferred_element_type=F32)


def tn(a, b):
    return lax.dot_general(a, b, (((0,), (0,)), ((), ())), preferred_element_type=F32)


def split(x):
    high = x.astype(BF16)
    return high, (x - high.astype(F32)).astype(BF16)


def split3(x):
    high = x.astype(BF16)
    rest = x - high.astype(F32)
    mid = rest.astype(BF16)
    return high, mid, (rest - mid.astype(F32)).astype(BF16)


def mm(dot, a, b):
    ah, al = a if isinstance(a, tuple) else split(a)
    bh, bl = b if isinstance(b, tuple) else split(b)
    return dot(ah, bh) + (dot(ah, bl) + dot(al, bh))


def flip_matrix(size):
    rows = lax.broadcasted_iota(jnp.int32, (size, size), 0)
    cols = lax.broadcasted_iota(jnp.int32, (size, size), 1)
    return jnp.where(rows + cols == size - 1, 1.0, 0.0).astype(BF16)


def flipped(x):
    flip = flip_matrix(x.shape[1])
    high, mid, low = split3(x)
    return nn(high, flip) + (nn(mid, flip) + nn(low, flip))


def order_matrix(length):
    steps = length // CH
    rows = lax.broadcasted_iota(jnp.int32, (length, length), 0)
    cols = lax.broadcasted_iota(jnp.int32, (length, length), 1)
    token = (rows & (CH - 1)) * steps + (rows >> 3)
    return jnp.where(cols == token, 1.0, 0.0)


def exact(dot, order, x):
    high, mid, low = split3(x)
    order = order.astype(BF16)
    return dot(order, high) + (dot(order, mid) + dot(order, low))


def ordered(ref):
    return exact(nn, order_matrix(ref.shape[0]), ref[...])


def store_ordered(ref, value):
    ref[...] = exact(tn, order_matrix(ref.shape[0]), value)


def spread(row, order=None):
    length = row.shape[1]
    picked = ((order_matrix(length) if order is None else order) * row).astype(BF16)
    return nn(picked, jnp.ones((length, LANE), BF16))


def sigmoid(x):
    return 1.0 / (1.0 + jnp.exp(-x))


def normalize(x, gain):
    factor = lax.rsqrt(jnp.mean(x * x, axis=1, keepdims=True) + EPS)
    return factor, x * factor * gain


def both_orders(normed):
    flip = flip_matrix(normed.shape[1])
    high, low = split(normed)
    return (
        jnp.concatenate([high, nn(high, flip).astype(BF16)], axis=0),
        jnp.concatenate([low, nn(low, flip).astype(BF16)], axis=0),
    )


def params(mib):
    return pltpu.CompilerParams(vmem_limit_bytes=mib * MIB)


def in_hbm(*arrays):
    return tuple(pltpu.with_memory_space_constraint(x, pltpu.HBM) for x in arrays)


def edges_kernel(*refs):
    count = (len(refs) - 3) // 2
    far, to_sib, to_oth, near, arrived = refs[:count], refs[count], refs[count + 1], refs[count + 2 : -1], refs[-1]
    copies = [pltpu.make_async_copy(one, two, arrived.at[i]) for i, (one, two) in enumerate(zip(far, near))]
    for copy in copies:
        copy.start()
    for copy in copies[:3]:
        copy.wait()
    tok, resets, pad = near[:3]
    length, feat = tok.shape
    sub = lax.broadcasted_iota(jnp.int32, (CH, length), 0)
    lane = lax.broadcasted_iota(jnp.int32, (CH, length), 1)
    real = pad[...].astype(F32)
    row = lax.broadcasted_iota(jnp.int32, (CH, feat), 0)
    flags = 1.0 - resets[...].astype(F32)
    flags = jnp.concatenate([flags, jnp.zeros((1, feat - length), F32)], axis=1)

    def message(rows, start):
        col = jnp.sum(jnp.where(lane == sub + start, real, 0.0), axis=1, keepdims=True)
        return jnp.where(row < 3, rows * col, jnp.where(row == 3, flags, 0.0))

    first = message(tok[:CH, :], 0)
    last = message(pltpu.roll(tok[length - CH :, :], 3, 0), length - 3)
    odd = (lax.axis_index("seq") & 1) == 1
    to_sib[...] = jnp.where(odd, first, last)
    to_oth[...] = jnp.where(odd, last, first)
    for copy in copies[3:]:
        copy.wait()


def edges(*arrays):
    shape = jax.ShapeDtypeStruct((CH, arrays[0].shape[1]), F32)
    found = pl.pallas_call(
        edges_kernel,
        in_specs=[pl.BlockSpec(memory_space=pl.ANY)] * len(arrays),
        out_specs=(pl.BlockSpec(memory_space=pltpu.VMEM),) * (2 + len(arrays)),
        out_shape=(shape, shape) + tuple(jax.ShapeDtypeStruct(x.shape, x.dtype) for x in arrays),
        scratch_shapes=[pltpu.SemaphoreType.DMA((len(arrays),))],
        compiler_params=params(8),
        name="edges",
    )(*in_hbm(*arrays))
    return found[0], found[1], found[2:]


def project_kernel(tok, pad, gain, w_in, gout, w_out, a_log, xb_o, z_o, go_o, gy_o, wih_o, wil_o, spread_o, a2_o):
    inner = w_out.shape[0]
    x = ordered(tok)
    normed = normalize(x, gain[...])[1]
    w_parts = split(w_in[...])
    wih_o[...], wil_o[...] = w_parts
    proj = mm(nn, both_orders(normed), w_parts)
    pad_col = spread(pad[...].astype(F32))
    pad_all = jnp.concatenate([pad_col, pad_col], axis=0)
    g = ordered(gout)
    gh, gl = both_orders(g)
    go = mm(nt, (gh, gl), split(w_out[...]))
    for lt in range(inner // LANE):
        cols = slice(lt * LANE, (lt + 1) * LANE)
        z = proj[:, inner + lt * LANE : inner + (lt + 1) * LANE]
        xb_o[:, cols] = proj[:, cols] * pad_all
        z_o[:, cols] = z
        go_o[:, cols] = go[:, cols]
        gy_o[:, cols] = go[:, cols] * (z * sigmoid(z))
    width = spread_o.shape[0] // 3
    row = lax.broadcasted_iota(jnp.int32, spread_o.shape, 0)
    entry = lax.broadcasted_iota(jnp.int32, spread_o.shape, 1) >> 7
    row = jnp.where(row >= 2 * width, row - 2 * width, jnp.where(row >= width, row - width, row))
    spread_o[...] = jnp.where(row == entry, 1.0, 0.0).astype(BF16)
    a2 = jnp.exp(a_log[...]) * (-LOG2E)
    for n in range(a2.shape[0]):
        a2_o[n] = jnp.broadcast_to(a2[n : n + 1], (CH, inner))


def project(tok, pad, gain, w_in, gout, w_out, a_log):
    big = jax.ShapeDtypeStruct((2 * tok.shape[0], w_out.shape[0]), F32)
    part = jax.ShapeDtypeStruct(w_in.shape, BF16)
    state, inner = a_log.shape
    return pl.pallas_call(
        project_kernel,
        out_shape=(
            big, big, big, big, part, part,
            jax.ShapeDtypeStruct((6 * state, 2 * state * LANE), BF16),
            jax.ShapeDtypeStruct((state, CH, inner), F32),
        ),
        compiler_params=params(8),
        name="project",
    )(tok, pad, gain, w_in, gout, w_out, a_log)


def pick_sides(from_sibling, from_other):
    odd = (lax.axis_index("seq") & 1) == 1
    left = jnp.where(odd, from_sibling, from_other)
    right = jnp.where(odd, from_other, from_sibling)
    return left, right


def rows_of(ref, first, count, cols):
    block = ref[pl.ds(pl.multiple_of(first, CH), count), cols]
    return [jnp.broadcast_to(block[n : n + 1], (CH, LANE)) for n in range(count)]


def sub_iota():
    return lax.broadcasted_iota(jnp.int32, (CH, LANE), 0)


def shifted(value, up):
    return pltpu.roll(value, 1 if up else CH - 1, 0)


def chunk_weights(total, up):
    sub = sub_iota()
    found = []
    width = total
    for reach in (1, 2, 4):
        inside = (sub >= reach) if up else (sub < CH - reach)
        found.append(jnp.where(inside, width, BIG))
        width = width + pltpu.roll(width, reach if up else CH - reach, 0)
    return found


def outside_sum(total, up):
    sub = sub_iota()
    value = jnp.where((sub >= 1) if up else (sub < CH - 1), shifted(total, up), 0.0)
    for reach in (1, 2, 4):
        inside = (sub >= reach) if up else (sub < CH - reach)
        value = value + jnp.where(inside, pltpu.roll(value, reach if up else CH - reach, 0), 0.0)
    return value


def chunk_scan(value, weights, a2, up):
    for reach, weight in zip((1, 2, 4), weights):
        value = value + jnp.exp2(weight * a2) * pltpu.roll(value, reach if up else CH - reach, 0)
    sub = sub_iota()
    enter = jnp.where((sub >= 1) if up else (sub < CH - 1), shifted(value, up), 0.0)
    leave = value[CH - 1 : CH] if up else value[0:1]
    return enter, leave


def prepare_kernel(
    sib, oth, keep, gain, wih, wil, conv_w, conv_b, w_x, w_dt, dt_bias, spread_s, a2_s, xb, gy,
    xc_o, dt_o, pre_o, conv_o, mask_o, dbl_o, xbh_o, sx_o, mx_o, sum_o, de_s, dx_s, bc_s, decay_o, drive_o,
    leave_s,
):
    inner, rank = w_x.shape[1], w_dt.shape[0]
    state = a2_s.shape[0]
    length = xb.shape[0] // 2
    steps = length // CH
    tiles = inner // LANE
    left, right = pick_sides(sib[...], oth[...])
    hn_l = normalize(left, gain[...])[1]
    hn_r = normalize(right, gain[...])[1]
    flip = flip_matrix(hn_r.shape[1])
    lh, ll = split(hn_l)
    rh, rl = split(hn_r)
    halo = (
        jnp.concatenate([lh, nn(rh, flip).astype(BF16)], axis=0),
        jnp.concatenate([ll, nn(rl, flip).astype(BF16)], axis=0),
    )
    xbh = mm(nn, halo, (wih[:, :inner], wil[:, :inner]))
    xbh_o[...] = xbh
    lane = lax.broadcasted_iota(jnp.int32, (1, length), 1)
    here = 1.0 - keep[...].astype(F32)
    before, after = left[3:4, :length], right[3:4, :length]

    def back(k):
        return jnp.where(lane < k, pltpu.roll(before, k, 1), pltpu.roll(here, k, 1))

    def ahead(k):
        return jnp.where(
            lane >= length - k,
            pltpu.roll(after, length - k, 1),
            pltpu.roll(here, length - k, 1),
        )

    f1 = here
    f2 = f1 * back(1)
    f3 = f2 * back(2)
    r1 = ahead(1)
    r2 = r1 * ahead(2)
    r3 = r2 * ahead(3)
    token_order = order_matrix(length)
    for i, row in enumerate((f1, f2, f3, r1, r2, r3)):
        mask_o[i * length : (i + 1) * length, :] = spread(row, token_order)

    sub = sub_iota()

    def conv_tile(lt, carry):
        cols = pl.ds(pl.multiple_of(lt * LANE, LANE), LANE)
        xbh_t = xbh_o[:, cols]
        taps = [conv_w[k : k + 1, cols] for k in range(4)]
        bias = conv_b[:, cols]
        xf = [xb[j * CH : (j + 1) * CH, cols] for j in range(steps)]
        edge = [
            jnp.where(sub == 0, xbh_t[b : b + 1], pltpu.roll(xf[steps - 3 + b], 1, 0))
            for b in range(3)
        ]
        xf = edge + xf
        for j in range(steps):
            rows = slice(j * CH, (j + 1) * CH)
            v = bias + taps[0] * xf[j + 3]
            for k in range(1, 4):
                v = v + taps[k] * (mask_o[(k - 1) * length + j * CH : (k - 1) * length + (j + 1) * CH, :] * xf[j + 3 - k])
            conv_o[rows, cols] = v
            xc_o[rows, cols] = v * sigmoid(v)
        xr = [xb[length + j * CH : length + (j + 1) * CH, cols] for j in range(steps)]
        xr = xr + [
            jnp.where(sub == CH - 1, xbh_t[8 + b : 9 + b], pltpu.roll(xr[b], CH - 1, 0))
            for b in range(3)
        ]
        for j in range(steps):
            rows = slice(length + j * CH, length + (j + 1) * CH)
            v = bias + taps[0] * xr[j]
            for k in range(1, 4):
                v = v + taps[k] * (mask_o[(k + 2) * length + j * CH : (k + 2) * length + (j + 1) * CH, :] * xr[j + k])
            conv_o[rows, cols] = v
            xc_o[rows, cols] = v * sigmoid(v)
        return carry

    lax.fori_loop(0, tiles, conv_tile, 0)
    dbl = mm(nt, xc_o[...], w_x[...])
    dbl_o[...] = dbl
    pre_all = mm(nn, dbl[:, :rank], w_dt[...])
    bc_s[...] = nn(jnp.concatenate(split3(dbl[:, rank:]), axis=1), spread_s[...])
    for lt in range(tiles):
        cols = slice(lt * LANE, (lt + 1) * LANE)
        pre = pre_all[:, cols] + dt_bias[:, cols]
        e = jnp.exp(-jnp.abs(pre))
        u = 1.0 + e
        log1p = jnp.where(u == 1.0, e, jnp.log(u) * (e / (u - 1.0)))
        dt = jnp.maximum(pre, 0.0) + log1p
        dt_o[:, cols] = dt
        pre_o[:, cols] = pre
        dx_s[:, cols] = dt * xc_o[:, cols]
        cut = jnp.concatenate([mask_o[:length], mask_o[3 * length : 4 * length]], axis=0)
        de_s[:, cols] = dt + BIG * (1.0 - cut)

    group = 8
    cols_of = [slice(t * LANE, (t + 1) * LANE) for t in range(tiles)]
    for dirn in range(2):
        order = list(range(steps)) if dirn == 0 else list(range(steps - 1, -1, -1))
        base = dirn * length
        up = dirn == 0
        s_row, m_row = (0, 3) if dirn == 0 else (2, 1)
        totals = []
        for cols in cols_of:
            total = jnp.zeros((CH, LANE), F32)
            for j in range(steps):
                total = total + de_s[base + j * CH : base + (j + 1) * CH, cols]
            sum_o[4 * state + dirn : 4 * state + dirn + 1, cols] = jnp.sum(total, axis=0, keepdims=True)
            totals.append(total)

        def some(g, carry, order=order, base=base, up=up, dirn=dirn, s_row=s_row, m_row=m_row, totals=totals):
            n0 = g * group
            at_b, at_c = lanes_of(n0, group), lanes_of(state + n0, group)
            keys = [(n, t) for n in range(group) for t in range(tiles)]
            a2 = {(n, t): a2_s[n0 + n, :, cols_of[t]] for n, t in keys}
            h, m = {}, {}
            for at, j in enumerate(order):
                rows = slice(base + j * CH, base + (j + 1) * CH)
                de = [de_s[rows, c] for c in cols_of]
                dx = [dx_s[rows, c] for c in cols_of]
                for n in range(group):
                    b_n = bc_s[rows, at_b[n]]
                    for t, cols in enumerate(cols_of):
                        d = jnp.exp2(de[t] * a2[n, t])
                        decay_o[dirn, at, n0 + n, :, cols] = d
                        drive = dx[t] * b_n
                        drive_o[dirn, at, n0 + n, :, cols] = drive
                        h[n, t] = drive if at == 0 else d * h[n, t] + drive
            for at in range(steps - 1, -1, -1):
                rows = slice(base + order[at] * CH, base + (order[at] + 1) * CH)
                gyj = [gy[rows, c] for c in cols_of]
                for n in range(group):
                    c_n = bc_s[rows, at_c[n]]
                    for t, cols in enumerate(cols_of):
                        own = gyj[t] * c_n
                        d = decay_o[dirn, at, n0 + n, :, cols]
                        m[n, t] = d * (own if at == steps - 1 else own + m[n, t])
            for t in range(tiles):
                w_s, w_m = chunk_weights(totals[t], up), chunk_weights(totals[t], not up)
                for n in range(group):
                    enter, leave = chunk_scan(h[n, t], w_s, a2[n, t], up)
                    sx_o[dirn, n0 + n, :, cols_of[t]] = enter
                    leave_s[s_row * state + n0 + n, :, cols_of[t]] = jnp.broadcast_to(leave, (CH, LANE))
                    enter, leave = chunk_scan(m[n, t], w_m, a2[n, t], not up)
                    mx_o[dirn, n0 + n, :, cols_of[t]] = enter
                    leave_s[m_row * state + n0 + n, :, cols_of[t]] = jnp.broadcast_to(leave, (CH, LANE))
            return carry

        lax.fori_loop(0, state // group, some, 0)
    for row in range(0, 4 * state, CH):
        for cols in cols_of:
            sum_o[row : row + CH, cols] = jnp.concatenate([leave_s[row + i, 0:1, cols] for i in range(CH)], axis=0)
    sum_o[4 * state + 2 :, :] = jnp.zeros((sum_o.shape[0] - 4 * state - 2, inner), F32)


def lanes_of(first, count):
    return [pl.ds(pl.multiple_of((first + n) * LANE, LANE), LANE) for n in range(count)]


def prepare(sib, oth, keep, gain, wih, wil, conv_w, conv_b, w_x, w_dt, dt_bias, spread_s, a2, xb, gy):
    rows, inner = xb.shape
    state, width = a2.shape[0], w_x.shape[0]
    big = pltpu.VMEM((rows, inner), F32)
    edge = pltpu.VMEM((2, state, CH, inner), F32)
    return pl.pallas_call(
        prepare_kernel,
        out_shape=(
            big, big, big, big,
            pltpu.VMEM((3 * rows, LANE), F32),
            pltpu.VMEM((rows, width), F32),
            pltpu.VMEM((2 * CH, inner), F32),
            edge, edge,
            pltpu.VMEM((4 * state + 8, inner), F32),
            big, big,
            pltpu.VMEM((rows, 2 * state * LANE), F32),
            pltpu.VMEM((2, rows // 2 // CH, state, CH, inner), F32),
            pltpu.VMEM((2, rows // 2 // CH, state, CH, inner), F32),
        ),
        scratch_shapes=[pltpu.VMEM((4 * state, CH, inner), F32)],
        compiler_params=params(8),
        name="prepare",
    )(sib, oth, keep, gain, wih, wil, conv_w, conv_b, w_x, w_dt, dt_bias, spread_s, a2, xb, gy)


def summary_parts(ref_value, state):
    return [ref_value[i * state : (i + 1) * state] for i in range(4)]


def pair_kernel(a2_s, mine, theirs, out):
    state, half = a2_s.shape[0], out.shape[1]
    core = lax.axis_index("seq") & 1
    cols = pl.ds(pl.multiple_of(core * half, half), half)
    a2 = half_a2(a2_s, half)
    me, it = mine[:, cols], theirs[:, cols]
    low, high = jnp.where(core == 1, it, me), jnp.where(core == 1, me, it)
    put_total(out, joined(low, high, a2, state), state)


def joined(low, high, a2, state):
    low_f, low_r = low[4 * state : 4 * state + 1], low[4 * state + 1 : 4 * state + 2]
    high_f, high_r = high[4 * state : 4 * state + 1], high[4 * state + 1 : 4 * state + 2]
    lows, highs = summary_parts(low, state), summary_parts(high, state)
    return [
        lows[0] * jnp.exp2(high_f * a2) + highs[0],
        lows[1] * jnp.exp2(high_r * a2) + highs[1],
        highs[2] * jnp.exp2(low_r * a2) + lows[2],
        highs[3] * jnp.exp2(low_f * a2) + lows[3],
        low_f + high_f,
        low_r + high_r,
    ]


def put_total(out, parts, state):
    for i in range(4):
        out[i * state : (i + 1) * state] = parts[i]
    rest = jnp.zeros((out.shape[0] - 4 * state - 2, out.shape[1]), F32)
    out[4 * state :] = jnp.concatenate([parts[4], parts[5], rest], axis=0)


def half_a2(a2_s, half):
    core = lax.axis_index("seq") & 1
    cols = pl.ds(pl.multiple_of(core * half, half), half)
    return jnp.concatenate([a2_s[n, 0:1, cols] for n in range(a2_s.shape[0])], axis=0)


def stage_kernel(first, halves, a2_s, *refs):
    outs = 1 + len(halves) if halves else 2
    members, out, held = refs[: -outs - 1], refs[-outs - 1 : -1], refs[-1]
    count = len(members)
    state, half = a2_s.shape[0], out[0].shape[1]
    a2 = half_a2(a2_s, half)
    at = (lax.axis_index("seq") >> first) & (count - 1)
    for i, ref in enumerate(members):
        held[at ^ i] = ref[...]
    zero, none = jnp.zeros((state, half), F32), jnp.zeros((1, half), F32)

    def run_through(order, rows, reach):
        run = [zero, zero, none, none]
        seen = list(run)
        for i in order:
            seen = [jnp.where(at == i, now, old) for now, old in zip(run, seen)]
            df, dr = held[i, 4 * state : 4 * state + 1], held[i, 4 * state + 1 : 4 * state + 2]
            decays = [jnp.exp2((df, dr)[w] * a2) for w in reach]
            run = [run[k] * decays[k] + held[i, rows[k] * state : (rows[k] + 1) * state] for k in range(2)] + [
                run[2] + df,
                run[3] + dr,
            ]
        return run, seen

    right, seen = run_through(range(count), (0, 1), (0, 1))
    left, seen_left = run_through(range(count - 1, -1, -1), (2, 3), (1, 0))
    enter = out[0]
    enter[:state], enter[state : 2 * state] = seen[0], seen[1]
    enter[2 * state : 3 * state], enter[3 * state : 4 * state] = seen_left[0], seen_left[1]
    blank = jnp.zeros((CH, half), F32)
    enter[4 * state :] = jnp.concatenate([seen[2], seen[3], seen_left[2], seen_left[3], blank[:4]], axis=0)
    sums = jnp.concatenate([right[2], right[3], blank[:6]], axis=0)
    if halves:
        me = lax.axis_index("seq")
        for ref, apart in zip(out[1:], halves):
            later = (me ^ apart) > me
            ref[:state] = jnp.where(later, right[0], left[0])
            ref[state : 2 * state] = jnp.where(later, right[1], left[1])
            ref[2 * state :] = sums
    else:
        for i, value in enumerate((right[0], right[1], left[0], left[1])):
            out[1][i * state : (i + 1) * state] = value
        out[1][4 * state :] = sums


def last_kernel(first, a2_s, *refs):
    theirs, out, held = refs[:-2], refs[-2], refs[-1]
    count = len(theirs) + 1
    state, half = a2_s.shape[0], out.shape[1]
    a2 = half_a2(a2_s, half)
    at = (lax.axis_index("seq") >> first) & (count - 1)
    held[at] = jnp.zeros(held.shape[1:], F32)
    for i, ref in enumerate(theirs):
        held[at ^ (i + 1)] = ref[...]

    def run_through(order, reach, inside):
        run = [jnp.zeros((state, half), F32)] * 2
        for i in order:
            sums = held[i, 2 * state : 2 * state + 1], held[i, 2 * state + 1 : 2 * state + 2]
            for k in range(2):
                longer = run[k] * jnp.exp2(sums[reach[k]] * a2) + held[i, k * state : (k + 1) * state]
                run[k] = jnp.where(inside(i), longer, run[k])
        return run

    found = run_through(range(count - 1), (0, 1), lambda i: i < at)
    found = found + run_through(range(count - 1, 0, -1), (1, 0), lambda i: i > at)
    for i in range(4):
        out[i * state : (i + 1) * state] = found[i]


def pair(a2_s, mine, theirs):
    rows, inner = mine.shape
    return pl.pallas_call(
        pair_kernel,
        out_shape=jax.ShapeDtypeStruct((rows, inner // 2), F32),
        compiler_params=params(2),
        name="pair",
    )(a2_s, mine, theirs)


def stage(first, halves, a2_s, members):
    shape = jax.ShapeDtypeStruct(members[0].shape, F32)
    part = jax.ShapeDtypeStruct((2 * a2_s.shape[0] + CH, members[0].shape[1]), F32)
    return pl.pallas_call(
        lambda *refs: stage_kernel(first, halves, *refs),
        out_shape=(shape,) + (part,) * len(halves) if halves else (shape, shape),
        scratch_shapes=[pltpu.VMEM((len(members),) + members[0].shape, F32)],
        compiler_params=params(4),
        name="stage",
    )(a2_s, *members)


def last_stage(first, a2_s, theirs):
    return pl.pallas_call(
        lambda *refs: last_kernel(first, *refs),
        out_shape=jax.ShapeDtypeStruct((4 * a2_s.shape[0], theirs[0].shape[1]), F32),
        scratch_shapes=[pltpu.VMEM((len(theirs) + 1,) + theirs[0].shape, F32)],
        compiler_params=params(4),
        name="stage",
    )(a2_s, *theirs)


def enter_kernel(a2_s, *refs):
    stages, out = refs[:-1], refs[-1]
    state, half = a2_s.shape[0], out.shape[1]
    a2 = half_a2(a2_s, half)
    value = [stages[-1][i * state : (i + 1) * state] for i in range(4)]
    for ref in reversed(stages[:-1]):
        reach = [ref[4 * state + i : 4 * state + i + 1] for i in range(4)]
        value = [
            ref[i * state : (i + 1) * state] + value[i] * jnp.exp2(reach[w] * a2)
            for i, w in ((0, 0), (1, 1), (2, 3), (3, 2))
        ]
    for i in range(4):
        out[i * state : (i + 1) * state] = value[i]


def enter(a2_s, stages):
    half = stages[0].shape[1]
    return pl.pallas_call(
        enter_kernel,
        out_shape=jax.ShapeDtypeStruct((4 * a2_s.shape[0], half), F32),
        compiler_params=params(2),
        name="enter",
    )(a2_s, *stages)


def carry_in(car_s, a2_s, mine_half, other_half, sibling):
    state, inner = a2_s.shape[0], a2_s.shape[2]
    half = inner // 2
    odd = (lax.axis_index("seq") & 1) == 1
    a2 = jnp.concatenate([a2_s[n, 0:1, :] for n in range(state)], axis=0)
    left, right = jnp.where(odd, other_half[...], mine_half[...]), jnp.where(odd, mine_half[...], other_half[...])
    into = jnp.concatenate([left, right], axis=1)
    df, dr = sibling[4 * state : 4 * state + 1], sibling[4 * state + 1 : 4 * state + 2]
    for i, reach, through in ((0, df, odd), (1, dr, odd), (2, dr, ~odd), (3, df, ~odd)):
        rows = slice(i * state, (i + 1) * state)
        value = jnp.where(through, into[rows] * jnp.exp2(reach * a2) + sibling[rows], into[rows])
        for n in range(state):
            car_s[i * state + n] = jnp.broadcast_to(value[n : n + 1], (CH, inner))


def forward_kernel(
    mine_half, other_half, sibling, sx, de_s, dx_s, bc_s, a2_s, decay, drive,
    y_s, h_s, car_o,
    before_s,
):
    rows2, inner = de_s.shape
    length = rows2 // 2
    steps = length // CH
    tiles = inner // LANE
    state = a2_s.shape[0]
    carry_in(car_o, a2_s, mine_half, other_half, sibling)
    y_s[...] = jnp.zeros(y_s.shape, F32)
    group = 8
    cols_of = [slice(t * LANE, (t + 1) * LANE) for t in range(tiles)]
    for dirn in range(2):
        order = list(range(steps)) if dirn == 0 else list(range(steps - 1, -1, -1))
        base = dirn * length
        s_row = 0 if dirn == 0 else 2
        for cols in cols_of:
            total = jnp.zeros((CH, LANE), F32)
            for j in range(steps):
                total = total + de_s[base + j * CH : base + (j + 1) * CH, cols]
            before_s[:, cols] = outside_sum(total, dirn == 0)

        def some(g, carry, dirn=dirn, order=order, base=base, s_row=s_row):
            n0 = g * group
            at_b, at_c = lanes_of(n0, group), lanes_of(state + n0, group)
            h = {}
            for n in range(group):
                for t, cols in enumerate(cols_of):
                    into = jnp.exp2(before_s[:, cols] * a2_s[n0 + n, :, cols]) * car_o[s_row * state + n0 + n, :, cols]
                    h[n, t] = sx[dirn, n0 + n, :, cols] + into
                    h_s[dirn, 0, n0 + n, :, cols] = h[n, t]
            for at, j in enumerate(order):
                rows = slice(base + j * CH, base + (j + 1) * CH)
                dx = [dx_s[rows, c] for c in cols_of]
                y = [None] * tiles
                for n in range(group):
                    c_n = bc_s[rows, at_c[n]]
                    for t, cols in enumerate(cols_of):
                        h[n, t] = decay[dirn, at, n0 + n, :, cols] * h[n, t] + drive[dirn, at, n0 + n, :, cols]
                        h_s[dirn, at + 1, n0 + n, :, cols] = h[n, t]
                        term = h[n, t] * c_n
                        y[t] = term if n == 0 else y[t] + term
                for t, cols in enumerate(cols_of):
                    y_s[rows, cols] += y[t]
            return carry

        lax.fori_loop(0, state // group, some, 0)


def forward(mine_half, other_half, sibling, sx, de, dx, bc, a2, decay, drive):
    rows2, inner = de.shape
    state = a2.shape[0]
    steps = rows2 // 2 // CH
    return pl.pallas_call(
        forward_kernel,
        out_shape=(
            jax.ShapeDtypeStruct((rows2, inner), F32),
            jax.ShapeDtypeStruct((2, steps + 1, state, CH, inner), F32),
            jax.ShapeDtypeStruct((4 * state, CH, inner), F32),
        ),
        scratch_shapes=[pltpu.VMEM((CH, inner), F32)],
        compiler_params=params(4),
        name="forward",
    )(mine_half, other_half, sibling, sx, de, dx, bc, a2, decay, drive)


def ready_kernel(
    rank, tok, gout, gain, wih, wil, w_out, d_skip, z, go, conv, pre, xc, gy,
    x_o, g_o, nth_o, ntl_o, gh_o, gl_o, wfh_o, wfl_o, woh_o, wol_o, vfh_o, vfl_o,
    gate_o, zgrad_o, cgrad_o, sig_o, xch_o, xcl_o, skip_o, pickb_o, pickc_o,
):
    feat, inner = gain.shape[1], w_out.shape[0]
    x = ordered(tok)
    x_o[...] = x
    g = ordered(gout)
    g_o[...] = g
    high, low = both_orders(normalize(x, gain[...])[1])
    nth_o[...] = high.astype(F32).T.astype(BF16)
    ntl_o[...] = low.astype(F32).T.astype(BF16)
    gh_o[...], gl_o[...] = both_orders(g)
    flip = flip_matrix(feat)
    wfh_o[...], wfl_o[...] = nn(flip, wih[...]).astype(BF16), nn(flip, wil[...]).astype(BF16)
    high, low = split(w_out[...])
    woh_o[...], wol_o[...] = high, low
    vfh_o[...], vfl_o[...] = nn(high, flip).astype(BF16), nn(low, flip).astype(BF16)
    xch_o[...], xcl_o[...] = split(xc[...])
    for lt in range(inner // LANE):
        cols = slice(lt * LANE, (lt + 1) * LANE)
        zt, v = z[:, cols], conv[:, cols]
        s = sigmoid(zt)
        gate_o[:, cols] = zt * s
        zgrad_o[:, cols] = go[:, cols] * (s * (1.0 + zt * (1.0 - s)))
        s = sigmoid(v)
        cgrad_o[:, cols] = s * (1.0 + v * (1.0 - s))
        sig_o[:, cols] = sigmoid(pre[:, cols])
        skip_o[:, cols] = jnp.sum(gy[:, cols] * xc[:, cols], axis=0, keepdims=True)
    row = lax.broadcasted_iota(jnp.int32, pickb_o.shape, 0) >> 6
    col = lax.broadcasted_iota(jnp.int32, pickb_o.shape, 1)
    pickb_o[...] = jnp.where(col == row + rank, 1.0, 0.0).astype(BF16)
    pickc_o[...] = jnp.where(col == row + (rank + pickb_o.shape[0] // (LANE // 2)), 1.0, 0.0).astype(BF16)


def ready(rank, state, tok, gout, gain, wih, wil, w_out, d_skip, z, go, conv, pre, xc, gy):
    length, feat = tok.shape
    rows2, inner = z.shape
    f32 = lambda *dims: jax.ShapeDtypeStruct(dims, F32)
    b16 = lambda *dims: jax.ShapeDtypeStruct(dims, BF16)
    both = lambda *dims: (b16(*dims), b16(*dims))
    return pl.pallas_call(
        lambda *refs: ready_kernel(rank, *refs),
        out_shape=(f32(length, feat), f32(length, feat))
        + both(feat, rows2) + both(rows2, feat) + both(feat, 2 * inner)
        + both(inner, feat) + both(inner, feat)
        + (f32(rows2, inner),) * 4
        + both(rows2, inner) + (f32(1, inner),) + both(state * LANE // 2, LANE),
        compiler_params=params(8),
        name="ready",
    )(tok, gout, gain, wih, wil, w_out, d_skip, z, go, conv, pre, xc, gy)


def early_kernel(
    rs_bits, nth, ntl, gh, gl, gate, zgrad, d_skip, xc, y_s, gzh_o, gzl_o, outh_o, outl_o, pieces_o,
):
    y = y_s[...] + d_skip[...] * xc[...]
    gz = split(zgrad[...] * y)
    gzh_o[...], gzl_o[...] = gz
    out = split(y * gate[...])
    gw_out = mm(tn, out, (gh[...], gl[...]))
    gw_in = mm(nn, (nth[...], ntl[...]), gz)
    outh_o[...], outl_o[...] = out
    put_pieces(rs_bits, pieces_o, [(gw_in, None), (gw_out, None)])


def early(rs_bits, nth, ntl, gh, gl, gate, zgrad, d_skip, xc, y):
    feat = nth.shape[0]
    rows2, inner = xc.shape
    pieces = 1 << rs_bits
    tall = 2 * feat * inner // LANE // pieces
    gz = jax.ShapeDtypeStruct((rows2, inner), BF16)
    return pl.pallas_call(
        lambda *refs: early_kernel(rs_bits, *refs),
        out_shape=(gz, gz, gz, gz, jax.ShapeDtypeStruct((pieces, tall, LANE), F32)),
        compiler_params=params(8),
        name="early",
    )(nth, ntl, gh, gl, gate, zgrad, d_skip, xc, y)


def put_pieces(rs_bits, pieces_o, arrays, few=None):
    pieces = 1 << rs_bits
    mine = reverse_bits(lax.axis_index("seq"), rs_bits)
    for p in range(pieces):
        slot = mine ^ reverse_bits(p, rs_bits)
        at = 0
        for value, more in arrays:
            tall = value.shape[0] // pieces
            for lt in range(value.shape[1] // LANE):
                where = (slice(p * tall, (p + 1) * tall), slice(lt * LANE, (lt + 1) * LANE))
                block = value[where] if more is None else value[where] + more[where]
                pieces_o[slot, at : at + tall, :] = block
                at += tall
        if few is not None:
            tiles = few.shape[1] // LANE
            top = pieces // tiles * CH
            rest = (few.shape[0] - top) * tiles // pieces
            rb, lt = p // tiles, p % tiles
            pieces_o[slot, at : at + CH, :] = few[rb * CH : (rb + 1) * CH, lt * LANE : (lt + 1) * LANE]
            rows = []
            for v in range(rest * p, rest * (p + 1)):
                rb, lt = top + v // tiles, v % tiles
                rows.append(few[rb : rb + 1, lt * LANE : (lt + 1) * LANE])
            zeros = jnp.zeros((4, LANE), F32)
            rows = [zeros] + rows + [zeros[: 4 - rest]]
            pieces_o[slot, at + CH : at + 2 * CH, :] = jnp.concatenate(rows, axis=0)
            pieces_o[slot, at + 2 * CH : at + 3 * CH, :] = jnp.zeros((CH, LANE), F32)


def row_vectors(rows):
    return jnp.concatenate(
        [rows[b : b + 1, lt * LANE : (lt + 1) * LANE] for b in range(3) for lt in range(rows.shape[1] // LANE)],
        axis=0,
    )


def backward_kernel(
    dirn, mx, car, h_s, de_s, dx_s, bc_s, a2_s, decay, gy,
    sb_s, sa_s, accb, accc, ga_s,
    after_s,
):
    rows2, inner = de_s.shape
    length = rows2 // 2
    steps = length // CH
    tiles = inner // LANE
    state = a2_s.shape[0]
    order = list(range(steps)) if dirn == 0 else list(range(steps - 1, -1, -1))
    base = dirn * length
    m_row = 3 if dirn == 0 else 1
    group = 8
    low = lax.broadcasted_iota(jnp.int32, (CH, LANE), 1) < LANE // 2
    cols_of = [slice(t * LANE, (t + 1) * LANE) for t in range(tiles)]
    sb_s[...] = jnp.zeros(sb_s.shape, F32)
    sa_s[...] = jnp.zeros(sa_s.shape, F32)
    for cols in cols_of:
        total = jnp.zeros((CH, LANE), F32)
        for j in range(steps):
            total = total + de_s[base + j * CH : base + (j + 1) * CH, cols]
        after_s[:, cols] = outside_sum(total, dirn != 0)

    def some(g, carry):
        n0 = g * group
        at_b, at_c = lanes_of(n0, group), lanes_of(state + n0, group)
        a2, q, ga, now = {}, {}, {}, {}
        for n in range(group):
            for t, cols in enumerate(cols_of):
                a2[n, t] = a2_s[n0 + n, :, cols]
                into = jnp.exp2(after_s[:, cols] * a2[n, t]) * car[m_row * state + n0 + n, :, cols]
                q[n, t] = mx[dirn, n0 + n, :, cols] + into
                ga[n, t] = jnp.zeros((CH, LANE), F32)
                now[n, t] = h_s[dirn, steps, n0 + n, :, cols]
        for time in range(steps - 1, -1, -1):
            j = order[time]
            rows = slice(base + j * CH, base + (j + 1) * CH)
            here = slice(j * CH, (j + 1) * CH)
            de = [de_s[rows, c] for c in cols_of]
            dx = [dx_s[rows, c] for c in cols_of]
            gyj = [gy[rows, c] for c in cols_of]
            sb, sa = [None] * tiles, [None] * tiles
            sums = []
            for n in range(group):
                b_n, c_n = bc_s[rows, at_b[n]], bc_s[rows, at_c[n]]
                to_b = to_c = None
                for t, cols in enumerate(cols_of):
                    gh = gyj[t] * c_n + q[n, t]
                    term_c = gyj[t] * now[n, t]
                    term_b = gh * dx[t]
                    to_b = term_b if t == 0 else to_b + term_b
                    to_c = term_c if t == 0 else to_c + term_c
                    q[n, t] = decay[dirn, time, n0 + n, :, cols] * gh
                    now[n, t] = h_s[dirn, time, n0 + n, :, cols]
                    r = q[n, t] * now[n, t]
                    ga[n, t] = ga[n, t] + de[t] * r
                    sb[t] = gh * b_n if n == 0 else sb[t] + gh * b_n
                    sa[t] = a2[n, t] * r if n == 0 else sa[t] + a2[n, t] * r
                sums.append((to_b, to_c))
            for i, at in enumerate(lanes_of(g * (group // 2), group // 2)):
                for acc, one, two in zip((accb, accc), sums[2 * i], sums[2 * i + 1]):
                    acc[here, at] = jnp.where(low, one, two) + pltpu.roll(jnp.where(low, two, one), LANE // 2, 1)
            for t, cols in enumerate(cols_of):
                sb_s[here, cols] += sb[t]
                sa_s[here, cols] += sa[t]
        for n in range(group):
            for t, cols in enumerate(cols_of):
                ga_s[n0 + n, :, cols] = ga[n, t]
        return carry

    lax.fori_loop(0, state // group, some, 0)


def backward(dirn, mx, car, h, de, dx, bc, a2, decay, gy):
    rows2, inner = de.shape
    state = a2.shape[0]
    length = rows2 // 2
    half = jax.ShapeDtypeStruct((length, inner), F32)
    acc = jax.ShapeDtypeStruct((length, state * LANE // 2), F32)
    return pl.pallas_call(
        lambda *refs: backward_kernel(dirn, *refs),
        out_shape=(half, half, acc, acc, jax.ShapeDtypeStruct((state, CH, inner), F32)),
        scratch_shapes=[pltpu.VMEM((CH, inner), F32)],
        compiler_params=params(4),
        name="backward",
    )(mx, car, h, de, dx, bc, a2, decay, gy)


def inner_kernel(
    pad, conv_w, w_x, w_dt, d_skip, a2_s,
    xb, gy, xc, dt, sig, cgrad, mask, dbl, xbh, xch, xcl, skip_sum, pick_b, pick_c,
    sb_f, sa_f, accb_f, accc_f, ga_f, sb_r, sa_r, accb_r, accc_r, ga_r,
    gxh_o, gxl_o, halo_o, few_o,
    gp_s, gpre_s, xcg_s,
):
    inner, rank = w_x.shape[1], w_dt.shape[0]
    state = a2_s.shape[0]
    rows2 = xb.shape[0]
    length = rows2 // 2
    steps = length // CH
    tiles = inner // LANE
    sub = sub_iota()

    bias_rows = []
    for lt in range(tiles):
        cols = slice(lt * LANE, (lt + 1) * LANE)
        bias = jnp.zeros((1, LANE), F32)
        for dirn, sb, sa in ((0, sb_f, sa_f), (1, sb_r, sa_r)):
            rows = slice(dirn * length, (dirn + 1) * length)
            g_pre = (xc[rows, cols] * sb[:, cols] + LN2 * sa[:, cols]) * sig[rows, cols]
            gpre_s[rows, cols] = g_pre
            xcg_s[rows, cols] = d_skip[:, cols] * gy[rows, cols] + dt[rows, cols] * sb[:, cols]
            bias = bias + jnp.sum(g_pre, axis=0, keepdims=True)
        bias_rows.append(bias)

    b_parts = split(jnp.concatenate([accb_f[...], accb_r[...]], axis=0))
    c_parts = split(jnp.concatenate([accc_f[...], accc_r[...]], axis=0))
    g_bc = (nn(b_parts[0], pick_b[...]) + nn(b_parts[1], pick_b[...])) + (
        nn(c_parts[0], pick_c[...]) + nn(c_parts[1], pick_c[...])
    )
    gpre_parts = split(gpre_s[...])
    w_dt_parts = split(w_dt[...])
    g_rank = mm(nt, gpre_parts, w_dt_parts)
    width = rank + 2 * state
    g_dbl = jnp.concatenate([g_rank, g_bc[:, rank:width]], axis=1)
    g_dbl_parts = split(g_dbl)
    few_o[width + state : width + state + rank, :] = mm(tn, split(dbl[:, :rank]), gpre_parts)
    few_o[:width, :] = mm(tn, g_dbl_parts, (xch[...], xcl[...]))
    xcg_s[...] += mm(nn, g_dbl_parts, split(w_x[...]))

    cw_rows = [[] for _ in range(4)]
    cb_rows = []
    halo_f, halo_r = [], []
    for lt in range(tiles):
        cols = slice(lt * LANE, (lt + 1) * LANE)
        taps = [conv_w[k : k + 1, cols] for k in range(4)]
        xbh_t = xbh[:, cols]
        xf = [xb[j * CH : (j + 1) * CH, cols] for j in range(steps)]
        xf = [
            jnp.where(sub == 0, xbh_t[b : b + 1], pltpu.roll(xf[steps - 3 + b], 1, 0))
            for b in range(3)
        ] + xf
        gcw = [jnp.zeros((CH, LANE), F32) for _ in range(4)]
        gcb = jnp.zeros((CH, LANE), F32)
        grads = [None] * (steps + 3)
        for j in range(steps):
            rows = slice(j * CH, (j + 1) * CH)
            u = xcg_s[rows, cols] * cgrad[rows, cols]
            gcb = gcb + u
            for k in range(4):
                uk = u if k == 0 else u * mask[(k - 1) * length + j * CH : (k - 1) * length + (j + 1) * CH, :]
                gcw[k] = gcw[k] + uk * xf[j + 3 - k]
                add = taps[k] * uk
                at = j + 3 - k
                grads[at] = add if grads[at] is None else grads[at] + add
        for b in range(3):
            halo_f.append(grads[b][0:1])
            at = steps + b
            grads[at] = grads[at] + jnp.where(sub == CH - 1, 0.0, pltpu.roll(grads[b], CH - 1, 0))
        for j in range(steps):
            gp_s[j * CH : (j + 1) * CH, cols] = grads[j + 3]
        xr = [xb[length + j * CH : length + (j + 1) * CH, cols] for j in range(steps)]
        xr = xr + [
            jnp.where(sub == CH - 1, xbh_t[8 + b : 9 + b], pltpu.roll(xr[b], CH - 1, 0))
            for b in range(3)
        ]
        grads = [None] * (steps + 3)
        for j in range(steps):
            rows = slice(length + j * CH, length + (j + 1) * CH)
            u = xcg_s[rows, cols] * cgrad[rows, cols]
            gcb = gcb + u
            for k in range(4):
                uk = u if k == 0 else u * mask[(k + 2) * length + j * CH : (k + 2) * length + (j + 1) * CH, :]
                gcw[k] = gcw[k] + uk * xr[j + k]
                add = taps[k] * uk
                grads[j + k] = add if grads[j + k] is None else grads[j + k] + add
        for b in range(3):
            halo_r.append(grads[steps + b][CH - 1 : CH])
            grads[b] = grads[b] + jnp.where(sub == 0, 0.0, pltpu.roll(grads[steps + b], 1, 0))
        for j in range(steps):
            gp_s[length + j * CH : length + (j + 1) * CH, cols] = grads[j]
        for k in range(4):
            cw_rows[k].append(jnp.sum(gcw[k], axis=0, keepdims=True))
        cb_rows.append(jnp.sum(gcb, axis=0, keepdims=True))
    pad_col = spread(pad[...].astype(F32))
    pad_all = jnp.concatenate([pad_col, pad_col], axis=0)
    for lt in range(tiles):
        cols = slice(lt * LANE, (lt + 1) * LANE)
        gxh_o[:, cols], gxl_o[:, cols] = split(gp_s[:, cols] * pad_all)

    blank = jnp.zeros((5, inner), F32)

    def gather(found):
        return jnp.concatenate(
            [jnp.concatenate([found[lt * 3 + b] for lt in range(tiles)], axis=1) for b in range(3)]
            + [blank],
            axis=0,
        )

    halo_o[...] = jnp.concatenate([gather(halo_f), gather(halo_r)], axis=0)
    ga = jnp.concatenate(
        [jnp.sum(ga_f[n] + ga_r[n], axis=0, keepdims=True) * (a2_s[n, 0:1, :] * LN2) for n in range(state)], axis=0
    )
    few_o[width : width + state, :] = ga
    few_o[width + state + rank :, :] = jnp.concatenate(
        [jnp.concatenate(cw_rows[k], axis=1) for k in range(4)]
        + [
            jnp.concatenate(cb_rows, axis=1),
            jnp.concatenate(bias_rows, axis=1),
            skip_sum[...],
            jnp.zeros((1, inner), F32),
        ],
        axis=0,
    )


def inner_back(*arrays):
    w_x, w_dt, a2, xb = arrays[2], arrays[3], arrays[5], arrays[6]
    rows2, inner = xb.shape
    few = w_x.shape[0] + a2.shape[0] + w_dt.shape[0] + CH
    big = pltpu.VMEM((rows2, inner), F32)
    part = jax.ShapeDtypeStruct((rows2, inner), BF16)
    return pl.pallas_call(
        inner_kernel,
        out_shape=(
            part, part,
            jax.ShapeDtypeStruct((2 * CH, inner), F32),
            jax.ShapeDtypeStruct((few, inner), F32),
        ),
        scratch_shapes=[big, big, big],
        compiler_params=params(8),
        name="inner",
    )(*arrays)


def tail_kernel(
    rs_bits, sib, oth, gain, x_s, nth, ntl, wih, wil, wfh, wfl, gzh, gzl, gxh, gxl, halo, few,
    normed_o, pieces_o, *edges_o,
):
    feat = gain.shape[1]
    rows2, inner = gxh.shape
    length = rows2 // 2
    left, right = pick_sides(sib[...], oth[...])
    factor_l, hn_l = normalize(left, gain[...])
    factor_r, hn_r = normalize(right, gain[...])
    flip = flip_matrix(feat)
    lh, ll = split(hn_l)
    rh, rl = split(hn_r)
    edge = (
        jnp.concatenate([lh, nn(rh, flip).astype(BF16)], axis=0),
        jnp.concatenate([ll, nn(rl, flip).astype(BF16)], axis=0),
    )
    x = x_s[...]
    factor = normalize(x, gain[...])[0]
    gh_parts = split(halo[...])
    gw_in = mm(nn, (nth[...], ntl[...]), (gxh[...], gxl[...]))
    gw_in_halo = mm(tn, edge, gh_parts)
    w_xb = (wih[:, :inner], wil[:, :inner])
    g_normed = (
        mm(nt, (gxh[:length], gxl[:length]), w_xb)
        + mm(nt, (gzh[:length], gzl[:length]), (wih[:, inner:], wil[:, inner:]))
    ) + (
        mm(nt, (gxh[length:], gxl[length:]), (wfh[:, :inner], wfl[:, :inner]))
        + mm(nt, (gzh[length:], gzl[length:]), (wfh[:, inner:], wfl[:, inner:]))
    )
    back_h = mm(nt, gh_parts, w_xb)
    gn_l = back_h[:CH]
    gn_r = flipped(back_h[CH:])

    normed_o[...] = g_normed
    to_left = norm_back(left, factor_l, gn_l, gain[...])
    to_right = norm_back(right, factor_r, gn_r, gain[...])
    for ref, value in zip(edges_o, (to_left, to_right)):
        ref[...] = value
    three = lax.broadcasted_iota(jnp.int32, (CH, feat), 0) < 3
    g_gain = (
        jnp.sum(g_normed * (x * factor), axis=0, keepdims=True)
        + jnp.sum(jnp.where(three, gn_l * (left * factor_l) + gn_r * (right * factor_r), 0.0), axis=0, keepdims=True)
    )
    few_all = jnp.concatenate(
        [few[: few.shape[0] - CH, :], few[few.shape[0] - CH : few.shape[0] - 1, :]]
        + [jnp.concatenate([g_gain, jnp.zeros((1, inner - feat), F32)], axis=1)],
        axis=0,
    )
    put_pieces(rs_bits, pieces_o, [(gw_in, gw_in_halo)], few_all)
    pieces = 1 << rs_bits
    me = lax.axis_index("seq") & (pieces - 1)
    mine = reverse_bits(me, rs_bits)
    at = pieces_o.shape[1] - 2 * CH

    @pl.when(me < pieces - 1)
    def _():
        slot = mine ^ reverse_bits(me + 1, rs_bits)
        vectors = row_vectors(to_right)
        pieces_o[slot, at : at + 4, :] = vectors[:4]
        pieces_o[slot, at + CH : at + CH + 2, :] = vectors[4:]

    @pl.when(me > 0)
    def _():
        slot = mine ^ reverse_bits(me - 1, rs_bits)
        pieces_o[slot, at + CH + 2 : at + 2 * CH, :] = row_vectors(to_left)


def reverse_bits(value, bits):
    found = 0
    for i in range(bits):
        found = found | (((value >> i) & 1) << (bits - 1 - i))
    return found


def norm_back(x, factor, gn, gain):
    scaled = gn * gain
    return factor * scaled - x * (factor * factor * factor * jnp.mean(scaled * x, axis=1, keepdims=True))


def finish_kernel(x_s, g, gain, g_normed, outh, outl, woh, wol, vfh, vfl, mixed_o, gtok_o):
    length = x_s.shape[0]
    x = x_s[...]
    fwd = mm(nn, (outh[:length], outl[:length]), (woh[...], wol[...]))
    rev = mm(nn, (outh[length:], outl[length:]), (vfh[...], vfl[...]))
    store_ordered(mixed_o, x + (fwd + rev))
    factor = normalize(x, gain[...])[0]
    store_ordered(gtok_o, g[...] + norm_back(x, factor, g_normed[...], gain[...]))


def finish(*arrays):
    shape = jax.ShapeDtypeStruct(arrays[0].shape, F32)
    return pl.pallas_call(
        finish_kernel,
        out_shape=(shape, shape),
        compiler_params=params(6),
        name="finish",
    )(*arrays)


def tail(rs_bits, alone, *arrays):
    x, gxh = arrays[3], arrays[12]
    length, feat = x.shape
    inner = gxh.shape[1]
    pieces = 1 << rs_bits
    tall = feat * inner // LANE // pieces + 3 * CH
    return pl.pallas_call(
        lambda *refs: tail_kernel(rs_bits, *refs),
        out_shape=(
            jax.ShapeDtypeStruct((length, feat), F32),
            jax.ShapeDtypeStruct((pieces, tall, LANE), F32),
        )
        + (jax.ShapeDtypeStruct((CH, feat), F32),) * (2 if alone else 0),
        compiler_params=params(8),
        name="tail",
    )(*arrays)


def unpack_kernel(rs_bits, parts, *refs):
    sources, refs = refs[:parts], refs[parts:]
    (gain_o, w_in_o, conv_w_o, conv_b_o, w_x_o, w_dt_o, dt_bias_o, a_log_o, d_skip_o, w_out_o,
     few_s, rest_s) = refs
    feat = w_in_o.shape[0]
    inner = w_out_o.shape[0]
    tiles = inner // LANE
    pieces = 1 << rs_bits
    mine = reverse_bits(lax.axis_index("seq"), rs_bits)
    in_rows, out_rows = feat // pieces, inner // pieces
    for slot in range(pieces):
        source = sources[slot * parts // pieces]
        i = slot % (pieces // parts)
        p = reverse_bits(mine ^ slot, rs_bits)
        at = 0
        in_at = pl.ds(pl.multiple_of(p * in_rows, in_rows), in_rows)
        out_at = pl.ds(pl.multiple_of(p * out_rows, out_rows), out_rows)
        for lt in range(tiles):
            w_in_o[in_at, inner + lt * LANE : inner + (lt + 1) * LANE] = source[i, at : at + in_rows, :]
            at += in_rows
        for lt in range(feat // LANE):
            w_out_o[out_at, lt * LANE : (lt + 1) * LANE] = source[i, at : at + out_rows, :]
            at += out_rows
        for lt in range(tiles):
            w_in_o[in_at, lt * LANE : (lt + 1) * LANE] = source[i, at : at + in_rows, :]
            at += in_rows
        few_s[p] = source[i, at : at + CH, :]
        rest_s[p] = source[i, at + CH : at + 2 * CH, :]

    top = pieces // tiles * CH
    total = w_x_o.shape[0] + a_log_o.shape[0] + w_dt_o.shape[0] + CH
    rest = (total - top) * tiles // pieces

    def few_rows(first, count):
        found = []
        for lt in range(tiles):
            if first < top:
                found.append(few_s[first // CH * tiles + lt])
                continue
            rows = []
            for row in range(first, first + count):
                v = (row - top) * tiles + lt
                rows.append(rest_s[v // rest, 4 + v % rest : 5 + v % rest, :])
            found.append(jnp.concatenate(rows, axis=0) if count > 1 else rows[0])
        return jnp.concatenate(found, axis=1)

    width, state = w_x_o.shape[0], a_log_o.shape[0]
    rank = w_dt_o.shape[0]
    w_x_o[...] = jnp.concatenate([few_rows(r, CH) for r in range(0, width, CH)], axis=0)
    at = width
    a_log_o[...] = jnp.concatenate([few_rows(r, CH) for r in range(at, at + state, CH)], axis=0)
    at += state
    w_dt_o[...] = jnp.concatenate([few_rows(r, CH) for r in range(at, at + rank, CH)], axis=0)
    at += rank
    conv_w_o[...] = few_rows(at, 4)
    conv_b_o[...] = few_rows(at + 4, 1)
    dt_bias_o[...] = few_rows(at + 5, 1)
    d_skip_o[...] = few_rows(at + 6, 1)
    gain_o[...] = few_rows(at + 7, 1)[:, :feat]


def close_kernel(gtok, halo, pad, gtok_o):
    feat = gtok.shape[1]
    length = gtok.shape[0]
    per = feat // LANE
    padded = spread_plain(pad[...].astype(F32), feat)

    def three(first):
        rows = [
            jnp.concatenate([halo[first + b * per + lt : first + b * per + lt + 1, :] for lt in range(per)], axis=1)
            for b in range(3)
        ]
        return rows, jnp.zeros((CH - 3, feat), F32)

    rows, blank = three(0)
    first = jnp.concatenate(rows + [blank], axis=0)
    rows, blank = three(3 * per)
    last = jnp.concatenate([blank] + rows, axis=0)
    gtok_o[...] = gtok[...]
    gtok_o[:CH] = gtok[:CH] + padded[:CH] * first
    gtok_o[length - CH :] = gtok[length - CH :] + padded[length - CH :] * last


def close(*arrays):
    return pl.pallas_call(
        close_kernel,
        out_shape=jax.ShapeDtypeStruct(arrays[0].shape, F32),
        compiler_params=params(4),
        name="close",
    )(*arrays)


def spread_plain(row, width):
    length = row.shape[1]
    rows = lax.broadcasted_iota(jnp.int32, (length, length), 0)
    cols = lax.broadcasted_iota(jnp.int32, (length, length), 1)
    picked = (jnp.where(rows == cols, 1.0, 0.0) * row).astype(BF16)
    return nn(picked, jnp.ones((length, width), BF16))


def unpack(rs_bits, parts, feat, state, rank):
    pieces = 1 << rs_bits
    inner = state[1]
    width = rank + 2 * state[0]
    shape = lambda *dims: jax.ShapeDtypeStruct(dims, F32)
    return pl.pallas_call(
        lambda *refs: unpack_kernel(rs_bits, len(parts), *refs),
        out_shape=(
            shape(1, feat),
            shape(feat, 2 * inner),
            shape(4, inner),
            shape(1, inner),
            shape(width, inner),
            shape(rank, inner),
            shape(1, inner),
            shape(state[0], inner),
            shape(1, inner),
            shape(inner, feat),
        ),
        scratch_shapes=[pltpu.VMEM((pieces, CH, LANE), F32)] * 2,
        compiler_params=params(6),
        name="unpack",
    )(*parts)


def body(tokens, resets, pad_mask, norm_gain, w_in, conv_w, conv_b, w_x, w_dt, dt_bias, a_log, d_skip, w_out, grad_out):
    count = lax.axis_size("seq")
    bits = count.bit_length() - 1
    rs_bits = min(5, bits)
    length = tokens.shape[0]
    keep_row, pad_row = resets.reshape(1, length), pad_mask.reshape(1, length)

    def exchange(value, apart):
        return lax.ppermute(value, "seq", [(i, i ^ apart) for i in range(count)])

    def swap(value, bit):
        return exchange(value, 1 << bit)

    across = [(i, i + 1) for i in range(1, count - 1, 2)] + [(i + 1, i) for i in range(1, count - 1, 2)]

    def swap_across(value):
        return lax.ppermute(value, "seq", across)

    to_sib, to_oth, kept = edges(
        tokens, keep_row, pad_row, norm_gain, w_in[0], grad_out, w_out[0],
        conv_w[0], conv_b, w_x[0].T, w_dt[0], dt_bias, a_log[0].T, d_skip,
    )
    (tok, keep, pad, gain, w_in_0, gout, w_out_0, conv_w_0, conv_b_0, w_x_t, w_dt_0, dt_bias_0, a_log_t, skip) = kept
    oth = swap_across(to_oth)
    sib = swap(to_sib, 0)
    xb, z, go, gy, wih, wil, spread_s, a2 = project(tok, pad, gain, w_in_0, gout, w_out_0, a_log_t)
    xc, dt, pre, conv, mask, dbl, xbh, sx, mx, total, de, dx, bc, decay, drive = prepare(
        sib, oth, keep, gain, wih, wil, conv_w_0, conv_b_0, w_x_t, w_dt_0, dt_bias_0, spread_s, a2, xb, gy
    )

    sibling = swap(total, 0)
    group = pair(a2, total, sibling)
    group, gate_in = lax.optimization_barrier((group, (z, go, conv, pre, xc, gy)))
    at_hand = ready(w_dt.shape[1], a_log.shape[2], tok, gout, gain, wih, wil, w_out_0, skip, *gate_in)
    stages = []
    steps = [range(first, min(first + 2, bits)) for first in range(1, bits, 2)]
    step = steps[-1]
    distances = [i << step[0] for i in range(1, 1 << len(step))]
    for first_step in steps[:-1]:
        members = [group] + [exchange(group, i << first_step[0]) for i in range(1, 1 << len(first_step))]
        halves = distances if first_step is steps[-2] else ()
        entering, *group = stage(first_step[0], halves, a2, members)
        stages.append(entering)
        if not halves:
            (group,) = group
    group, at_hand = lax.optimization_barrier((group, at_hand))
    theirs = [exchange(value, apart) for value, apart in zip(group, distances)]
    stages.append(last_stage(step[0], a2, theirs))
    mine_half = enter(a2, stages)
    other_half = swap(mine_half, 0)

    y, h, car = forward(mine_half, other_half, sibling, sx, de, dx, bc, a2, decay, drive)
    def reduced(part, step):
        size = part.shape[0] >> len(step)
        total = part[:size]
        for i in ((2, 3, 1) if len(step) == 2 else (1,)):
            slot = reverse_bits(i, len(step))
            total = total + exchange(part[slot * size : (slot + 1) * size], i << step[0])
        return total

    (x, g, nth, ntl, gh, gl, wfh, wfl, woh, wol, vfh, vfl, gate, zgrad, cgrad, sig, xch, xcl, skip_sum,
     pick_b, pick_c) = at_hand
    rs_steps = [range(0, 1)] + [range(first, min(first + 2, rs_bits)) for first in range(1, rs_bits, 2)]
    gzh, gzl, outh, outl, part_a = early(rs_bits, nth, ntl, gh, gl, gate, zgrad, skip, xc, y)
    part_a, h = lax.optimization_barrier((part_a, h))
    part_a = reduced(part_a, range(0, 1))
    back_f = backward(0, mx, car, h, de, dx, bc, a2, decay, gy)
    part_a, back_f, h = lax.optimization_barrier((part_a, back_f, h))
    part_a = reduced(part_a, range(1, 2))
    back_r = backward(1, mx, car, h, de, dx, bc, a2, decay, gy)
    gxh, gxl, halo_g, few = inner_back(
        pad, conv_w_0, w_x_t, w_dt_0, skip, a2,
        xb, gy, xc, dt, sig, cgrad, mask, dbl, xbh, xch, xcl, skip_sum, pick_b, pick_c, *back_f, *back_r,
    )
    g_normed, part_b, *to_sides = tail(
        rs_bits, bits > rs_bits, sib, oth, gain, x, nth, ntl, wih, wil, wfh, wfl, gzh, gzl, gxh, gxl, halo_g, few
    )
    part_a, part_b = lax.optimization_barrier((part_a, part_b))
    part_a, part_b = reduced(part_a, range(2, 3)), reduced(part_b, rs_steps[0])
    part_b, g_normed = lax.optimization_barrier((part_b, g_normed))
    part_b = reduced(part_b, rs_steps[1])
    mixed, gtok = finish(x, g, gain, g_normed, outh, outl, woh, wol, vfh, vfl)
    part_b, mixed, gtok = lax.optimization_barrier((part_b, mixed, gtok))
    own = jnp.concatenate([part_a, part_b], axis=1)
    for step in rs_steps[2:]:
        own = reduced(own, step)
    for bit in range(rs_bits, bits):
        own = own + swap(own, bit)
    tall = own.shape[1]
    halo = jnp.concatenate([own[0, tall - 16 : tall - 12], own[0, tall - 8 :]], axis=0)
    if bits > rs_bits:
        pairs = [(i, i + 1) for i in range(count - 1)]
        from_left = lax.ppermute(to_sides[1], "seq", pairs)[:3]
        from_right = lax.ppermute(to_sides[0], "seq", [(j, i) for i, j in pairs])[:3]
        halo = jnp.concatenate([from_left.reshape(-1, LANE), from_right.reshape(-1, LANE)], axis=0)
    own = own[:, : tall - 8]
    gtok = close(gtok, halo, pad)
    for step in reversed(rs_steps[1:]):
        near = [exchange(own, reverse_bits(i, len(step)) << step[0]) for i in range((1 << len(step)) - 1, 0, -1)]
        near = [own] + near[::-1]
        if step is not rs_steps[1]:
            own, gtok = lax.optimization_barrier((jnp.concatenate(near, axis=0), gtok))
    far = [swap(part, 0) for part in near]
    outs = unpack(rs_bits, near + far, tokens.shape[1], a_log_t.shape, w_dt.shape[1])
    g_gain, g_w_in, g_conv_w, g_conv_b, g_w_x, g_w_dt, g_dt_bias, g_a_log, g_d_skip, g_w_out = outs
    return (
        mixed, gtok, g_gain, g_w_in[None], g_conv_w[None], g_conv_b, g_w_x.T[None], g_w_dt[None],
        g_dt_bias, g_a_log.T[None], g_d_skip, g_w_out[None],
    )


def solution(mesh):
    rows, whole = P("seq", None), P()
    return jax.shard_map(
        body,
        mesh=mesh,
        in_specs=(rows, P("seq"), P("seq")) + (whole,) * 10 + (rows,),
        out_specs=(rows, rows) + (whole,) * 10,
        check_vma=False,
    )
```

```python
import jax
import jax.numpy as jnp
from jax import lax
from jax.experimental import pallas as pl
from jax.experimental.pallas import tpu as pltpu
from jax.sharding import PartitionSpec as P

F32 = jnp.float32
BF16 = jnp.bfloat16
EPS = 1e-05
LOG2E = 1.4426950408889634
LN2 = 0.6931471805599453
BIG = 1e9
CH = 8
LANE = 128
MIB = 1024 * 1024


def nn(a, b):
    return lax.dot_general(a, b, (((1,), (0,)), ((), ())), preferred_element_type=F32)


def nt(a, b):
    return lax.dot_general(a, b, (((1,), (1,)), ((), ())), preferred_element_type=F32)


def tn(a, b):
    return lax.dot_general(a, b, (((0,), (0,)), ((), ())), preferred_element_type=F32)


def split(x):
    high = x.astype(BF16)
    return high, (x - high.astype(F32)).astype(BF16)


def split3(x):
    high = x.astype(BF16)
    rest = x - high.astype(F32)
    mid = rest.astype(BF16)
    return high, mid, (rest - mid.astype(F32)).astype(BF16)


def mm(dot, a, b):
    ah, al = a if isinstance(a, tuple) else split(a)
    bh, bl = b if isinstance(b, tuple) else split(b)
    return dot(ah, bh) + (dot(ah, bl) + dot(al, bh))


def flip_matrix(size):
    rows = lax.broadcasted_iota(jnp.int32, (size, size), 0)
    cols = lax.broadcasted_iota(jnp.int32, (size, size), 1)
    return jnp.where(rows + cols == size - 1, 1.0, 0.0).astype(BF16)


def flipped(x):
    flip = flip_matrix(x.shape[1])
    high, mid, low = split3(x)
    return nn(high, flip) + (nn(mid, flip) + nn(low, flip))


def order_matrix(length):
    steps = length // CH
    rows = lax.broadcasted_iota(jnp.int32, (length, length), 0)
    cols = lax.broadcasted_iota(jnp.int32, (length, length), 1)
    token = (rows & (CH - 1)) * steps + (rows >> 3)
    return jnp.where(cols == token, 1.0, 0.0)


def exact(dot, order, x):
    high, mid, low = split3(x)
    order = order.astype(BF16)
    return dot(order, high) + (dot(order, mid) + dot(order, low))


def ordered(ref):
    return exact(nn, order_matrix(ref.shape[0]), ref[...])


def store_ordered(ref, value):
    ref[...] = exact(tn, order_matrix(ref.shape[0]), value)


def spread(row, order=None):
    length = row.shape[1]
    picked = ((order_matrix(length) if order is None else order) * row).astype(BF16)
    return nn(picked, jnp.ones((length, LANE), BF16))


def sigmoid(x):
    return 1.0 / (1.0 + jnp.exp(-x))


def normalize(x, gain):
    factor = lax.rsqrt(jnp.mean(x * x, axis=1, keepdims=True) + EPS)
    return factor, x * factor * gain


def both_orders(normed):
    flip = flip_matrix(normed.shape[1])
    high, low = split(normed)
    return (
        jnp.concatenate([high, nn(high, flip).astype(BF16)], axis=0),
        jnp.concatenate([low, nn(low, flip).astype(BF16)], axis=0),
    )


def params(mib):
    return pltpu.CompilerParams(vmem_limit_bytes=mib * MIB)


def in_hbm(*arrays):
    return tuple(pltpu.with_memory_space_constraint(x, pltpu.HBM) for x in arrays)


def edges_kernel(*refs):
    count = (len(refs) - 3) // 2
    far, to_sib, to_oth, near, arrived = refs[:count], refs[count], refs[count + 1], refs[count + 2 : -1], refs[-1]
    copies = [pltpu.make_async_copy(one, two, arrived.at[i]) for i, (one, two) in enumerate(zip(far, near))]
    for copy in copies:
        copy.start()
    for copy in copies[:3]:
        copy.wait()
    tok, resets, pad = near[:3]
    length, feat = tok.shape
    sub = lax.broadcasted_iota(jnp.int32, (CH, length), 0)
    lane = lax.broadcasted_iota(jnp.int32, (CH, length), 1)
    real = pad[...].astype(F32)
    row = lax.broadcasted_iota(jnp.int32, (CH, feat), 0)
    flags = 1.0 - resets[...].astype(F32)
    flags = jnp.concatenate([flags, jnp.zeros((1, feat - length), F32)], axis=1)

    def message(rows, start):
        col = jnp.sum(jnp.where(lane == sub + start, real, 0.0), axis=1, keepdims=True)
        return jnp.where(row < 3, rows * col, jnp.where(row == 3, flags, 0.0))

    first = message(tok[:CH, :], 0)
    last = message(pltpu.roll(tok[length - CH :, :], 3, 0), length - 3)
    odd = (lax.axis_index("seq") & 1) == 1
    to_sib[...] = jnp.where(odd, first, last)
    to_oth[...] = jnp.where(odd, last, first)
    for copy in copies[3:]:
        copy.wait()


def edges(*arrays):
    shape = jax.ShapeDtypeStruct((CH, arrays[0].shape[1]), F32)
    found = pl.pallas_call(
        edges_kernel,
        in_specs=[pl.BlockSpec(memory_space=pl.ANY)] * len(arrays),
        out_specs=(pl.BlockSpec(memory_space=pltpu.VMEM),) * (2 + len(arrays)),
        out_shape=(shape, shape) + tuple(jax.ShapeDtypeStruct(x.shape, x.dtype) for x in arrays),
        scratch_shapes=[pltpu.SemaphoreType.DMA((len(arrays),))],
        compiler_params=params(8),
        name="edges",
    )(*in_hbm(*arrays))
    return found[0], found[1], found[2:]


def project_kernel(tok, pad, gain, w_in, gout, w_out, a_log, xb_o, z_o, go_o, gy_o, wih_o, wil_o, spread_o, a2_o):
    inner = w_out.shape[0]
    x = ordered(tok)
    normed = normalize(x, gain[...])[1]
    w_parts = split(w_in[...])
    wih_o[...], wil_o[...] = w_parts
    proj = mm(nn, both_orders(normed), w_parts)
    pad_col = spread(pad[...].astype(F32))
    pad_all = jnp.concatenate([pad_col, pad_col], axis=0)
    g = ordered(gout)
    gh, gl = both_orders(g)
    go = mm(nt, (gh, gl), split(w_out[...]))
    for lt in range(inner // LANE):
        cols = slice(lt * LANE, (lt + 1) * LANE)
        z = proj[:, inner + lt * LANE : inner + (lt + 1) * LANE]
        xb_o[:, cols] = proj[:, cols] * pad_all
        z_o[:, cols] = z
        go_o[:, cols] = go[:, cols]
        gy_o[:, cols] = go[:, cols] * (z * sigmoid(z))
    width = spread_o.shape[0] // 3
    row = lax.broadcasted_iota(jnp.int32, spread_o.shape, 0)
    entry = lax.broadcasted_iota(jnp.int32, spread_o.shape, 1) >> 7
    row = jnp.where(row >= 2 * width, row - 2 * width, jnp.where(row >= width, row - width, row))
    spread_o[...] = jnp.where(row == entry, 1.0, 0.0).astype(BF16)
    a2 = jnp.exp(a_log[...]) * (-LOG2E)
    for n in range(a2.shape[0]):
        a2_o[n] = jnp.broadcast_to(a2[n : n + 1], (CH, inner))


def project(tok, pad, gain, w_in, gout, w_out, a_log):
    big = jax.ShapeDtypeStruct((2 * tok.shape[0], w_out.shape[0]), F32)
    part = jax.ShapeDtypeStruct(w_in.shape, BF16)
    state, inner = a_log.shape
    return pl.pallas_call(
        project_kernel,
        out_shape=(
            big, big, big, big, part, part,
            jax.ShapeDtypeStruct((6 * state, 2 * state * LANE), BF16),
            jax.ShapeDtypeStruct((state, CH, inner), F32),
        ),
        compiler_params=params(8),
        name="project",
    )(tok, pad, gain, w_in, gout, w_out, a_log)


def pick_sides(from_sibling, from_other):
    odd = (lax.axis_index("seq") & 1) == 1
    left = jnp.where(odd, from_sibling, from_other)
    right = jnp.where(odd, from_other, from_sibling)
    return left, right


def rows_of(ref, first, count, cols):
    block = ref[pl.ds(pl.multiple_of(first, CH), count), cols]
    return [jnp.broadcast_to(block[n : n + 1], (CH, LANE)) for n in range(count)]


def sub_iota():
    return lax.broadcasted_iota(jnp.int32, (CH, LANE), 0)


def shifted(value, up):
    return pltpu.roll(value, 1 if up else CH - 1, 0)


def chunk_weights(total, up):
    sub = sub_iota()
    found = []
    width = total
    for reach in (1, 2, 4):
        inside = (sub >= reach) if up else (sub < CH - reach)
        found.append(jnp.where(inside, width, BIG))
        width = width + pltpu.roll(width, reach if up else CH - reach, 0)
    return found


def outside_sum(total, up):
    sub = sub_iota()
    value = jnp.where((sub >= 1) if up else (sub < CH - 1), shifted(total, up), 0.0)
    for reach in (1, 2, 4):
        inside = (sub >= reach) if up else (sub < CH - reach)
        value = value + jnp.where(inside, pltpu.roll(value, reach if up else CH - reach, 0), 0.0)
    return value


def chunk_scan(value, weights, a2, up):
    for reach, weight in zip((1, 2, 4), weights):
        value = value + jnp.exp2(weight * a2) * pltpu.roll(value, reach if up else CH - reach, 0)
    sub = sub_iota()
    enter = jnp.where((sub >= 1) if up else (sub < CH - 1), shifted(value, up), 0.0)
    leave = value[CH - 1 : CH] if up else value[0:1]
    return enter, leave


def prepare_kernel(
    sib, oth, keep, gain, wih, wil, conv_w, conv_b, w_x, w_dt, dt_bias, spread_s, a2_s, xb, gy,
    xc_o, dt_o, pre_o, conv_o, mask_o, dbl_o, xbh_o, sx_o, mx_o, sum_o, de_s, dx_s, bc_s, decay_o, drive_o,
    leave_s,
):
    inner, rank = w_x.shape[1], w_dt.shape[0]
    state = a2_s.shape[0]
    length = xb.shape[0] // 2
    steps = length // CH
    tiles = inner // LANE
    left, right = pick_sides(sib[...], oth[...])
    hn_l = normalize(left, gain[...])[1]
    hn_r = normalize(right, gain[...])[1]
    flip = flip_matrix(hn_r.shape[1])
    lh, ll = split(hn_l)
    rh, rl = split(hn_r)
    halo = (
        jnp.concatenate([lh, nn(rh, flip).astype(BF16)], axis=0),
        jnp.concatenate([ll, nn(rl, flip).astype(BF16)], axis=0),
    )
    xbh = mm(nn, halo, (wih[:, :inner], wil[:, :inner]))
    xbh_o[...] = xbh
    lane = lax.broadcasted_iota(jnp.int32, (1, length), 1)
    here = 1.0 - keep[...].astype(F32)
    before, after = left[3:4, :length], right[3:4, :length]

    def back(k):
        return jnp.where(lane < k, pltpu.roll(before, k, 1), pltpu.roll(here, k, 1))

    def ahead(k):
        return jnp.where(
            lane >= length - k,
            pltpu.roll(after, length - k, 1),
            pltpu.roll(here, length - k, 1),
        )

    f1 = here
    f2 = f1 * back(1)
    f3 = f2 * back(2)
    r1 = ahead(1)
    r2 = r1 * ahead(2)
    r3 = r2 * ahead(3)
    token_order = order_matrix(length)
    picked = [(token_order * row).astype(BF16) for row in (f1, f2, f3, r1, r2, r3)]
    mask_o[...] = nn(jnp.concatenate(picked, axis=0), jnp.ones((length, LANE), BF16))

    sub = sub_iota()

    def conv_tile(lt, carry):
        cols = pl.ds(pl.multiple_of(lt * LANE, LANE), LANE)
        xbh_t = xbh_o[:, cols]
        taps = [conv_w[k : k + 1, cols] for k in range(4)]
        bias = conv_b[:, cols]
        xf = [xb[j * CH : (j + 1) * CH, cols] for j in range(steps)]
        edge = [
            jnp.where(sub == 0, xbh_t[b : b + 1], pltpu.roll(xf[steps - 3 + b], 1, 0))
            for b in range(3)
        ]
        xf = edge + xf
        for j in range(steps):
            rows = slice(j * CH, (j + 1) * CH)
            v = bias + taps[0] * xf[j + 3]
            for k in range(1, 4):
                v = v + taps[k] * (mask_o[(k - 1) * length + j * CH : (k - 1) * length + (j + 1) * CH, :] * xf[j + 3 - k])
            conv_o[rows, cols] = v
            xc_o[rows, cols] = v * sigmoid(v)
        xr = [xb[length + j * CH : length + (j + 1) * CH, cols] for j in range(steps)]
        xr = xr + [
            jnp.where(sub == CH - 1, xbh_t[8 + b : 9 + b], pltpu.roll(xr[b], CH - 1, 0))
            for b in range(3)
        ]
        for j in range(steps):
            rows = slice(length + j * CH, length + (j + 1) * CH)
            v = bias + taps[0] * xr[j]
            for k in range(1, 4):
                v = v + taps[k] * (mask_o[(k + 2) * length + j * CH : (k + 2) * length + (j + 1) * CH, :] * xr[j + k])
            conv_o[rows, cols] = v
            xc_o[rows, cols] = v * sigmoid(v)
        return carry

    lax.fori_loop(0, tiles, conv_tile, 0)
    dbl = mm(nt, xc_o[...], w_x[...])
    dbl_o[...] = dbl
    pre_all = mm(nn, dbl[:, :rank], w_dt[...])
    bc_s[...] = nn(jnp.concatenate(split3(dbl[:, rank:]), axis=1), spread_s[...])
    for lt in range(tiles):
        cols = slice(lt * LANE, (lt + 1) * LANE)
        pre = pre_all[:, cols] + dt_bias[:, cols]
        e = jnp.exp(-jnp.abs(pre))
        u = 1.0 + e
        log1p = jnp.where(u == 1.0, e, jnp.log(u) * (e / (u - 1.0)))
        dt = jnp.maximum(pre, 0.0) + log1p
        dt_o[:, cols] = dt
        pre_o[:, cols] = pre
        dx_s[:, cols] = dt * xc_o[:, cols]
        cut = jnp.concatenate([mask_o[:length], mask_o[3 * length : 4 * length]], axis=0)
        de_s[:, cols] = dt + BIG * (1.0 - cut)

    group = 8
    cols_of = [slice(t * LANE, (t + 1) * LANE) for t in range(tiles)]
    for dirn in range(2):
        order = list(range(steps)) if dirn == 0 else list(range(steps - 1, -1, -1))
        base = dirn * length
        up = dirn == 0
        s_row, m_row = (0, 3) if dirn == 0 else (2, 1)
        totals = []
        for cols in cols_of:
            total = jnp.zeros((CH, LANE), F32)
            for j in range(steps):
                total = total + de_s[base + j * CH : base + (j + 1) * CH, cols]
            sum_o[4 * state + dirn : 4 * state + dirn + 1, cols] = jnp.sum(total, axis=0, keepdims=True)
            totals.append(total)

        def some(g, carry, order=order, base=base, up=up, dirn=dirn, s_row=s_row, m_row=m_row, totals=totals):
            n0 = g * group
            at_b, at_c = lanes_of(n0, group), lanes_of(state + n0, group)
            keys = [(n, t) for n in range(group) for t in range(tiles)]
            a2 = {(n, t): a2_s[n0 + n, :, cols_of[t]] for n, t in keys}
            h, m = {}, {}
            for at, j in enumerate(order):
                rows = slice(base + j * CH, base + (j + 1) * CH)
                de = [de_s[rows, c] for c in cols_of]
                dx = [dx_s[rows, c] for c in cols_of]
                for n in range(group):
                    b_n = bc_s[rows, at_b[n]]
                    for t, cols in enumerate(cols_of):
                        d = jnp.exp2(de[t] * a2[n, t])
                        decay_o[dirn, at, n0 + n, :, cols] = d
                        drive = dx[t] * b_n
                        drive_o[dirn, at, n0 + n, :, cols] = drive
                        h[n, t] = drive if at == 0 else d * h[n, t] + drive
            for at in range(steps - 1, -1, -1):
                rows = slice(base + order[at] * CH, base + (order[at] + 1) * CH)
                gyj = [gy[rows, c] for c in cols_of]
                for n in range(group):
                    c_n = bc_s[rows, at_c[n]]
                    for t, cols in enumerate(cols_of):
                        own = gyj[t] * c_n
                        d = decay_o[dirn, at, n0 + n, :, cols]
                        m[n, t] = d * (own if at == steps - 1 else own + m[n, t])
            for t in range(tiles):
                w_s, w_m = chunk_weights(totals[t], up), chunk_weights(totals[t], not up)
                for n in range(group):
                    enter, leave = chunk_scan(h[n, t], w_s, a2[n, t], up)
                    sx_o[dirn, n0 + n, :, cols_of[t]] = enter
                    leave_s[s_row * state + n0 + n, :, cols_of[t]] = jnp.broadcast_to(leave, (CH, LANE))
                    enter, leave = chunk_scan(m[n, t], w_m, a2[n, t], not up)
                    mx_o[dirn, n0 + n, :, cols_of[t]] = enter
                    leave_s[m_row * state + n0 + n, :, cols_of[t]] = jnp.broadcast_to(leave, (CH, LANE))
            return carry

        lax.fori_loop(0, state // group, some, 0)
    for row in range(0, 4 * state, CH):
        for cols in cols_of:
            sum_o[row : row + CH, cols] = jnp.concatenate([leave_s[row + i, 0:1, cols] for i in range(CH)], axis=0)
    sum_o[4 * state + 2 :, :] = jnp.zeros((sum_o.shape[0] - 4 * state - 2, inner), F32)


def lanes_of(first, count):
    return [pl.ds(pl.multiple_of((first + n) * LANE, LANE), LANE) for n in range(count)]


def prepare(sib, oth, keep, gain, wih, wil, conv_w, conv_b, w_x, w_dt, dt_bias, spread_s, a2, xb, gy):
    rows, inner = xb.shape
    state, width = a2.shape[0], w_x.shape[0]
    big = pltpu.VMEM((rows, inner), F32)
    edge = pltpu.VMEM((2, state, CH, inner), F32)
    return pl.pallas_call(
        prepare_kernel,
        out_shape=(
            big, big, big, big,
            pltpu.VMEM((3 * rows, LANE), F32),
            pltpu.VMEM((rows, width), F32),
            pltpu.VMEM((2 * CH, inner), F32),
            edge, edge,
            pltpu.VMEM((4 * state + 8, inner), F32),
            big, big,
            pltpu.VMEM((rows, 2 * state * LANE), F32),
            pltpu.VMEM((2, rows // 2 // CH, state, CH, inner), F32),
            pltpu.VMEM((2, rows // 2 // CH, state, CH, inner), F32),
        ),
        scratch_shapes=[pltpu.VMEM((4 * state, CH, inner), F32)],
        compiler_params=params(8),
        name="prepare",
    )(sib, oth, keep, gain, wih, wil, conv_w, conv_b, w_x, w_dt, dt_bias, spread_s, a2, xb, gy)


def summary_parts(ref_value, state):
    return [ref_value[i * state : (i + 1) * state] for i in range(4)]


def pair_kernel(a2_s, mine, theirs, out):
    state, half = a2_s.shape[0], out.shape[1]
    core = lax.axis_index("seq") & 1
    cols = pl.ds(pl.multiple_of(core * half, half), half)
    a2 = half_a2(a2_s, half)
    me, it = mine[:, cols], theirs[:, cols]
    low, high = jnp.where(core == 1, it, me), jnp.where(core == 1, me, it)
    put_total(out, joined(low, high, a2, state), state)


def joined(low, high, a2, state):
    low_f, low_r = low[4 * state : 4 * state + 1], low[4 * state + 1 : 4 * state + 2]
    high_f, high_r = high[4 * state : 4 * state + 1], high[4 * state + 1 : 4 * state + 2]
    lows, highs = summary_parts(low, state), summary_parts(high, state)
    return [
        lows[0] * jnp.exp2(high_f * a2) + highs[0],
        lows[1] * jnp.exp2(high_r * a2) + highs[1],
        highs[2] * jnp.exp2(low_r * a2) + lows[2],
        highs[3] * jnp.exp2(low_f * a2) + lows[3],
        low_f + high_f,
        low_r + high_r,
    ]


def put_total(out, parts, state):
    for i in range(4):
        out[i * state : (i + 1) * state] = parts[i]
    rest = jnp.zeros((out.shape[0] - 4 * state - 2, out.shape[1]), F32)
    out[4 * state :] = jnp.concatenate([parts[4], parts[5], rest], axis=0)


def half_a2(a2_s, half):
    core = lax.axis_index("seq") & 1
    cols = pl.ds(pl.multiple_of(core * half, half), half)
    return jnp.concatenate([a2_s[n, 0:1, cols] for n in range(a2_s.shape[0])], axis=0)


def stage_kernel(first, halves, a2_s, *refs):
    outs = 1 + len(halves) if halves else 2
    members, out, held = refs[: -outs - 1], refs[-outs - 1 : -1], refs[-1]
    count = len(members)
    state, half = a2_s.shape[0], out[0].shape[1]
    a2 = half_a2(a2_s, half)
    at = (lax.axis_index("seq") >> first) & (count - 1)
    for i, ref in enumerate(members):
        held[at ^ i] = ref[...]
    zero, none = jnp.zeros((state, half), F32), jnp.zeros((1, half), F32)

    def run_through(order, rows, reach):
        run = [zero, zero, none, none]
        seen = list(run)
        for i in order:
            seen = [jnp.where(at == i, now, old) for now, old in zip(run, seen)]
            df, dr = held[i, 4 * state : 4 * state + 1], held[i, 4 * state + 1 : 4 * state + 2]
            decays = [jnp.exp2((df, dr)[w] * a2) for w in reach]
            run = [run[k] * decays[k] + held[i, rows[k] * state : (rows[k] + 1) * state] for k in range(2)] + [
                run[2] + df,
                run[3] + dr,
            ]
        return run, seen

    right, seen = run_through(range(count), (0, 1), (0, 1))
    left, seen_left = run_through(range(count - 1, -1, -1), (2, 3), (1, 0))
    enter = out[0]
    enter[:state], enter[state : 2 * state] = seen[0], seen[1]
    enter[2 * state : 3 * state], enter[3 * state : 4 * state] = seen_left[0], seen_left[1]
    blank = jnp.zeros((CH, half), F32)
    enter[4 * state :] = jnp.concatenate([seen[2], seen[3], seen_left[2], seen_left[3], blank[:4]], axis=0)
    sums = jnp.concatenate([right[2], right[3], blank[:6]], axis=0)
    if halves:
        me = lax.axis_index("seq")
        for ref, apart in zip(out[1:], halves):
            later = (me ^ apart) > me
            ref[:state] = jnp.where(later, right[0], left[0])
            ref[state : 2 * state] = jnp.where(later, right[1], left[1])
            ref[2 * state :] = sums
    else:
        for i, value in enumerate((right[0], right[1], left[0], left[1])):
            out[1][i * state : (i + 1) * state] = value
        out[1][4 * state :] = sums


def last_kernel(first, a2_s, *refs):
    theirs, out, held = refs[:-2], refs[-2], refs[-1]
    count = len(theirs) + 1
    state, half = a2_s.shape[0], out.shape[1]
    a2 = half_a2(a2_s, half)
    at = (lax.axis_index("seq") >> first) & (count - 1)
    held[at] = jnp.zeros(held.shape[1:], F32)
    for i, ref in enumerate(theirs):
        held[at ^ (i + 1)] = ref[...]

    def run_through(order, reach, inside):
        run = [jnp.zeros((state, half), F32)] * 2
        for i in order:
            sums = held[i, 2 * state : 2 * state + 1], held[i, 2 * state + 1 : 2 * state + 2]
            for k in range(2):
                longer = run[k] * jnp.exp2(sums[reach[k]] * a2) + held[i, k * state : (k + 1) * state]
                run[k] = jnp.where(inside(i), longer, run[k])
        return run

    found = run_through(range(count - 1), (0, 1), lambda i: i < at)
    found = found + run_through(range(count - 1, 0, -1), (1, 0), lambda i: i > at)
    for i in range(4):
        out[i * state : (i + 1) * state] = found[i]


def pair(a2_s, mine, theirs):
    rows, inner = mine.shape
    return pl.pallas_call(
        pair_kernel,
        out_shape=jax.ShapeDtypeStruct((rows, inner // 2), F32),
        compiler_params=params(2),
        name="pair",
    )(a2_s, mine, theirs)


def stage(first, halves, a2_s, members):
    shape = jax.ShapeDtypeStruct(members[0].shape, F32)
    part = jax.ShapeDtypeStruct((2 * a2_s.shape[0] + CH, members[0].shape[1]), F32)
    return pl.pallas_call(
        lambda *refs: stage_kernel(first, halves, *refs),
        out_shape=(shape,) + (part,) * len(halves) if halves else (shape, shape),
        scratch_shapes=[pltpu.VMEM((len(members),) + members[0].shape, F32)],
        compiler_params=params(4),
        name="stage",
    )(a2_s, *members)


def last_stage(first, a2_s, theirs):
    return pl.pallas_call(
        lambda *refs: last_kernel(first, *refs),
        out_shape=jax.ShapeDtypeStruct((4 * a2_s.shape[0], theirs[0].shape[1]), F32),
        scratch_shapes=[pltpu.VMEM((len(theirs) + 1,) + theirs[0].shape, F32)],
        compiler_params=params(4),
        name="stage",
    )(a2_s, *theirs)


def enter_kernel(a2_s, *refs):
    stages, out = refs[:-1], refs[-1]
    state, half = a2_s.shape[0], out.shape[1]
    a2 = half_a2(a2_s, half)
    value = [stages[-1][i * state : (i + 1) * state] for i in range(4)]
    for ref in reversed(stages[:-1]):
        reach = [ref[4 * state + i : 4 * state + i + 1] for i in range(4)]
        value = [
            ref[i * state : (i + 1) * state] + value[i] * jnp.exp2(reach[w] * a2)
            for i, w in ((0, 0), (1, 1), (2, 3), (3, 2))
        ]
    for i in range(4):
        out[i * state : (i + 1) * state] = value[i]


def enter(a2_s, stages):
    half = stages[0].shape[1]
    return pl.pallas_call(
        enter_kernel,
        out_shape=jax.ShapeDtypeStruct((4 * a2_s.shape[0], half), F32),
        compiler_params=params(2),
        name="enter",
    )(a2_s, *stages)


def carry_in(car_s, a2_s, mine_half, other_half, sibling):
    state, inner = a2_s.shape[0], a2_s.shape[2]
    half = inner // 2
    odd = (lax.axis_index("seq") & 1) == 1
    a2 = jnp.concatenate([a2_s[n, 0:1, :] for n in range(state)], axis=0)
    left, right = jnp.where(odd, other_half[...], mine_half[...]), jnp.where(odd, mine_half[...], other_half[...])
    into = jnp.concatenate([left, right], axis=1)
    df, dr = sibling[4 * state : 4 * state + 1], sibling[4 * state + 1 : 4 * state + 2]
    for i, reach, through in ((0, df, odd), (1, dr, odd), (2, dr, ~odd), (3, df, ~odd)):
        rows = slice(i * state, (i + 1) * state)
        value = jnp.where(through, into[rows] * jnp.exp2(reach * a2) + sibling[rows], into[rows])
        for n in range(state):
            car_s[i * state + n] = jnp.broadcast_to(value[n : n + 1], (CH, inner))


def forward_kernel(
    mine_half, other_half, sibling, sx, de_s, dx_s, bc_s, a2_s, decay, drive,
    y_s, h_s, car_o,
    before_s,
):
    rows2, inner = de_s.shape
    length = rows2 // 2
    steps = length // CH
    tiles = inner // LANE
    state = a2_s.shape[0]
    carry_in(car_o, a2_s, mine_half, other_half, sibling)
    y_s[...] = jnp.zeros(y_s.shape, F32)
    group = 8
    cols_of = [slice(t * LANE, (t + 1) * LANE) for t in range(tiles)]
    for dirn in range(2):
        order = list(range(steps)) if dirn == 0 else list(range(steps - 1, -1, -1))
        base = dirn * length
        s_row = 0 if dirn == 0 else 2
        for cols in cols_of:
            total = jnp.zeros((CH, LANE), F32)
            for j in range(steps):
                total = total + de_s[base + j * CH : base + (j + 1) * CH, cols]
            before_s[:, cols] = outside_sum(total, dirn == 0)

        def some(g, carry, dirn=dirn, order=order, base=base, s_row=s_row):
            n0 = g * group
            at_b, at_c = lanes_of(n0, group), lanes_of(state + n0, group)
            h = {}
            for n in range(group):
                for t, cols in enumerate(cols_of):
                    into = jnp.exp2(before_s[:, cols] * a2_s[n0 + n, :, cols]) * car_o[s_row * state + n0 + n, :, cols]
                    h[n, t] = sx[dirn, n0 + n, :, cols] + into
                    h_s[dirn, 0, n0 + n, :, cols] = h[n, t]
            for at, j in enumerate(order):
                rows = slice(base + j * CH, base + (j + 1) * CH)
                dx = [dx_s[rows, c] for c in cols_of]
                y = [None] * tiles
                for n in range(group):
                    c_n = bc_s[rows, at_c[n]]
                    for t, cols in enumerate(cols_of):
                        h[n, t] = decay[dirn, at, n0 + n, :, cols] * h[n, t] + drive[dirn, at, n0 + n, :, cols]
                        h_s[dirn, at + 1, n0 + n, :, cols] = h[n, t]
                        term = h[n, t] * c_n
                        y[t] = term if n == 0 else y[t] + term
                for t, cols in enumerate(cols_of):
                    y_s[rows, cols] += y[t]
            return carry

        lax.fori_loop(0, state // group, some, 0)


def forward(mine_half, other_half, sibling, sx, de, dx, bc, a2, decay, drive):
    rows2, inner = de.shape
    state = a2.shape[0]
    steps = rows2 // 2 // CH
    return pl.pallas_call(
        forward_kernel,
        out_shape=(
            jax.ShapeDtypeStruct((rows2, inner), F32),
            jax.ShapeDtypeStruct((2, steps + 1, state, CH, inner), F32),
            jax.ShapeDtypeStruct((4 * state, CH, inner), F32),
        ),
        scratch_shapes=[pltpu.VMEM((CH, inner), F32)],
        compiler_params=params(4),
        name="forward",
    )(mine_half, other_half, sibling, sx, de, dx, bc, a2, decay, drive)


def ready_kernel(
    rank, tok, gout, gain, wih, wil, w_out, d_skip, z, go, conv, pre, xc, gy,
    x_o, g_o, nth_o, ntl_o, gh_o, gl_o, wfh_o, wfl_o, woh_o, wol_o, vfh_o, vfl_o,
    gate_o, zgrad_o, cgrad_o, sig_o, xch_o, xcl_o, skip_o, pickb_o, pickc_o,
):
    feat, inner = gain.shape[1], w_out.shape[0]
    x = ordered(tok)
    x_o[...] = x
    g = ordered(gout)
    g_o[...] = g
    high, low = both_orders(normalize(x, gain[...])[1])
    nth_o[...] = high.astype(F32).T.astype(BF16)
    ntl_o[...] = low.astype(F32).T.astype(BF16)
    gh_o[...], gl_o[...] = both_orders(g)
    flip = flip_matrix(feat)
    wfh_o[...], wfl_o[...] = nn(flip, wih[...]).astype(BF16), nn(flip, wil[...]).astype(BF16)
    high, low = split(w_out[...])
    woh_o[...], wol_o[...] = high, low
    vfh_o[...], vfl_o[...] = nn(high, flip).astype(BF16), nn(low, flip).astype(BF16)
    xch_o[...], xcl_o[...] = split(xc[...])
    for lt in range(inner // LANE):
        cols = slice(lt * LANE, (lt + 1) * LANE)
        zt, v = z[:, cols], conv[:, cols]
        s = sigmoid(zt)
        gate_o[:, cols] = zt * s
        zgrad_o[:, cols] = go[:, cols] * (s * (1.0 + zt * (1.0 - s)))
        s = sigmoid(v)
        cgrad_o[:, cols] = s * (1.0 + v * (1.0 - s))
        sig_o[:, cols] = sigmoid(pre[:, cols])
        skip_o[:, cols] = jnp.sum(gy[:, cols] * xc[:, cols], axis=0, keepdims=True)
    row = lax.broadcasted_iota(jnp.int32, pickb_o.shape, 0) >> 6
    col = lax.broadcasted_iota(jnp.int32, pickb_o.shape, 1)
    pickb_o[...] = jnp.where(col == row + rank, 1.0, 0.0).astype(BF16)
    pickc_o[...] = jnp.where(col == row + (rank + pickb_o.shape[0] // (LANE // 2)), 1.0, 0.0).astype(BF16)


def ready(rank, state, tok, gout, gain, wih, wil, w_out, d_skip, z, go, conv, pre, xc, gy):
    length, feat = tok.shape
    rows2, inner = z.shape
    f32 = lambda *dims: jax.ShapeDtypeStruct(dims, F32)
    b16 = lambda *dims: jax.ShapeDtypeStruct(dims, BF16)
    both = lambda *dims: (b16(*dims), b16(*dims))
    return pl.pallas_call(
        lambda *refs: ready_kernel(rank, *refs),
        out_shape=(f32(length, feat), f32(length, feat))
        + both(feat, rows2) + both(rows2, feat) + both(feat, 2 * inner)
        + both(inner, feat) + both(inner, feat)
        + (f32(rows2, inner),) * 4
        + both(rows2, inner) + (f32(1, inner),) + both(state * LANE // 2, LANE),
        compiler_params=params(8),
        name="ready",
    )(tok, gout, gain, wih, wil, w_out, d_skip, z, go, conv, pre, xc, gy)


def early_kernel(
    rs_bits, nth, ntl, gh, gl, gate, zgrad, d_skip, xc, y_s, gzh_o, gzl_o, outh_o, outl_o, pieces_o,
):
    y = y_s[...] + d_skip[...] * xc[...]
    gz = split(zgrad[...] * y)
    gzh_o[...], gzl_o[...] = gz
    out = split(y * gate[...])
    gw_out = mm(tn, out, (gh[...], gl[...]))
    gw_in = mm(nn, (nth[...], ntl[...]), gz)
    outh_o[...], outl_o[...] = out
    put_pieces(rs_bits, pieces_o, [(gw_in, None), (gw_out, None)])


def early(rs_bits, nth, ntl, gh, gl, gate, zgrad, d_skip, xc, y):
    feat = nth.shape[0]
    rows2, inner = xc.shape
    pieces = 1 << rs_bits
    tall = 2 * feat * inner // LANE // pieces
    gz = jax.ShapeDtypeStruct((rows2, inner), BF16)
    return pl.pallas_call(
        lambda *refs: early_kernel(rs_bits, *refs),
        out_shape=(gz, gz, gz, gz, jax.ShapeDtypeStruct((pieces, tall, LANE), F32)),
        compiler_params=params(8),
        name="early",
    )(nth, ntl, gh, gl, gate, zgrad, d_skip, xc, y)


def put_pieces(rs_bits, pieces_o, arrays, few=None):
    pieces = 1 << rs_bits
    mine = reverse_bits(lax.axis_index("seq"), rs_bits)
    for p in range(pieces):
        slot = mine ^ reverse_bits(p, rs_bits)
        at = 0
        for value, more in arrays:
            tall = value.shape[0] // pieces
            for lt in range(value.shape[1] // LANE):
                where = (slice(p * tall, (p + 1) * tall), slice(lt * LANE, (lt + 1) * LANE))
                block = value[where] if more is None else value[where] + more[where]
                pieces_o[slot, at : at + tall, :] = block
                at += tall
        if few is not None:
            tiles = few.shape[1] // LANE
            top = pieces // tiles * CH
            rest = (few.shape[0] - top) * tiles // pieces
            rb, lt = p // tiles, p % tiles
            pieces_o[slot, at : at + CH, :] = few[rb * CH : (rb + 1) * CH, lt * LANE : (lt + 1) * LANE]
            rows = []
            for v in range(rest * p, rest * (p + 1)):
                rb, lt = top + v // tiles, v % tiles
                rows.append(few[rb : rb + 1, lt * LANE : (lt + 1) * LANE])
            zeros = jnp.zeros((4, LANE), F32)
            rows = [zeros] + rows + [zeros[: 4 - rest]]
            pieces_o[slot, at + CH : at + 2 * CH, :] = jnp.concatenate(rows, axis=0)
            pieces_o[slot, at + 2 * CH : at + 3 * CH, :] = jnp.zeros((CH, LANE), F32)


def row_vectors(rows):
    return jnp.concatenate(
        [rows[b : b + 1, lt * LANE : (lt + 1) * LANE] for b in range(3) for lt in range(rows.shape[1] // LANE)],
        axis=0,
    )


def backward_kernel(
    dirn, mx, car, h_s, de_s, dx_s, bc_s, a2_s, decay, gy,
    sb_s, sa_s, accb, accc, ga_s,
    after_s,
):
    rows2, inner = de_s.shape
    length = rows2 // 2
    steps = length // CH
    tiles = inner // LANE
    state = a2_s.shape[0]
    order = list(range(steps)) if dirn == 0 else list(range(steps - 1, -1, -1))
    base = dirn * length
    m_row = 3 if dirn == 0 else 1
    group = 8
    low = lax.broadcasted_iota(jnp.int32, (CH, LANE), 1) < LANE // 2
    cols_of = [slice(t * LANE, (t + 1) * LANE) for t in range(tiles)]
    sb_s[...] = jnp.zeros(sb_s.shape, F32)
    sa_s[...] = jnp.zeros(sa_s.shape, F32)
    for cols in cols_of:
        total = jnp.zeros((CH, LANE), F32)
        for j in range(steps):
            total = total + de_s[base + j * CH : base + (j + 1) * CH, cols]
        after_s[:, cols] = outside_sum(total, dirn != 0)

    def some(g, carry):
        n0 = g * group
        at_b, at_c = lanes_of(n0, group), lanes_of(state + n0, group)
        a2, q, ga, now = {}, {}, {}, {}
        for n in range(group):
            for t, cols in enumerate(cols_of):
                a2[n, t] = a2_s[n0 + n, :, cols]
                into = jnp.exp2(after_s[:, cols] * a2[n, t]) * car[m_row * state + n0 + n, :, cols]
                q[n, t] = mx[dirn, n0 + n, :, cols] + into
                ga[n, t] = jnp.zeros((CH, LANE), F32)
                now[n, t] = h_s[dirn, steps, n0 + n, :, cols]
        for time in range(steps - 1, -1, -1):
            j = order[time]
            rows = slice(base + j * CH, base + (j + 1) * CH)
            here = slice(j * CH, (j + 1) * CH)
            de = [de_s[rows, c] for c in cols_of]
            dx = [dx_s[rows, c] for c in cols_of]
            gyj = [gy[rows, c] for c in cols_of]
            sb, sa = [None] * tiles, [None] * tiles
            sums = []
            for n in range(group):
                b_n, c_n = bc_s[rows, at_b[n]], bc_s[rows, at_c[n]]
                to_b = to_c = None
                for t, cols in enumerate(cols_of):
                    gh = gyj[t] * c_n + q[n, t]
                    term_c = gyj[t] * now[n, t]
                    term_b = gh * dx[t]
                    to_b = term_b if t == 0 else to_b + term_b
                    to_c = term_c if t == 0 else to_c + term_c
                    q[n, t] = decay[dirn, time, n0 + n, :, cols] * gh
                    now[n, t] = h_s[dirn, time, n0 + n, :, cols]
                    r = q[n, t] * now[n, t]
                    ga[n, t] = ga[n, t] + de[t] * r
                    sb[t] = gh * b_n if n == 0 else sb[t] + gh * b_n
                    sa[t] = a2[n, t] * r if n == 0 else sa[t] + a2[n, t] * r
                sums.append((to_b, to_c))
            for i, at in enumerate(lanes_of(g * (group // 2), group // 2)):
                for acc, one, two in zip((accb, accc), sums[2 * i], sums[2 * i + 1]):
                    acc[here, at] = jnp.where(low, one, two) + pltpu.roll(jnp.where(low, two, one), LANE // 2, 1)
            for t, cols in enumerate(cols_of):
                sb_s[here, cols] += sb[t]
                sa_s[here, cols] += sa[t]
        for n in range(group):
            for t, cols in enumerate(cols_of):
                ga_s[n0 + n, :, cols] = ga[n, t]
        return carry

    lax.fori_loop(0, state // group, some, 0)


def backward(dirn, mx, car, h, de, dx, bc, a2, decay, gy):
    rows2, inner = de.shape
    state = a2.shape[0]
    length = rows2 // 2
    half = jax.ShapeDtypeStruct((length, inner), F32)
    acc = jax.ShapeDtypeStruct((length, state * LANE // 2), F32)
    return pl.pallas_call(
        lambda *refs: backward_kernel(dirn, *refs),
        out_shape=(half, half, acc, acc, jax.ShapeDtypeStruct((state, CH, inner), F32)),
        scratch_shapes=[pltpu.VMEM((CH, inner), F32)],
        compiler_params=params(4),
        name="backward",
    )(mx, car, h, de, dx, bc, a2, decay, gy)


def inner_kernel(
    pad, conv_w, w_x, w_dt, d_skip, a2_s,
    xb, gy, xc, dt, sig, cgrad, mask, dbl, xbh, xch, xcl, skip_sum, pick_b, pick_c,
    sb_f, sa_f, accb_f, accc_f, ga_f, sb_r, sa_r, accb_r, accc_r, ga_r,
    gxh_o, gxl_o, halo_o, few_o,
    gp_s, gpre_s, xcg_s,
):
    inner, rank = w_x.shape[1], w_dt.shape[0]
    state = a2_s.shape[0]
    rows2 = xb.shape[0]
    length = rows2 // 2
    steps = length // CH
    tiles = inner // LANE
    sub = sub_iota()

    bias_rows = []
    for lt in range(tiles):
        cols = slice(lt * LANE, (lt + 1) * LANE)
        bias = jnp.zeros((1, LANE), F32)
        for dirn, sb, sa in ((0, sb_f, sa_f), (1, sb_r, sa_r)):
            rows = slice(dirn * length, (dirn + 1) * length)
            g_pre = (xc[rows, cols] * sb[:, cols] + LN2 * sa[:, cols]) * sig[rows, cols]
            gpre_s[rows, cols] = g_pre
            xcg_s[rows, cols] = d_skip[:, cols] * gy[rows, cols] + dt[rows, cols] * sb[:, cols]
            bias = bias + jnp.sum(g_pre, axis=0, keepdims=True)
        bias_rows.append(bias)

    b_parts = split(jnp.concatenate([accb_f[...], accb_r[...]], axis=0))
    c_parts = split(jnp.concatenate([accc_f[...], accc_r[...]], axis=0))
    g_bc = (nn(b_parts[0], pick_b[...]) + nn(b_parts[1], pick_b[...])) + (
        nn(c_parts[0], pick_c[...]) + nn(c_parts[1], pick_c[...])
    )
    gpre_parts = split(gpre_s[...])
    w_dt_parts = split(w_dt[...])
    g_rank = mm(nt, gpre_parts, w_dt_parts)
    width = rank + 2 * state
    g_dbl = jnp.concatenate([g_rank, g_bc[:, rank:width]], axis=1)
    g_dbl_parts = split(g_dbl)
    few_o[width + state : width + state + rank, :] = mm(tn, split(dbl[:, :rank]), gpre_parts)
    few_o[:width, :] = mm(tn, g_dbl_parts, (xch[...], xcl[...]))
    xcg_s[...] += mm(nn, g_dbl_parts, split(w_x[...]))

    cw_rows = [[] for _ in range(4)]
    cb_rows = []
    halo_f, halo_r = [], []
    for lt in range(tiles):
        cols = slice(lt * LANE, (lt + 1) * LANE)
        taps = [conv_w[k : k + 1, cols] for k in range(4)]
        xbh_t = xbh[:, cols]
        xf = [xb[j * CH : (j + 1) * CH, cols] for j in range(steps)]
        xf = [
            jnp.where(sub == 0, xbh_t[b : b + 1], pltpu.roll(xf[steps - 3 + b], 1, 0))
            for b in range(3)
        ] + xf
        gcw = [jnp.zeros((CH, LANE), F32) for _ in range(4)]
        gcb = jnp.zeros((CH, LANE), F32)
        grads = [None] * (steps + 3)
        for j in range(steps):
            rows = slice(j * CH, (j + 1) * CH)
            u = xcg_s[rows, cols] * cgrad[rows, cols]
            gcb = gcb + u
            for k in range(4):
                uk = u if k == 0 else u * mask[(k - 1) * length + j * CH : (k - 1) * length + (j + 1) * CH, :]
                gcw[k] = gcw[k] + uk * xf[j + 3 - k]
                add = taps[k] * uk
                at = j + 3 - k
                grads[at] = add if grads[at] is None else grads[at] + add
        for b in range(3):
            halo_f.append(grads[b][0:1])
            at = steps + b
            grads[at] = grads[at] + jnp.where(sub == CH - 1, 0.0, pltpu.roll(grads[b], CH - 1, 0))
        for j in range(steps):
            gp_s[j * CH : (j + 1) * CH, cols] = grads[j + 3]
        xr = [xb[length + j * CH : length + (j + 1) * CH, cols] for j in range(steps)]
        xr = xr + [
            jnp.where(sub == CH - 1, xbh_t[8 + b : 9 + b], pltpu.roll(xr[b], CH - 1, 0))
            for b in range(3)
        ]
        grads = [None] * (steps + 3)
        for j in range(steps):
            rows = slice(length + j * CH, length + (j + 1) * CH)
            u = xcg_s[rows, cols] * cgrad[rows, cols]
            gcb = gcb + u
            for k in range(4):
                uk = u if k == 0 else u * mask[(k + 2) * length + j * CH : (k + 2) * length + (j + 1) * CH, :]
                gcw[k] = gcw[k] + uk * xr[j + k]
                add = taps[k] * uk
                grads[j + k] = add if grads[j + k] is None else grads[j + k] + add
        for b in range(3):
            halo_r.append(grads[steps + b][CH - 1 : CH])
            grads[b] = grads[b] + jnp.where(sub == 0, 0.0, pltpu.roll(grads[steps + b], 1, 0))
        for j in range(steps):
            gp_s[length + j * CH : length + (j + 1) * CH, cols] = grads[j]
        for k in range(4):
            cw_rows[k].append(jnp.sum(gcw[k], axis=0, keepdims=True))
        cb_rows.append(jnp.sum(gcb, axis=0, keepdims=True))
    pad_col = spread(pad[...].astype(F32))
    pad_all = jnp.concatenate([pad_col, pad_col], axis=0)
    for lt in range(tiles):
        cols = slice(lt * LANE, (lt + 1) * LANE)
        gxh_o[:, cols], gxl_o[:, cols] = split(gp_s[:, cols] * pad_all)

    blank = jnp.zeros((5, inner), F32)

    def gather(found):
        return jnp.concatenate(
            [jnp.concatenate([found[lt * 3 + b] for lt in range(tiles)], axis=1) for b in range(3)]
            + [blank],
            axis=0,
        )

    halo_o[...] = jnp.concatenate([gather(halo_f), gather(halo_r)], axis=0)
    ga = jnp.concatenate(
        [jnp.sum(ga_f[n] + ga_r[n], axis=0, keepdims=True) * (a2_s[n, 0:1, :] * LN2) for n in range(state)], axis=0
    )
    few_o[width : width + state, :] = ga
    few_o[width + state + rank :, :] = jnp.concatenate(
        [jnp.concatenate(cw_rows[k], axis=1) for k in range(4)]
        + [
            jnp.concatenate(cb_rows, axis=1),
            jnp.concatenate(bias_rows, axis=1),
            skip_sum[...],
            jnp.zeros((1, inner), F32),
        ],
        axis=0,
    )


def inner_back(*arrays):
    w_x, w_dt, a2, xb = arrays[2], arrays[3], arrays[5], arrays[6]
    rows2, inner = xb.shape
    few = w_x.shape[0] + a2.shape[0] + w_dt.shape[0] + CH
    big = pltpu.VMEM((rows2, inner), F32)
    part = jax.ShapeDtypeStruct((rows2, inner), BF16)
    return pl.pallas_call(
        inner_kernel,
        out_shape=(
            part, part,
            jax.ShapeDtypeStruct((2 * CH, inner), F32),
            jax.ShapeDtypeStruct((few, inner), F32),
        ),
        scratch_shapes=[big, big, big],
        compiler_params=params(8),
        name="inner",
    )(*arrays)


def tail_kernel(
    rs_bits, sib, oth, gain, x_s, nth, ntl, wih, wil, wfh, wfl, gzh, gzl, gxh, gxl, halo, few,
    normed_o, pieces_o, *edges_o,
):
    feat = gain.shape[1]
    rows2, inner = gxh.shape
    length = rows2 // 2
    left, right = pick_sides(sib[...], oth[...])
    factor_l, hn_l = normalize(left, gain[...])
    factor_r, hn_r = normalize(right, gain[...])
    flip = flip_matrix(feat)
    lh, ll = split(hn_l)
    rh, rl = split(hn_r)
    edge = (
        jnp.concatenate([lh, nn(rh, flip).astype(BF16)], axis=0),
        jnp.concatenate([ll, nn(rl, flip).astype(BF16)], axis=0),
    )
    x = x_s[...]
    factor = normalize(x, gain[...])[0]
    gh_parts = split(halo[...])
    gw_in = mm(nn, (nth[...], ntl[...]), (gxh[...], gxl[...]))
    gw_in_halo = mm(tn, edge, gh_parts)
    w_xb = (wih[:, :inner], wil[:, :inner])
    g_normed = (
        mm(nt, (gxh[:length], gxl[:length]), w_xb)
        + mm(nt, (gzh[:length], gzl[:length]), (wih[:, inner:], wil[:, inner:]))
    ) + (
        mm(nt, (gxh[length:], gxl[length:]), (wfh[:, :inner], wfl[:, :inner]))
        + mm(nt, (gzh[length:], gzl[length:]), (wfh[:, inner:], wfl[:, inner:]))
    )
    back_h = mm(nt, gh_parts, w_xb)
    gn_l = back_h[:CH]
    gn_r = flipped(back_h[CH:])

    normed_o[...] = g_normed
    to_left = norm_back(left, factor_l, gn_l, gain[...])
    to_right = norm_back(right, factor_r, gn_r, gain[...])
    for ref, value in zip(edges_o, (to_left, to_right)):
        ref[...] = value
    three = lax.broadcasted_iota(jnp.int32, (CH, feat), 0) < 3
    g_gain = (
        jnp.sum(g_normed * (x * factor), axis=0, keepdims=True)
        + jnp.sum(jnp.where(three, gn_l * (left * factor_l) + gn_r * (right * factor_r), 0.0), axis=0, keepdims=True)
    )
    few_all = jnp.concatenate(
        [few[: few.shape[0] - CH, :], few[few.shape[0] - CH : few.shape[0] - 1, :]]
        + [jnp.concatenate([g_gain, jnp.zeros((1, inner - feat), F32)], axis=1)],
        axis=0,
    )
    put_pieces(rs_bits, pieces_o, [(gw_in, gw_in_halo)], few_all)
    pieces = 1 << rs_bits
    me = lax.axis_index("seq") & (pieces - 1)
    mine = reverse_bits(me, rs_bits)
    at = pieces_o.shape[1] - 2 * CH

    @pl.when(me < pieces - 1)
    def _():
        slot = mine ^ reverse_bits(me + 1, rs_bits)
        vectors = row_vectors(to_right)
        pieces_o[slot, at : at + 4, :] = vectors[:4]
        pieces_o[slot, at + CH : at + CH + 2, :] = vectors[4:]

    @pl.when(me > 0)
    def _():
        slot = mine ^ reverse_bits(me - 1, rs_bits)
        pieces_o[slot, at + CH + 2 : at + 2 * CH, :] = row_vectors(to_left)


def reverse_bits(value, bits):
    found = 0
    for i in range(bits):
        found = found | (((value >> i) & 1) << (bits - 1 - i))
    return found


def norm_back(x, factor, gn, gain):
    scaled = gn * gain
    return factor * scaled - x * (factor * factor * factor * jnp.mean(scaled * x, axis=1, keepdims=True))


def finish_kernel(x_s, g, gain, g_normed, outh, outl, woh, wol, vfh, vfl, mixed_o, gtok_o):
    length = x_s.shape[0]
    x = x_s[...]
    fwd = mm(nn, (outh[:length], outl[:length]), (woh[...], wol[...]))
    rev = mm(nn, (outh[length:], outl[length:]), (vfh[...], vfl[...]))
    store_ordered(mixed_o, x + (fwd + rev))
    factor = normalize(x, gain[...])[0]
    store_ordered(gtok_o, g[...] + norm_back(x, factor, g_normed[...], gain[...]))


def finish(*arrays):
    shape = jax.ShapeDtypeStruct(arrays[0].shape, F32)
    return pl.pallas_call(
        finish_kernel,
        out_shape=(shape, shape),
        compiler_params=params(6),
        name="finish",
    )(*arrays)


def tail(rs_bits, alone, *arrays):
    x, gxh = arrays[3], arrays[12]
    length, feat = x.shape
    inner = gxh.shape[1]
    pieces = 1 << rs_bits
    tall = feat * inner // LANE // pieces + 3 * CH
    return pl.pallas_call(
        lambda *refs: tail_kernel(rs_bits, *refs),
        out_shape=(
            jax.ShapeDtypeStruct((length, feat), F32),
            jax.ShapeDtypeStruct((pieces, tall, LANE), F32),
        )
        + (jax.ShapeDtypeStruct((CH, feat), F32),) * (2 if alone else 0),
        compiler_params=params(8),
        name="tail",
    )(*arrays)


def unpack_kernel(rs_bits, parts, *refs):
    sources, refs = refs[:parts], refs[parts:]
    (gain_o, w_in_o, conv_w_o, conv_b_o, w_x_o, w_dt_o, dt_bias_o, a_log_o, d_skip_o, w_out_o,
     few_s, rest_s) = refs
    feat = w_in_o.shape[0]
    inner = w_out_o.shape[0]
    tiles = inner // LANE
    pieces = 1 << rs_bits
    mine = reverse_bits(lax.axis_index("seq"), rs_bits)
    in_rows, out_rows = feat // pieces, inner // pieces
    for slot in range(pieces):
        source = sources[slot * parts // pieces]
        i = slot % (pieces // parts)
        p = reverse_bits(mine ^ slot, rs_bits)
        at = 0
        in_at = pl.ds(pl.multiple_of(p * in_rows, in_rows), in_rows)
        out_at = pl.ds(pl.multiple_of(p * out_rows, out_rows), out_rows)
        for lt in range(tiles):
            w_in_o[in_at, inner + lt * LANE : inner + (lt + 1) * LANE] = source[i, at : at + in_rows, :]
            at += in_rows
        for lt in range(feat // LANE):
            w_out_o[out_at, lt * LANE : (lt + 1) * LANE] = source[i, at : at + out_rows, :]
            at += out_rows
        for lt in range(tiles):
            w_in_o[in_at, lt * LANE : (lt + 1) * LANE] = source[i, at : at + in_rows, :]
            at += in_rows
        few_s[p] = source[i, at : at + CH, :]
        rest_s[p] = source[i, at + CH : at + 2 * CH, :]

    top = pieces // tiles * CH
    total = w_x_o.shape[0] + a_log_o.shape[0] + w_dt_o.shape[0] + CH
    rest = (total - top) * tiles // pieces

    def few_rows(first, count):
        found = []
        for lt in range(tiles):
            if first < top:
                found.append(few_s[first // CH * tiles + lt])
                continue
            rows = []
            for row in range(first, first + count):
                v = (row - top) * tiles + lt
                rows.append(rest_s[v // rest, 4 + v % rest : 5 + v % rest, :])
            found.append(jnp.concatenate(rows, axis=0) if count > 1 else rows[0])
        return jnp.concatenate(found, axis=1)

    width, state = w_x_o.shape[0], a_log_o.shape[0]
    rank = w_dt_o.shape[0]
    w_x_o[...] = jnp.concatenate([few_rows(r, CH) for r in range(0, width, CH)], axis=0)
    at = width
    a_log_o[...] = jnp.concatenate([few_rows(r, CH) for r in range(at, at + state, CH)], axis=0)
    at += state
    w_dt_o[...] = jnp.concatenate([few_rows(r, CH) for r in range(at, at + rank, CH)], axis=0)
    at += rank
    conv_w_o[...] = few_rows(at, 4)
    conv_b_o[...] = few_rows(at + 4, 1)
    dt_bias_o[...] = few_rows(at + 5, 1)
    d_skip_o[...] = few_rows(at + 6, 1)
    gain_o[...] = few_rows(at + 7, 1)[:, :feat]


def close_kernel(gtok, halo, pad, gtok_o):
    feat = gtok.shape[1]
    length = gtok.shape[0]
    per = feat // LANE
    padded = spread_plain(pad[...].astype(F32), feat)

    def three(first):
        rows = [
            jnp.concatenate([halo[first + b * per + lt : first + b * per + lt + 1, :] for lt in range(per)], axis=1)
            for b in range(3)
        ]
        return rows, jnp.zeros((CH - 3, feat), F32)

    rows, blank = three(0)
    first = jnp.concatenate(rows + [blank], axis=0)
    rows, blank = three(3 * per)
    last = jnp.concatenate([blank] + rows, axis=0)
    gtok_o[...] = gtok[...]
    gtok_o[:CH] = gtok[:CH] + padded[:CH] * first
    gtok_o[length - CH :] = gtok[length - CH :] + padded[length - CH :] * last


def close(*arrays):
    return pl.pallas_call(
        close_kernel,
        out_shape=jax.ShapeDtypeStruct(arrays[0].shape, F32),
        compiler_params=params(4),
        name="close",
    )(*arrays)


def spread_plain(row, width):
    length = row.shape[1]
    rows = lax.broadcasted_iota(jnp.int32, (length, length), 0)
    cols = lax.broadcasted_iota(jnp.int32, (length, length), 1)
    picked = (jnp.where(rows == cols, 1.0, 0.0) * row).astype(BF16)
    return nn(picked, jnp.ones((length, width), BF16))


def unpack(rs_bits, parts, feat, state, rank):
    pieces = 1 << rs_bits
    inner = state[1]
    width = rank + 2 * state[0]
    shape = lambda *dims: jax.ShapeDtypeStruct(dims, F32)
    return pl.pallas_call(
        lambda *refs: unpack_kernel(rs_bits, len(parts), *refs),
        out_shape=(
            shape(1, feat),
            shape(feat, 2 * inner),
            shape(4, inner),
            shape(1, inner),
            shape(width, inner),
            shape(rank, inner),
            shape(1, inner),
            shape(state[0], inner),
            shape(1, inner),
            shape(inner, feat),
        ),
        scratch_shapes=[pltpu.VMEM((pieces, CH, LANE), F32)] * 2,
        compiler_params=params(6),
        name="unpack",
    )(*parts)


def body(tokens, resets, pad_mask, norm_gain, w_in, conv_w, conv_b, w_x, w_dt, dt_bias, a_log, d_skip, w_out, grad_out):
    count = lax.axis_size("seq")
    bits = count.bit_length() - 1
    rs_bits = min(5, bits)
    length = tokens.shape[0]
    keep_row, pad_row = resets.reshape(1, length), pad_mask.reshape(1, length)

    def exchange(value, apart):
        return lax.ppermute(value, "seq", [(i, i ^ apart) for i in range(count)])

    def swap(value, bit):
        return exchange(value, 1 << bit)

    across = [(i, i + 1) for i in range(1, count - 1, 2)] + [(i + 1, i) for i in range(1, count - 1, 2)]

    def swap_across(value):
        return lax.ppermute(value, "seq", across)

    to_sib, to_oth, kept = edges(
        tokens, keep_row, pad_row, norm_gain, w_in[0], grad_out, w_out[0],
        conv_w[0], conv_b, w_x[0].T, w_dt[0], dt_bias, a_log[0].T, d_skip,
    )
    (tok, keep, pad, gain, w_in_0, gout, w_out_0, conv_w_0, conv_b_0, w_x_t, w_dt_0, dt_bias_0, a_log_t, skip) = kept
    oth = swap_across(to_oth)
    sib = swap(to_sib, 0)
    xb, z, go, gy, wih, wil, spread_s, a2 = project(tok, pad, gain, w_in_0, gout, w_out_0, a_log_t)
    xc, dt, pre, conv, mask, dbl, xbh, sx, mx, total, de, dx, bc, decay, drive = prepare(
        sib, oth, keep, gain, wih, wil, conv_w_0, conv_b_0, w_x_t, w_dt_0, dt_bias_0, spread_s, a2, xb, gy
    )

    sibling = swap(total, 0)
    group = pair(a2, total, sibling)
    group, gate_in = lax.optimization_barrier((group, (z, go, conv, pre, xc, gy)))
    at_hand = ready(w_dt.shape[1], a_log.shape[2], tok, gout, gain, wih, wil, w_out_0, skip, *gate_in)
    stages = []
    steps = [range(first, min(first + 2, bits)) for first in range(1, bits, 2)]
    step = steps[-1]
    distances = [i << step[0] for i in range(1, 1 << len(step))]
    for first_step in steps[:-1]:
        members = [group] + [exchange(group, i << first_step[0]) for i in range(1, 1 << len(first_step))]
        halves = distances if first_step is steps[-2] else ()
        entering, *group = stage(first_step[0], halves, a2, members)
        stages.append(entering)
        if not halves:
            (group,) = group
    group, at_hand = lax.optimization_barrier((group, at_hand))
    theirs = [exchange(value, apart) for value, apart in zip(group, distances)]
    stages.append(last_stage(step[0], a2, theirs))
    mine_half = enter(a2, stages)
    other_half = swap(mine_half, 0)

    y, h, car = forward(mine_half, other_half, sibling, sx, de, dx, bc, a2, decay, drive)
    def reduced(part, step):
        size = part.shape[0] >> len(step)
        total = part[:size]
        for i in ((2, 3, 1) if len(step) == 2 else (1,)):
            slot = reverse_bits(i, len(step))
            total = total + exchange(part[slot * size : (slot + 1) * size], i << step[0])
        return total

    (x, g, nth, ntl, gh, gl, wfh, wfl, woh, wol, vfh, vfl, gate, zgrad, cgrad, sig, xch, xcl, skip_sum,
     pick_b, pick_c) = at_hand
    rs_steps = [range(0, 1)] + [range(first, min(first + 2, rs_bits)) for first in range(1, rs_bits, 2)]
    gzh, gzl, outh, outl, part_a = early(rs_bits, nth, ntl, gh, gl, gate, zgrad, skip, xc, y)
    part_a, h = lax.optimization_barrier((part_a, h))
    part_a = reduced(part_a, range(0, 1))
    back_f = backward(0, mx, car, h, de, dx, bc, a2, decay, gy)
    part_a, back_f, h = lax.optimization_barrier((part_a, back_f, h))
    part_a = reduced(part_a, range(1, 2))
    back_r = backward(1, mx, car, h, de, dx, bc, a2, decay, gy)
    gxh, gxl, halo_g, few = inner_back(
        pad, conv_w_0, w_x_t, w_dt_0, skip, a2,
        xb, gy, xc, dt, sig, cgrad, mask, dbl, xbh, xch, xcl, skip_sum, pick_b, pick_c, *back_f, *back_r,
    )
    g_normed, part_b, *to_sides = tail(
        rs_bits, bits > rs_bits, sib, oth, gain, x, nth, ntl, wih, wil, wfh, wfl, gzh, gzl, gxh, gxl, halo_g, few
    )
    part_a, part_b = lax.optimization_barrier((part_a, part_b))
    part_a, part_b = reduced(part_a, range(2, 3)), reduced(part_b, rs_steps[0])
    part_b, g_normed = lax.optimization_barrier((part_b, g_normed))
    part_b = reduced(part_b, rs_steps[1])
    mixed, gtok = finish(x, g, gain, g_normed, outh, outl, woh, wol, vfh, vfl)
    part_b, mixed, gtok = lax.optimization_barrier((part_b, mixed, gtok))
    own = jnp.concatenate([part_a, part_b], axis=1)
    for step in rs_steps[2:]:
        own = reduced(own, step)
    for bit in range(rs_bits, bits):
        own = own + swap(own, bit)
    tall = own.shape[1]
    halo = jnp.concatenate([own[0, tall - 16 : tall - 12], own[0, tall - 8 :]], axis=0)
    if bits > rs_bits:
        pairs = [(i, i + 1) for i in range(count - 1)]
        from_left = lax.ppermute(to_sides[1], "seq", pairs)[:3]
        from_right = lax.ppermute(to_sides[0], "seq", [(j, i) for i, j in pairs])[:3]
        halo = jnp.concatenate([from_left.reshape(-1, LANE), from_right.reshape(-1, LANE)], axis=0)
    own = own[:, : tall - 8]
    gtok = close(gtok, halo, pad)
    for step in reversed(rs_steps[1:]):
        near = [exchange(own, reverse_bits(i, len(step)) << step[0]) for i in range((1 << len(step)) - 1, 0, -1)]
        near = [own] + near[::-1]
        if step is not rs_steps[1]:
            own, gtok = lax.optimization_barrier((jnp.concatenate(near, axis=0), gtok))
    far = [swap(part, 0) for part in near]
    outs = unpack(rs_bits, near + far, tokens.shape[1], a_log_t.shape, w_dt.shape[1])
    g_gain, g_w_in, g_conv_w, g_conv_b, g_w_x, g_w_dt, g_dt_bias, g_a_log, g_d_skip, g_w_out = outs
    return (
        mixed, gtok, g_gain, g_w_in[None], g_conv_w[None], g_conv_b, g_w_x.T[None], g_w_dt[None],
        g_dt_bias, g_a_log.T[None], g_d_skip, g_w_out[None],
    )


def solution(mesh):
    rows, whole = P("seq", None), P()
    return jax.shard_map(
        body,
        mesh=mesh,
        in_specs=(rows, P("seq"), P("seq")) + (whole,) * 10 + (rows,),
        out_specs=(rows, rows) + (whole,) * 10,
        check_vma=False,
    )
```
